32 devices in a mesh: batch: 16 (over z, y, core), pix: 2 (over x).
Axes of the slice: x: 2, y: 2, z: 4, core: 2. Of those that a mesh axis runs over, the one named last changes fastest.
Arguments:
- images: bfloat16 [16, 32, 32, 384], P('batch', 'pix'), may hold values from -6 to 6
- target: bfloat16 [16, 16, 16, 576], P('batch', 'pix'), may hold values from -6 to 6
- clean_images: bfloat16 [16, 16, 16, 576], P('batch', 'pix'), may hold values from -6 to 6
- levels: int32 [16], P('batch'), may hold values from 0 to 39
- labels: int32 [16], P('batch'), may hold values from 0 to 999
- null_mask: int32 [16], P('batch'), may hold values 0 or 1
- vgg_proj: bfloat16 [576, 256], replicated, may hold values from -0.25 to 0.25
- lpips_lin: float32 [256], replicated, may hold values from 0.1 to 1
- master: float32 [6598656], P(('batch', 'pix')), may hold values from -2 to 2.16
- first_moment: float32 [6598656], P(('batch', 'pix')), may hold values from -1.73039e-05 to 1.73039e-05
- second_moment: float32 [6598656], P(('batch', 'pix')), may hold values from 1.5169756e-14 to 6.0679023e-12
Outputs:
- new_master: float32 [6598656], P(('batch', 'pix'))
- new_first: float32 [6598656], P(('batch', 'pix'))
- new_second: float32 [6598656], P(('batch', 'pix'))
- master_copy: bfloat16 [6598656], P(('batch', 'pix'))
- norm_before: float32 [], replicated
- level_sums: float32 [2, 40], replicated
The draws below stay inside these ranges and needn't reach their ends.
All inputs are finite; a program needn't handle non-finite values. No bound on the sum of `null_mask` on one device may be relied on, other than what follows from the above.
Results may differ from the reference program's by a relative error of at most 0.0072.
Values may be sent and summed in bfloat16 or wider, within the bound.
A program may use at most 192 MiB of HBM per device.

```python
import math
import jax
import jax.numpy as jnp
import numpy as np
from jax import lax

RES = 32
RES2 = 16
CH = 384
CH2 = 576
GROUPS = 32
HEADS = 6
HEAD = 64
TEMB = 768
CLASSES = 1000
FEAT = 256
LEVELS = 40
STEP = 10
IMAGES = 16
PARAMS = 6598656


CLIP_LEVEL = 0.01


def segment_ends():
    sizes_list = [9 * CH * CH, 9 * CH * CH, 3 * CH * CH, CH * CH, 9 * CH * CH2, TEMB * 2 * CH, (CLASSES + 1) * TEMB, 6 * CH]
    ends = []
    running = 0
    for piece in sizes_list:
        running += piece
        ends.append(running)
    return ends


def kind_factor(position, ends):
    return jnp.where((position >= ends[6]) & (position < ends[7]), 10.0, 1.0).astype(jnp.float32)


def signed_noise(key, spread_value):
    return jax.random.truncated_normal(key, -4.0, 4.0, (PARAMS,), jnp.float32) * spread_value


def draw_master(key, part):
    key = jax.random.fold_in(key, 11)
    position = jnp.arange(PARAMS, dtype=jnp.int32)
    ends = segment_ends()
    spreads = [(9 * CH) ** (-0.5), (9 * CH) ** (-0.5), CH ** (-0.5), 4.0 * CH ** (-0.5), (9 * CH) ** (-0.5), TEMB ** (-0.5), TEMB ** (-0.5), 0.3, 0.02]
    spread = jnp.full((PARAMS,), spreads[-1], jnp.float32)
    for index_pos in reversed(range(8)):
        spread = jnp.where(position < ends[index_pos], spreads[index_pos], spread)
    values = signed_noise(key, 1.0) * spread
    offset = jnp.maximum(position - ends[6], 0)
    in_norms = (position >= ends[6]) & (position < ends[7])
    row_even = offset // CH % 2 == 0
    column_share = (offset % CH).astype(jnp.float32) / CH
    is_gain = in_norms & row_even
    rise = 0.6 + 1.2 * column_share
    gain_noise = jax.random.uniform(jax.random.fold_in(key, 1), (PARAMS,), jnp.float32, 0.8, 1.2)
    return jnp.where(is_gain, rise * gain_noise, values)


def draw_first_moment(key, part):
    key = jax.random.fold_in(key, 12)
    position = jnp.arange(PARAMS, dtype=jnp.int32)
    entry = CLIP_LEVEL / PARAMS ** 0.5 * kind_factor(position, segment_ends())
    return signed_noise(key, 0.1111) * entry


def draw_second_moment(key, part):
    key = jax.random.fold_in(key, 13)
    position = jnp.arange(PARAMS, dtype=jnp.int32)
    entry = CLIP_LEVEL / PARAMS ** 0.5 * kind_factor(position, segment_ends())
    factor = jax.random.uniform(key, (PARAMS,), jnp.float32, 1.0, 4.0)
    return 0.001001 * entry * entry * factor


def touch_ends(entries, key, smallest, largest):
    shape = entries.shape
    index_at = [jax.random.randint(jax.random.fold_in(key, axis), (), 0, shape[axis]) for axis in range(len(shape))]
    entries = entries.at[tuple(index_at)].set(smallest)
    longest = shape.index(max(shape))
    index_at[longest] = (index_at[longest] + 1) % shape[longest]
    return entries.at[tuple(index_at)].set(largest)


def block_scale(key, extent, cuts, smallest, high):
    factor_of, own = 1.0, jax.random.fold_in(key, 6)
    for dim, parts in cuts:
        steps = jnp.exp(jax.random.uniform(jax.random.fold_in(own, dim), (parts,), jnp.float32, smallest / len(cuts), high / len(cuts)))
        factor_of = factor_of * jnp.repeat(steps, extent[dim] // parts).reshape([-1 if axis == dim else 1 for axis in range(len(extent))])
    return factor_of


def rank_bounds(number_of, skew):
    portions = [(1 << 20) // math.isqrt(standing ** skew) + 1 for standing in range(1, number_of + 1)]
    scale = 1 + sum(portions) // (1 << 30)
    return np.cumsum(np.array([max(1, weight // scale) for weight in portions]))


def ranked(key, extent, amount, skew):
    table = rank_bounds(amount, skew)
    pick = jax.random.randint(jax.random.fold_in(key, 1), extent, 0, int(table[amount - 1]))
    standing = jnp.searchsorted(jnp.asarray(table, jnp.int32), pick, side="right")
    return jax.random.permutation(jax.random.fold_in(key, 2), amount)[standing].astype(jnp.int32)


def noise(stream_key, shape, deviation, limit, shards=(), held_as=jnp.bfloat16):
    loudness = block_scale(stream_key, shape, shards, -0.22, 0.18) if shards else 1.0
    entries = jax.random.normal(stream_key, shape, jnp.float32) * deviation * loudness
    return jnp.minimum(jnp.maximum(entries, -limit), limit).astype(held_as)


def setup_inputs(seed: int = 0) -> dict:
    key_of = jax.random.split(jax.random.key(seed), 12)
    images = noise(key_of[0], (IMAGES, RES, RES, CH), 1.0, 6.0, ((0, 16), (1, 2)))
    target = noise(key_of[1], (IMAGES, RES2, RES2, CH2), 1.0, 6.0, ((0, 16), (1, 2)))
    clean_images = noise(key_of[2], (IMAGES, RES2, RES2, CH2), 1.0, 6.0, ((0, 16), (1, 2)))
    levels = touch_ends(jax.random.randint(key_of[3], (IMAGES,), 0, LEVELS), jax.random.fold_in(key_of[3], 1), 0, LEVELS - 1).astype(jnp.int32)
    labels = touch_ends(ranked(key_of[4], (IMAGES,), CLASSES, 2), jax.random.fold_in(key_of[4], 3), 0, CLASSES - 1).astype(jnp.int32)
    null_mask = touch_ends((jax.random.randint(key_of[5], (IMAGES,), 0, 10) < 1).astype(jnp.int32), jax.random.fold_in(key_of[5], 1), 0, 1)
    vgg_proj = noise(key_of[6], (CH2, FEAT), CH2 ** -0.5, 0.25)
    lpips_lin = jnp.clip(jnp.exp(jax.random.uniform(key_of[7], (FEAT,), jnp.float32, math.log(0.1), math.log(1.0))), 0.1, 1.0)
    master = draw_master(jax.random.fold_in(key_of[11], 71), 0)
    first_moment = draw_first_moment(jax.random.fold_in(key_of[11], 71), 0)
    second_moment = draw_second_moment(jax.random.fold_in(key_of[11], 71), 0)
    return {"images": images, "target": target, "clean_images": clean_images, "levels": levels, "labels": labels, "null_mask": null_mask, "vgg_proj": vgg_proj, "lpips_lin": lpips_lin, "master": master, "first_moment": first_moment, "second_moment": second_moment}


@jax.custom_vjp
def low(v):
    return lax.optimization_barrier(v.astype(jnp.bfloat16)).astype(jnp.float32)

@jax.custom_vjp
def low_back(v):
    return v

def low_keep(v):
    return (low(v), None)

def low_pass(kept, grad):
    return (grad,)

def back_keep(v):
    return (v, None)

def back_low(kept, grad):
    return (low(grad),)
low.defvjp(low_keep, low_pass)
low_back.defvjp(back_keep, back_low)
EPS_NORM = 1e-05
EPS_FEAT = 1e-06
BETA_ONE = 0.9
BETA_TWO = 0.999
EPS_ADAM = 1e-08
RATE = 0.02
DECAY = 0.01
CLIP = 0.01
precise = lax.Precision.HIGHEST

def unpack(flat_vec):
    layout = [(9 * CH, CH), (9 * CH, CH), (CH, 3 * CH), (CH, CH), (9 * CH, CH2), (TEMB, 2 * CH), (CLASSES + 1, TEMB), (6, CH)]
    pieces = []
    offset = 0
    for rows_n, cols_n in layout:
        pieces.append(flat_vec[offset:offset + rows_n * cols_n].reshape(rows_n, cols_n))
        offset += rows_n * cols_n
    return pieces

def time_vector(level_ids):
    half_width = TEMB // 2
    frequency = jnp.exp(-math.log(10000.0) * jnp.arange(half_width, dtype=jnp.float32) / half_width)
    angles = level_ids.astype(jnp.float32)[..., None] * (1000.0 / LEVELS) * frequency
    return jnp.concatenate([jnp.cos(angles), jnp.sin(angles)], -1)

def group_norm(values, gain_row, biases):
    pixel_n, chan_n = values.shape
    grouped = values.reshape(pixel_n, GROUPS, chan_n // GROUPS)
    center = lax.optimization_barrier(jnp.mean(grouped, axis=(0, 2), keepdims=True))
    spread = lax.optimization_barrier(jnp.mean((grouped - center) ** 2, axis=(0, 2), keepdims=True))
    normed = ((grouped - center) * lax.rsqrt(spread + EPS_NORM)).reshape(values.shape)
    return normed * gain_row + biases

def conv_same(values, weight, stride):
    side_in = values.shape[0]
    side_out = side_in // stride
    span = stride * (side_out - 1) + 1
    padded = jnp.pad(values, ((1, 1), (1, 1), (0, 0)))
    columns = jnp.concatenate([padded[row_off:row_off + span:stride, col_off:col_off + span:stride, :] for row_off in range(3) for col_off in range(3)], -1)
    return jnp.dot(columns.reshape(side_out * side_out, -1), weight, precision=precise)

def res_block(values, side, w_a, w_b, gain_rows, scale, shift):
    chan_n = values.shape[1]
    act = low(jax.nn.silu(group_norm(values, gain_rows[0], gain_rows[1])))
    inner = low_back(conv_same(act.reshape(side, side, chan_n), w_a, 1))
    modulated = group_norm(inner, gain_rows[2], gain_rows[3]) * (1.0 + scale) + shift
    second = low(jax.nn.silu(modulated))
    return values + low_back(conv_same(second.reshape(side, side, chan_n), w_b, 1))

def unit_rows(feature):
    return feature * lax.rsqrt(lax.optimization_barrier(jnp.mean(feature * feature, -1, keepdims=True)) + EPS_FEAT)

def image_loss(pieces, picture, target, clean_img, level_id, label_id, unlabeled, zero_count, vgg_proj, lpips_lin):
    w_one, w_two, w_qkv, w_proj, w_down, w_emb, class_table, gains_one = pieces
    row_index = jnp.where(unlabeled == 1, CLASSES, label_id)
    embedded = jax.nn.silu(time_vector(level_id) + class_table[row_index])
    scale_shift = jnp.dot(embedded, w_emb, precision=precise)
    middle = res_block(picture.reshape(RES * RES, CH), RES, w_one, w_two, gains_one[:4], scale_shift[:CH], scale_shift[CH:2 * CH])
    attn_in = low(group_norm(middle, gains_one[4], gains_one[5]))
    triples = low_back(low(jnp.dot(attn_in, w_qkv, precision=precise)))
    triples = triples.reshape(RES * RES, HEADS, 3, HEAD).transpose(2, 1, 0, 3)
    scores = low_back(jnp.einsum('hqd,hkd->hqk', triples[0], triples[1], precision=precise) / math.sqrt(HEAD))
    attn_probs = low(jax.nn.softmax(scores, axis=-1))
    attended = jnp.einsum('hqk,hkd->hqd', attn_probs, triples[2], precision=precise)
    attended = low_back(low(attended.transpose(1, 0, 2).reshape(RES * RES, CH)))
    output = middle + low_back(jnp.dot(attended, w_proj, precision=precise))
    final_out = low_back(conv_same(low(output).reshape(RES, RES, CH), w_down, 2))
    online_feat = unit_rows(low_back(jnp.dot(low(final_out), vgg_proj, precision=precise)))
    target_feat = unit_rows(jnp.dot(target.reshape(RES2 * RES2, CH2), vgg_proj, precision=precise))
    consist = jnp.mean(lax.optimization_barrier(jnp.sum(lpips_lin * (online_feat - target_feat) ** 2, -1))) / FEAT
    denoise = jnp.mean((final_out - clean_img.reshape(RES2 * RES2, CH2)) ** 2)
    loss_term = consist / IMAGES + jnp.where(level_id == 0, denoise, 0.0) / jnp.maximum(zero_count, 1.0)
    return (loss_term, consist)

def reference(images, target, clean_images, levels, labels, null_mask, vgg_proj, lpips_lin, master, first_moment, second_moment):
    rounded = lax.optimization_barrier(master.astype(jnp.bfloat16)).astype(jnp.float32)
    pictures = images.astype(jnp.float32)
    targets = target.astype(jnp.float32)
    cleans = clean_images.astype(jnp.float32)
    vgg_wide = vgg_proj.astype(jnp.float32)
    zero_count = jnp.sum((levels == 0).astype(jnp.float32))
    checked = jax.checkpoint(image_loss)

    def total_loss(flat_vec):
        pieces = unpack(flat_vec)

        def one_image(running, bundle):
            loss_term, consist = checked(pieces, *bundle, zero_count, vgg_wide, lpips_lin)
            return (running + loss_term, consist)
        return lax.scan(one_image, jnp.zeros((), jnp.float32), (pictures, targets, cleans, levels, labels, null_mask))
    loss_sum, pullback, consists = jax.vjp(total_loss, rounded, has_aux=True)
    gradient, = pullback(jnp.ones((), jnp.float32))
    norm_before = jnp.sqrt(jnp.sum(gradient * gradient))
    clipped = gradient * jnp.minimum(1.0, CLIP / norm_before)
    new_first = BETA_ONE * first_moment + (1.0 - BETA_ONE) * clipped
    new_second = BETA_TWO * second_moment + (1.0 - BETA_TWO) * clipped * clipped
    fixed_first = new_first / (1.0 - BETA_ONE ** STEP)
    fixed_second = new_second / (1.0 - BETA_TWO ** STEP)
    new_master = master - RATE * (fixed_first / (jnp.sqrt(fixed_second) + EPS_ADAM) + DECAY * master)
    level_hot = (levels[:, None] == jnp.arange(LEVELS, dtype=jnp.int32)[None, :]).astype(jnp.float32)
    level_sums = jnp.stack([lax.optimization_barrier(jnp.sum(consists[:, None] * level_hot, 0)), lax.optimization_barrier(jnp.sum(level_hot, 0))])
    return (new_master, new_first, new_second, new_master.astype(jnp.bfloat16), norm_before, level_sums)
```

```python
import functools
import math

import jax
import jax.numpy as jnp
from jax import lax
from jax.experimental import pallas as pl
from jax.experimental.pallas import tpu as pltpu
from jax.sharding import PartitionSpec as P

CH = 384
CH2 = 576
GROUPS = 32
HEAD = 64
TEMB = 768
CLASSES = 1000
LEVELS = 40
STEP = 10


EPS_NORM = 1e-05
EPS_FEAT = 1e-06
BETA_ONE = 0.9
BETA_TWO = 0.999
EPS_ADAM = 1e-08
RATE = 0.02
DECAY = 0.01
CLIP = 0.01
precise = lax.Precision.HIGHEST


def extended(shard, sides, width):
    for axis, dim in sides:
        size, length = (lax.axis_size(axis), shard.shape[dim])
        up = [(i, (i + 1) % size) for i in range(size - 1)]
        down = [(j, i) for i, j in up]
        last = lax.slice_in_dim(shard, length - width, length, axis=dim)
        initial = lax.slice_in_dim(shard, 0, width, axis=dim)
        before = lax.ppermute(last, axis, up)
        after = lax.ppermute(initial, axis, down)
        shard = jnp.concatenate([before, shard, after], axis=dim)
    return shard


def unpack(flat_vec):
    layout = [
        (9 * CH, CH),
        (9 * CH, CH),
        (CH, 3 * CH),
        (CH, CH),
        (9 * CH, CH2),
        (TEMB, 2 * CH),
        (CLASSES + 1, TEMB),
        (6, CH),
    ]
    pieces = []
    offset = 0
    for rows_n, cols_n in layout:
        pieces.append(flat_vec[offset : offset + rows_n * cols_n].reshape(rows_n, cols_n))
        offset += rows_n * cols_n
    return (pieces, offset)


def time_vector(level_ids):
    half_width = TEMB // 2
    frequency = jnp.exp(-math.log(10000.0) * jnp.arange(half_width, dtype=jnp.float32) / half_width)
    angles = level_ids.astype(jnp.float32)[..., None] * (1000.0 / LEVELS) * frequency
    return jnp.concatenate([jnp.cos(angles), jnp.sin(angles)], -1)


def silu_slope(values):
    sigmoid = jax.nn.sigmoid(values)
    return sigmoid * (1.0 + values * (1.0 - sigmoid))


def pix_sums(pair_sums):
    return lax.psum((pair_sums[0], pair_sums[1]), "pix")


def group_forward(values, pixels_all):
    grouped = values.reshape(values.shape[0], values.shape[1], GROUPS, -1)
    totals = pix_sums((jnp.sum(grouped, (1, 3)), jnp.sum(grouped * grouped, (1, 3))))
    per_group = pixels_all * grouped.shape[3]
    center = totals[0] / per_group
    spread = totals[1] / per_group - center * center
    inverse = lax.rsqrt(spread + EPS_NORM)
    normed = (grouped - center[:, None, :, None]) * inverse[:, None, :, None]
    return (normed.reshape(values.shape), inverse)


def group_backward(grad_normed, normed, inverse, pixels_all):
    grad_grouped = grad_normed.reshape(normed.shape[0], normed.shape[1], GROUPS, -1)
    val_grouped = normed.reshape(grad_grouped.shape)
    totals = pix_sums((jnp.sum(grad_grouped, (1, 3)), jnp.sum(grad_grouped * val_grouped, (1, 3))))
    per_group = pixels_all * grad_grouped.shape[3]
    result = (
        grad_grouped
        - (totals[0] / per_group)[:, None, :, None]
        - val_grouped * (totals[1] / per_group)[:, None, :, None]
    )
    return (result * inverse[:, None, :, None]).reshape(normed.shape)


def columns_of(values, stride):
    rows_out = values.shape[1] // stride
    cols_out = values.shape[2] // stride
    span_rows = stride * (rows_out - 1) + 1
    span_cols = stride * (cols_out - 1) + 1
    padded = extended(values, (("pix", 1),), 1)
    padded = jnp.pad(padded, ((0, 0), (0, 0), (1, 1), (0, 0)))
    return jnp.concatenate(
        [
            padded[
                :, row_off : row_off + span_rows : stride, col_off : col_off + span_cols : stride, :
            ]
            for row_off in range(3)
            for col_off in range(3)
        ],
        -1,
    )


def conv_forward(values, weight, rows_in, stride):
    n_img, pixels_in, in_chan = values.shape
    columns = columns_of(values.reshape(n_img, rows_in, -1, in_chan), stride)
    result = jnp.dot(columns.reshape(-1, 9 * in_chan), weight, preferred_element_type=jnp.float32)
    return (result.reshape(n_img, -1, weight.shape[1]), columns)


def conv_back(columns, grad_low, weight, rows_in, stride):
    n_img, pix_out, out_chan = grad_low.shape
    in_chan = weight.shape[0] // 9
    d_weight = jnp.einsum(
        "rk,rc->kc",
        columns.reshape(-1, 9 * in_chan),
        grad_low.reshape(-1, out_chan),
        preferred_element_type=jnp.float32,
    )
    flipped = (
        weight.reshape(3, 3, in_chan, out_chan)[::-1, ::-1]
        .transpose(0, 1, 3, 2)
        .reshape(9 * out_chan, in_chan)
    )
    rows_out = rows_in // stride
    grid_grad = grad_low.reshape(n_img, rows_out, pix_out // rows_out, out_chan)
    if stride > 1:
        grid_grad = jnp.pad(
            grid_grad[:, :, None, :, None, :],
            ((0, 0), (0, 0), (0, stride - 1), (0, 0), (0, stride - 1), (0, 0)),
        )
        grid_grad = grid_grad.reshape(n_img, rows_in, -1, out_chan)
    grad_columns = columns_of(grid_grad, 1)
    grad_input = jnp.dot(
        grad_columns.reshape(-1, 9 * out_chan), flipped, preferred_element_type=jnp.float32
    )
    return (d_weight, grad_input.reshape(n_img, -1, in_chan))


def res_forward(values, gain_rows, scale, shift, w_first, w_second, rows_in, pixels_all):
    normed_a, inverse_a = group_forward(values, pixels_all)
    pre_a = normed_a * gain_rows[0] + gain_rows[1]
    act_a = jax.nn.silu(pre_a).astype(jnp.bfloat16)
    inner, columns_a = conv_forward(act_a, w_first, rows_in, 1)
    normed_b, inverse_b = group_forward(inner, pixels_all)
    affine_b = normed_b * gain_rows[2] + gain_rows[3]
    pre_b = affine_b * (1.0 + scale) + shift
    second = jax.nn.silu(pre_b).astype(jnp.bfloat16)
    branch, columns_b = conv_forward(second, w_second, rows_in, 1)
    kept_state = (
        normed_a,
        inverse_a,
        pre_a,
        columns_a,
        normed_b,
        inverse_b,
        affine_b,
        pre_b,
        columns_b,
    )
    return (values + branch, kept_state)


def res_back(grad_result, kept_state, gain_rows, scale, w_first, w_second, rows_in, pixels_all):
    normed_a, inverse_a, pre_a, columns_a, normed_b, inverse_b, affine_b, pre_b, columns_b = (
        kept_state
    )
    d_w_second, grad_second = conv_back(
        columns_b, grad_result.astype(jnp.bfloat16), w_second, rows_in, 1
    )
    grad_pre_b = grad_second * silu_slope(pre_b)
    d_scale = jnp.sum(grad_pre_b * affine_b, 1)
    d_shift = jnp.sum(grad_pre_b, 1)
    grad_affine = grad_pre_b * (1.0 + scale)
    d_gain_b = jnp.sum(grad_affine * normed_b, (0, 1))
    d_bias_b = jnp.sum(grad_affine, (0, 1))
    grad_inner = group_backward(grad_affine * gain_rows[2], normed_b, inverse_b, pixels_all).astype(
        jnp.bfloat16
    )
    d_w_first, grad_act = conv_back(columns_a, grad_inner, w_first, rows_in, 1)
    grad_pre_a = grad_act * silu_slope(pre_a)
    d_gain_a = jnp.sum(grad_pre_a * normed_a, (0, 1))
    d_bias_a = jnp.sum(grad_pre_a, (0, 1))
    grad_values = None
    d_gains = jnp.stack([d_gain_a, d_bias_a, d_gain_b, d_bias_b])
    return (d_w_first, d_w_second, d_gains, d_scale, d_shift, grad_values)


def to_heads(values):
    return lax.all_to_all(values, "pix", split_axis=2, concat_axis=1, tiled=True)


def to_pixels(values):
    return lax.all_to_all(values, "pix", split_axis=1, concat_axis=2, tiled=True)


def flat_heads(values):
    return values.reshape(-1, values.shape[2], values.shape[3])


def attend(queries, keys, values):
    root_dim = math.sqrt(queries.shape[-1])

    def single(bundle):
        q_one, k_one, v_one = bundle
        scores = (
            jnp.einsum("qd,kd->qk", q_one, k_one, preferred_element_type=jnp.float32) / root_dim
        )
        row_peak = jnp.max(scores, -1, keepdims=True)
        exp_scores = jnp.exp(scores - row_peak)
        sum_exp = jnp.sum(exp_scores, -1, keepdims=True)
        probabilities = (exp_scores / sum_exp).astype(jnp.bfloat16)
        attended = jnp.einsum("qk,kd->qd", probabilities, v_one, preferred_element_type=jnp.float32)
        return (attended.astype(jnp.bfloat16), row_peak + jnp.log(sum_exp))

    attended, log_total = lax.map(
        single, (flat_heads(queries), flat_heads(keys), flat_heads(values))
    )
    return (attended.reshape(queries.shape), log_total)


def attend_back(queries, keys, values, log_total, grad_out):
    root_dim = math.sqrt(queries.shape[-1])

    def single(bundle):
        q_one, k_one, v_one, lse_one, g_one = bundle
        scores = (
            jnp.einsum("qd,kd->qk", q_one, k_one, preferred_element_type=jnp.float32) / root_dim
        )
        probabilities = jnp.exp(scores - lse_one)
        grad_v = jnp.einsum(
            "qk,qd->kd",
            probabilities.astype(jnp.bfloat16),
            g_one,
            preferred_element_type=jnp.float32,
        )
        grad_p = jnp.einsum("qd,kd->qk", g_one, v_one, preferred_element_type=jnp.float32)
        inner_sum = jnp.sum(probabilities * grad_p, -1, keepdims=True)
        grad_s = (probabilities * (grad_p - inner_sum)).astype(jnp.bfloat16)
        grad_q = (
            jnp.einsum("qk,kd->qd", grad_s, k_one, preferred_element_type=jnp.float32) / root_dim
        )
        grad_k = (
            jnp.einsum("qk,qd->kd", grad_s, q_one, preferred_element_type=jnp.float32) / root_dim
        )
        return (grad_q, grad_k, grad_v)

    grad_q, grad_k, grad_v = lax.map(
        single,
        (
            flat_heads(queries),
            flat_heads(keys),
            flat_heads(values),
            log_total,
            flat_heads(grad_out),
        ),
    )
    return (grad_q.reshape(queries.shape), grad_k.reshape(keys.shape), grad_v.reshape(values.shape))


def local(
    images,
    target,
    clean_images,
    levels,
    labels,
    null_mask,
    vgg_proj,
    lpips_lin,
    master,
    first_moment,
    second_moment,
):
    gathered = lax.all_gather(master.astype(jnp.bfloat16), ("batch", "pix"), axis=0, tiled=True)
    pieces, used_len = unpack(gathered)
    w_one, w_two, w_qkv, w_proj, w_down, w_emb, class_table, gains_low = pieces
    gains_one = gains_low.astype(jnp.float32)
    n_img, rows_local, cols_local, channels = images.shape
    wide_channels = w_down.shape[1]
    pix_count = lax.axis_size("pix")
    batch_count = lax.axis_size("batch")
    pixels_here = rows_local * cols_local
    pixels_all = pixels_here * pix_count
    pixels_all_two = pixels_all // 4
    images_all = n_img * batch_count
    row_index = jnp.where(null_mask == 1, class_table.shape[0] - 1, labels)
    one_hot = (
        row_index[:, None] == jnp.arange(class_table.shape[0], dtype=jnp.int32)[None, :]
    ).astype(jnp.float32)
    pre_embed = time_vector(levels) + jnp.dot(
        one_hot, class_table.astype(jnp.float32), precision=precise
    )
    embedded = jax.nn.silu(pre_embed)
    w_emb_wide = w_emb.astype(jnp.float32)
    scale_shift = jnp.dot(embedded, w_emb_wide, precision=precise)
    scale_one = scale_shift[:, None, :channels]
    shift_one = scale_shift[:, None, channels:]
    flat_in = images.astype(jnp.float32).reshape(n_img, pixels_here, channels)
    middle, kept_one = res_forward(
        flat_in, gains_one, scale_one, shift_one, w_one, w_two, rows_local, pixels_all
    )
    normed_three, inverse_three = group_forward(middle, pixels_all)
    attn_in = (normed_three * gains_one[4] + gains_one[5]).astype(jnp.bfloat16)
    triples = jnp.dot(attn_in.reshape(-1, channels), w_qkv, preferred_element_type=jnp.float32)
    triples = triples.astype(jnp.bfloat16).reshape(n_img, pixels_here, 3 * channels)
    spread_heads = to_heads(triples)
    local_heads = spread_heads.shape[2] // (3 * HEAD)
    split_heads = spread_heads.reshape(n_img, -1, local_heads, 3, HEAD).transpose(3, 0, 2, 1, 4)
    queries, keys, values = (split_heads[0], split_heads[1], split_heads[2])
    attended, log_total = attend(queries, keys, values)
    attended_px = to_pixels(attended.transpose(0, 2, 1, 3).reshape(n_img, -1, local_heads * HEAD))
    projected = jnp.dot(
        attended_px.reshape(-1, channels), w_proj, preferred_element_type=jnp.float32
    )
    output = middle + projected.reshape(n_img, pixels_here, channels)
    final_out, columns_down = conv_forward(output.astype(jnp.bfloat16), w_down, rows_local, 2)
    pixels_two = final_out.shape[1]
    feat_width = vgg_proj.shape[1]
    online_feat = jnp.dot(
        final_out.astype(jnp.bfloat16).reshape(-1, wide_channels),
        vgg_proj,
        preferred_element_type=jnp.float32,
    )
    online_feat = online_feat.reshape(n_img, pixels_two, feat_width)
    target_feat = jnp.dot(
        target.reshape(-1, wide_channels), vgg_proj, preferred_element_type=jnp.float32
    )
    target_feat = target_feat.reshape(n_img, pixels_two, feat_width)
    target_unit = target_feat * lax.rsqrt(
        jnp.mean(target_feat * target_feat, -1, keepdims=True) + EPS_FEAT
    )
    clean_wide = clean_images.astype(jnp.float32).reshape(n_img, pixels_two, wide_channels)

    def loss_terms(feature, out_value):
        unit = feature * lax.rsqrt(jnp.mean(feature * feature, -1, keepdims=True) + EPS_FEAT)
        consist = jnp.sum(lpips_lin * (unit - target_unit) ** 2, (1, 2)) / (
            feat_width * pixels_all_two
        )
        denoise = jnp.sum((out_value - clean_wide) ** 2, (1, 2)) / (pixels_all_two * wide_channels)
        return (consist, denoise)

    (consist, denoise), pullback = jax.vjp(loss_terms, online_feat, final_out)
    level_hot = (levels[:, None] == jnp.arange(LEVELS, dtype=jnp.int32)[None, :]).astype(
        jnp.float32
    )
    level_pair = lax.psum(
        (jnp.sum(consist[:, None] * level_hot, 0), jnp.sum(level_hot / pix_count, 0)),
        ("batch", "pix"),
    )
    zero_count = level_pair[1][0]
    is_zero = (levels == 0).astype(jnp.float32)
    grad_feat, grad_out = pullback(
        (jnp.full_like(consist, 1.0 / images_all), is_zero / jnp.maximum(zero_count, 1.0))
    )
    grad_feat_low = grad_feat.astype(jnp.bfloat16).reshape(-1, feat_width)
    grad_final = grad_out + jnp.einsum(
        "rf,cf->rc", grad_feat_low, vgg_proj, preferred_element_type=jnp.float32
    ).reshape(n_img, pixels_two, wide_channels)
    d_w_down, grad_output = conv_back(
        columns_down, grad_final.astype(jnp.bfloat16), w_down, rows_local, 2
    )
    grad_proj = grad_output.astype(jnp.bfloat16).reshape(-1, channels)
    d_w_proj = jnp.einsum(
        "rc,rd->cd",
        attended_px.reshape(-1, channels),
        grad_proj,
        preferred_element_type=jnp.float32,
    )
    grad_att_px = jnp.einsum("rd,cd->rc", grad_proj, w_proj, preferred_element_type=jnp.float32)
    grad_att_px = grad_att_px.astype(jnp.bfloat16).reshape(n_img, pixels_here, channels)
    grad_heads = to_heads(grad_att_px)
    grad_split = grad_heads.reshape(n_img, -1, local_heads, HEAD).transpose(0, 2, 1, 3)
    grad_q, grad_k, grad_v = attend_back(queries, keys, values, log_total, grad_split)
    grad_triples = jnp.stack([grad_q, grad_k, grad_v], 3).transpose(0, 2, 1, 3, 4)
    grad_triples = grad_triples.reshape(n_img, -1, local_heads * 3 * HEAD).astype(jnp.bfloat16)
    grad_triples = to_pixels(grad_triples)
    grad_rows = grad_triples.reshape(-1, 3 * channels)
    d_w_qkv = jnp.einsum(
        "rc,rd->cd", attn_in.reshape(-1, channels), grad_rows, preferred_element_type=jnp.float32
    )
    grad_attn_in = jnp.einsum(
        "rd,cd->rc", grad_rows, w_qkv, preferred_element_type=jnp.float32
    ).reshape(n_img, pixels_here, channels)
    d_gain_three = jnp.sum(grad_attn_in * normed_three, (0, 1))
    d_bias_three = jnp.sum(grad_attn_in, (0, 1))
    grad_middle = grad_output + group_backward(
        grad_attn_in * gains_one[4], normed_three, inverse_three, pixels_all
    )
    d_w_one, d_w_two, d_gains_one, d_scale_one, d_shift_one, unused_grad = res_back(
        grad_middle, kept_one, gains_one, scale_one, w_one, w_two, rows_local, pixels_all
    )
    grad_scale_shift = jnp.concatenate([d_scale_one, d_shift_one], 1)
    d_w_emb = jnp.dot(embedded.T, grad_scale_shift, precision=precise)
    grad_embedded = jnp.dot(grad_scale_shift, w_emb_wide.T, precision=precise)
    d_table = jnp.dot(one_hot.T, grad_embedded * silu_slope(pre_embed), precision=precise)
    d_norms_one = jnp.concatenate([d_gains_one, jnp.stack([d_gain_three, d_bias_three])], 0)
    flat_grad = jnp.concatenate(
        [
            d_w_one.ravel(),
            d_w_two.ravel(),
            d_w_qkv.ravel(),
            d_w_proj.ravel(),
            d_w_down.ravel(),
            d_w_emb.ravel(),
            d_table.ravel(),
            d_norms_one.ravel(),
            jnp.zeros((gathered.shape[0] - used_len,), jnp.float32),
        ]
    )
    own_grad = lax.psum_scatter(flat_grad, ("batch", "pix"), scatter_dimension=0, tiled=True)
    norm_before = jnp.sqrt(lax.psum(jnp.sum(own_grad * own_grad), ("batch", "pix")))
    clipped = own_grad * jnp.minimum(1.0, CLIP / norm_before)
    new_first = BETA_ONE * first_moment + (1.0 - BETA_ONE) * clipped
    new_second = BETA_TWO * second_moment + (1.0 - BETA_TWO) * clipped * clipped
    fixed_first = new_first / (1.0 - BETA_ONE**STEP)
    fixed_second = new_second / (1.0 - BETA_TWO**STEP)
    new_master = master - RATE * (
        fixed_first / (jnp.sqrt(fixed_second) + EPS_ADAM) + DECAY * master
    )
    level_sums = jnp.stack([level_pair[0], level_pair[1]])
    return (
        new_master,
        new_first,
        new_second,
        new_master.astype(jnp.bfloat16),
        norm_before,
        level_sums,
    )


MESH = pl.DeviceIdType.MESH
ROWS=537; BLK=560; HALF=288

class Comm:
    def __init__(self): self.sent=[]
    def go(self, cond, src, dst, ssem, rsem, b, p):
        c = pltpu.make_async_remote_copy(src_ref=src,dst_ref=dst,send_sem=ssem,recv_sem=rsem,device_id=(b,p),device_id_type=MESH)
        if cond is None: c.start()
        else: pl.when(cond)(lambda: c.start())
        self.sent.append((cond,c))
    def drain(self):
        for cond,c in self.sent:
            if cond is None: c.wait_send()
            else: pl.when(cond)(lambda c=c: c.wait_send())
        self.sent=[]

def place():
    b=lax.axis_index("batch"); p=lax.axis_index("pix")
    core=lax.rem(b,2); y=lax.rem(lax.div(b,2),2); z=lax.div(b,4)
    return b,p,core,y,z

def ag_kernel(x_ref, flag_ref, out_ref, f_ref, blk_ref, own_sem, zs, zr, xs, xr, ys, yr, das, dar, dbs, dbr, ss, sr, ss2, sr2):
    b,p,core,y,z=place()
    s=b*2+p
    yn=b+2-4*y; sib=b+1-2*core; xn=1-p
    up_ok=z<3; dn_ok=z>0
    barrier=pltpu.get_barrier_semaphore()
    def sig(bb,pp): pl.semaphore_signal(barrier,inc=1,device_id=(bb,pp),device_id_type=MESH)
    sig(b,xn); sig(yn,p); sig(sib,p)
    pl.when(up_ok)(lambda: sig(b+4,p))
    pl.when(dn_ok)(lambda: sig(b-4,p))
    shift=lax.rem(9*s,16)
    f_ref[...]=jnp.zeros_like(f_ref)
    for j in range(3):
        f_ref[0:ROWS,128*j:128*j+128]=x_ref[pl.ds(j,ROWS,stride=3),:]
    at=lax.broadcasted_iota(jnp.int32,(BLK,384),0)
    blk_ref[...]=jnp.where(at==BLK-4,flag_ref[...],pltpu.roll(f_ref[...],shift,0)).astype(jnp.bfloat16)
    own=pltpu.make_async_copy(blk_ref,out_ref.at[s],own_sem)
    own.start()
    pl.semaphore_wait(barrier,3+up_ok.astype(jnp.int32)+dn_ok.astype(jnp.int32))
    cm=Comm()
    def slot(zz,yy,pp,cc=core): return ((zz*2+yy)*2+cc)*2+pp
    A=pl.ds(0,HALF); B=pl.ds(HALF,BLK-HALF)
    def valid(zz): return (zz>=0)&(zz<4)
    def z_arrive(k):
        for d in ((1,) if k==0 else (1,-1)):
            zz=z-k*d
            ok=None if k==0 else valid(zz)
            if k==0: zz=z
            sl=slot(zz,y,p)
            src=blk_ref if k==0 else out_ref.at[sl]
            if k>0:
                def w(): pltpu.make_async_remote_copy(src_ref=blk_ref,dst_ref=out_ref.at[sl],send_sem=zs.at[zz,0],recv_sem=zr.at[zz],device_id=(b,xn),device_id_type=MESH).wait_recv()
                pl.when(ok)(w)
            if k==0:
                cm.go(up_ok,src,out_ref.at[sl],zs.at[zz,0],zr.at[zz],b+4,p)
                cm.go(dn_ok,src,out_ref.at[sl],zs.at[zz,1],zr.at[zz],b-4,p)
            elif k<3:
                cm.go(ok&(up_ok if d==1 else dn_ok),src,out_ref.at[sl],zs.at[zz,0],zr.at[zz],b+4*d,p)
            cm.go(ok,src,out_ref.at[sl],xs.at[zz],xr.at[zz],b,xn)
            cm.go(ok,src,out_ref.at[sl],ys.at[zz],yr.at[zz],yn,p)
            cm.go(ok,src,out_ref.at[sl],ss.at[zz,y,p],sr.at[zz,y,p],sib,p)
    def when(ok,f):
        if ok is None: f()
        else: pl.when(ok)(f)
    def each(k):
        if k==0: return [(None,z)]
        return [(valid(z-k),z-k),(valid(z+k),z+k)]
    def wait_in(ref,sem,like):
        pltpu.make_async_remote_copy(src_ref=ref,dst_ref=ref,send_sem=sem,recv_sem=sem,device_id=(b,xn),device_id_type=MESH).wait_recv()
    def xy_arrive(k):
        for ok,zz in each(k):
            sx=slot(zz,y,xn); sy=slot(zz,1-y,p)
            when(ok,lambda: wait_in(out_ref.at[sx],xr.at[zz],None))
            cm.go(ok,out_ref.at[sx,A],out_ref.at[sx,A],das.at[zz],dar.at[zz],yn,p)
            cm.go(ok,out_ref.at[sx],out_ref.at[sx],ss.at[zz,y,xn],sr.at[zz,y,xn],sib,p)
            when(ok,lambda: wait_in(out_ref.at[sy],yr.at[zz],None))
            cm.go(ok,out_ref.at[sy,B],out_ref.at[sy,B],dbs.at[zz],dbr.at[zz],b,xn)
            cm.go(ok,out_ref.at[sy],out_ref.at[sy],ss.at[zz,1-y,p],sr.at[zz,1-y,p],sib,p)
    def d_arrive(k):
        for ok,zz in each(k):
            sd=slot(zz,1-y,xn)
            when(ok,lambda: wait_in(out_ref.at[sd,A],dar.at[zz],None))
            cm.go(ok,out_ref.at[sd,A],out_ref.at[sd,A],ss.at[zz,1-y,xn],sr.at[zz,1-y,xn],sib,p)
            when(ok,lambda: wait_in(out_ref.at[sd,B],dbr.at[zz],None))
            cm.go(ok,out_ref.at[sd,B],out_ref.at[sd,B],ss2.at[zz],sr2.at[zz],sib,p)
    for k in range(6):
        if k<=3: z_arrive(k)
        if 0<=k-1<=3: xy_arrive(k-1)
        if 0<=k-2<=3: d_arrive(k-2)
    oc=1-core
    for zz in range(4):
        for yy in range(2):
            for pp in range(2):
                sl=slot(zz,yy,pp,oc)
                isd=(yy!=y)&(pp!=p)
                def full(): wait_in(out_ref.at[sl],sr.at[zz,yy,pp],None)
                def part():
                    wait_in(out_ref.at[sl,A],sr.at[zz,yy,pp],None)
                    wait_in(out_ref.at[sl,B],sr2.at[zz],None)
                pl.when(isd)(part)
                pl.when(jnp.logical_not(isd))(full)
    cm.drain()
    own.wait()

def all_gather_weights(x, flag):
    D=pltpu.SemaphoreType.DMA
    return pl.pallas_call(ag_kernel,
        out_shape=jax.ShapeDtypeStruct((32,BLK,384),jnp.bfloat16),
        in_specs=[pl.BlockSpec(memory_space=pltpu.VMEM)]*2,
        out_specs=pl.BlockSpec(memory_space=pl.ANY),
        scratch_shapes=[pltpu.VMEM((BLK,384),jnp.float32),pltpu.VMEM((BLK,384),jnp.bfloat16),D,
            D((4,2)),D((4,)),D((4,)),D((4,)),D((4,)),D((4,)),D((4,)),D((4,)),D((4,)),D((4,)),D((4,2,2)),D((4,2,2)),D((4,)),D((4,))],
        compiler_params=pltpu.CompilerParams(collective_id=0,has_side_effects=True,vmem_limit_bytes=40<<20),
        name="gather_weights",
    )(x, flag)
f32=jnp.float32; bf=jnp.bfloat16
CH=384; CH2=576
PX=512
EPS_NORM=1e-5; EPS_FEAT=1e-6
R_ONE,R_TWO,R_QKV,R_PROJ,R_DOWN,R_EMB,R_TAB,R_GAIN,R_END=0,3456,6912,8064,8448,13632,15168,17170,17184
GROWS=13984
def base_of(s): return 16*((ROWS*s)//16)
def dg(a,b,ca,cb): return lax.dot_general(a,b,(((ca,),(cb,)),((),())),preferred_element_type=f32)
def nn(a,b): return dg(a,b,1,0)
def nt(a,b): return dg(a,b,1,1)
def tn(a,b): return dg(a,b,0,0)
def split3(v):
    hi=v.astype(bf); r=v-hi.astype(f32); mid=r.astype(bf); lo=(r-mid.astype(f32)).astype(bf)
    return hi,mid,lo
def exact(v,w,dot):
    hi,mid,lo=split3(v)
    return dot(hi,w)+dot(mid,w)+dot(lo,w)
def sigmoid(v): return 1.0/(1.0+jnp.exp(-v))
def silu(v): return v*sigmoid(v)
def slope(v):
    s=sigmoid(v)
    return s*(1.0+v*(1.0-s))
def cloop(n,chunk,body,init):
    return lax.fori_loop(0,n//chunk,lambda i,c: body(pl.multiple_of(i*chunk,chunk),c),init)
def col8(v): return jnp.sum(v.reshape(-1,8,v.shape[-1]),axis=0)
Z8=lambda: jnp.zeros((8,CH),f32)
def ld(ref,sl): return jnp.concatenate([ref[j,sl,:] for j in range(ref.shape[0])],1)
def put3(ref,sl,v):
    for j in range(v.shape[1]//128): ref[j,sl,:]=v[:,128*j:128*j+128]
def every(start,n,step): return pl.ds(start,n,stride=step)
def row(v): return jnp.sum(v,axis=0,keepdims=True)

def core_kernel(images_all,
    g_ref,img,tgt,cln,vgg,lin,tvec,rowid,iszero,gm,
    grad_ref,aux_ref,
    wv,tails,cvt,cvt2,wd,wee,weo,wqT,x3a,x3b,z3,inner,middle,gout,gsec,out32,ain,trT,dtrT,attT,gv,xd,lse,gai,dattT,dkv,
    ssend,srecv,hsend,hrecv,himg,dzs,dzr,geo,oth,
    wsem,tsem,gsem,xs,xr):
    b=lax.axis_index("batch"); p=lax.axis_index("pix"); q=1-p
    pf=p.astype(f32); qf=1.0-pf
    barrier=pltpu.get_barrier_semaphore()
    pl.semaphore_signal(barrier,inc=1,device_id=(b,q),device_id_type=MESH)
    loads=[]
    for s in range(32):
        lo=base_of(s); n=(base_of(s+1) if s<31 else R_END)-lo
        c=pltpu.make_async_copy(g_ref.at[s,pl.ds(0,n)],wv.at[pl.ds(lo,n)],wsem.at[s]); c.start(); loads.append(c)
    tl=pltpu.make_async_copy(g_ref.at[:,pl.ds(528,32)],tails,tsem); tl.start()
    state={"k":0,"loaded":0}
    def xchg(src,dst,dst_like=None):
        k=state["k"]; state["k"]=k+1
        c=pltpu.make_async_remote_copy(src_ref=src,dst_ref=dst,send_sem=xs.at[k],recv_sem=xr.at[k],device_id=(b,q),device_id_type=MESH)
        c.start()
        return c
    edge=pl.ds(pl.multiple_of(q*480,32),32)
    pl.semaphore_wait(barrier,1)
    c_img=xchg(img.at[edge],himg)
    def need_rows(upto):
        while state["loaded"]<32 and base_of(state["loaded"])<upto:
            s=state["loaded"]; loads[s].wait()
            if s==0: tl.wait()
            if s>0:
                off=(base_of(s)-base_of(s-1))-528
                t=tails[s-1,off:off+16].astype(f32)
                if off: t=jnp.where(lax.broadcasted_iota(jnp.int32,(16,CH),0)<8,t,0.0)
                lo=base_of(s)
                wv[lo:lo+16]=(wv[lo:lo+16].astype(f32)+t).astype(bf)
            state["loaded"]=s+1
    def gsum(v): return exact(v,gm[...],nn)
    def swap_sums(k,s1,s2):
        ssend[k]=jnp.concatenate([s1,s2,jnp.zeros((6,CH),f32)],0)
        return xchg(ssend.at[k],srecv.at[k])
    def total_sums(k):
        t=gsum(ssend[k]+srecv[k])*(1.0/(12*2*PX))
        return t[0:1],t[1:2]
    def norm_of(t):
        mean,sq=t
        return mean,lax.rsqrt(sq-mean*mean+EPS_NORM)
    def fill3(dst,at,a):
        col=lax.broadcasted_iota(jnp.int32,a.shape,0)&31
        n=a.shape[0]
        dst[pl.ds(at,n),CH:2*CH]=a.astype(bf)
        dst[pl.ds(at,n),0:CH]=jnp.where(col==0,0.0,pltpu.roll(a,1,0)).astype(bf)
        dst[pl.ds(at,n),2*CH:3*CH]=jnp.where(col==31,0.0,pltpu.roll(a,n-1,0)).astype(bf)
    def fill_edges(dst,h):
        fill3(dst,0,h*pf); fill3(dst,544,h*qf)
    def conv_to(dst,x3,wrow,add=None):
        for dr in range(3):
            d=nn(x3[32*dr:32*dr+PX],wv[wrow+1152*dr:wrow+1152*dr+1152])
            if dr==0: dst[...]=d if add is None else add()+d
            else: dst[...]+=d
    def conv_dw(x3,dz,grow):
        for dr in range(3):
            gv[grow+1152*dr:grow+1152*dr+1152]=tn(x3[32*dr:32*dr+PX],dz).astype(bf)
    def conv_dx(dst,wrow):
        first=True
        for dr in range(3):
            for dc in range(3):
                d=nt(z3[32*(2-dr):32*(2-dr)+PX,CH*(2-dc):CH*(2-dc)+CH],wv[wrow+CH*(3*dr+dc):wrow+CH*(3*dr+dc)+CH])
                if first: dst[...]=d
                else: dst[...]+=d
                first=False
    def st(i,c):
        v=img[pl.ds(i,64)].astype(f32)
        return c[0]+col8(v),c[1]+col8(v*v)
    a1,a2=cloop(PX,64,st,(Z8(),Z8()))
    c=swap_sums(0,row(a1),row(a2))
    need_rows(R_END)
    g6=wv[R_TAB+2000-(R_TAB+2000)%16:R_END].astype(f32)
    o=R_GAIN-(R_TAB+2000-(R_TAB+2000)%16)
    g1,b1,g2,b2,g3,b3=[g6[o+i:o+i+1] for i in range(6)]
    ids=rowid[...]
    pre=[]
    tcol=lax.broadcasted_iota(jnp.int32,(16,R_END-R_TAB),1)
    for h in range(2):
        hot=(tcol==2*ids+h).astype(f32).astype(bf)
        pre.append(nn(hot,wv[R_TAB:R_END])[0:1]+tvec[:,CH*h:CH*h+CH])
    emb=[silu(v) for v in pre]
    put3(cvt,pl.ds(0,1536),wv[R_EMB:R_TAB].astype(f32))
    wee[...]=ld(cvt,every(0,768,2)).astype(bf)
    weo[...]=ld(cvt,every(1,768,2)).astype(bf)
    def emb_dot(w):
        r=None
        for h in range(2):
            e=jnp.broadcast_to(emb[h],(16,CH))
            d=exact(e,w[CH*h:CH*h+CH],nn)[0:1]
            r=d if r is None else r+d
        return r
    sc1=1.0+emb_dot(wee); sh=emb_dot(weo)
    c.wait()
    mean1,inv1=norm_of(total_sums(0))
    def act_of(v): return silu((v-mean1)*inv1*g1+b1)
    def fa(i,_):
        fill3(x3a,pl.multiple_of(i+32,32),act_of(img[pl.ds(i,64)].astype(f32)))
        return 0
    cloop(PX,64,fa,0)
    c_img.wait()
    fill_edges(x3a,act_of(himg[...].astype(f32)))
    conv_to(inner,x3a,R_ONE)
    def st2(i,c):
        v=inner[pl.ds(i,64)]
        return c[0]+col8(v),c[1]+col8(v*v)
    a1,a2=cloop(PX,64,st2,(Z8(),Z8()))
    c1=swap_sums(1,row(a1),row(a2))
    c2=xchg(inner.at[edge],hrecv.at[0])
    c1.wait()
    mean2,inv2=norm_of(total_sums(1))
    def pre_b(v):
        n=(v-mean2)*inv2
        af=n*g2+b2
        return n,af,af*sc1+sh
    def fb(i,_):
        fill3(x3b,pl.multiple_of(i+32,32),silu(pre_b(inner[pl.ds(i,64)])[2]))
        return 0
    cloop(PX,64,fb,0)
    c2.wait()
    fill_edges(x3b,silu(pre_b(hrecv[0])[2]))
    conv_to(middle,x3b,R_TWO,lambda: img[...].astype(f32))
    def st3(i,c):
        v=middle[pl.ds(i,64)]
        return c[0]+col8(v),c[1]+col8(v*v)
    a1,a2=cloop(PX,64,st3,(Z8(),Z8()))
    c1=swap_sums(2,row(a1),row(a2))
    put3(cvt,pl.ds(0,1152),wv[R_QKV:R_PROJ].astype(f32))
    for j in range(3):
        wqT[CH*j:CH*j+CH]=ld(cvt,every(j,CH,3)).T.astype(bf)
    c1.wait()
    mean3,inv3=norm_of(total_sums(2))
    def fc(i,_):
        n=(middle[pl.ds(i,64)]-mean3)*inv3
        ain[pl.ds(i,64)]=(n*g3+b3).astype(bf)
        return 0
    cloop(PX,64,fc,0)
    c1=xchg(ain.at[pl.ds(0,PX)],ain.at[pl.ds(PX,PX)])
    trT[:,0:PX]=nt(wqT[...],ain[0:PX]).astype(bf)
    for off in range(9):
        put3(cvt,pl.ds(0,576),wv[R_DOWN+576*off:R_DOWN+576*off+576].astype(f32))
        v0,v1,v2=[ld(cvt,every(i,192,3)) for i in range(3)]
        put3(cvt2,every(0,192,2),jnp.concatenate([v0,v1[:,0:256]],1))
        w=jnp.concatenate([v1[:,128:384],v2],1)
        w=pltpu.roll(w,w.shape[1]-64,1)
        put3(cvt2,every(1,192,2),w)
        wd[CH*off:CH*off+CH]=ld(cvt2,pl.ds(0,CH))[:,0:576].astype(bf)
    c1.wait()
    trT[:,PX:2*PX]=nt(wqT[...],ain[PX:2*PX]).astype(bf)
    QC=256
    def fh(h,_):
        r0=pl.multiple_of(h*192,64)
        qT=trT[pl.ds(r0,64),0:PX]
        k=trT[pl.ds(pl.multiple_of(r0+64,64),64),:].T
        vT=trT[pl.ds(pl.multiple_of(r0+128,64),64),:]
        for c in range(PX//QC):
            s=nn(k,qT[:,QC*c:QC*c+QC])*0.125
            m=jnp.max(s,0,keepdims=True)
            e=jnp.exp(s-m)
            l=jnp.sum(e,0,keepdims=True)
            pT=(e*(1.0/l)).astype(bf)
            attT[pl.ds(pl.multiple_of(h*64,64),64),QC*c:QC*c+QC]=nn(vT,pT).astype(bf)
            lse[h,0:1,QC*c:QC*c+QC]=m+jnp.log(l)
        return 0
    lax.fori_loop(0,6,fh,0)
    put3(out32,pl.ds(0,PX),middle[...]+tn(attT[...],wv[R_PROJ:R_DOWN]))
    hsend[0]=ld(out32,edge).astype(bf)
    c1=xchg(hsend.at[0],oth.at[0])
    def parts(ref,n):
        e=ld(ref,every(0,n//2,2)); o=ld(ref,every(1,n//2,2))
        col=lax.broadcasted_iota(jnp.int32,o.shape,0)&15
        return jnp.where(col==0,0.0,pltpu.roll(o,1,0)).astype(bf),e.astype(bf),o.astype(bf)
    for dc,v in enumerate(parts(out32,PX)):
        v=v.reshape(8,32,CH)
        even=v[:,0:16].reshape(128,CH); odd=v[:,16:32].reshape(128,CH)
        xd[:,CH*(3+dc):CH*(3+dc)+CH]=even
        xd[:,CH*(6+dc):CH*(6+dc)+CH]=odd
        xd[16:128,CH*dc:CH*dc+CH]=odd[0:112]
    c1.wait()
    put3(geo,pl.ds(0,32),oth[0].astype(f32)*pf)
    for dc,v in enumerate(parts(geo,32)):
        xd[0:16,CH*dc:CH*dc+CH]=v
    fin=nn(xd[...],wd[...])
    feat=nn(fin.astype(bf),vgg[...]); tf=nn(tgt[...],vgg[...])
    ir=lax.rsqrt(jnp.mean(feat*feat,-1,keepdims=True)+EPS_FEAT)
    unit=feat*ir
    diff=unit-tf*lax.rsqrt(jnp.mean(tf*tf,-1,keepdims=True)+EPS_FEAT)
    wl=lin[...]*diff
    consist=jnp.sum(row(wl*diff),1,keepdims=True)*(1.0/(256*256))
    du=wl*(2.0/(256*256*images_all))
    dfeat=(ir*(du-unit*jnp.mean(du*unit,-1,keepdims=True))).astype(bf)
    zc=jnp.zeros((16,128),f32)
    for s in range(0,32,2): zc=zc+tails[s,16:32,0:128].astype(f32)
    zc=zc[12:13,0:1]
    seed=iszero[...]/jnp.maximum(zc,1.0)*(2.0/(256*CH2))
    gfin=nt(dfeat,vgg[...])+seed*(fin-cln[...].astype(f32))
    dz=gfin.astype(bf)
    dzs[...]=dz[0:16]
    c1=xchg(dzs,dzr)
    for off in range(9):
        dw=tn(xd[:,CH*off:CH*off+CH],dz)
        put3(cvt2,pl.ds(0,CH),jnp.concatenate([dw,jnp.zeros((CH,64),f32)],1))
        e=ld(cvt2,every(0,192,2)); o_=pltpu.roll(ld(cvt2,every(1,192,2)),64,1)
        lane=lax.broadcasted_iota(jnp.int32,(192,128),1)
        put3(cvt,every(0,192,3),e[:,0:384])
        put3(cvt,every(1,192,3),jnp.concatenate([e[:,384:512],jnp.where(lane<64,e[:,512:640],o_[:,0:128]),o_[:,128:256]],1))
        put3(cvt,every(2,192,3),o_[:,256:640])
        wv[R_DOWN+576*off:R_DOWN+576*off+576]=ld(cvt,pl.ds(0,576)).astype(bf)
    store_down=pltpu.make_async_copy(wv.at[pl.ds(R_DOWN,GROWS-R_DOWN)],grad_ref.at[pl.ds(R_DOWN,GROWS-R_DOWN)],gsem.at[0])
    store_down.start()
    c1.wait()
    z32=dz.astype(f32)
    down=jnp.concatenate([z32[16:128],dzr[...].astype(f32)*qf],0)
    def left(v):
        col=lax.broadcasted_iota(jnp.int32,v.shape,0)&15
        return jnp.where(col==15,0.0,pltpu.roll(v,127,0)).astype(bf)
    s00,s01,s10,s11=dz,left(z32),down.astype(bf),left(down)
    W=lambda a,c: wd[CH*(3*a+c):CH*(3*a+c)+CH]
    def put(a,c,v):
        for i in range(8):
            put3(gout,every((2*i+a)*32+c,16,2),v[16*i:16*i+16])
    put(0,0,nt(s00,W(1,1)))
    put(0,1,nt(s00,W(1,2))+nt(s01,W(1,0)))
    put(1,0,nt(s00,W(2,1))+nt(s10,W(0,1)))
    put(1,1,nt(s00,W(2,2))+nt(s01,W(2,0))+nt(s10,W(0,2))+nt(s11,W(0,0)))
    gp=ld(gout,pl.ds(0,PX)).astype(bf)
    gv[R_PROJ:R_DOWN]=nn(attT[...],gp).astype(bf)
    dattT[...]=nt(wv[R_PROJ:R_DOWN],gp).astype(bf)
    def bh(h,_):
        r0=pl.multiple_of(h*192,64); r1=pl.multiple_of(r0+64,64); r2=pl.multiple_of(r0+128,64)
        qT=trT[pl.ds(r0,64),0:PX]
        kT=trT[pl.ds(r1,64),:]
        k=kT.T
        v=trT[pl.ds(r2,64),:].T
        gT=dattT[pl.ds(pl.multiple_of(h*64,64),64),:]
        for c in range(PX//QC):
            qs=slice(QC*c,QC*c+QC)
            s=nn(k,qT[:,qs])*0.125
            pr=jnp.exp(s-lse[h,0:1,qs])
            dp=nn(v,gT[:,qs])
            de=jnp.sum(pr*dp,0,keepdims=True)
            ds=(pr*(dp-de)).astype(bf)
            dk=nt(qT[:,qs],ds)*0.125; dv=nt(gT[:,qs],pr.astype(bf))
            if c==0: dkv[0:64]=dk; dkv[64:128]=dv
            else: dkv[0:64]+=dk; dkv[64:128]+=dv
            dtrT[pl.ds(r0,64),qs]=(nn(kT,ds)*0.125).astype(bf)
        dtrT[pl.ds(r0,64),PX:2*PX]=jnp.zeros((64,PX),bf)
        dtrT[pl.ds(r1,64),:]=dkv[0:64].astype(bf)
        dtrT[pl.ds(r2,64),:]=dkv[64:128].astype(bf)
        return 0
    lax.fori_loop(0,6,bh,0)
    oth[1:17]=tn(dtrT[:,PX:2*PX],wqT[...]).astype(bf).reshape(16,32,CH)
    c1=xchg(oth.at[pl.ds(1,16)],oth.at[pl.ds(17,16)])
    gai[...]=tn(dtrT[:,0:PX],wqT[...])
    dq=nt(ain[...].T,dtrT[...])
    for j in range(3):
        put3(cvt,every(j,CH,3),dq[:,CH*j:CH*j+CH])
    gv[R_QKV:R_PROJ]=ld(cvt,pl.ds(0,1152)).astype(bf)
    c1.wait()
    def n3_of(i): return (middle[pl.ds(i,64)]-mean3)*inv3
    def s3(i,c):
        j=pl.multiple_of(17+lax.div(i,32),1)
        v=gai[pl.ds(i,64)]+oth[pl.ds(j,2)].reshape(64,CH).astype(f32)
        gai[pl.ds(i,64)]=v
        return c[0]+col8(v),c[1]+col8(v*n3_of(i))
    a1,a2=cloop(PX,64,s3,(Z8(),Z8()))
    db3,dg3=row(a1),row(a2)
    c1=swap_sums(3,db3*g3,dg3*g3)
    c1.wait()
    m1,m2=total_sums(3)
    def f3(i,_):
        v=ld(gout,pl.ds(i,64))+inv3*(gai[pl.ds(i,64)]*g3-m1-n3_of(i)*m2)
        fill3(z3,pl.multiple_of(i+32,32),v)
        return 0
    cloop(PX,64,f3,0)
    zedge=pl.ds(pl.multiple_of(q*480+32,32),32)
    hsend[1]=z3[zedge,CH:2*CH]
    c1=xchg(hsend.at[1],oth.at[33])
    conv_dw(x3b,z3[32:32+PX,CH:2*CH],R_TWO)
    store_two=pltpu.make_async_copy(gv.at[pl.ds(R_TWO,R_DOWN-R_TWO)],grad_ref.at[pl.ds(R_TWO,R_DOWN-R_TWO)],gsem.at[1])
    store_two.start()
    c1.wait()
    fill_edges(z3,oth[33].astype(f32))
    conv_dx(gsec,R_TWO)
    def s2(i,c):
        n,af,pb=pre_b(inner[pl.ds(i,64)])
        gpre=gsec[pl.ds(i,64)]*slope(pb)
        gaff=gpre*sc1
        gsec[pl.ds(i,64)]=gaff
        return c[0]+col8(gpre*af),c[1]+col8(gpre),c[2]+col8(gaff*n),c[3]+col8(gaff)
    a1,a2,a3,a4=cloop(PX,64,s2,(Z8(),Z8(),Z8(),Z8()))
    dsc,dsh,dg2,db2=row(a1),row(a2),row(a3),row(a4)
    c1=swap_sums(4,db2*g2,dg2*g2)
    c1.wait()
    m1,m2=total_sums(4)
    def f2(i,_):
        n=(inner[pl.ds(i,64)]-mean2)*inv2
        fill3(z3,pl.multiple_of(i+32,32),inv2*(gsec[pl.ds(i,64)]*g2-m1-n*m2))
        return 0
    cloop(PX,64,f2,0)
    hsend[2]=z3[zedge,CH:2*CH]
    c1=xchg(hsend.at[2],oth.at[34])
    conv_dw(x3a,z3[32:32+PX,CH:2*CH],R_ONE)
    store_one=pltpu.make_async_copy(gv.at[pl.ds(0,R_TWO)],grad_ref.at[pl.ds(0,R_TWO)],gsem.at[2])
    store_one.start()
    c1.wait()
    fill_edges(z3,oth[34].astype(f32))
    conv_dx(gsec,R_ONE)
    def s1(i,c):
        n=(img[pl.ds(i,64)].astype(f32)-mean1)*inv1
        gpre=gsec[pl.ds(i,64)]*slope(n*g1+b1)
        return c[0]+col8(gpre*n),c[1]+col8(gpre)
    a1,a2=cloop(PX,64,s1,(Z8(),Z8()))
    ge=[]
    for h in range(2):
        d=exact(jnp.broadcast_to(dsc,(16,CH)),wee[CH*h:CH*h+CH],nt)+exact(jnp.broadcast_to(dsh,(16,CH)),weo[CH*h:CH*h+CH],nt)
        ge.append(d[0:1]*slope(pre[h]))
    aux_ref[...]=jnp.concatenate([row(a1),row(a2),dg2,db2,dg3,db3,dsc,dsh,ge[0],ge[1],emb[0],emb[1],jnp.broadcast_to(consist,(1,CH)),jnp.zeros((3,CH),f32)],0)
    store_down.wait(); store_two.wait(); store_one.wait()

def core(images_all,G,img,tgt,cln,vgg,lin,tvec,rowid,iszero,gm):
    D=pltpu.SemaphoreType.DMA
    V=lambda *s: pltpu.VMEM(s,bf)
    F=lambda *s: pltpu.VMEM(s,f32)
    vm=pl.BlockSpec(memory_space=pltpu.VMEM)
    import functools
    return pl.pallas_call(functools.partial(core_kernel,images_all),
        out_shape=(jax.ShapeDtypeStruct((GROWS,CH),bf),jax.ShapeDtypeStruct((16,CH),f32)),
        in_specs=[pl.BlockSpec(memory_space=pl.ANY)]+[vm]*9,
        out_specs=(pl.BlockSpec(memory_space=pl.ANY),vm),
        scratch_shapes=[V(17184,CH),V(32,32,CH),F(3,1536,128),F(5,CH,128),V(3456,CH2),V(768,CH),V(768,CH),V(1152,CH),V(576,1152),V(576,1152),V(576,1152),
            F(PX,CH),F(PX,CH),F(3,PX,128),F(PX,CH),F(3,PX,128),V(1024,CH),V(1152,1024),V(1152,1024),V(CH,PX),V(R_DOWN,CH),V(128,3456),F(6,8,PX),F(PX,CH),V(CH,PX),F(128,1024),
            F(5,8,CH),F(5,8,CH),V(3,32,CH),F(1,32,CH),V(32,CH),V(16,CH2),V(16,CH2),F(3,32,128),V(35,32,CH),
            D((32,)),D,D((3,)),D((16,)),D((16,))],
        compiler_params=pltpu.CompilerParams(collective_id=2,has_side_effects=True,vmem_limit_bytes=62<<20),
        name="image_step",
    )(G,img,tgt,cln,vgg,lin,tvec,rowid,iszero,gm)
LAST=25
def rs_kernel(g_ref, out_ref, own, sibr, ra, rb, rx, ry, zu, zd, ld, s1s, s1r, das, dar, dbs, dbr, xs, xr, ys, yr, zs, zur, zdr):
    b,p,core,y,z=place()
    s=b*2+p
    yn=b+2-4*y; sib=b+1-2*core; xn=1-p
    up_ok=z<3; dn_ok=z>0
    barrier=pltpu.get_barrier_semaphore()
    def sig(bb,pp): pl.semaphore_signal(barrier,inc=1,device_id=(bb,pp),device_id_type=MESH)
    sig(b,xn); sig(yn,p); sig(sib,p)
    pl.when(up_ok)(lambda: sig(b+4,p))
    pl.when(dn_ok)(lambda: sig(b-4,p))
    def slot(zz,yy,pp,cc=core): return ((zz*2+yy)*2+cc)*2+pp
    def rows(sl): return g_ref.at[pl.ds(pl.multiple_of(16*lax.div(ROWS*sl,16),16),BLK)]
    def valid(zz): return (zz>=0)&(zz<4)
    def each(k):
        if k==0: return [(None,z,0)]
        return [(valid(z-k),z-k,-1),(valid(z+k),z+k,1)]
    def AND(*c):
        r=None
        for q in c:
            if q is not None: r=q if r is None else r&q
        return r
    def when(ok,f):
        if ok is None: f()
        else: pl.when(ok)(f)
    def need(zz,yy,pp,cc=core): return slot(zz,yy,pp,cc)<=LAST
    order=[3,2,1,0]
    four=((1-y,xn),(y,xn),(1-y,p),(y,p))
    def local(zz,yy,pp):
        return pltpu.make_async_copy(rows(slot(zz,yy,pp)),own.at[zz,yy,pp],ld.at[zz,yy,pp])
    for k in order:
        for ok,zz,_ in each(k):
            for yy,pp in four:
                when(AND(ok,need(zz,yy,pp)),lambda: local(zz,yy,pp).start())
    pl.semaphore_wait(barrier,3+up_ok.astype(jnp.int32)+dn_ok.astype(jnp.int32))
    cm=Comm()
    oc=1-core
    for k in order:
        for ok,zz,_ in each(k):
            for yy,pp in four:
                cm.go(AND(ok,need(zz,yy,pp,oc)),rows(slot(zz,yy,pp,oc)),sibr.at[zz,yy,pp],s1s.at[zz,yy,pp],s1r.at[zz,yy,pp],sib,p)
    def wait_in(ref,sem):
        pltpu.make_async_remote_copy(src_ref=ref,dst_ref=ref,send_sem=sem,recv_sem=sem,device_id=(b,xn),device_id_type=MESH).wait_recv()
    f32=jnp.float32
    A=pl.ds(0,HALF); B=pl.ds(HALF,BLK-HALF)
    def ready(zz,yy,pp):
        local(zz,yy,pp).wait()
        wait_in(sibr.at[zz,yy,pp],s1r.at[zz,yy,pp])
    def stage1(k):
        for ok,zz,_ in each(k):
            yy,pp=1-y,xn
            c=AND(ok,need(zz,yy,pp))
            def f():
                ready(zz,yy,pp)
                own[zz,yy,pp]=(own[zz,yy,pp].astype(f32)+sibr[zz,yy,pp].astype(f32)).astype(jnp.bfloat16)
            when(c,f)
            cm.go(c,own.at[zz,yy,pp,A],ra.at[zz],das.at[zz],dar.at[zz],b,xn)
            cm.go(c,own.at[zz,yy,pp,B],rb.at[zz],dbs.at[zz],dbr.at[zz],yn,p)
    def stage2(k):
        for ok,zz,_ in each(k):
            yy,pp=y,xn
            c=AND(ok,need(zz,yy,pp))
            def f():
                ready(zz,yy,pp)
                own[zz,yy,pp,A]=(own[zz,yy,pp,A].astype(f32)+sibr[zz,yy,pp,A].astype(f32)).astype(jnp.bfloat16)
                wait_in(rb.at[zz],dbr.at[zz])
                own[zz,yy,pp,B]=(own[zz,yy,pp,B].astype(f32)+sibr[zz,yy,pp,B].astype(f32)+rb[zz].astype(f32)).astype(jnp.bfloat16)
            when(c,f)
            cm.go(c,own.at[zz,yy,pp],rx.at[zz],xs.at[zz],xr.at[zz],b,xn)
            yy2,pp2=1-y,p
            c2=AND(ok,need(zz,yy2,pp2))
            def f2():
                ready(zz,yy2,pp2)
                own[zz,yy2,pp2,B]=(own[zz,yy2,pp2,B].astype(f32)+sibr[zz,yy2,pp2,B].astype(f32)).astype(jnp.bfloat16)
                wait_in(ra.at[zz],dar.at[zz])
                own[zz,yy2,pp2,A]=(own[zz,yy2,pp2,A].astype(f32)+sibr[zz,yy2,pp2,A].astype(f32)+ra[zz].astype(f32)).astype(jnp.bfloat16)
            when(c2,f2)
            cm.go(c2,own.at[zz,yy2,pp2],ry.at[zz],ys.at[zz],yr.at[zz],yn,p)
    def stage3(k):
        for ok,zz,d in each(k):
            c=AND(ok,need(zz,y,p))
            def f():
                ready(zz,y,p)
                wait_in(rx.at[zz],xr.at[zz])
                wait_in(ry.at[zz],yr.at[zz])
                t=own[zz,y,p].astype(f32)+sibr[zz,y,p].astype(f32)+rx[zz].astype(f32)+ry[zz].astype(f32)
                if k>0: own[zz,y,p]=t.astype(jnp.bfloat16)
                else: out_ref[...]=t
            when(c,f)
            if k>0:
                behind=dn_ok if d==1 else up_ok
                zbuf,zsem=(zu,zur) if d==1 else (zd,zdr)
                def f2():
                    wait_in(zbuf.at[zz],zsem.at[zz])
                    own[zz,y,p]=(own[zz,y,p].astype(f32)+zbuf[zz].astype(f32)).astype(jnp.bfloat16)
                if k<3: when(AND(c,behind),f2)
                cm.go(c,own.at[zz,y,p],zbuf.at[zz],zs.at[zz],zsem.at[zz],b+4*d,p)
            else:
                def f3():
                    wait_in(zu.at[zz],zur.at[zz])
                    out_ref[...]+=zu[zz].astype(f32)
                def f4():
                    wait_in(zd.at[zz],zdr.at[zz])
                    out_ref[...]+=zd[zz].astype(f32)
                when(AND(c,dn_ok),f3)
                when(AND(c,up_ok),f4)
    n=len(order)
    for i in range(n+2):
        if i<n: stage1(order[i])
        if 0<=i-1<n: stage2(order[i-1])
        if 0<=i-2<n: stage3(order[i-2])
    pl.when(jnp.logical_not(need(z,y,p)))(lambda: out_ref.__setitem__(Ellipsis,jnp.zeros(out_ref.shape,f32)))
    cm.drain()

def reduce_scatter(g):
    D=pltpu.SemaphoreType.DMA
    V=lambda *s: pltpu.VMEM(s,jnp.bfloat16)
    return pl.pallas_call(rs_kernel,
        out_shape=jax.ShapeDtypeStruct((BLK,384),jnp.float32),
        in_specs=[pl.BlockSpec(memory_space=pl.ANY)],
        out_specs=pl.BlockSpec(memory_space=pltpu.VMEM),
        scratch_shapes=[V(4,2,2,BLK,384),V(4,2,2,BLK,384),V(4,HALF,384),V(4,BLK-HALF,384),V(4,BLK,384),V(4,BLK,384),V(4,BLK,384),V(4,BLK,384),
            D((4,2,2)),D((4,2,2)),D((4,2,2)),D((4,)),D((4,)),D((4,)),D((4,)),D((4,)),D((4,)),D((4,)),D((4,)),D((4,)),D((4,)),D((4,))],
        compiler_params=pltpu.CompilerParams(collective_id=1,has_side_effects=True,vmem_limit_bytes=50<<20),
        name="scatter_gradient",
    )(g)


def tail_gradient(packs, s):
    gains = jnp.sum(packs[:, 0:6], 0)
    gss = packs[:, 6:8]
    gpre = packs[:, 8:10]
    rowids = packs[:, 13, 0]
    n = packs.shape[0]
    r = ROWS * s + jnp.arange(ROWS, dtype=jnp.int32)
    emb_all = packs[:, 10:12].reshape(n, TEMB).T
    wide = jnp.repeat(emb_all, 2, axis=0)
    wide = jnp.pad(wide, ((ROWS, ROWS), (0, 0)))
    start = jnp.clip(ROWS * s - R_EMB + ROWS, 0, 1536 + ROWS)
    part = lax.dynamic_slice(wide, (start, 0), (ROWS, n))
    inside = (r >= R_EMB) & (r < R_TAB)
    rel = r - R_EMB
    even = (inside & (rel % 2 == 0)).astype(jnp.float32)[:, None]
    odd = (inside & (rel % 2 == 1)).astype(jnp.float32)[:, None]
    t = (r - R_TAB)[:, None]
    ids = rowids.astype(jnp.int32)[None, :]
    in_table = ((r >= R_TAB) & (r < R_GAIN))[:, None]
    hot0 = ((t == 2 * ids) & in_table).astype(jnp.float32)
    hot1 = ((t == 2 * ids + 1) & in_table).astype(jnp.float32)
    g = (r[:, None] - R_GAIN == jnp.arange(6)[None, :]).astype(jnp.float32)
    left = jnp.concatenate([part * even, part * odd, hot0, hot1, g], 1)
    right = jnp.concatenate([gss[:, 0], gss[:, 1], gpre[:, 0], gpre[:, 1], gains], 0)
    return jnp.dot(left, right, precision=precise)


def fast(images, target, clean_images, levels, labels, null_mask, vgg_proj, lpips_lin, master, first_moment, second_moment):
    s = lax.axis_index("batch") * 2 + lax.axis_index("pix")
    is_zero = (levels == 0).astype(jnp.float32).reshape(1, 1)
    row_index = jnp.where(null_mask == 1, CLASSES, labels).reshape(1, 1)
    tvec = time_vector(levels)
    gathered = all_gather_weights(master.reshape(1611, 128), is_zero)
    lane = jnp.arange(CH, dtype=jnp.int32) // 12
    gm = (lane[:, None] == lane[None, :]).astype(jnp.bfloat16)
    grad, aux = core(
        16,
        gathered,
        images.reshape(PX, CH),
        target.reshape(128, CH2),
        clean_images.reshape(128, CH2),
        vgg_proj,
        lpips_lin.reshape(1, 256),
        tvec,
        row_index,
        is_zero,
        gm,
    )
    level_hot = (levels[:, None] == jnp.arange(CH, dtype=jnp.int32)[None, :]).astype(jnp.float32)
    pack = jnp.concatenate(
        [
            aux[0:12],
            aux[12:13] * level_hot,
            jnp.broadcast_to(row_index.astype(jnp.float32), (1, CH)),
            level_hot * 0.5,
            jnp.zeros((1, CH), jnp.float32),
        ],
        0,
    )
    packs = lax.all_gather(pack, ("batch", "pix"), axis=0, tiled=False)
    packs = packs.reshape(32, 16, CH)
    level_sums = jnp.stack([jnp.sum(packs[:, 12, :LEVELS], 0), jnp.sum(packs[:, 14, :LEVELS], 0)])
    summed = reduce_scatter(grad)
    summed = lax.dynamic_slice(summed, (lax.rem(9 * s, 16), 0), (ROWS, CH))
    r = ROWS * s + jnp.arange(ROWS, dtype=jnp.int32)
    own_grad = jnp.where((r < R_EMB)[:, None], summed, 0.0) + tail_gradient(packs, s)
    own_grad = own_grad.reshape(-1)
    norm_before = jnp.sqrt(lax.psum(jnp.sum(own_grad * own_grad), ("batch", "pix")))
    clipped = own_grad * jnp.minimum(1.0, CLIP / norm_before)
    new_first = BETA_ONE * first_moment + (1.0 - BETA_ONE) * clipped
    new_second = BETA_TWO * second_moment + (1.0 - BETA_TWO) * clipped * clipped
    fixed_first = new_first / (1.0 - BETA_ONE**STEP)
    fixed_second = new_second / (1.0 - BETA_TWO**STEP)
    new_master = master - RATE * (fixed_first / (jnp.sqrt(fixed_second) + EPS_ADAM) + DECAY * master)
    return (new_master, new_first, new_second, new_master.astype(jnp.bfloat16), norm_before, level_sums)


def solution(mesh):
    small = mesh.shape["batch"] == 16 and mesh.shape["pix"] == 2
    return jax.shard_map(
        fast if small else local,
        mesh=mesh,
        in_specs=(
            P("batch", "pix", None, None),
            P("batch", "pix", None, None),
            P("batch", "pix", None, None),
            P("batch"),
            P("batch"),
            P("batch"),
            P(),
            P(),
            P(("batch", "pix")),
            P(("batch", "pix")),
            P(("batch", "pix")),
        ),
        out_specs=(
            P(("batch", "pix")),
            P(("batch", "pix")),
            P(("batch", "pix")),
            P(("batch", "pix")),
            P(),
            P(),
        ),
        check_vma=False,
    )
```

```python
import functools
import math

import jax
import jax.numpy as jnp
from jax import lax
from jax.experimental import pallas as pl
from jax.experimental.pallas import tpu as pltpu
from jax.sharding import PartitionSpec as P

CH = 384
CH2 = 576
GROUPS = 32
HEAD = 64
TEMB = 768
CLASSES = 1000
LEVELS = 40
STEP = 10


EPS_NORM = 1e-05
EPS_FEAT = 1e-06
BETA_ONE = 0.9
BETA_TWO = 0.999
EPS_ADAM = 1e-08
RATE = 0.02
DECAY = 0.01
CLIP = 0.01
precise = lax.Precision.HIGHEST


def extended(shard, sides, width):
    for axis, dim in sides:
        size, length = (lax.axis_size(axis), shard.shape[dim])
        up = [(i, (i + 1) % size) for i in range(size - 1)]
        down = [(j, i) for i, j in up]
        last = lax.slice_in_dim(shard, length - width, length, axis=dim)
        initial = lax.slice_in_dim(shard, 0, width, axis=dim)
        before = lax.ppermute(last, axis, up)
        after = lax.ppermute(initial, axis, down)
        shard = jnp.concatenate([before, shard, after], axis=dim)
    return shard


def unpack(flat_vec):
    layout = [
        (9 * CH, CH),
        (9 * CH, CH),
        (CH, 3 * CH),
        (CH, CH),
        (9 * CH, CH2),
        (TEMB, 2 * CH),
        (CLASSES + 1, TEMB),
        (6, CH),
    ]
    pieces = []
    offset = 0
    for rows_n, cols_n in layout:
        pieces.append(flat_vec[offset : offset + rows_n * cols_n].reshape(rows_n, cols_n))
        offset += rows_n * cols_n
    return (pieces, offset)


def time_vector(level_ids):
    half_width = TEMB // 2
    frequency = jnp.exp(-math.log(10000.0) * jnp.arange(half_width, dtype=jnp.float32) / half_width)
    angles = level_ids.astype(jnp.float32)[..., None] * (1000.0 / LEVELS) * frequency
    return jnp.concatenate([jnp.cos(angles), jnp.sin(angles)], -1)


def silu_slope(values):
    sigmoid = jax.nn.sigmoid(values)
    return sigmoid * (1.0 + values * (1.0 - sigmoid))


def pix_sums(pair_sums):
    return lax.psum((pair_sums[0], pair_sums[1]), "pix")


def group_forward(values, pixels_all):
    grouped = values.reshape(values.shape[0], values.shape[1], GROUPS, -1)
    totals = pix_sums((jnp.sum(grouped, (1, 3)), jnp.sum(grouped * grouped, (1, 3))))
    per_group = pixels_all * grouped.shape[3]
    center = totals[0] / per_group
    spread = totals[1] / per_group - center * center
    inverse = lax.rsqrt(spread + EPS_NORM)
    normed = (grouped - center[:, None, :, None]) * inverse[:, None, :, None]
    return (normed.reshape(values.shape), inverse)


def group_backward(grad_normed, normed, inverse, pixels_all):
    grad_grouped = grad_normed.reshape(normed.shape[0], normed.shape[1], GROUPS, -1)
    val_grouped = normed.reshape(grad_grouped.shape)
    totals = pix_sums((jnp.sum(grad_grouped, (1, 3)), jnp.sum(grad_grouped * val_grouped, (1, 3))))
    per_group = pixels_all * grad_grouped.shape[3]
    result = (
        grad_grouped
        - (totals[0] / per_group)[:, None, :, None]
        - val_grouped * (totals[1] / per_group)[:, None, :, None]
    )
    return (result * inverse[:, None, :, None]).reshape(normed.shape)


def columns_of(values, stride):
    rows_out = values.shape[1] // stride
    cols_out = values.shape[2] // stride
    span_rows = stride * (rows_out - 1) + 1
    span_cols = stride * (cols_out - 1) + 1
    padded = extended(values, (("pix", 1),), 1)
    padded = jnp.pad(padded, ((0, 0), (0, 0), (1, 1), (0, 0)))
    return jnp.concatenate(
        [
            padded[
                :, row_off : row_off + span_rows : stride, col_off : col_off + span_cols : stride, :
            ]
            for row_off in range(3)
            for col_off in range(3)
        ],
        -1,
    )


def conv_forward(values, weight, rows_in, stride):
    n_img, pixels_in, in_chan = values.shape
    columns = columns_of(values.reshape(n_img, rows_in, -1, in_chan), stride)
    result = jnp.dot(columns.reshape(-1, 9 * in_chan), weight, preferred_element_type=jnp.float32)
    return (result.reshape(n_img, -1, weight.shape[1]), columns)


def conv_back(columns, grad_low, weight, rows_in, stride):
    n_img, pix_out, out_chan = grad_low.shape
    in_chan = weight.shape[0] // 9
    d_weight = jnp.einsum(
        "rk,rc->kc",
        columns.reshape(-1, 9 * in_chan),
        grad_low.reshape(-1, out_chan),
        preferred_element_type=jnp.float32,
    )
    flipped = (
        weight.reshape(3, 3, in_chan, out_chan)[::-1, ::-1]
        .transpose(0, 1, 3, 2)
        .reshape(9 * out_chan, in_chan)
    )
    rows_out = rows_in // stride
    grid_grad = grad_low.reshape(n_img, rows_out, pix_out // rows_out, out_chan)
    if stride > 1:
        grid_grad = jnp.pad(
            grid_grad[:, :, None, :, None, :],
            ((0, 0), (0, 0), (0, stride - 1), (0, 0), (0, stride - 1), (0, 0)),
        )
        grid_grad = grid_grad.reshape(n_img, rows_in, -1, out_chan)
    grad_columns = columns_of(grid_grad, 1)
    grad_input = jnp.dot(
        grad_columns.reshape(-1, 9 * out_chan), flipped, preferred_element_type=jnp.float32
    )
    return (d_weight, grad_input.reshape(n_img, -1, in_chan))


def res_forward(values, gain_rows, scale, shift, w_first, w_second, rows_in, pixels_all):
    normed_a, inverse_a = group_forward(values, pixels_all)
    pre_a = normed_a * gain_rows[0] + gain_rows[1]
    act_a = jax.nn.silu(pre_a).astype(jnp.bfloat16)
    inner, columns_a = conv_forward(act_a, w_first, rows_in, 1)
    normed_b, inverse_b = group_forward(inner, pixels_all)
    affine_b = normed_b * gain_rows[2] + gain_rows[3]
    pre_b = affine_b * (1.0 + scale) + shift
    second = jax.nn.silu(pre_b).astype(jnp.bfloat16)
    branch, columns_b = conv_forward(second, w_second, rows_in, 1)
    kept_state = (
        normed_a,
        inverse_a,
        pre_a,
        columns_a,
        normed_b,
        inverse_b,
        affine_b,
        pre_b,
        columns_b,
    )
    return (values + branch, kept_state)


def res_back(grad_result, kept_state, gain_rows, scale, w_first, w_second, rows_in, pixels_all):
    normed_a, inverse_a, pre_a, columns_a, normed_b, inverse_b, affine_b, pre_b, columns_b = (
        kept_state
    )
    d_w_second, grad_second = conv_back(
        columns_b, grad_result.astype(jnp.bfloat16), w_second, rows_in, 1
    )
    grad_pre_b = grad_second * silu_slope(pre_b)
    d_scale = jnp.sum(grad_pre_b * affine_b, 1)
    d_shift = jnp.sum(grad_pre_b, 1)
    grad_affine = grad_pre_b * (1.0 + scale)
    d_gain_b = jnp.sum(grad_affine * normed_b, (0, 1))
    d_bias_b = jnp.sum(grad_affine, (0, 1))
    grad_inner = group_backward(grad_affine * gain_rows[2], normed_b, inverse_b, pixels_all).astype(
        jnp.bfloat16
    )
    d_w_first, grad_act = conv_back(columns_a, grad_inner, w_first, rows_in, 1)
    grad_pre_a = grad_act * silu_slope(pre_a)
    d_gain_a = jnp.sum(grad_pre_a * normed_a, (0, 1))
    d_bias_a = jnp.sum(grad_pre_a, (0, 1))
    grad_values = None
    d_gains = jnp.stack([d_gain_a, d_bias_a, d_gain_b, d_bias_b])
    return (d_w_first, d_w_second, d_gains, d_scale, d_shift, grad_values)


def to_heads(values):
    return lax.all_to_all(values, "pix", split_axis=2, concat_axis=1, tiled=True)


def to_pixels(values):
    return lax.all_to_all(values, "pix", split_axis=1, concat_axis=2, tiled=True)


def flat_heads(values):
    return values.reshape(-1, values.shape[2], values.shape[3])


def attend(queries, keys, values):
    root_dim = math.sqrt(queries.shape[-1])

    def single(bundle):
        q_one, k_one, v_one = bundle
        scores = (
            jnp.einsum("qd,kd->qk", q_one, k_one, preferred_element_type=jnp.float32) / root_dim
        )
        row_peak = jnp.max(scores, -1, keepdims=True)
        exp_scores = jnp.exp(scores - row_peak)
        sum_exp = jnp.sum(exp_scores, -1, keepdims=True)
        probabilities = (exp_scores / sum_exp).astype(jnp.bfloat16)
        attended = jnp.einsum("qk,kd->qd", probabilities, v_one, preferred_element_type=jnp.float32)
        return (attended.astype(jnp.bfloat16), row_peak + jnp.log(sum_exp))

    attended, log_total = lax.map(
        single, (flat_heads(queries), flat_heads(keys), flat_heads(values))
    )
    return (attended.reshape(queries.shape), log_total)


def attend_back(queries, keys, values, log_total, grad_out):
    root_dim = math.sqrt(queries.shape[-1])

    def single(bundle):
        q_one, k_one, v_one, lse_one, g_one = bundle
        scores = (
            jnp.einsum("qd,kd->qk", q_one, k_one, preferred_element_type=jnp.float32) / root_dim
        )
        probabilities = jnp.exp(scores - lse_one)
        grad_v = jnp.einsum(
            "qk,qd->kd",
            probabilities.astype(jnp.bfloat16),
            g_one,
            preferred_element_type=jnp.float32,
        )
        grad_p = jnp.einsum("qd,kd->qk", g_one, v_one, preferred_element_type=jnp.float32)
        inner_sum = jnp.sum(probabilities * grad_p, -1, keepdims=True)
        grad_s = (probabilities * (grad_p - inner_sum)).astype(jnp.bfloat16)
        grad_q = (
            jnp.einsum("qk,kd->qd", grad_s, k_one, preferred_element_type=jnp.float32) / root_dim
        )
        grad_k = (
            jnp.einsum("qk,qd->kd", grad_s, q_one, preferred_element_type=jnp.float32) / root_dim
        )
        return (grad_q, grad_k, grad_v)

    grad_q, grad_k, grad_v = lax.map(
        single,
        (
            flat_heads(queries),
            flat_heads(keys),
            flat_heads(values),
            log_total,
            flat_heads(grad_out),
        ),
    )
    return (grad_q.reshape(queries.shape), grad_k.reshape(keys.shape), grad_v.reshape(values.shape))


def local(
    images,
    target,
    clean_images,
    levels,
    labels,
    null_mask,
    vgg_proj,
    lpips_lin,
    master,
    first_moment,
    second_moment,
):
    gathered = lax.all_gather(master.astype(jnp.bfloat16), ("batch", "pix"), axis=0, tiled=True)
    pieces, used_len = unpack(gathered)
    w_one, w_two, w_qkv, w_proj, w_down, w_emb, class_table, gains_low = pieces
    gains_one = gains_low.astype(jnp.float32)
    n_img, rows_local, cols_local, channels = images.shape
    wide_channels = w_down.shape[1]
    pix_count = lax.axis_size("pix")
    batch_count = lax.axis_size("batch")
    pixels_here = rows_local * cols_local
    pixels_all = pixels_here * pix_count
    pixels_all_two = pixels_all // 4
    images_all = n_img * batch_count
    row_index = jnp.where(null_mask == 1, class_table.shape[0] - 1, labels)
    one_hot = (
        row_index[:, None] == jnp.arange(class_table.shape[0], dtype=jnp.int32)[None, :]
    ).astype(jnp.float32)
    pre_embed = time_vector(levels) + jnp.dot(
        one_hot, class_table.astype(jnp.float32), precision=precise
    )
    embedded = jax.nn.silu(pre_embed)
    w_emb_wide = w_emb.astype(jnp.float32)
    scale_shift = jnp.dot(embedded, w_emb_wide, precision=precise)
    scale_one = scale_shift[:, None, :channels]
    shift_one = scale_shift[:, None, channels:]
    flat_in = images.astype(jnp.float32).reshape(n_img, pixels_here, channels)
    middle, kept_one = res_forward(
        flat_in, gains_one, scale_one, shift_one, w_one, w_two, rows_local, pixels_all
    )
    normed_three, inverse_three = group_forward(middle, pixels_all)
    attn_in = (normed_three * gains_one[4] + gains_one[5]).astype(jnp.bfloat16)
    triples = jnp.dot(attn_in.reshape(-1, channels), w_qkv, preferred_element_type=jnp.float32)
    triples = triples.astype(jnp.bfloat16).reshape(n_img, pixels_here, 3 * channels)
    spread_heads = to_heads(triples)
    local_heads = spread_heads.shape[2] // (3 * HEAD)
    split_heads = spread_heads.reshape(n_img, -1, local_heads, 3, HEAD).transpose(3, 0, 2, 1, 4)
    queries, keys, values = (split_heads[0], split_heads[1], split_heads[2])
    attended, log_total = attend(queries, keys, values)
    attended_px = to_pixels(attended.transpose(0, 2, 1, 3).reshape(n_img, -1, local_heads * HEAD))
    projected = jnp.dot(
        attended_px.reshape(-1, channels), w_proj, preferred_element_type=jnp.float32
    )
    output = middle + projected.reshape(n_img, pixels_here, channels)
    final_out, columns_down = conv_forward(output.astype(jnp.bfloat16), w_down, rows_local, 2)
    pixels_two = final_out.shape[1]
    feat_width = vgg_proj.shape[1]
    online_feat = jnp.dot(
        final_out.astype(jnp.bfloat16).reshape(-1, wide_channels),
        vgg_proj,
        preferred_element_type=jnp.float32,
    )
    online_feat = online_feat.reshape(n_img, pixels_two, feat_width)
    target_feat = jnp.dot(
        target.reshape(-1, wide_channels), vgg_proj, preferred_element_type=jnp.float32
    )
    target_feat = target_feat.reshape(n_img, pixels_two, feat_width)
    target_unit = target_feat * lax.rsqrt(
        jnp.mean(target_feat * target_feat, -1, keepdims=True) + EPS_FEAT
    )
    clean_wide = clean_images.astype(jnp.float32).reshape(n_img, pixels_two, wide_channels)

    def loss_terms(feature, out_value):
        unit = feature * lax.rsqrt(jnp.mean(feature * feature, -1, keepdims=True) + EPS_FEAT)
        consist = jnp.sum(lpips_lin * (unit - target_unit) ** 2, (1, 2)) / (
            feat_width * pixels_all_two
        )
        denoise = jnp.sum((out_value - clean_wide) ** 2, (1, 2)) / (pixels_all_two * wide_channels)
        return (consist, denoise)

    (consist, denoise), pullback = jax.vjp(loss_terms, online_feat, final_out)
    level_hot = (levels[:, None] == jnp.arange(LEVELS, dtype=jnp.int32)[None, :]).astype(
        jnp.float32
    )
    level_pair = lax.psum(
        (jnp.sum(consist[:, None] * level_hot, 0), jnp.sum(level_hot / pix_count, 0)),
        ("batch", "pix"),
    )
    zero_count = level_pair[1][0]
    is_zero = (levels == 0).astype(jnp.float32)
    grad_feat, grad_out = pullback(
        (jnp.full_like(consist, 1.0 / images_all), is_zero / jnp.maximum(zero_count, 1.0))
    )
    grad_feat_low = grad_feat.astype(jnp.bfloat16).reshape(-1, feat_width)
    grad_final = grad_out + jnp.einsum(
        "rf,cf->rc", grad_feat_low, vgg_proj, preferred_element_type=jnp.float32
    ).reshape(n_img, pixels_two, wide_channels)
    d_w_down, grad_output = conv_back(
        columns_down, grad_final.astype(jnp.bfloat16), w_down, rows_local, 2
    )
    grad_proj = grad_output.astype(jnp.bfloat16).reshape(-1, channels)
    d_w_proj = jnp.einsum(
        "rc,rd->cd",
        attended_px.reshape(-1, channels),
        grad_proj,
        preferred_element_type=jnp.float32,
    )
    grad_att_px = jnp.einsum("rd,cd->rc", grad_proj, w_proj, preferred_element_type=jnp.float32)
    grad_att_px = grad_att_px.astype(jnp.bfloat16).reshape(n_img, pixels_here, channels)
    grad_heads = to_heads(grad_att_px)
    grad_split = grad_heads.reshape(n_img, -1, local_heads, HEAD).transpose(0, 2, 1, 3)
    grad_q, grad_k, grad_v = attend_back(queries, keys, values, log_total, grad_split)
    grad_triples = jnp.stack([grad_q, grad_k, grad_v], 3).transpose(0, 2, 1, 3, 4)
    grad_triples = grad_triples.reshape(n_img, -1, local_heads * 3 * HEAD).astype(jnp.bfloat16)
    grad_triples = to_pixels(grad_triples)
    grad_rows = grad_triples.reshape(-1, 3 * channels)
    d_w_qkv = jnp.einsum(
        "rc,rd->cd", attn_in.reshape(-1, channels), grad_rows, preferred_element_type=jnp.float32
    )
    grad_attn_in = jnp.einsum(
        "rd,cd->rc", grad_rows, w_qkv, preferred_element_type=jnp.float32
    ).reshape(n_img, pixels_here, channels)
    d_gain_three = jnp.sum(grad_attn_in * normed_three, (0, 1))
    d_bias_three = jnp.sum(grad_attn_in, (0, 1))
    grad_middle = grad_output + group_backward(
        grad_attn_in * gains_one[4], normed_three, inverse_three, pixels_all
    )
    d_w_one, d_w_two, d_gains_one, d_scale_one, d_shift_one, unused_grad = res_back(
        grad_middle, kept_one, gains_one, scale_one, w_one, w_two, rows_local, pixels_all
    )
    grad_scale_shift = jnp.concatenate([d_scale_one, d_shift_one], 1)
    d_w_emb = jnp.dot(embedded.T, grad_scale_shift, precision=precise)
    grad_embedded = jnp.dot(grad_scale_shift, w_emb_wide.T, precision=precise)
    d_table = jnp.dot(one_hot.T, grad_embedded * silu_slope(pre_embed), precision=precise)
    d_norms_one = jnp.concatenate([d_gains_one, jnp.stack([d_gain_three, d_bias_three])], 0)
    flat_grad = jnp.concatenate(
        [
            d_w_one.ravel(),
            d_w_two.ravel(),
            d_w_qkv.ravel(),
            d_w_proj.ravel(),
            d_w_down.ravel(),
            d_w_emb.ravel(),
            d_table.ravel(),
            d_norms_one.ravel(),
            jnp.zeros((gathered.shape[0] - used_len,), jnp.float32),
        ]
    )
    own_grad = lax.psum_scatter(flat_grad, ("batch", "pix"), scatter_dimension=0, tiled=True)
    norm_before = jnp.sqrt(lax.psum(jnp.sum(own_grad * own_grad), ("batch", "pix")))
    clipped = own_grad * jnp.minimum(1.0, CLIP / norm_before)
    new_first = BETA_ONE * first_moment + (1.0 - BETA_ONE) * clipped
    new_second = BETA_TWO * second_moment + (1.0 - BETA_TWO) * clipped * clipped
    fixed_first = new_first / (1.0 - BETA_ONE**STEP)
    fixed_second = new_second / (1.0 - BETA_TWO**STEP)
    new_master = master - RATE * (
        fixed_first / (jnp.sqrt(fixed_second) + EPS_ADAM) + DECAY * master
    )
    level_sums = jnp.stack([level_pair[0], level_pair[1]])
    return (
        new_master,
        new_first,
        new_second,
        new_master.astype(jnp.bfloat16),
        norm_before,
        level_sums,
    )


MESH = pl.DeviceIdType.MESH
ROWS=537; BLK=560; HALF=288

class Comm:
    def __init__(self): self.sent=[]
    def go(self, cond, src, dst, ssem, rsem, b, p):
        c = pltpu.make_async_remote_copy(src_ref=src,dst_ref=dst,send_sem=ssem,recv_sem=rsem,device_id=(b,p),device_id_type=MESH)
        if cond is None: c.start()
        else: pl.when(cond)(lambda: c.start())
        self.sent.append((cond,c))
    def drain(self):
        for cond,c in self.sent:
            if cond is None: c.wait_send()
            else: pl.when(cond)(lambda c=c: c.wait_send())
        self.sent=[]

def place():
    b=lax.axis_index("batch"); p=lax.axis_index("pix")
    core=lax.rem(b,2); y=lax.rem(lax.div(b,2),2); z=lax.div(b,4)
    return b,p,core,y,z

def ag_kernel(x_ref, flag_ref, out_ref, f_ref, blk_ref, own_sem, zs, zr, xs, xr, ys, yr, das, dar, dbs, dbr, ss, sr, ss2, sr2):
    b,p,core,y,z=place()
    s=b*2+p
    yn=b+2-4*y; sib=b+1-2*core; xn=1-p
    up_ok=z<3; dn_ok=z>0
    barrier=pltpu.get_barrier_semaphore()
    def sig(bb,pp): pl.semaphore_signal(barrier,inc=1,device_id=(bb,pp),device_id_type=MESH)
    sig(b,xn); sig(yn,p); sig(sib,p)
    pl.when(up_ok)(lambda: sig(b+4,p))
    pl.when(dn_ok)(lambda: sig(b-4,p))
    shift=lax.rem(9*s,16)
    f_ref[...]=jnp.zeros_like(f_ref)
    for j in range(3):
        f_ref[0:ROWS,128*j:128*j+128]=x_ref[pl.ds(j,ROWS,stride=3),:]
    at=lax.broadcasted_iota(jnp.int32,(BLK,384),0)
    blk_ref[...]=jnp.where(at==BLK-4,flag_ref[...],pltpu.roll(f_ref[...],shift,0)).astype(jnp.bfloat16)
    own=pltpu.make_async_copy(blk_ref,out_ref.at[s],own_sem)
    own.start()
    pl.semaphore_wait(barrier,3+up_ok.astype(jnp.int32)+dn_ok.astype(jnp.int32))
    cm=Comm()
    def slot(zz,yy,pp,cc=core): return ((zz*2+yy)*2+cc)*2+pp
    A=pl.ds(0,HALF); B=pl.ds(HALF,BLK-HALF)
    def valid(zz): return (zz>=0)&(zz<4)
    def z_arrive(k):
        for d in ((1,) if k==0 else (1,-1)):
            zz=z-k*d
            ok=None if k==0 else valid(zz)
            if k==0: zz=z
            sl=slot(zz,y,p)
            src=blk_ref if k==0 else out_ref.at[sl]
            if k>0:
                def w(): pltpu.make_async_remote_copy(src_ref=blk_ref,dst_ref=out_ref.at[sl],send_sem=zs.at[zz,0],recv_sem=zr.at[zz],device_id=(b,xn),device_id_type=MESH).wait_recv()
                pl.when(ok)(w)
            if k==0:
                cm.go(up_ok,src,out_ref.at[sl],zs.at[zz,0],zr.at[zz],b+4,p)
                cm.go(dn_ok,src,out_ref.at[sl],zs.at[zz,1],zr.at[zz],b-4,p)
            elif k<3:
                cm.go(ok&(up_ok if d==1 else dn_ok),src,out_ref.at[sl],zs.at[zz,0],zr.at[zz],b+4*d,p)
            cm.go(ok,src,out_ref.at[sl],xs.at[zz],xr.at[zz],b,xn)
            cm.go(ok,src,out_ref.at[sl],ys.at[zz],yr.at[zz],yn,p)
            cm.go(ok,src,out_ref.at[sl],ss.at[zz,y,p],sr.at[zz,y,p],sib,p)
    def when(ok,f):
        if ok is None: f()
        else: pl.when(ok)(f)
    def each(k):
        if k==0: return [(None,z)]
        return [(valid(z-k),z-k),(valid(z+k),z+k)]
    def wait_in(ref,sem,like):
        pltpu.make_async_remote_copy(src_ref=ref,dst_ref=ref,send_sem=sem,recv_sem=sem,device_id=(b,xn),device_id_type=MESH).wait_recv()
    def xy_arrive(k):
        for ok,zz in each(k):
            sx=slot(zz,y,xn); sy=slot(zz,1-y,p)
            when(ok,lambda: wait_in(out_ref.at[sx],xr.at[zz],None))
            cm.go(ok,out_ref.at[sx,A],out_ref.at[sx,A],das.at[zz],dar.at[zz],yn,p)
            cm.go(ok,out_ref.at[sx],out_ref.at[sx],ss.at[zz,y,xn],sr.at[zz,y,xn],sib,p)
            when(ok,lambda: wait_in(out_ref.at[sy],yr.at[zz],None))
            cm.go(ok,out_ref.at[sy,B],out_ref.at[sy,B],dbs.at[zz],dbr.at[zz],b,xn)
            cm.go(ok,out_ref.at[sy],out_ref.at[sy],ss.at[zz,1-y,p],sr.at[zz,1-y,p],sib,p)
    def d_arrive(k):
        for ok,zz in each(k):
            sd=slot(zz,1-y,xn)
            when(ok,lambda: wait_in(out_ref.at[sd,A],dar.at[zz],None))
            cm.go(ok,out_ref.at[sd,A],out_ref.at[sd,A],ss.at[zz,1-y,xn],sr.at[zz,1-y,xn],sib,p)
            when(ok,lambda: wait_in(out_ref.at[sd,B],dbr.at[zz],None))
            cm.go(ok,out_ref.at[sd,B],out_ref.at[sd,B],ss2.at[zz],sr2.at[zz],sib,p)
    for k in range(6):
        if k<=3: z_arrive(k)
        if 0<=k-1<=3: xy_arrive(k-1)
        if 0<=k-2<=3: d_arrive(k-2)
    oc=1-core
    for zz in range(4):
        for yy in range(2):
            for pp in range(2):
                sl=slot(zz,yy,pp,oc)
                isd=(yy!=y)&(pp!=p)
                def full(): wait_in(out_ref.at[sl],sr.at[zz,yy,pp],None)
                def part():
                    wait_in(out_ref.at[sl,A],sr.at[zz,yy,pp],None)
                    wait_in(out_ref.at[sl,B],sr2.at[zz],None)
                pl.when(isd)(part)
                pl.when(jnp.logical_not(isd))(full)
    cm.drain()
    own.wait()

def all_gather_weights(x, flag):
    D=pltpu.SemaphoreType.DMA
    return pl.pallas_call(ag_kernel,
        out_shape=jax.ShapeDtypeStruct((32,BLK,384),jnp.bfloat16),
        in_specs=[pl.BlockSpec(memory_space=pltpu.VMEM)]*2,
        out_specs=pl.BlockSpec(memory_space=pl.ANY),
        scratch_shapes=[pltpu.VMEM((BLK,384),jnp.float32),pltpu.VMEM((BLK,384),jnp.bfloat16),D,
            D((4,2)),D((4,)),D((4,)),D((4,)),D((4,)),D((4,)),D((4,)),D((4,)),D((4,)),D((4,)),D((4,2,2)),D((4,2,2)),D((4,)),D((4,))],
        compiler_params=pltpu.CompilerParams(collective_id=0,has_side_effects=True,vmem_limit_bytes=40<<20),
        name="gather_weights",
    )(x, flag)
f32=jnp.float32; bf=jnp.bfloat16
CH=384; CH2=576
PX=512
EPS_NORM=1e-5; EPS_FEAT=1e-6
R_ONE,R_TWO,R_QKV,R_PROJ,R_DOWN,R_EMB,R_TAB,R_GAIN,R_END=0,3456,6912,8064,8448,13632,15168,17170,17184
GROWS=13984
def base_of(s): return 16*((ROWS*s)//16)
def dg(a,b,ca,cb): return lax.dot_general(a,b,(((ca,),(cb,)),((),())),preferred_element_type=f32)
def nn(a,b): return dg(a,b,1,0)
def nt(a,b): return dg(a,b,1,1)
def tn(a,b): return dg(a,b,0,0)
def split3(v):
    hi=v.astype(bf); r=v-hi.astype(f32); mid=r.astype(bf); lo=(r-mid.astype(f32)).astype(bf)
    return hi,mid,lo
def exact(v,w,dot):
    hi,mid,lo=split3(v)
    return dot(hi,w)+dot(mid,w)+dot(lo,w)
def sigmoid(v): return 1.0/(1.0+jnp.exp(-v))
def silu(v): return v*sigmoid(v)
def slope(v):
    s=sigmoid(v)
    return s*(1.0+v*(1.0-s))
def cloop(n,chunk,body,init):
    return lax.fori_loop(0,n//chunk,lambda i,c: body(pl.multiple_of(i*chunk,chunk),c),init)
def col8(v): return jnp.sum(v.reshape(-1,8,v.shape[-1]),axis=0)
Z8=lambda: jnp.zeros((8,CH),f32)
def ld(ref,sl): return jnp.concatenate([ref[j,sl,:] for j in range(ref.shape[0])],1)
def put3(ref,sl,v):
    for j in range(v.shape[1]//128): ref[j,sl,:]=v[:,128*j:128*j+128]
def every(start,n,step): return pl.ds(start,n,stride=step)
def row(v): return jnp.sum(v,axis=0,keepdims=True)

def core_kernel(images_all,
    g_ref,img,tgt,cln,vgg,lin,tvec,rowid,level,gm,
    grad_ref,aux_ref,
    wv,tails,cvt,cvt2,wd,wee,weo,wqT,x3a,x3b,z3,inner,middle,gout,gsec,out32,ain,trT,dtrT,attT,gv,xd,lse,gai,dattT,dkv,
    ssend,srecv,hsend,hrecv,himg,dzs,dzr,geo,oth,
    wsem,tsem,gsem,xs,xr):
    b=lax.axis_index("batch"); p=lax.axis_index("pix"); q=1-p
    pf=p.astype(f32); qf=1.0-pf
    barrier=pltpu.get_barrier_semaphore()
    pl.semaphore_signal(barrier,inc=1,device_id=(b,q),device_id_type=MESH)
    loads=[]
    for s in range(32):
        lo=base_of(s); n=(base_of(s+1) if s<31 else R_END)-lo
        c=pltpu.make_async_copy(g_ref.at[s,pl.ds(0,n)],wv.at[pl.ds(lo,n)],wsem.at[s]); c.start(); loads.append(c)
    tl=pltpu.make_async_copy(g_ref.at[:,pl.ds(528,32)],tails,tsem); tl.start()
    state={"k":0,"loaded":0}
    def xchg(src,dst,dst_like=None):
        k=state["k"]; state["k"]=k+1
        c=pltpu.make_async_remote_copy(src_ref=src,dst_ref=dst,send_sem=xs.at[k],recv_sem=xr.at[k],device_id=(b,q),device_id_type=MESH)
        c.start()
        return c
    edge=pl.ds(pl.multiple_of(q*480,32),32)
    pl.semaphore_wait(barrier,1)
    c_img=xchg(img.at[edge],himg)
    def need_rows(upto):
        while state["loaded"]<32 and base_of(state["loaded"])<upto:
            s=state["loaded"]; loads[s].wait()
            if s==0: tl.wait()
            if s>0:
                off=(base_of(s)-base_of(s-1))-528
                t=tails[s-1,off:off+16].astype(f32)
                if off: t=jnp.where(lax.broadcasted_iota(jnp.int32,(16,CH),0)<8,t,0.0)
                lo=base_of(s)
                wv[lo:lo+16]=(wv[lo:lo+16].astype(f32)+t).astype(bf)
            state["loaded"]=s+1
    def gsum(v): return exact(v,gm[...],nn)
    def swap_sums(k,s1,s2):
        ssend[k]=jnp.concatenate([s1,s2,jnp.zeros((6,CH),f32)],0)
        return xchg(ssend.at[k],srecv.at[k])
    def total_sums(k):
        t=gsum(ssend[k]+srecv[k])*(1.0/(12*2*PX))
        return t[0:1],t[1:2]
    def norm_of(t):
        mean,sq=t
        return mean,lax.rsqrt(sq-mean*mean+EPS_NORM)
    def fill3(dst,at,a):
        col=lax.broadcasted_iota(jnp.int32,a.shape,0)&31
        n=a.shape[0]
        dst[pl.ds(at,n),CH:2*CH]=a.astype(bf)
        dst[pl.ds(at,n),0:CH]=jnp.where(col==0,0.0,pltpu.roll(a,1,0)).astype(bf)
        dst[pl.ds(at,n),2*CH:3*CH]=jnp.where(col==31,0.0,pltpu.roll(a,n-1,0)).astype(bf)
    def fill_edges(dst,h):
        fill3(dst,0,h*pf); fill3(dst,544,h*qf)
    def conv_to(dst,x3,wrow,add=None):
        for dr in range(3):
            d=nn(x3[32*dr:32*dr+PX],wv[wrow+1152*dr:wrow+1152*dr+1152])
            if dr==0: dst[...]=d if add is None else add()+d
            else: dst[...]+=d
    def conv_dw(x3,dz,grow):
        for dr in range(3):
            gv[grow+1152*dr:grow+1152*dr+1152]=tn(x3[32*dr:32*dr+PX],dz).astype(bf)
    def conv_dx(dst,wrow):
        first=True
        for dr in range(3):
            for dc in range(3):
                d=nt(z3[32*(2-dr):32*(2-dr)+PX,CH*(2-dc):CH*(2-dc)+CH],wv[wrow+CH*(3*dr+dc):wrow+CH*(3*dr+dc)+CH])
                if first: dst[...]=d
                else: dst[...]+=d
                first=False
    def st(i,c):
        v=img[pl.ds(i,64)].astype(f32)
        return c[0]+col8(v),c[1]+col8(v*v)
    a1,a2=cloop(PX,64,st,(Z8(),Z8()))
    c=swap_sums(0,row(a1),row(a2))
    need_rows(R_END)
    g6=wv[R_TAB+2000-(R_TAB+2000)%16:R_END].astype(f32)
    o=R_GAIN-(R_TAB+2000-(R_TAB+2000)%16)
    g1,b1,g2,b2,g3,b3=[g6[o+i:o+i+1] for i in range(6)]
    ids=rowid[...]
    pre=[]
    tcol=lax.broadcasted_iota(jnp.int32,(16,R_END-R_TAB),1)
    for h in range(2):
        hot=(tcol==2*ids+h).astype(f32).astype(bf)
        pre.append(nn(hot,wv[R_TAB:R_END])[0:1]+tvec[:,CH*h:CH*h+CH])
    emb=[silu(v) for v in pre]
    put3(cvt,pl.ds(0,1536),wv[R_EMB:R_TAB].astype(f32))
    wee[...]=ld(cvt,every(0,768,2)).astype(bf)
    weo[...]=ld(cvt,every(1,768,2)).astype(bf)
    def emb_dot(w):
        r=None
        for h in range(2):
            e=jnp.broadcast_to(emb[h],(16,CH))
            d=exact(e,w[CH*h:CH*h+CH],nn)[0:1]
            r=d if r is None else r+d
        return r
    sc1=1.0+emb_dot(wee); sh=emb_dot(weo)
    c.wait()
    mean1,inv1=norm_of(total_sums(0))
    def act_of(v): return silu((v-mean1)*inv1*g1+b1)
    def fa(i,_):
        fill3(x3a,pl.multiple_of(i+32,32),act_of(img[pl.ds(i,64)].astype(f32)))
        return 0
    cloop(PX,64,fa,0)
    c_img.wait()
    fill_edges(x3a,act_of(himg[...].astype(f32)))
    conv_to(inner,x3a,R_ONE)
    def st2(i,c):
        v=inner[pl.ds(i,64)]
        return c[0]+col8(v),c[1]+col8(v*v)
    a1,a2=cloop(PX,64,st2,(Z8(),Z8()))
    c1=swap_sums(1,row(a1),row(a2))
    c2=xchg(inner.at[edge],hrecv.at[0])
    c1.wait()
    mean2,inv2=norm_of(total_sums(1))
    def pre_b(v):
        n=(v-mean2)*inv2
        af=n*g2+b2
        return n,af,af*sc1+sh
    def fb(i,_):
        fill3(x3b,pl.multiple_of(i+32,32),silu(pre_b(inner[pl.ds(i,64)])[2]))
        return 0
    cloop(PX,64,fb,0)
    c2.wait()
    fill_edges(x3b,silu(pre_b(hrecv[0])[2]))
    conv_to(middle,x3b,R_TWO,lambda: img[...].astype(f32))
    def st3(i,c):
        v=middle[pl.ds(i,64)]
        return c[0]+col8(v),c[1]+col8(v*v)
    a1,a2=cloop(PX,64,st3,(Z8(),Z8()))
    c1=swap_sums(2,row(a1),row(a2))
    put3(cvt,pl.ds(0,1152),wv[R_QKV:R_PROJ].astype(f32))
    for j in range(3):
        wqT[CH*j:CH*j+CH]=ld(cvt,every(j,CH,3)).T.astype(bf)
    c1.wait()
    mean3,inv3=norm_of(total_sums(2))
    def fc(i,_):
        n=(middle[pl.ds(i,64)]-mean3)*inv3
        ain[pl.ds(i,64)]=(n*g3+b3).astype(bf)
        return 0
    cloop(PX,64,fc,0)
    c1=xchg(ain.at[pl.ds(0,PX)],ain.at[pl.ds(PX,PX)])
    trT[:,0:PX]=nt(wqT[...],ain[0:PX]).astype(bf)
    for off in range(9):
        put3(cvt,pl.ds(0,576),wv[R_DOWN+576*off:R_DOWN+576*off+576].astype(f32))
        v0,v1,v2=[ld(cvt,every(i,192,3)) for i in range(3)]
        put3(cvt2,every(0,192,2),jnp.concatenate([v0,v1[:,0:256]],1))
        w=jnp.concatenate([v1[:,128:384],v2],1)
        w=pltpu.roll(w,w.shape[1]-64,1)
        put3(cvt2,every(1,192,2),w)
        wd[CH*off:CH*off+CH]=ld(cvt2,pl.ds(0,CH))[:,0:576].astype(bf)
    c1.wait()
    trT[:,PX:2*PX]=nt(wqT[...],ain[PX:2*PX]).astype(bf)
    QC=256
    def fh(h,_):
        r0=pl.multiple_of(h*192,64)
        qT=trT[pl.ds(r0,64),0:PX]
        k=trT[pl.ds(pl.multiple_of(r0+64,64),64),:].T
        vT=trT[pl.ds(pl.multiple_of(r0+128,64),64),:]
        for c in range(PX//QC):
            s=nn(k,qT[:,QC*c:QC*c+QC])*0.125
            m=jnp.max(s,0,keepdims=True)
            e=jnp.exp(s-m)
            l=jnp.sum(e,0,keepdims=True)
            pT=(e*(1.0/l)).astype(bf)
            attT[pl.ds(pl.multiple_of(h*64,64),64),QC*c:QC*c+QC]=nn(vT,pT).astype(bf)
            lse[h,0:1,QC*c:QC*c+QC]=m+jnp.log(l)
        return 0
    lax.fori_loop(0,6,fh,0)
    put3(out32,pl.ds(0,PX),middle[...]+tn(attT[...],wv[R_PROJ:R_DOWN]))
    hsend[0]=ld(out32,edge).astype(bf)
    c1=xchg(hsend.at[0],oth.at[0])
    def parts(ref,n):
        e=ld(ref,every(0,n//2,2)); o=ld(ref,every(1,n//2,2))
        col=lax.broadcasted_iota(jnp.int32,o.shape,0)&15
        return jnp.where(col==0,0.0,pltpu.roll(o,1,0)).astype(bf),e.astype(bf),o.astype(bf)
    for dc,v in enumerate(parts(out32,PX)):
        v=v.reshape(8,32,CH)
        even=v[:,0:16].reshape(128,CH); odd=v[:,16:32].reshape(128,CH)
        xd[:,CH*(3+dc):CH*(3+dc)+CH]=even
        xd[:,CH*(6+dc):CH*(6+dc)+CH]=odd
        xd[16:128,CH*dc:CH*dc+CH]=odd[0:112]
    c1.wait()
    put3(geo,pl.ds(0,32),oth[0].astype(f32)*pf)
    for dc,v in enumerate(parts(geo,32)):
        xd[0:16,CH*dc:CH*dc+CH]=v
    fin=nn(xd[...],wd[...])
    feat=nn(fin.astype(bf),vgg[...]); tf=nn(tgt[...],vgg[...])
    ir=lax.rsqrt(jnp.mean(feat*feat,-1,keepdims=True)+EPS_FEAT)
    unit=feat*ir
    diff=unit-tf*lax.rsqrt(jnp.mean(tf*tf,-1,keepdims=True)+EPS_FEAT)
    wl=lin[...]*diff
    consist=jnp.sum(row(wl*diff),1,keepdims=True)*(1.0/(256*256))
    du=wl*(2.0/(256*256*images_all))
    dfeat=(ir*(du-unit*jnp.mean(du*unit,-1,keepdims=True))).astype(bf)
    zc=jnp.zeros((16,128),f32)
    for s in range(0,32,2): zc=zc+tails[s,16:32,0:128].astype(f32)
    zc=zc[12:13,0:1]
    seed=(level[...]==0).astype(f32)/jnp.maximum(zc,1.0)*(2.0/(256*CH2))
    gfin=nt(dfeat,vgg[...])+seed*(fin-cln[...].astype(f32))
    dz=gfin.astype(bf)
    dzs[...]=dz[0:16]
    c1=xchg(dzs,dzr)
    for off in range(9):
        dw=tn(xd[:,CH*off:CH*off+CH],dz)
        put3(cvt2,pl.ds(0,CH),jnp.concatenate([dw,jnp.zeros((CH,64),f32)],1))
        e=ld(cvt2,every(0,192,2)); o_=pltpu.roll(ld(cvt2,every(1,192,2)),64,1)
        lane=lax.broadcasted_iota(jnp.int32,(192,128),1)
        put3(cvt,every(0,192,3),e[:,0:384])
        put3(cvt,every(1,192,3),jnp.concatenate([e[:,384:512],jnp.where(lane<64,e[:,512:640],o_[:,0:128]),o_[:,128:256]],1))
        put3(cvt,every(2,192,3),o_[:,256:640])
        wv[R_DOWN+576*off:R_DOWN+576*off+576]=ld(cvt,pl.ds(0,576)).astype(bf)
    store_down=pltpu.make_async_copy(wv.at[pl.ds(R_DOWN,GROWS-R_DOWN)],grad_ref.at[pl.ds(R_DOWN,GROWS-R_DOWN)],gsem.at[0])
    store_down.start()
    c1.wait()
    z32=dz.astype(f32)
    down=jnp.concatenate([z32[16:128],dzr[...].astype(f32)*qf],0)
    def left(v):
        col=lax.broadcasted_iota(jnp.int32,v.shape,0)&15
        return jnp.where(col==15,0.0,pltpu.roll(v,127,0)).astype(bf)
    s00,s01,s10,s11=dz,left(z32),down.astype(bf),left(down)
    W=lambda a,c: wd[CH*(3*a+c):CH*(3*a+c)+CH]
    def put(a,c,v):
        for i in range(8):
            put3(gout,every((2*i+a)*32+c,16,2),v[16*i:16*i+16])
    put(0,0,nt(s00,W(1,1)))
    put(0,1,nt(s00,W(1,2))+nt(s01,W(1,0)))
    put(1,0,nt(s00,W(2,1))+nt(s10,W(0,1)))
    put(1,1,nt(s00,W(2,2))+nt(s01,W(2,0))+nt(s10,W(0,2))+nt(s11,W(0,0)))
    gp=ld(gout,pl.ds(0,PX)).astype(bf)
    gv[R_PROJ:R_DOWN]=nn(attT[...],gp).astype(bf)
    dattT[...]=nt(wv[R_PROJ:R_DOWN],gp).astype(bf)
    def bh(h,_):
        r0=pl.multiple_of(h*192,64); r1=pl.multiple_of(r0+64,64); r2=pl.multiple_of(r0+128,64)
        qT=trT[pl.ds(r0,64),0:PX]
        kT=trT[pl.ds(r1,64),:]
        k=kT.T
        v=trT[pl.ds(r2,64),:].T
        gT=dattT[pl.ds(pl.multiple_of(h*64,64),64),:]
        for c in range(PX//QC):
            qs=slice(QC*c,QC*c+QC)
            s=nn(k,qT[:,qs])*0.125
            pr=jnp.exp(s-lse[h,0:1,qs])
            dp=nn(v,gT[:,qs])
            de=jnp.sum(pr*dp,0,keepdims=True)
            ds=(pr*(dp-de)).astype(bf)
            dk=nt(qT[:,qs],ds)*0.125; dv=nt(gT[:,qs],pr.astype(bf))
            if c==0: dkv[0:64]=dk; dkv[64:128]=dv
            else: dkv[0:64]+=dk; dkv[64:128]+=dv
            dtrT[pl.ds(r0,64),qs]=(nn(kT,ds)*0.125).astype(bf)
        dtrT[pl.ds(r0,64),PX:2*PX]=jnp.zeros((64,PX),bf)
        dtrT[pl.ds(r1,64),:]=dkv[0:64].astype(bf)
        dtrT[pl.ds(r2,64),:]=dkv[64:128].astype(bf)
        return 0
    lax.fori_loop(0,6,bh,0)
    oth[1:17]=tn(dtrT[:,PX:2*PX],wqT[...]).astype(bf).reshape(16,32,CH)
    c1=xchg(oth.at[pl.ds(1,16)],oth.at[pl.ds(17,16)])
    gai[...]=tn(dtrT[:,0:PX],wqT[...])
    dq=nt(ain[...].T,dtrT[...])
    for j in range(3):
        put3(cvt,every(j,CH,3),dq[:,CH*j:CH*j+CH])
    gv[R_QKV:R_PROJ]=ld(cvt,pl.ds(0,1152)).astype(bf)
    c1.wait()
    def n3_of(i): return (middle[pl.ds(i,64)]-mean3)*inv3
    def s3(i,c):
        j=pl.multiple_of(17+lax.div(i,32),1)
        v=gai[pl.ds(i,64)]+oth[pl.ds(j,2)].reshape(64,CH).astype(f32)
        gai[pl.ds(i,64)]=v
        return c[0]+col8(v),c[1]+col8(v*n3_of(i))
    a1,a2=cloop(PX,64,s3,(Z8(),Z8()))
    db3,dg3=row(a1),row(a2)
    c1=swap_sums(3,db3*g3,dg3*g3)
    c1.wait()
    m1,m2=total_sums(3)
    def f3(i,_):
        v=ld(gout,pl.ds(i,64))+inv3*(gai[pl.ds(i,64)]*g3-m1-n3_of(i)*m2)
        fill3(z3,pl.multiple_of(i+32,32),v)
        return 0
    cloop(PX,64,f3,0)
    zedge=pl.ds(pl.multiple_of(q*480+32,32),32)
    hsend[1]=z3[zedge,CH:2*CH]
    c1=xchg(hsend.at[1],oth.at[33])
    conv_dw(x3b,z3[32:32+PX,CH:2*CH],R_TWO)
    store_two=pltpu.make_async_copy(gv.at[pl.ds(R_TWO,R_DOWN-R_TWO)],grad_ref.at[pl.ds(R_TWO,R_DOWN-R_TWO)],gsem.at[1])
    store_two.start()
    c1.wait()
    fill_edges(z3,oth[33].astype(f32))
    conv_dx(gsec,R_TWO)
    def s2(i,c):
        n,af,pb=pre_b(inner[pl.ds(i,64)])
        gpre=gsec[pl.ds(i,64)]*slope(pb)
        gaff=gpre*sc1
        gsec[pl.ds(i,64)]=gaff
        return c[0]+col8(gpre*af),c[1]+col8(gpre),c[2]+col8(gaff*n),c[3]+col8(gaff)
    a1,a2,a3,a4=cloop(PX,64,s2,(Z8(),Z8(),Z8(),Z8()))
    dsc,dsh,dg2,db2=row(a1),row(a2),row(a3),row(a4)
    c1=swap_sums(4,db2*g2,dg2*g2)
    c1.wait()
    m1,m2=total_sums(4)
    def f2(i,_):
        n=(inner[pl.ds(i,64)]-mean2)*inv2
        fill3(z3,pl.multiple_of(i+32,32),inv2*(gsec[pl.ds(i,64)]*g2-m1-n*m2))
        return 0
    cloop(PX,64,f2,0)
    hsend[2]=z3[zedge,CH:2*CH]
    c1=xchg(hsend.at[2],oth.at[34])
    conv_dw(x3a,z3[32:32+PX,CH:2*CH],R_ONE)
    store_one=pltpu.make_async_copy(gv.at[pl.ds(0,R_TWO)],grad_ref.at[pl.ds(0,R_TWO)],gsem.at[2])
    store_one.start()
    c1.wait()
    fill_edges(z3,oth[34].astype(f32))
    conv_dx(gsec,R_ONE)
    def s1(i,c):
        n=(img[pl.ds(i,64)].astype(f32)-mean1)*inv1
        gpre=gsec[pl.ds(i,64)]*slope(n*g1+b1)
        return c[0]+col8(gpre*n),c[1]+col8(gpre)
    a1,a2=cloop(PX,64,s1,(Z8(),Z8()))
    ge=[]
    for h in range(2):
        d=exact(jnp.broadcast_to(dsc,(16,CH)),wee[CH*h:CH*h+CH],nt)+exact(jnp.broadcast_to(dsh,(16,CH)),weo[CH*h:CH*h+CH],nt)
        ge.append(d[0:1]*slope(pre[h]))
    hot_level=(lax.broadcasted_iota(jnp.int32,(1,CH),1)==level[...]).astype(f32)
    aux_ref[...]=jnp.concatenate([row(a1),row(a2),dg2,db2,dg3,db3,dsc,dsh,ge[0],ge[1],emb[0],emb[1],consist*hot_level,jnp.broadcast_to(ids.astype(f32),(1,CH)),0.5*hot_level,jnp.zeros((1,CH),f32)],0)
    store_down.wait(); store_two.wait(); store_one.wait()

def core(images_all,G,img,tgt,cln,vgg,lin,tvec,rowid,level,gm):
    D=pltpu.SemaphoreType.DMA
    V=lambda *s: pltpu.VMEM(s,bf)
    F=lambda *s: pltpu.VMEM(s,f32)
    vm=pl.BlockSpec(memory_space=pltpu.VMEM)
    import functools
    return pl.pallas_call(functools.partial(core_kernel,images_all),
        out_shape=(jax.ShapeDtypeStruct((GROWS,CH),bf),jax.ShapeDtypeStruct((16,CH),f32)),
        in_specs=[pl.BlockSpec(memory_space=pl.ANY)]+[vm]*9,
        out_specs=(pl.BlockSpec(memory_space=pl.ANY),vm),
        scratch_shapes=[V(17184,CH),V(32,32,CH),F(3,1536,128),F(5,CH,128),V(3456,CH2),V(768,CH),V(768,CH),V(1152,CH),V(576,1152),V(576,1152),V(576,1152),
            F(PX,CH),F(PX,CH),F(3,PX,128),F(PX,CH),F(3,PX,128),V(1024,CH),V(1152,1024),V(1152,1024),V(CH,PX),V(R_DOWN,CH),V(128,3456),F(6,8,PX),F(PX,CH),V(CH,PX),F(128,1024),
            F(5,8,CH),F(5,8,CH),V(3,32,CH),F(1,32,CH),V(32,CH),V(16,CH2),V(16,CH2),F(3,32,128),V(35,32,CH),
            D((32,)),D,D((3,)),D((16,)),D((16,))],
        compiler_params=pltpu.CompilerParams(collective_id=2,has_side_effects=True,vmem_limit_bytes=62<<20),
        name="image_step",
    )(G,img,tgt,cln,vgg,lin,tvec,rowid,level,gm)
LAST=25
f32=jnp.float32
def rs_kernel(g_ref, pack_ref, flat_ref, all_ref, total, lpk, ppk, ex, red1, red2, tile, lps, lpr, pps, ppr, n1s, n1r, n2s, n2r, own, sibr, ra, rb, rx, ry, zu, zd, ld, s1s, s1r, das, dar, dbs, dbr, xs, xr, ys, yr, zs, zur, zdr):
    b,p,core,y,z=place()
    s=b*2+p
    yn=b+2-4*y; sib=b+1-2*core; xn=1-p
    up_ok=z<3; dn_ok=z>0
    barrier=pltpu.get_barrier_semaphore()
    def sig(bb,pp): pl.semaphore_signal(barrier,inc=1,device_id=(bb,pp),device_id_type=MESH)
    mine=(y*2+core)*2+p
    plane=[]
    for dy in range(2):
        for dc in range(2):
            for dp in range(2):
                if dy+dc+dp: plane.append((4*dy+2*dc+dp,z*4+lax.rem(y+dy,2)*2+lax.rem(core+dc,2),lax.rem(p+dp,2)))
    line=[(k,lax.rem(z+k,4)) for k in range(1,4)]
    for _,bb,pp in plane: sig(bb,pp)
    for _,zz in line: sig(b+4*(zz-z),p)
    def slot(zz,yy,pp,cc=core): return ((zz*2+yy)*2+cc)*2+pp
    def rows(sl): return g_ref.at[pl.ds(pl.multiple_of(16*lax.div(ROWS*sl,16),16),BLK)]
    def valid(zz): return (zz>=0)&(zz<4)
    def each(k):
        if k==0: return [(None,z,0)]
        return [(valid(z-k),z-k,-1),(valid(z+k),z+k,1)]
    def AND(*c):
        r=None
        for q in c:
            if q is not None: r=q if r is None else r&q
        return r
    def when(ok,f):
        if ok is None: f()
        else: pl.when(ok)(f)
    def need(zz,yy,pp,cc=core): return slot(zz,yy,pp,cc)<=LAST
    order=[3,2,1,0]
    four=((1-y,xn),(y,xn),(1-y,p),(y,p))
    def local(zz,yy,pp):
        return pltpu.make_async_copy(rows(slot(zz,yy,pp)),own.at[zz,yy,pp],ld.at[zz,yy,pp])
    for k in order:
        for ok,zz,_ in each(k):
            for yy,pp in four:
                when(AND(ok,need(zz,yy,pp)),lambda: local(zz,yy,pp).start())
    pl.semaphore_wait(barrier,10)
    cm=Comm()
    top=z==3
    low=jnp.logical_not(top)
    cm.go(low,pack_ref,lpk.at[z],lps,lpr.at[z],b+4*(3-z),p)
    oc=1-core
    for k in order:
        for ok,zz,_ in each(k):
            for yy,pp in four:
                cm.go(AND(ok,need(zz,yy,pp,oc)),rows(slot(zz,yy,pp,oc)),sibr.at[zz,yy,pp],s1s.at[zz,yy,pp],s1r.at[zz,yy,pp],sib,p)
    def wait_in(ref,sem):
        pltpu.make_async_remote_copy(src_ref=ref,dst_ref=ref,send_sem=sem,recv_sem=sem,device_id=(b,xn),device_id_type=MESH).wait_recv()
    A=pl.ds(0,HALF); B=pl.ds(HALF,BLK-HALF)
    def ready(zz,yy,pp):
        local(zz,yy,pp).wait()
        wait_in(sibr.at[zz,yy,pp],s1r.at[zz,yy,pp])
    def stage1(k):
        for ok,zz,_ in each(k):
            yy,pp=1-y,xn
            c=AND(ok,need(zz,yy,pp))
            def f():
                ready(zz,yy,pp)
                own[zz,yy,pp]=(own[zz,yy,pp].astype(f32)+sibr[zz,yy,pp].astype(f32)).astype(jnp.bfloat16)
            when(c,f)
            cm.go(c,own.at[zz,yy,pp,A],ra.at[zz],das.at[zz],dar.at[zz],b,xn)
            cm.go(c,own.at[zz,yy,pp,B],rb.at[zz],dbs.at[zz],dbr.at[zz],yn,p)
    def stage2(k):
        for ok,zz,_ in each(k):
            yy,pp=y,xn
            c=AND(ok,need(zz,yy,pp))
            def f():
                ready(zz,yy,pp)
                own[zz,yy,pp,A]=(own[zz,yy,pp,A].astype(f32)+sibr[zz,yy,pp,A].astype(f32)).astype(jnp.bfloat16)
                wait_in(rb.at[zz],dbr.at[zz])
                own[zz,yy,pp,B]=(own[zz,yy,pp,B].astype(f32)+sibr[zz,yy,pp,B].astype(f32)+rb[zz].astype(f32)).astype(jnp.bfloat16)
            when(c,f)
            cm.go(c,own.at[zz,yy,pp],rx.at[zz],xs.at[zz],xr.at[zz],b,xn)
            yy2,pp2=1-y,p
            c2=AND(ok,need(zz,yy2,pp2))
            def f2():
                ready(zz,yy2,pp2)
                own[zz,yy2,pp2,B]=(own[zz,yy2,pp2,B].astype(f32)+sibr[zz,yy2,pp2,B].astype(f32)).astype(jnp.bfloat16)
                wait_in(ra.at[zz],dar.at[zz])
                own[zz,yy2,pp2,A]=(own[zz,yy2,pp2,A].astype(f32)+sibr[zz,yy2,pp2,A].astype(f32)+ra[zz].astype(f32)).astype(jnp.bfloat16)
            when(c2,f2)
            cm.go(c2,own.at[zz,yy2,pp2],ry.at[zz],ys.at[zz],yr.at[zz],yn,p)
    def stage3(k):
        for ok,zz,d in each(k):
            c=AND(ok,need(zz,y,p))
            def f():
                ready(zz,y,p)
                wait_in(rx.at[zz],xr.at[zz])
                wait_in(ry.at[zz],yr.at[zz])
                t=own[zz,y,p].astype(f32)+sibr[zz,y,p].astype(f32)+rx[zz].astype(f32)+ry[zz].astype(f32)
                if k>0: own[zz,y,p]=t.astype(jnp.bfloat16)
                else: total[...]=t
            when(c,f)
            if k>0:
                behind=dn_ok if d==1 else up_ok
                zbuf,zsem=(zu,zur) if d==1 else (zd,zdr)
                def f2():
                    wait_in(zbuf.at[zz],zsem.at[zz])
                    own[zz,y,p]=(own[zz,y,p].astype(f32)+zbuf[zz].astype(f32)).astype(jnp.bfloat16)
                if k<3: when(AND(c,behind),f2)
                cm.go(c,own.at[zz,y,p],zbuf.at[zz],zs.at[zz],zsem.at[zz],b+4*d,p)
            else:
                def f3():
                    wait_in(zu.at[zz],zur.at[zz])
                    total[...]+=zu[zz].astype(f32)
                def f4():
                    wait_in(zd.at[zz],zdr.at[zz])
                    total[...]+=zd[zz].astype(f32)
                when(AND(c,dn_ok),f3)
                when(AND(c,up_ok),f4)
    n=len(order)
    for i in range(n+2):
        if i<n: stage1(order[i])
        if 0<=i-1<n: stage2(order[i-1])
        if 0<=i-2<n: stage3(order[i-2])
    pl.when(jnp.logical_not(need(z,y,p)))(lambda: total.__setitem__(Ellipsis,jnp.zeros(total.shape,f32)))

    def packs_line():
        lpk[3]=pack_ref[...]
        for zz in range(3): wait_in(lpk.at[zz],lpr.at[zz])
    pl.when(top)(packs_line)
    for d,bb,pp in plane:
        cm.go(top,lpk,ppk.at[mine],pps.at[d],ppr.at[mine],bb,pp)
    def packs_plane():
        ppk[mine]=lpk[...]
        for d,bb,pp in plane:
            o=(lax.rem(lax.div(bb,2),2)*2+lax.rem(bb,2))*2+pp
            wait_in(ppk.at[o],ppr.at[o])
        a_s=16*lax.div(ROWS*s,16)
        rows_at=lambda k: ppk[:,:,k,:].reshape(32,384)
        zero=jnp.zeros((64,384),f32)
        for h in range(2):
            e=rows_at(10+h)
            t=jnp.concatenate([e,e,zero],0).T
            ex[pl.ds(BLK+768*h,384,stride=2),:]=t
            ex[pl.ds(BLK+768*h+1,384,stride=2),:]=t
        r=a_s+lax.broadcasted_iota(jnp.int32,(BLK,128),0)
        l=lax.broadcasted_iota(jnp.int32,(BLK,128),1)
        inside=(r>=R_EMB)&(r<R_TAB)
        start=pl.multiple_of(jnp.clip(a_s-R_EMB+BLK,0,BLK+1536),16)
        lf=jnp.where(inside&(((r&1)==1)==(l>=32))&(l<64),ex[pl.ds(start,BLK),:],0.0)
        ids=rows_at(13)[:,0:128].astype(jnp.int32)
        ids=jnp.concatenate([ids]*4,0).astype(f32).T[0:1].astype(jnp.int32)
        hot=(r-R_TAB==2*ids+(l>=96).astype(jnp.int32))&(l>=64)&(r>=R_TAB)
        lf=jnp.where(hot,1.0,lf)
        rg=jnp.concatenate([rows_at(6),rows_at(7),rows_at(8),rows_at(9)],0)
        gains=[jnp.sum(rows_at(k),0,keepdims=True) for k in range(6)]
        hi=lax.Precision.HIGHEST
        add=lax.dot_general(lf,rg,(((1,),(0,)),((),())),precision=hi,preferred_element_type=f32)
        for k in range(6): add=add+jnp.where(r[:,0:1]-R_GAIN==k,gains[k],0.0)
        rr=a_s+lax.broadcasted_iota(jnp.int32,(BLK,384),0)
        total[...]=jnp.where(rr<R_EMB,total[...],add)
    pl.when(top)(packs_plane)
    shift=lax.rem(9*s,16)
    t=pltpu.roll(total[...],lax.rem(BLK-shift,BLK),0)[0:ROWS]
    for j in range(3): flat_ref[pl.ds(j,ROWS,stride=3),:]=t[:,128*j:128*j+128]
    sq=jnp.sum(jnp.sum(t*t,0,keepdims=True),1,keepdims=True)
    tile[...]=jnp.concatenate([jnp.broadcast_to(sq,(1,128)),pack_ref[12:13,0:128],pack_ref[14:15,0:128],jnp.zeros((5,128),f32)],0)
    red1[mine]=tile[...]
    for d,bb,pp in plane: cm.go(None,tile,red1.at[mine],n1s.at[d],n1r.at[mine],bb,pp)
    for d,bb,pp in plane:
        o=(lax.rem(lax.div(bb,2),2)*2+lax.rem(bb,2))*2+pp
        wait_in(red1.at[o],n1r.at[o])
    v=red1[0]
    for k in range(1,8): v=v+red1[k]
    red2[z]=v
    for k,zz in line: cm.go(None,red2.at[z],red2.at[z],n2s.at[k],n2r.at[z],b+4*(zz-z),p)
    for k,zz in line: wait_in(red2.at[zz],n2r.at[zz])
    all_ref[...]=red2[0]+red2[1]+red2[2]+red2[3]
    cm.drain()

def reduce_scatter(g,pack):
    D=pltpu.SemaphoreType.DMA
    V=lambda *s: pltpu.VMEM(s,jnp.bfloat16)
    F=lambda *s: pltpu.VMEM(s,f32)
    return pl.pallas_call(rs_kernel,
        out_shape=(jax.ShapeDtypeStruct((1611,128),f32),jax.ShapeDtypeStruct((8,128),f32)),
        in_specs=[pl.BlockSpec(memory_space=pl.ANY),pl.BlockSpec(memory_space=pltpu.VMEM)],
        out_specs=(pl.BlockSpec(memory_space=pltpu.VMEM),)*2,
        scratch_shapes=[F(BLK,384),F(4,16,384),F(8,4,16,384),F(2*BLK+1536,128),F(8,8,128),F(4,8,128),F(8,128),D,D((4,)),D((8,)),D((8,)),D((8,)),D((8,)),D((4,)),D((4,)),
            V(4,2,2,BLK,384),V(4,2,2,BLK,384),V(4,HALF,384),V(4,BLK-HALF,384),V(4,BLK,384),V(4,BLK,384),V(4,BLK,384),V(4,BLK,384),
            D((4,2,2)),D((4,2,2)),D((4,2,2)),D((4,)),D((4,)),D((4,)),D((4,)),D((4,)),D((4,)),D((4,)),D((4,)),D((4,)),D((4,)),D((4,))],
        compiler_params=pltpu.CompilerParams(collective_id=1,has_side_effects=True,vmem_limit_bytes=50<<20),
        name="scatter_gradient",
    )(g,pack)


def fast(images, target, clean_images, levels, labels, null_mask, vgg_proj, lpips_lin, master, first_moment, second_moment):
    is_zero = (levels == 0).astype(jnp.float32).reshape(1, 1)
    row_index = jnp.where(null_mask == 1, CLASSES, labels).reshape(1, 1)
    tvec = time_vector(levels)
    gathered = all_gather_weights(master.reshape(1611, 128), is_zero)
    lane = jnp.arange(CH, dtype=jnp.int32) // 12
    gm = (lane[:, None] == lane[None, :]).astype(jnp.bfloat16)
    grad, pack = core(
        16,
        gathered,
        images.reshape(PX, CH),
        target.reshape(128, CH2),
        clean_images.reshape(128, CH2),
        vgg_proj,
        lpips_lin.reshape(1, 256),
        tvec,
        row_index,
        levels.reshape(1, 1),
        gm,
    )
    own_grad, sums = reduce_scatter(grad, pack)
    own_grad = own_grad.reshape(-1)
    level_sums = sums[1:3, :LEVELS]
    norm_before = jnp.sqrt(sums[0, 0])
    clipped = own_grad * jnp.minimum(1.0, CLIP / norm_before)
    new_first = BETA_ONE * first_moment + (1.0 - BETA_ONE) * clipped
    new_second = BETA_TWO * second_moment + (1.0 - BETA_TWO) * clipped * clipped
    fixed_first = new_first / (1.0 - BETA_ONE**STEP)
    fixed_second = new_second / (1.0 - BETA_TWO**STEP)
    new_master = master - RATE * (fixed_first / (jnp.sqrt(fixed_second) + EPS_ADAM) + DECAY * master)
    return (new_master, new_first, new_second, new_master.astype(jnp.bfloat16), norm_before, level_sums)


def solution(mesh):
    small = mesh.shape["batch"] == 16 and mesh.shape["pix"] == 2
    return jax.shard_map(
        fast if small else local,
        mesh=mesh,
        in_specs=(
            P("batch", "pix", None, None),
            P("batch", "pix", None, None),
            P("batch", "pix", None, None),
            P("batch"),
            P("batch"),
            P("batch"),
            P(),
            P(),
            P(("batch", "pix")),
            P(("batch", "pix")),
            P(("batch", "pix")),
        ),
        out_specs=(
            P(("batch", "pix")),
            P(("batch", "pix")),
            P(("batch", "pix")),
            P(("batch", "pix")),
            P(),
            P(),
        ),
        check_vma=False,
    )
```

```python
import functools
import math

import jax
import jax.numpy as jnp
from jax import lax
from jax.experimental import pallas as pl
from jax.experimental.pallas import tpu as pltpu
from jax.sharding import PartitionSpec as P

CH = 384
CH2 = 576
GROUPS = 32
HEAD = 64
TEMB = 768
CLASSES = 1000
LEVELS = 40
STEP = 10


EPS_NORM = 1e-05
EPS_FEAT = 1e-06
BETA_ONE = 0.9
BETA_TWO = 0.999
EPS_ADAM = 1e-08
RATE = 0.02
DECAY = 0.01
CLIP = 0.01
precise = lax.Precision.HIGHEST


def extended(shard, sides, width):
    for axis, dim in sides:
        size, length = (lax.axis_size(axis), shard.shape[dim])
        up = [(i, (i + 1) % size) for i in range(size - 1)]
        down = [(j, i) for i, j in up]
        last = lax.slice_in_dim(shard, length - width, length, axis=dim)
        initial = lax.slice_in_dim(shard, 0, width, axis=dim)
        before = lax.ppermute(last, axis, up)
        after = lax.ppermute(initial, axis, down)
        shard = jnp.concatenate([before, shard, after], axis=dim)
    return shard


def unpack(flat_vec):
    layout = [
        (9 * CH, CH),
        (9 * CH, CH),
        (CH, 3 * CH),
        (CH, CH),
        (9 * CH, CH2),
        (TEMB, 2 * CH),
        (CLASSES + 1, TEMB),
        (6, CH),
    ]
    pieces = []
    offset = 0
    for rows_n, cols_n in layout:
        pieces.append(flat_vec[offset : offset + rows_n * cols_n].reshape(rows_n, cols_n))
        offset += rows_n * cols_n
    return (pieces, offset)


def time_vector(level_ids):
    half_width = TEMB // 2
    frequency = jnp.exp(-math.log(10000.0) * jnp.arange(half_width, dtype=jnp.float32) / half_width)
    angles = level_ids.astype(jnp.float32)[..., None] * (1000.0 / LEVELS) * frequency
    return jnp.concatenate([jnp.cos(angles), jnp.sin(angles)], -1)


def silu_slope(values):
    sigmoid = jax.nn.sigmoid(values)
    return sigmoid * (1.0 + values * (1.0 - sigmoid))


def pix_sums(pair_sums):
    return lax.psum((pair_sums[0], pair_sums[1]), "pix")


def group_forward(values, pixels_all):
    grouped = values.reshape(values.shape[0], values.shape[1], GROUPS, -1)
    totals = pix_sums((jnp.sum(grouped, (1, 3)), jnp.sum(grouped * grouped, (1, 3))))
    per_group = pixels_all * grouped.shape[3]
    center = totals[0] / per_group
    spread = totals[1] / per_group - center * center
    inverse = lax.rsqrt(spread + EPS_NORM)
    normed = (grouped - center[:, None, :, None]) * inverse[:, None, :, None]
    return (normed.reshape(values.shape), inverse)


def group_backward(grad_normed, normed, inverse, pixels_all):
    grad_grouped = grad_normed.reshape(normed.shape[0], normed.shape[1], GROUPS, -1)
    val_grouped = normed.reshape(grad_grouped.shape)
    totals = pix_sums((jnp.sum(grad_grouped, (1, 3)), jnp.sum(grad_grouped * val_grouped, (1, 3))))
    per_group = pixels_all * grad_grouped.shape[3]
    result = (
        grad_grouped
        - (totals[0] / per_group)[:, None, :, None]
        - val_grouped * (totals[1] / per_group)[:, None, :, None]
    )
    return (result * inverse[:, None, :, None]).reshape(normed.shape)


def columns_of(values, stride):
    rows_out = values.shape[1] // stride
    cols_out = values.shape[2] // stride
    span_rows = stride * (rows_out - 1) + 1
    span_cols = stride * (cols_out - 1) + 1
    padded = extended(values, (("pix", 1),), 1)
    padded = jnp.pad(padded, ((0, 0), (0, 0), (1, 1), (0, 0)))
    return jnp.concatenate(
        [
            padded[
                :, row_off : row_off + span_rows : stride, col_off : col_off + span_cols : stride, :
            ]
            for row_off in range(3)
            for col_off in range(3)
        ],
        -1,
    )


def conv_forward(values, weight, rows_in, stride):
    n_img, pixels_in, in_chan = values.shape
    columns = columns_of(values.reshape(n_img, rows_in, -1, in_chan), stride)
    result = jnp.dot(columns.reshape(-1, 9 * in_chan), weight, preferred_element_type=jnp.float32)
    return (result.reshape(n_img, -1, weight.shape[1]), columns)


def conv_back(columns, grad_low, weight, rows_in, stride):
    n_img, pix_out, out_chan = grad_low.shape
    in_chan = weight.shape[0] // 9
    d_weight = jnp.einsum(
        "rk,rc->kc",
        columns.reshape(-1, 9 * in_chan),
        grad_low.reshape(-1, out_chan),
        preferred_element_type=jnp.float32,
    )
    flipped = (
        weight.reshape(3, 3, in_chan, out_chan)[::-1, ::-1]
        .transpose(0, 1, 3, 2)
        .reshape(9 * out_chan, in_chan)
    )
    rows_out = rows_in // stride
    grid_grad = grad_low.reshape(n_img, rows_out, pix_out // rows_out, out_chan)
    if stride > 1:
        grid_grad = jnp.pad(
            grid_grad[:, :, None, :, None, :],
            ((0, 0), (0, 0), (0, stride - 1), (0, 0), (0, stride - 1), (0, 0)),
        )
        grid_grad = grid_grad.reshape(n_img, rows_in, -1, out_chan)
    grad_columns = columns_of(grid_grad, 1)
    grad_input = jnp.dot(
        grad_columns.reshape(-1, 9 * out_chan), flipped, preferred_element_type=jnp.float32
    )
    return (d_weight, grad_input.reshape(n_img, -1, in_chan))


def res_forward(values, gain_rows, scale, shift, w_first, w_second, rows_in, pixels_all):
    normed_a, inverse_a = group_forward(values, pixels_all)
    pre_a = normed_a * gain_rows[0] + gain_rows[1]
    act_a = jax.nn.silu(pre_a).astype(jnp.bfloat16)
    inner, columns_a = conv_forward(act_a, w_first, rows_in, 1)
    normed_b, inverse_b = group_forward(inner, pixels_all)
    affine_b = normed_b * gain_rows[2] + gain_rows[3]
    pre_b = affine_b * (1.0 + scale) + shift
    second = jax.nn.silu(pre_b).astype(jnp.bfloat16)
    branch, columns_b = conv_forward(second, w_second, rows_in, 1)
    kept_state = (
        normed_a,
        inverse_a,
        pre_a,
        columns_a,
        normed_b,
        inverse_b,
        affine_b,
        pre_b,
        columns_b,
    )
    return (values + branch, kept_state)


def res_back(grad_result, kept_state, gain_rows, scale, w_first, w_second, rows_in, pixels_all):
    normed_a, inverse_a, pre_a, columns_a, normed_b, inverse_b, affine_b, pre_b, columns_b = (
        kept_state
    )
    d_w_second, grad_second = conv_back(
        columns_b, grad_result.astype(jnp.bfloat16), w_second, rows_in, 1
    )
    grad_pre_b = grad_second * silu_slope(pre_b)
    d_scale = jnp.sum(grad_pre_b * affine_b, 1)
    d_shift = jnp.sum(grad_pre_b, 1)
    grad_affine = grad_pre_b * (1.0 + scale)
    d_gain_b = jnp.sum(grad_affine * normed_b, (0, 1))
    d_bias_b = jnp.sum(grad_affine, (0, 1))
    grad_inner = group_backward(grad_affine * gain_rows[2], normed_b, inverse_b, pixels_all).astype(
        jnp.bfloat16
    )
    d_w_first, grad_act = conv_back(columns_a, grad_inner, w_first, rows_in, 1)
    grad_pre_a = grad_act * silu_slope(pre_a)
    d_gain_a = jnp.sum(grad_pre_a * normed_a, (0, 1))
    d_bias_a = jnp.sum(grad_pre_a, (0, 1))
    grad_values = None
    d_gains = jnp.stack([d_gain_a, d_bias_a, d_gain_b, d_bias_b])
    return (d_w_first, d_w_second, d_gains, d_scale, d_shift, grad_values)


def to_heads(values):
    return lax.all_to_all(values, "pix", split_axis=2, concat_axis=1, tiled=True)


def to_pixels(values):
    return lax.all_to_all(values, "pix", split_axis=1, concat_axis=2, tiled=True)


def flat_heads(values):
    return values.reshape(-1, values.shape[2], values.shape[3])


def attend(queries, keys, values):
    root_dim = math.sqrt(queries.shape[-1])

    def single(bundle):
        q_one, k_one, v_one = bundle
        scores = (
            jnp.einsum("qd,kd->qk", q_one, k_one, preferred_element_type=jnp.float32) / root_dim
        )
        row_peak = jnp.max(scores, -1, keepdims=True)
        exp_scores = jnp.exp(scores - row_peak)
        sum_exp = jnp.sum(exp_scores, -1, keepdims=True)
        probabilities = (exp_scores / sum_exp).astype(jnp.bfloat16)
        attended = jnp.einsum("qk,kd->qd", probabilities, v_one, preferred_element_type=jnp.float32)
        return (attended.astype(jnp.bfloat16), row_peak + jnp.log(sum_exp))

    attended, log_total = lax.map(
        single, (flat_heads(queries), flat_heads(keys), flat_heads(values))
    )
    return (attended.reshape(queries.shape), log_total)


def attend_back(queries, keys, values, log_total, grad_out):
    root_dim = math.sqrt(queries.shape[-1])

    def single(bundle):
        q_one, k_one, v_one, lse_one, g_one = bundle
        scores = (
            jnp.einsum("qd,kd->qk", q_one, k_one, preferred_element_type=jnp.float32) / root_dim
        )
        probabilities = jnp.exp(scores - lse_one)
        grad_v = jnp.einsum(
            "qk,qd->kd",
            probabilities.astype(jnp.bfloat16),
            g_one,
            preferred_element_type=jnp.float32,
        )
        grad_p = jnp.einsum("qd,kd->qk", g_one, v_one, preferred_element_type=jnp.float32)
        inner_sum = jnp.sum(probabilities * grad_p, -1, keepdims=True)
        grad_s = (probabilities * (grad_p - inner_sum)).astype(jnp.bfloat16)
        grad_q = (
            jnp.einsum("qk,kd->qd", grad_s, k_one, preferred_element_type=jnp.float32) / root_dim
        )
        grad_k = (
            jnp.einsum("qk,qd->kd", grad_s, q_one, preferred_element_type=jnp.float32) / root_dim
        )
        return (grad_q, grad_k, grad_v)

    grad_q, grad_k, grad_v = lax.map(
        single,
        (
            flat_heads(queries),
            flat_heads(keys),
            flat_heads(values),
            log_total,
            flat_heads(grad_out),
        ),
    )
    return (grad_q.reshape(queries.shape), grad_k.reshape(keys.shape), grad_v.reshape(values.shape))


def local(
    images,
    target,
    clean_images,
    levels,
    labels,
    null_mask,
    vgg_proj,
    lpips_lin,
    master,
    first_moment,
    second_moment,
):
    gathered = lax.all_gather(master.astype(jnp.bfloat16), ("batch", "pix"), axis=0, tiled=True)
    pieces, used_len = unpack(gathered)
    w_one, w_two, w_qkv, w_proj, w_down, w_emb, class_table, gains_low = pieces
    gains_one = gains_low.astype(jnp.float32)
    n_img, rows_local, cols_local, channels = images.shape
    wide_channels = w_down.shape[1]
    pix_count = lax.axis_size("pix")
    batch_count = lax.axis_size("batch")
    pixels_here = rows_local * cols_local
    pixels_all = pixels_here * pix_count
    pixels_all_two = pixels_all // 4
    images_all = n_img * batch_count
    row_index = jnp.where(null_mask == 1, class_table.shape[0] - 1, labels)
    one_hot = (
        row_index[:, None] == jnp.arange(class_table.shape[0], dtype=jnp.int32)[None, :]
    ).astype(jnp.float32)
    pre_embed = time_vector(levels) + jnp.dot(
        one_hot, class_table.astype(jnp.float32), precision=precise
    )
    embedded = jax.nn.silu(pre_embed)
    w_emb_wide = w_emb.astype(jnp.float32)
    scale_shift = jnp.dot(embedded, w_emb_wide, precision=precise)
    scale_one = scale_shift[:, None, :channels]
    shift_one = scale_shift[:, None, channels:]
    flat_in = images.astype(jnp.float32).reshape(n_img, pixels_here, channels)
    middle, kept_one = res_forward(
        flat_in, gains_one, scale_one, shift_one, w_one, w_two, rows_local, pixels_all
    )
    normed_three, inverse_three = group_forward(middle, pixels_all)
    attn_in = (normed_three * gains_one[4] + gains_one[5]).astype(jnp.bfloat16)
    triples = jnp.dot(attn_in.reshape(-1, channels), w_qkv, preferred_element_type=jnp.float32)
    triples = triples.astype(jnp.bfloat16).reshape(n_img, pixels_here, 3 * channels)
    spread_heads = to_heads(triples)
    local_heads = spread_heads.shape[2] // (3 * HEAD)
    split_heads = spread_heads.reshape(n_img, -1, local_heads, 3, HEAD).transpose(3, 0, 2, 1, 4)
    queries, keys, values = (split_heads[0], split_heads[1], split_heads[2])
    attended, log_total = attend(queries, keys, values)
    attended_px = to_pixels(attended.transpose(0, 2, 1, 3).reshape(n_img, -1, local_heads * HEAD))
    projected = jnp.dot(
        attended_px.reshape(-1, channels), w_proj, preferred_element_type=jnp.float32
    )
    output = middle + projected.reshape(n_img, pixels_here, channels)
    final_out, columns_down = conv_forward(output.astype(jnp.bfloat16), w_down, rows_local, 2)
    pixels_two = final_out.shape[1]
    feat_width = vgg_proj.shape[1]
    online_feat = jnp.dot(
        final_out.astype(jnp.bfloat16).reshape(-1, wide_channels),
        vgg_proj,
        preferred_element_type=jnp.float32,
    )
    online_feat = online_feat.reshape(n_img, pixels_two, feat_width)
    target_feat = jnp.dot(
        target.reshape(-1, wide_channels), vgg_proj, preferred_element_type=jnp.float32
    )
    target_feat = target_feat.reshape(n_img, pixels_two, feat_width)
    target_unit = target_feat * lax.rsqrt(
        jnp.mean(target_feat * target_feat, -1, keepdims=True) + EPS_FEAT
    )
    clean_wide = clean_images.astype(jnp.float32).reshape(n_img, pixels_two, wide_channels)

    def loss_terms(feature, out_value):
        unit = feature * lax.rsqrt(jnp.mean(feature * feature, -1, keepdims=True) + EPS_FEAT)
        consist = jnp.sum(lpips_lin * (unit - target_unit) ** 2, (1, 2)) / (
            feat_width * pixels_all_two
        )
        denoise = jnp.sum((out_value - clean_wide) ** 2, (1, 2)) / (pixels_all_two * wide_channels)
        return (consist, denoise)

    (consist, denoise), pullback = jax.vjp(loss_terms, online_feat, final_out)
    level_hot = (levels[:, None] == jnp.arange(LEVELS, dtype=jnp.int32)[None, :]).astype(
        jnp.float32
    )
    level_pair = lax.psum(
        (jnp.sum(consist[:, None] * level_hot, 0), jnp.sum(level_hot / pix_count, 0)),
        ("batch", "pix"),
    )
    zero_count = level_pair[1][0]
    is_zero = (levels == 0).astype(jnp.float32)
    grad_feat, grad_out = pullback(
        (jnp.full_like(consist, 1.0 / images_all), is_zero / jnp.maximum(zero_count, 1.0))
    )
    grad_feat_low = grad_feat.astype(jnp.bfloat16).reshape(-1, feat_width)
    grad_final = grad_out + jnp.einsum(
        "rf,cf->rc", grad_feat_low, vgg_proj, preferred_element_type=jnp.float32
    ).reshape(n_img, pixels_two, wide_channels)
    d_w_down, grad_output = conv_back(
        columns_down, grad_final.astype(jnp.bfloat16), w_down, rows_local, 2
    )
    grad_proj = grad_output.astype(jnp.bfloat16).reshape(-1, channels)
    d_w_proj = jnp.einsum(
        "rc,rd->cd",
        attended_px.reshape(-1, channels),
        grad_proj,
        preferred_element_type=jnp.float32,
    )
    grad_att_px = jnp.einsum("rd,cd->rc", grad_proj, w_proj, preferred_element_type=jnp.float32)
    grad_att_px = grad_att_px.astype(jnp.bfloat16).reshape(n_img, pixels_here, channels)
    grad_heads = to_heads(grad_att_px)
    grad_split = grad_heads.reshape(n_img, -1, local_heads, HEAD).transpose(0, 2, 1, 3)
    grad_q, grad_k, grad_v = attend_back(queries, keys, values, log_total, grad_split)
    grad_triples = jnp.stack([grad_q, grad_k, grad_v], 3).transpose(0, 2, 1, 3, 4)
    grad_triples = grad_triples.reshape(n_img, -1, local_heads * 3 * HEAD).astype(jnp.bfloat16)
    grad_triples = to_pixels(grad_triples)
    grad_rows = grad_triples.reshape(-1, 3 * channels)
    d_w_qkv = jnp.einsum(
        "rc,rd->cd", attn_in.reshape(-1, channels), grad_rows, preferred_element_type=jnp.float32
    )
    grad_attn_in = jnp.einsum(
        "rd,cd->rc", grad_rows, w_qkv, preferred_element_type=jnp.float32
    ).reshape(n_img, pixels_here, channels)
    d_gain_three = jnp.sum(grad_attn_in * normed_three, (0, 1))
    d_bias_three = jnp.sum(grad_attn_in, (0, 1))
    grad_middle = grad_output + group_backward(
        grad_attn_in * gains_one[4], normed_three, inverse_three, pixels_all
    )
    d_w_one, d_w_two, d_gains_one, d_scale_one, d_shift_one, unused_grad = res_back(
        grad_middle, kept_one, gains_one, scale_one, w_one, w_two, rows_local, pixels_all
    )
    grad_scale_shift = jnp.concatenate([d_scale_one, d_shift_one], 1)
    d_w_emb = jnp.dot(embedded.T, grad_scale_shift, precision=precise)
    grad_embedded = jnp.dot(grad_scale_shift, w_emb_wide.T, precision=precise)
    d_table = jnp.dot(one_hot.T, grad_embedded * silu_slope(pre_embed), precision=precise)
    d_norms_one = jnp.concatenate([d_gains_one, jnp.stack([d_gain_three, d_bias_three])], 0)
    flat_grad = jnp.concatenate(
        [
            d_w_one.ravel(),
            d_w_two.ravel(),
            d_w_qkv.ravel(),
            d_w_proj.ravel(),
            d_w_down.ravel(),
            d_w_emb.ravel(),
            d_table.ravel(),
            d_norms_one.ravel(),
            jnp.zeros((gathered.shape[0] - used_len,), jnp.float32),
        ]
    )
    own_grad = lax.psum_scatter(flat_grad, ("batch", "pix"), scatter_dimension=0, tiled=True)
    norm_before = jnp.sqrt(lax.psum(jnp.sum(own_grad * own_grad), ("batch", "pix")))
    clipped = own_grad * jnp.minimum(1.0, CLIP / norm_before)
    new_first = BETA_ONE * first_moment + (1.0 - BETA_ONE) * clipped
    new_second = BETA_TWO * second_moment + (1.0 - BETA_TWO) * clipped * clipped
    fixed_first = new_first / (1.0 - BETA_ONE**STEP)
    fixed_second = new_second / (1.0 - BETA_TWO**STEP)
    new_master = master - RATE * (
        fixed_first / (jnp.sqrt(fixed_second) + EPS_ADAM) + DECAY * master
    )
    level_sums = jnp.stack([level_pair[0], level_pair[1]])
    return (
        new_master,
        new_first,
        new_second,
        new_master.astype(jnp.bfloat16),
        norm_before,
        level_sums,
    )


MESH = pl.DeviceIdType.MESH
ROWS=537; BLK=560; HALF=288
PX=512
R_ONE,R_TWO,R_QKV,R_PROJ,R_DOWN,R_EMB,R_TAB,R_GAIN,R_END=0,3456,6912,8064,8448,13632,15168,17170,17184
f32=jnp.float32; bf=jnp.bfloat16
class Comm:
    def __init__(self): self.sent=[]
    def go(self, cond, src, dst, ssem, rsem, b, p):
        c = pltpu.make_async_remote_copy(src_ref=src,dst_ref=dst,send_sem=ssem,recv_sem=rsem,device_id=(b,p),device_id_type=MESH)
        if cond is None: c.start()
        else: pl.when(cond)(lambda: c.start())
        self.sent.append((cond,c))
    def drain(self):
        for cond,c in self.sent:
            if cond is None: c.wait_send()
            else: pl.when(cond)(lambda c=c: c.wait_send())
        self.sent=[]

def place():
    b=lax.axis_index("batch"); p=lax.axis_index("pix")
    core=lax.rem(b,2); y=lax.rem(lax.div(b,2),2); z=lax.div(b,4)
    return b,p,core,y,z

def base_of(s): return 16*((ROWS*s)//16)
def dg(a,b,ca,cb): return lax.dot_general(a,b,(((ca,),(cb,)),((),())),preferred_element_type=f32)
def nn(a,b): return dg(a,b,1,0)
def nt(a,b): return dg(a,b,1,1)
def tn(a,b): return dg(a,b,0,0)
def split3(v):
    hi=v.astype(bf); r=v-hi.astype(f32); mid=r.astype(bf); lo=(r-mid.astype(f32)).astype(bf)
    return hi,mid,lo
def exact(v,w,dot):
    hi,mid,lo=split3(v)
    return dot(hi,w)+dot(mid,w)+dot(lo,w)
def sigmoid(v): return 1.0/(1.0+jnp.exp(-v))
def silu(v): return v*sigmoid(v)
def slope(v):
    s=sigmoid(v)
    return s*(1.0+v*(1.0-s))
def cloop(n,chunk,body,init):
    return lax.fori_loop(0,n//chunk,lambda i,c: body(pl.multiple_of(i*chunk,chunk),c),init)
def col8(v): return jnp.sum(v.reshape(-1,8,v.shape[-1]),axis=0)
Z8=lambda: jnp.zeros((8,CH),f32)
class Blocks:
    def __init__(self,ref,n): self.ref=ref; self.n=n
def at_block(ref,j,sl):
    if isinstance(ref,Blocks): return ref.ref,(pl.ds(ref.n*j+sl.start,sl.size,stride=sl.stride),slice(None))
    return ref,(j,sl,slice(None))
def ld(ref,sl):
    out=[]
    for j in range(ref.ref.shape[0]//ref.n if isinstance(ref,Blocks) else ref.shape[0]):
        r,k=at_block(ref,j,sl)
        out.append(r[k])
    return jnp.concatenate(out,1)
def put3(ref,sl,v):
    for j in range(v.shape[1]//128):
        r,k=at_block(ref,j,sl)
        r[k]=v[:,128*j:128*j+128]
def every(start,n,step): return pl.ds(start,n,stride=step)
def row(v): return jnp.sum(v,axis=0,keepdims=True)


LAST=25
def step_kernel(images_all,
    mast,img,tgt,cln,vgg,lin,tvec,rowid,level,gm,
    flat_ref,all_ref,g_ref,
    wv,gv,tails,cvt,cvt2,wd,wee,weo,wqT,x3a,x3b,z3,inner,middle,gout,gsec,ain,trT,dtrT,attT,xd,lse,dattT,dkv,ssend,srecv,hsend,hrecv,himg,dzs,dzr,geo,oth,wsem,tsem,xs,xr,total,blk,own_sem,azs,azr,axs,axr,ays,ayr,adas,adar,adbs,adbr,ass,asr,ass2,asr2,pack_ref,lpk,ppk,red1,red2,tile,lps,lpr,pps,ppr,n1s,n1r,n2s,n2r,sibr,ra,rb,rx,ry,zu,zd,s1s,s1r,das,dar,dbs,dbr,rxs,rxr,rys,ryr,zs,zur,zdr):
    b,p,core,y,z=place()
    q=1-p; xn=q; s=b*2+p
    pf=p.astype(f32); qf=1.0-pf
    yn=b+2-4*y; sib=b+1-2*core; oc=1-core
    up_ok=z<3; dn_ok=z>0
    top=z==3
    mine=(y*2+core)*2+p
    cvt3=Blocks(cvt,1536)
    mcopy=pltpu.make_async_copy(mast,cvt.at[pl.ds(0,1611)],own_sem)
    mcopy.start()
    barrier=pltpu.get_barrier_semaphore()
    plane=[]
    for dy in range(2):
        for dc in range(2):
            for dp in range(2):
                if dy+dc+dp: plane.append((4*dy+2*dc+dp,z*4+lax.rem(y+dy,2)*2+lax.rem(core+dc,2),lax.rem(p+dp,2)))
    line=[(k,lax.rem(z+k,4)) for k in range(1,4)]
    def sig(bb,pp): pl.semaphore_signal(barrier,inc=1,device_id=(bb,pp),device_id_type=MESH)
    for _,bb,pp in plane: sig(bb,pp)
    for _,zz in line: sig(b+4*(zz-z),p)
    def when(ok,f):
        if ok is None: f()
        else: pl.when(ok)(f)
    def AND(*c):
        r=None
        for k in c:
            if k is not None: r=k if r is None else r&k
        return r
    def wait_in(ref,sem):
        pltpu.make_async_remote_copy(src_ref=ref,dst_ref=ref,send_sem=sem,recv_sem=sem,device_id=(b,xn),device_id_type=MESH).wait_recv()
    def slot(zz,yy,pp,cc=core): return ((zz*2+yy)*2+cc)*2+pp
    A=pl.ds(0,HALF); B=pl.ds(HALF,BLK-HALF)
    cm=Comm()
    shift=lax.rem(9*s,16)
    total[ROWS-1:BLK]=jnp.zeros((BLK-ROWS+1,CH),f32)
    mcopy.wait()
    for j in range(3): total[0:ROWS,128*j:128*j+128]=cvt[pl.ds(j,ROWS,stride=3),:]
    at=lax.broadcasted_iota(jnp.int32,(BLK,CH),0)
    blk[...]=jnp.where(at==BLK-4,(level[...]==0).astype(f32),pltpu.roll(total[...],shift,0)).astype(bf)
    own=pltpu.make_async_copy(blk,g_ref.at[s],own_sem)
    own.start()
    pl.semaphore_wait(barrier,10)
    def valid(zz): return (zz>=0)&(zz<4)
    def pick(c0,c1,c2,c3): return jnp.where(z==0,c0,jnp.where(z==1,c1,jnp.where(z==2,c2,c3)))
    seq=[z,pick(1,0,3,2),pick(3,3,0,0),pick(2,2,1,1)]
    def xy_send(zz,src):
        sl=slot(zz,y,p)
        cm.go(None,src,g_ref.at[sl],axs.at[zz],axr.at[zz],b,xn)
        cm.go(None,src,g_ref.at[sl],ays.at[zz],ayr.at[zz],yn,p)
    def z_own():
        sl=slot(z,y,p)
        cm.go(up_ok,blk,g_ref.at[sl],azs.at[z,0],azr.at[z],b+4,p)
        cm.go(dn_ok,blk,g_ref.at[sl],azs.at[z,1],azr.at[z],b-4,p)
        xy_send(z,blk)
        cm.go(None,blk,g_ref.at[sl],ass.at[z,y,p],asr.at[z,y,p],sib,p)
    def z_arrive(k):
        for d in (1,-1):
            zz=z-k*d
            ok=valid(zz)
            sl=slot(zz,y,p)
            when(ok,lambda: wait_in(g_ref.at[sl],azr.at[zz]))
            if k<3: cm.go(ok&(up_ok if d==1 else dn_ok),g_ref.at[sl],g_ref.at[sl],azs.at[zz,0],azr.at[zz],b+4*d,p)
            cm.go(ok,g_ref.at[sl],g_ref.at[sl],ass.at[zz,y,p],asr.at[zz,y,p],sib,p)
    def xy_arrive(zz):
        sx=slot(zz,y,xn); sy=slot(zz,1-y,p)
        wait_in(g_ref.at[sx],axr.at[zz])
        cm.go(None,g_ref.at[sx,A],g_ref.at[sx,A],adas.at[zz],adar.at[zz],yn,p)
        cm.go(None,g_ref.at[sx],g_ref.at[sx],ass.at[zz,y,xn],asr.at[zz,y,xn],sib,p)
        wait_in(g_ref.at[sy],ayr.at[zz])
        cm.go(None,g_ref.at[sy,B],g_ref.at[sy,B],adbs.at[zz],adbr.at[zz],b,xn)
        cm.go(None,g_ref.at[sy],g_ref.at[sy],ass.at[zz,1-y,p],asr.at[zz,1-y,p],sib,p)
    def load(sl): return (pltpu.make_async_copy(g_ref.at[sl,pl.ds(0,528)],wv.at[pl.ds(pl.multiple_of(16*lax.div(ROWS*sl,16),16),528)],wsem.at[sl]),
                          pltpu.make_async_copy(g_ref.at[sl,pl.ds(528,32)],tails.at[sl],tsem.at[sl]))
    def d_arrive(zz):
        sd=slot(zz,1-y,xn)
        wait_in(g_ref.at[sd,A],adar.at[zz])
        cm.go(None,g_ref.at[sd,A],g_ref.at[sd,A],ass.at[zz,1-y,xn],asr.at[zz,1-y,xn],sib,p)
        wait_in(g_ref.at[sd,B],adbr.at[zz])
        cm.go(None,g_ref.at[sd,B],g_ref.at[sd,B],ass2.at[zz],asr2.at[zz],sib,p)
        for yy in range(2):
            for pp in range(2):
                for c in load(slot(zz,yy,pp)): c.start()
    def sib_arrive(zz):
        for yy,pp in ((y,p),(y,xn),(1-y,p)):
            wait_in(g_ref.at[slot(zz,yy,pp,oc)],asr.at[zz,yy,pp])
        sl=slot(zz,1-y,xn,oc)
        wait_in(g_ref.at[sl,A],asr.at[zz,1-y,xn])
        wait_in(g_ref.at[sl,B],asr2.at[zz])
        for yy in range(2):
            for pp in range(2):
                for c in load(slot(zz,yy,pp,oc)): c.start()
    def gather_first():
        z_arrive(1)
        xy_send(seq[1],g_ref.at[slot(seq[1],y,p)])
        own.wait()
        xy_arrive(seq[0])
        z_arrive(2)
        d_arrive(seq[0])
        xy_arrive(seq[1])
        z_arrive(3)
        xy_send(seq[2],g_ref.at[slot(seq[2],y,p)])
        sib_arrive(seq[0])
        d_arrive(seq[1])
        xy_arrive(seq[2])
        xy_send(seq[3],g_ref.at[slot(seq[3],y,p)])
        sib_arrive(seq[1])
        d_arrive(seq[2])
        sib_arrive(seq[2])
    def gather_rest():
        xy_arrive(seq[3])
        d_arrive(seq[3])
        sib_arrive(seq[3])
    seen=[]
    def take(shards):
        for k in shards:
            for c in load(k): c.wait()
            lo=base_of(k)
            if k<31 and base_of(k+1)-lo==544 or k==31: wv[lo+528:lo+544]=tails[k,0:16]
            seen.append(k)
        for k in range(1,32):
            if k in seen and k-1 in seen and (k in shards or k-1 in shards):
                off=base_of(k)-base_of(k-1)-528
                t=tails[k-1,off:off+16].astype(f32)
                if off: t=jnp.where(lax.broadcasted_iota(jnp.int32,(16,CH),0)<8,t,0.0)
                lo=base_of(k)
                wv[lo:lo+16]=(wv[lo:lo+16].astype(f32)+t).astype(bf)
    four=((1-y,xn),(y,xn),(1-y,p),(y,p))
    def rows(u,yy,pp,cc=core):
        return (gv if u==0 else wv).at[pl.ds(pl.multiple_of(16*lax.div(ROWS*slot(u,yy,pp,cc),16),16),BLK)]
    def need(u,yy,pp,cc=core): return None if u<3 else slot(u,yy,pp,cc)<=LAST
    def sibsend(u):
        for yy,pp in four:
            cm.go(need(u,yy,pp,oc),rows(u,yy,pp,oc),sibr.at[4*u+2*yy+pp],s1s.at[u,yy,pp],s1r.at[u,yy,pp],sib,p)
    def both(u,yy,pp,part):
        lo,n=(0,HALF) if part==0 else (HALF,BLK-HALF)
        r=gv if u==0 else wv
        a=pl.multiple_of(16*lax.div(ROWS*slot(u,yy,pp),16)+lo,16)
        return r[pl.ds(a,n)].astype(f32)+sibr[4*u+2*yy+pp,lo:lo+n].astype(f32)
    def stage1(u):
        yy,pp=1-y,xn
        c=need(u,yy,pp)
        def f():
            wait_in(sibr.at[4*u+2*yy+pp],s1r.at[u,yy,pp])
            sibr[4*u+2*yy+pp,0:HALF]=both(u,yy,pp,0).astype(bf)
            sibr[4*u+2*yy+pp,HALF:BLK]=both(u,yy,pp,1).astype(bf)
        when(c,f)
        cm.go(c,sibr.at[4*u+2*yy+pp,A],ra.at[u],das.at[u],dar.at[u],b,xn)
        cm.go(c,sibr.at[4*u+2*yy+pp,B],rb.at[u],dbs.at[u],dbr.at[u],yn,p)
    def stage2(u):
        yy,pp=y,xn
        c=need(u,yy,pp)
        def f():
            wait_in(sibr.at[4*u+2*yy+pp],s1r.at[u,yy,pp])
            sibr[4*u+2*yy+pp,0:HALF]=both(u,yy,pp,0).astype(bf)
            wait_in(rb.at[u],dbr.at[u])
            sibr[4*u+2*yy+pp,HALF:BLK]=(both(u,yy,pp,1)+rb[u].astype(f32)).astype(bf)
        when(c,f)
        cm.go(c,sibr.at[4*u+2*yy+pp],rx.at[u],rxs.at[u],rxr.at[u],b,xn)
        yy2,pp2=1-y,p
        c2=need(u,yy2,pp2)
        def f2():
            wait_in(sibr.at[4*u+2*yy2+pp2],s1r.at[u,yy2,pp2])
            sibr[4*u+2*yy2+pp2,HALF:BLK]=both(u,yy2,pp2,1).astype(bf)
            wait_in(ra.at[u],dar.at[u])
            sibr[4*u+2*yy2+pp2,0:HALF]=(both(u,yy2,pp2,0)+ra[u].astype(f32)).astype(bf)
        when(c2,f2)
        cm.go(c2,sibr.at[4*u+2*yy2+pp2],ry.at[u],rys.at[u],ryr.at[u],yn,p)
    def stage3(u):
        c=need(u,y,p)
        def f():
            wait_in(sibr.at[4*u+2*y+p],s1r.at[u,y,p])
            wait_in(rx.at[u],rxr.at[u])
            wait_in(ry.at[u],ryr.at[u])
        when(c,f)
        def part(i):
            lo,n=(0,HALF) if i==0 else (HALF,BLK-HALF)
            return lo,n,both(u,y,p,i)+rx[u,lo:lo+n].astype(f32)+ry[u,lo:lo+n].astype(f32)
        def end():
            if u>0: wait_in(zu.at[u-1],zur.at[u])
            if u<3: wait_in(zd.at[u],zdr.at[u])
            for i in range(2):
                lo,n,t=part(i)
                if u>0: t=t+zu[u-1,lo:lo+n].astype(f32)
                if u<3: t=t+zd[u,lo:lo+n].astype(f32)
                total[lo:lo+n]=t
        def pass_on(buf,bsem,more):
            for i in range(2):
                lo,n,t=part(i)
                sibr[4*u+2*y+p,lo:lo+n]=t.astype(bf)
            def f():
                wait_in(buf,bsem)
                sibr[4*u+2*y+p]=(sibr[4*u+2*y+p].astype(f32)+buf[...].astype(f32)).astype(bf)
            pl.when(more)(f)
        when(AND(c,z==u),end)
        if u>0:
            when(AND(c,z<u),lambda: pass_on(zu.at[u-1],zur.at[u],dn_ok))
            cm.go(AND(c,z<u),sibr.at[4*u+2*y+p],zu.at[u-1],zs.at[u],zur.at[u],b+4,p)
        if u<3:
            when(AND(c,z>u),lambda: pass_on(zd.at[u],zdr.at[u],up_ok))
            cm.go(AND(c,z>u),sibr.at[4*u+2*y+p],zd.at[u],zs.at[u],zdr.at[u],b-4,p)
    state={"k":0}
    def xchg(src,dst,dst_like=None):
        k=state["k"]; state["k"]=k+1
        c=pltpu.make_async_remote_copy(src_ref=src,dst_ref=dst,send_sem=xs.at[k],recv_sem=xr.at[k],device_id=(b,q),device_id_type=MESH)
        c.start()
        return c
    edge=pl.ds(pl.multiple_of(q*480,32),32)
    z_own()
    c_img=xchg(img.at[edge],himg)
    def gsum(v): return exact(v,gm[...],nn)
    def swap_sums(k,s1,s2):
        ssend[k]=jnp.concatenate([s1,s2,jnp.zeros((6,CH),f32)],0)
        return xchg(ssend.at[k],srecv.at[k])
    def total_sums(k):
        t=gsum(ssend[k]+srecv[k])*(1.0/(12*2*PX))
        return t[0:1],t[1:2]
    def norm_of(t):
        mean,sq=t
        return mean,lax.rsqrt(sq-mean*mean+EPS_NORM)
    def fill3(dst,at,a):
        col=lax.broadcasted_iota(jnp.int32,a.shape,0)&31
        n=a.shape[0]
        dst[pl.ds(at,n),CH:2*CH]=a.astype(bf)
        dst[pl.ds(at,n),0:CH]=jnp.where(col==0,0.0,pltpu.roll(a,1,0)).astype(bf)
        dst[pl.ds(at,n),2*CH:3*CH]=jnp.where(col==31,0.0,pltpu.roll(a,n-1,0)).astype(bf)
    def fill_edges(dst,h):
        fill3(dst,0,h*pf); fill3(dst,544,h*qf)
    def conv_to(dst,x3,wrow,add=None):
        for dr in range(3):
            d=nn(x3[32*dr:32*dr+PX],wv[wrow+1152*dr:wrow+1152*dr+1152])
            if dr==0: dst[...]=d if add is None else add()+d
            else: dst[...]+=d
    def conv_dx(dst,wrow):
        first=True
        for dr in range(3):
            for dc in range(3):
                d=nt(z3[32*(2-dr):32*(2-dr)+PX,CH*(2-dc):CH*(2-dc)+CH],wv[wrow+CH*(3*dr+dc):wrow+CH*(3*dr+dc)+CH])
                if first: dst[...]=d
                else: dst[...]+=d
                first=False
    def st(i,c):
        v=img[pl.ds(i,64)].astype(f32)
        return c[0]+col8(v),c[1]+col8(v*v)
    a1,a2=cloop(PX,64,st,(Z8(),Z8()))
    c=swap_sums(0,row(a1),row(a2))
    gather_first()
    take(range(24,32)); take(range(0,8))
    g6=wv[R_TAB+2000-(R_TAB+2000)%16:R_END].astype(f32)
    o=R_GAIN-(R_TAB+2000-(R_TAB+2000)%16)
    g1,b1,g2,b2,g3,b3=[g6[o+i:o+i+1] for i in range(6)]
    ids=rowid[...]
    pre=[]
    tcol=lax.broadcasted_iota(jnp.int32,(16,R_END-R_TAB),1)
    for h in range(2):
        hot=(tcol==2*ids+h).astype(f32).astype(bf)
        pre.append(nn(hot,wv[R_TAB:R_END])[0:1]+tvec[:,CH*h:CH*h+CH])
    emb=[silu(v) for v in pre]
    put3(cvt3,pl.ds(0,1536),wv[R_EMB:R_TAB].astype(f32))
    wee[...]=ld(cvt3,every(0,768,2)).astype(bf)
    weo[...]=ld(cvt3,every(1,768,2)).astype(bf)
    def emb_dot(w):
        r=None
        for h in range(2):
            e=jnp.broadcast_to(emb[h],(16,CH))
            d=exact(e,w[CH*h:CH*h+CH],nn)[0:1]
            r=d if r is None else r+d
        return r
    sc1=1.0+emb_dot(wee); sh=emb_dot(weo)
    c.wait()
    mean1,inv1=norm_of(total_sums(0))
    def act_of(v): return silu((v-mean1)*inv1*g1+b1)
    def fa(i,_):
        fill3(x3a,pl.multiple_of(i+32,32),act_of(img[pl.ds(i,64)].astype(f32)))
        return 0
    cloop(PX,64,fa,0)
    c_img.wait()
    fill_edges(x3a,act_of(himg[...].astype(f32)))
    conv_to(inner,x3a,R_ONE)
    def st2(i,c):
        v=inner[pl.ds(i,64)]
        return c[0]+col8(v),c[1]+col8(v*v)
    a1,a2=cloop(PX,64,st2,(Z8(),Z8()))
    c1=swap_sums(1,row(a1),row(a2))
    c2=xchg(inner.at[edge],hrecv.at[0])
    c1.wait()
    mean2,inv2=norm_of(total_sums(1))
    def pre_b(v):
        n=(v-mean2)*inv2
        af=n*g2+b2
        return n,af,af*sc1+sh
    def fb(i,_):
        fill3(x3b,pl.multiple_of(i+32,32),silu(pre_b(inner[pl.ds(i,64)])[2]))
        return 0
    cloop(PX,64,fb,0)
    c2.wait()
    fill_edges(x3b,silu(pre_b(hrecv[0])[2]))
    gather_rest()
    take(range(8,16)); take(range(16,24))
    conv_to(middle,x3b,R_TWO,lambda: img[...].astype(f32))
    def st3(i,c):
        v=middle[pl.ds(i,64)]
        return c[0]+col8(v),c[1]+col8(v*v)
    a1,a2=cloop(PX,64,st3,(Z8(),Z8()))
    c1=swap_sums(2,row(a1),row(a2))
    put3(cvt3,pl.ds(0,1152),wv[R_QKV:R_PROJ].astype(f32))
    for j in range(3):
        wqT[CH*j:CH*j+CH]=ld(cvt3,every(j,CH,3)).T.astype(bf)
    c1.wait()
    mean3,inv3=norm_of(total_sums(2))
    def fc(i,_):
        n=(middle[pl.ds(i,64)]-mean3)*inv3
        ain[pl.ds(i,64)]=(n*g3+b3).astype(bf)
        return 0
    cloop(PX,64,fc,0)
    c1=xchg(ain.at[pl.ds(0,PX)],ain.at[pl.ds(PX,PX)])
    trT[:,0:PX]=nt(wqT[...],ain[0:PX]).astype(bf)
    for off in range(9):
        put3(cvt3,pl.ds(0,576),wv[R_DOWN+576*off:R_DOWN+576*off+576].astype(f32))
        v0,v1,v2=[ld(cvt3,every(i,192,3)) for i in range(3)]
        put3(cvt2,every(0,192,2),jnp.concatenate([v0,v1[:,0:256]],1))
        w=jnp.concatenate([v1[:,128:384],v2],1)
        w=pltpu.roll(w,w.shape[1]-64,1)
        put3(cvt2,every(1,192,2),w)
        wd[CH*off:CH*off+CH]=ld(cvt2,pl.ds(0,CH))[:,0:576].astype(bf)
    c1.wait()
    trT[:,PX:2*PX]=nt(wqT[...],ain[PX:2*PX]).astype(bf)
    QC=256
    def fh(h,_):
        r0=pl.multiple_of(h*192,64)
        qT=trT[pl.ds(r0,64),0:PX]
        k=trT[pl.ds(pl.multiple_of(r0+64,64),64),:].T
        vT=trT[pl.ds(pl.multiple_of(r0+128,64),64),:]
        for c in range(PX//QC):
            s=nn(k,qT[:,QC*c:QC*c+QC])*0.125
            m=jnp.max(s,0,keepdims=True)
            e=jnp.exp(s-m)
            l=jnp.sum(e,0,keepdims=True)
            pT=(e*(1.0/l)).astype(bf)
            attT[pl.ds(pl.multiple_of(h*64,64),64),QC*c:QC*c+QC]=nn(vT,pT).astype(bf)
            lse[h,0:1,QC*c:QC*c+QC]=m+jnp.log(l)
        return 0
    lax.fori_loop(0,6,fh,0)
    put3(gout,pl.ds(0,PX),middle[...]+tn(attT[...],wv[R_PROJ:R_DOWN]))
    hsend[0]=ld(gout,edge).astype(bf)
    c1=xchg(hsend.at[0],oth.at[0])
    def parts(ref,n):
        e=ld(ref,every(0,n//2,2)); o=ld(ref,every(1,n//2,2))
        col=lax.broadcasted_iota(jnp.int32,o.shape,0)&15
        return jnp.where(col==0,0.0,pltpu.roll(o,1,0)).astype(bf),e.astype(bf),o.astype(bf)
    for dc,v in enumerate(parts(gout,PX)):
        v=v.reshape(8,32,CH)
        even=v[:,0:16].reshape(128,CH); odd=v[:,16:32].reshape(128,CH)
        xd[:,CH*(3+dc):CH*(3+dc)+CH]=even
        xd[:,CH*(6+dc):CH*(6+dc)+CH]=odd
        xd[16:128,CH*dc:CH*dc+CH]=odd[0:112]
    c1.wait()
    put3(geo,pl.ds(0,32),oth[0].astype(f32)*pf)
    for dc,v in enumerate(parts(geo,32)):
        xd[0:16,CH*dc:CH*dc+CH]=v
    fin=nn(xd[...],wd[...])
    feat=nn(fin.astype(bf),vgg[...]); tf=nn(tgt[...],vgg[...])
    ir=lax.rsqrt(jnp.mean(feat*feat,-1,keepdims=True)+EPS_FEAT)
    unit=feat*ir
    diff=unit-tf*lax.rsqrt(jnp.mean(tf*tf,-1,keepdims=True)+EPS_FEAT)
    wl=lin[...]*diff
    consist=jnp.sum(row(wl*diff),1,keepdims=True)*(1.0/(256*256))
    du=wl*(2.0/(256*256*images_all))
    dfeat=(ir*(du-unit*jnp.mean(du*unit,-1,keepdims=True))).astype(bf)
    zc=jnp.zeros((16,128),f32)
    for t_ in range(0,32,2): zc=zc+tails[t_,16:32,0:128].astype(f32)
    zc=zc[12:13,0:1]
    seed=(level[...]==0).astype(f32)/jnp.maximum(zc,1.0)*(2.0/(256*CH2))
    gfin=nt(dfeat,vgg[...])+seed*(fin-cln[...].astype(f32))
    dz=gfin.astype(bf)
    dzs[...]=dz[0:16]
    c1=xchg(dzs,dzr)
    for off in range(9):
        dw=tn(xd[:,CH*off:CH*off+CH],dz)
        put3(cvt2,pl.ds(0,CH),jnp.concatenate([dw,jnp.zeros((CH,64),f32)],1))
        e=ld(cvt2,every(0,192,2)); o_=pltpu.roll(ld(cvt2,every(1,192,2)),64,1)
        lane=lax.broadcasted_iota(jnp.int32,(192,128),1)
        put3(cvt3,every(0,192,3),e[:,0:384])
        put3(cvt3,every(1,192,3),jnp.concatenate([e[:,384:512],jnp.where(lane<64,e[:,512:640],o_[:,0:128]),o_[:,128:256]],1))
        put3(cvt3,every(2,192,3),o_[:,256:640])
        wv[R_DOWN+576*off:R_DOWN+576*off+576]=ld(cvt3,pl.ds(0,576)).astype(bf)
    sibsend(2); sibsend(3)
    c1.wait()
    z32=dz.astype(f32)
    down=jnp.concatenate([z32[16:128],dzr[...].astype(f32)*qf],0)
    def left(v):
        col=lax.broadcasted_iota(jnp.int32,v.shape,0)&15
        return jnp.where(col==15,0.0,pltpu.roll(v,127,0)).astype(bf)
    s00,s01,s10,s11=dz,left(z32),down.astype(bf),left(down)
    W=lambda a,c: wd[CH*(3*a+c):CH*(3*a+c)+CH]
    def put(a,c,v):
        for i in range(8):
            put3(gout,every((2*i+a)*32+c,16,2),v[16*i:16*i+16])
    put(0,0,nt(s00,W(1,1)))
    put(0,1,nt(s00,W(1,2))+nt(s01,W(1,0)))
    put(1,0,nt(s00,W(2,1))+nt(s10,W(0,1)))
    put(1,1,nt(s00,W(2,2))+nt(s01,W(2,0))+nt(s10,W(0,2))+nt(s11,W(0,0)))
    stage1(2); stage1(3)
    gp=ld(gout,pl.ds(0,PX)).astype(bf)
    dattT[...]=nt(wv[R_PROJ:R_DOWN],gp).astype(bf)
    wv[R_PROJ:R_DOWN]=nn(attT[...],gp).astype(bf)
    def bh(h,_):
        r0=pl.multiple_of(h*192,64); r1=pl.multiple_of(r0+64,64); r2=pl.multiple_of(r0+128,64)
        qT=trT[pl.ds(r0,64),0:PX]
        kT=trT[pl.ds(r1,64),:]
        k=kT.T
        v=trT[pl.ds(r2,64),:].T
        gT=dattT[pl.ds(pl.multiple_of(h*64,64),64),:]
        for c in range(PX//QC):
            qs=slice(QC*c,QC*c+QC)
            s=nn(k,qT[:,qs])*0.125
            pr=jnp.exp(s-lse[h,0:1,qs])
            dp=nn(v,gT[:,qs])
            de=jnp.sum(pr*dp,0,keepdims=True)
            ds=(pr*(dp-de)).astype(bf)
            dk=nt(qT[:,qs],ds)*0.125; dv=nt(gT[:,qs],pr.astype(bf))
            if c==0: dkv[0:64]=dk; dkv[64:128]=dv
            else: dkv[0:64]+=dk; dkv[64:128]+=dv
            dtrT[pl.ds(r0,64),qs]=(nn(kT,ds)*0.125).astype(bf)
        dtrT[pl.ds(r0,64),PX:2*PX]=jnp.zeros((64,PX),bf)
        dtrT[pl.ds(r1,64),:]=dkv[0:64].astype(bf)
        dtrT[pl.ds(r2,64),:]=dkv[64:128].astype(bf)
        return 0
    lax.fori_loop(0,3,bh,0)
    stage2(2); stage2(3)
    lax.fori_loop(3,6,bh,0)
    oth[1:17]=tn(dtrT[:,PX:2*PX],wqT[...]).astype(bf).reshape(16,32,CH)
    c1=xchg(oth.at[pl.ds(1,16)],oth.at[pl.ds(17,16)])
    gsec[...]=tn(dtrT[:,0:PX],wqT[...])
    dq=nt(ain[...].T,dtrT[...])
    for j in range(3):
        put3(cvt3,every(j,CH,3),dq[:,CH*j:CH*j+CH])
    wv[R_QKV:R_PROJ]=ld(cvt3,pl.ds(0,1152)).astype(bf)
    c1.wait()
    def n3_of(i): return (middle[pl.ds(i,64)]-mean3)*inv3
    def s3(i,c):
        j=pl.multiple_of(17+lax.div(i,32),1)
        v=gsec[pl.ds(i,64)]+oth[pl.ds(j,2)].reshape(64,CH).astype(f32)
        gsec[pl.ds(i,64)]=v
        return c[0]+col8(v),c[1]+col8(v*n3_of(i))
    a1,a2=cloop(PX,64,s3,(Z8(),Z8()))
    db3,dg3=row(a1),row(a2)
    c1=swap_sums(3,db3*g3,dg3*g3)
    stage3(2)
    c1.wait()
    m1,m2=total_sums(3)
    def f3(i,_):
        v=ld(gout,pl.ds(i,64))+inv3*(gsec[pl.ds(i,64)]*g3-m1-n3_of(i)*m2)
        fill3(z3,pl.multiple_of(i+32,32),v)
        return 0
    cloop(PX,64,f3,0)
    zedge=pl.ds(pl.multiple_of(q*480+32,32),32)
    hsend[1]=z3[zedge,CH:2*CH]
    c1=xchg(hsend.at[1],oth.at[33])
    stage3(3)
    c1.wait()
    fill_edges(z3,oth[33].astype(f32))
    conv_dx(gsec,R_TWO)
    for dr in range(3):
        d=tn(x3b[32*dr:32*dr+PX],z3[32:32+PX,CH:2*CH]).astype(bf)
        wv[R_TWO+1152*dr:R_TWO+1152*dr+1152]=d
        if dr==0: gv[R_TWO:4304]=d[0:4304-R_TWO]
    sibsend(1)
    def s2(i,c):
        n,af,pb=pre_b(inner[pl.ds(i,64)])
        gpre=gsec[pl.ds(i,64)]*slope(pb)
        gaff=gpre*sc1
        gsec[pl.ds(i,64)]=gaff
        return c[0]+col8(gpre*af),c[1]+col8(gpre),c[2]+col8(gaff*n),c[3]+col8(gaff)
    a1,a2,a3,a4=cloop(PX,64,s2,(Z8(),Z8(),Z8(),Z8()))
    dsc,dsh,dg2,db2=row(a1),row(a2),row(a3),row(a4)
    c1=swap_sums(4,db2*g2,dg2*g2)
    stage1(1)
    c1.wait()
    m1,m2=total_sums(4)
    def f2(i,_):
        n=(inner[pl.ds(i,64)]-mean2)*inv2
        fill3(z3,pl.multiple_of(i+32,32),inv2*(gsec[pl.ds(i,64)]*g2-m1-n*m2))
        return 0
    cloop(PX,64,f2,0)
    hsend[2]=z3[zedge,CH:2*CH]
    c1=xchg(hsend.at[2],oth.at[34])
    for dr in range(3):
        gv[1152*dr:1152*dr+1152]=tn(x3a[32*dr:32*dr+PX],z3[32:32+PX,CH:2*CH]).astype(bf)
    sibsend(0)
    stage2(1)
    c1.wait()
    fill_edges(z3,oth[34].astype(f32))
    stage1(0)
    conv_dx(gsec,R_ONE)
    def s1(i,c):
        n=(img[pl.ds(i,64)].astype(f32)-mean1)*inv1
        gpre=gsec[pl.ds(i,64)]*slope(n*g1+b1)
        return c[0]+col8(gpre*n),c[1]+col8(gpre)
    a1,a2=cloop(PX,64,s1,(Z8(),Z8()))
    stage2(0)
    ge=[]
    for h in range(2):
        d=exact(jnp.broadcast_to(dsc,(16,CH)),wee[CH*h:CH*h+CH],nt)+exact(jnp.broadcast_to(dsh,(16,CH)),weo[CH*h:CH*h+CH],nt)
        ge.append(d[0:1]*slope(pre[h]))
    hot_level=(lax.broadcasted_iota(jnp.int32,(1,CH),1)==level[...]).astype(f32)
    pack_ref[...]=jnp.concatenate([row(a1),row(a2),dg2,db2,dg3,db3,dsc,dsh,ge[0],ge[1],emb[0],emb[1],consist*hot_level,jnp.broadcast_to(ids.astype(f32),(1,CH)),0.5*hot_level,jnp.zeros((1,CH),f32)],0)
    low=jnp.logical_not(top)
    cm.go(low,pack_ref,lpk.at[z],lps,lpr.at[z],b+4*(3-z),p)
    stage3(1)
    def packs_line():
        pl.when(jnp.logical_not(slot(z,y,p)<=LAST))(lambda: total.__setitem__(Ellipsis,jnp.zeros(total.shape,f32)))
        lpk[3]=pack_ref[...]
        for zz in range(3): wait_in(lpk.at[zz],lpr.at[zz])
    pl.when(top)(packs_line)
    for d,bb,pp in plane:
        cm.go(top,lpk,ppk.at[mine],pps.at[d],ppr.at[mine],bb,pp)
    def packs_plane():
        ppk[mine]=lpk[...]
        for d,bb,pp in plane:
            o=(lax.rem(lax.div(bb,2),2)*2+lax.rem(bb,2))*2+pp
            wait_in(ppk.at[o],ppr.at[o])
        a_s=16*lax.div(ROWS*s,16)
        rows_at=lambda k: ppk[:,:,k,:].reshape(32,384)
        zero=jnp.zeros((64,384),f32)
        for h in range(2):
            e=rows_at(10+h)
            t=jnp.concatenate([e,e,zero],0).T
            cvt[pl.ds(BLK+768*h,384,stride=2),:]=t
            cvt[pl.ds(BLK+768*h+1,384,stride=2),:]=t
        r=a_s+lax.broadcasted_iota(jnp.int32,(BLK,128),0)
        l=lax.broadcasted_iota(jnp.int32,(BLK,128),1)
        inside=(r>=R_EMB)&(r<R_TAB)
        start=pl.multiple_of(jnp.clip(a_s-R_EMB+BLK,0,BLK+1536),16)
        lf=jnp.where(inside&(((r&1)==1)==(l>=32))&(l<64),cvt[pl.ds(start,BLK),:],0.0)
        ids=rows_at(13)[:,0:128].astype(jnp.int32)
        ids=jnp.concatenate([ids]*4,0).astype(f32).T[0:1].astype(jnp.int32)
        hot=(r-R_TAB==2*ids+(l>=96).astype(jnp.int32))&(l>=64)&(r>=R_TAB)
        lf=jnp.where(hot,1.0,lf)
        rg=jnp.concatenate([rows_at(6),rows_at(7),rows_at(8),rows_at(9)],0)
        gains=[jnp.sum(rows_at(k),0,keepdims=True) for k in range(6)]
        hi=lax.Precision.HIGHEST
        add=lax.dot_general(lf,rg,(((1,),(0,)),((),())),precision=hi,preferred_element_type=f32)
        for k in range(6): add=add+jnp.where(r[:,0:1]-R_GAIN==k,gains[k],0.0)
        rr=a_s+lax.broadcasted_iota(jnp.int32,(BLK,384),0)
        total[...]=jnp.where(rr<R_EMB,total[...],add)
    pl.when(top)(packs_plane)
    stage3(0)
    shift=lax.rem(9*s,16)
    t=pltpu.roll(total[...],lax.rem(BLK-shift,BLK),0)[0:ROWS]
    for j in range(3): cvt[pl.ds(j,ROWS,stride=3),:]=t[:,128*j:128*j+128]
    fcopy=pltpu.make_async_copy(cvt.at[pl.ds(0,1611)],flat_ref,own_sem)
    fcopy.start()
    sq=jnp.sum(jnp.sum(t*t,0,keepdims=True),1,keepdims=True)
    tile[...]=jnp.concatenate([jnp.broadcast_to(sq,(1,128)),pack_ref[12:13,0:128],pack_ref[14:15,0:128],jnp.zeros((5,128),f32)],0)
    red1[mine]=tile[...]
    for d,bb,pp in plane: cm.go(None,tile,red1.at[mine],n1s.at[d],n1r.at[mine],bb,pp)
    for d,bb,pp in plane:
        o=(lax.rem(lax.div(bb,2),2)*2+lax.rem(bb,2))*2+pp
        wait_in(red1.at[o],n1r.at[o])
    v=red1[0]
    for k in range(1,8): v=v+red1[k]
    red2[z]=v
    for k,zz in line: cm.go(None,red2.at[z],red2.at[z],n2s.at[k],n2r.at[z],b+4*(zz-z),p)
    for k,zz in line: wait_in(red2.at[zz],n2r.at[zz])
    all_ref[...]=red2[0]+red2[1]+red2[2]+red2[3]
    cm.drain()
    fcopy.wait()

def step(images_all,mast,img,tgt,cln,vgg,lin,tvec,rowid,level,gm):
    D=pltpu.SemaphoreType.DMA
    V=lambda *s: pltpu.VMEM(s,bf)
    F=lambda *s: pltpu.VMEM(s,f32)
    vm=pl.BlockSpec(memory_space=pltpu.VMEM)
    return pl.pallas_call(functools.partial(step_kernel,images_all),
        out_shape=(jax.ShapeDtypeStruct((1611,128),f32),jax.ShapeDtypeStruct((8,128),f32),jax.ShapeDtypeStruct((32,BLK,CH),bf)),
        in_specs=[pl.BlockSpec(memory_space=pl.ANY)]+[vm]*9,
        out_specs=(pl.BlockSpec(memory_space=pl.ANY),vm,pl.BlockSpec(memory_space=pl.ANY)),
        scratch_shapes=[V(17184,CH),V(4304,CH),V(32,32,CH),F(4608,128),F(5,CH,128),V(3456,CH2),V(768,CH),V(768,CH),V(1152,CH),V(576,1152),V(576,1152),V(576,1152),F(PX,CH),F(PX,CH),F(3,PX,128),F(PX,CH),V(1024,CH),V(1152,1024),V(1152,1024),V(CH,PX),V(128,3456),F(6,8,PX),V(CH,PX),F(128,1024),F(5,8,CH),F(5,8,CH),V(3,32,CH),F(1,32,CH),V(32,CH),V(16,CH2),V(16,CH2),F(3,32,128),V(35,32,CH),D((32,)),D((32,)),D((16,)),D((16,)),F(BLK,CH),V(BLK,CH),D,D((4,2)),D((4,)),D((4,)),D((4,)),D((4,)),D((4,)),D((4,)),D((4,)),D((4,)),D((4,)),D((4,2,2)),D((4,2,2)),D((4,)),D((4,)),F(16,CH),F(4,16,CH),F(8,4,16,CH),F(8,8,128),F(4,8,128),F(8,128),D,D((4,)),D((8,)),D((8,)),D((8,)),D((8,)),D((4,)),D((4,)),V(14,BLK,CH),V(4,HALF,CH),V(4,BLK-HALF,CH),V(4,BLK,CH),V(4,BLK,CH),V(3,BLK,CH),V(3,BLK,CH),D((4,2,2)),D((4,2,2)),D((4,)),D((4,)),D((4,)),D((4,)),D((4,)),D((4,)),D((4,)),D((4,)),D((4,)),D((4,)),D((4,))],
        compiler_params=pltpu.CompilerParams(collective_id=0,has_side_effects=True,vmem_limit_bytes=63<<20),
        name="train_step",
    )(mast,img,tgt,cln,vgg,lin,tvec,rowid,level,gm)


def fast(images, target, clean_images, levels, labels, null_mask, vgg_proj, lpips_lin, master, first_moment, second_moment):
    row_index = jnp.where(null_mask == 1, CLASSES, labels).reshape(1, 1)
    tvec = time_vector(levels)
    lane = jnp.arange(CH, dtype=jnp.int32) // 12
    gm = (lane[:, None] == lane[None, :]).astype(jnp.bfloat16)
    own_grad, sums, _ = step(
        16,
        master.reshape(1611, 128),
        images.reshape(PX, CH),
        target.reshape(128, CH2),
        clean_images.reshape(128, CH2),
        vgg_proj,
        lpips_lin.reshape(1, 256),
        tvec,
        row_index,
        levels.reshape(1, 1),
        gm,
    )
    own_grad = own_grad.reshape(-1)
    level_sums = sums[1:3, :LEVELS]
    norm_before = jnp.sqrt(sums[0, 0])
    clipped = own_grad * jnp.minimum(1.0, CLIP / norm_before)
    new_first = BETA_ONE * first_moment + (1.0 - BETA_ONE) * clipped
    new_second = BETA_TWO * second_moment + (1.0 - BETA_TWO) * clipped * clipped
    fixed_first = new_first / (1.0 - BETA_ONE**STEP)
    fixed_second = new_second / (1.0 - BETA_TWO**STEP)
    new_master = master - RATE * (fixed_first / (jnp.sqrt(fixed_second) + EPS_ADAM) + DECAY * master)
    return (new_master, new_first, new_second, new_master.astype(jnp.bfloat16), norm_before, level_sums)


def solution(mesh):
    small = mesh.shape["batch"] == 16 and mesh.shape["pix"] == 2
    return jax.shard_map(
        fast if small else local,
        mesh=mesh,
        in_specs=(
            P("batch", "pix", None, None),
            P("batch", "pix", None, None),
            P("batch", "pix", None, None),
            P("batch"),
            P("batch"),
            P("batch"),
            P(),
            P(),
            P(("batch", "pix")),
            P(("batch", "pix")),
            P(("batch", "pix")),
        ),
        out_specs=(
            P(("batch", "pix")),
            P(("batch", "pix")),
            P(("batch", "pix")),
            P(("batch", "pix")),
            P(),
            P(),
        ),
        check_vma=False,
    )
```

```python
import functools
import math

import jax
import jax.numpy as jnp
from jax import lax
from jax.experimental import pallas as pl
from jax.experimental.pallas import tpu as pltpu
from jax.sharding import PartitionSpec as P

CH = 384
CH2 = 576
GROUPS = 32
HEAD = 64
TEMB = 768
CLASSES = 1000
LEVELS = 40
STEP = 10


EPS_NORM = 1e-05
EPS_FEAT = 1e-06
BETA_ONE = 0.9
BETA_TWO = 0.999
EPS_ADAM = 1e-08
RATE = 0.02
DECAY = 0.01
CLIP = 0.01
precise = lax.Precision.HIGHEST


def extended(shard, sides, width):
    for axis, dim in sides:
        size, length = (lax.axis_size(axis), shard.shape[dim])
        up = [(i, (i + 1) % size) for i in range(size - 1)]
        down = [(j, i) for i, j in up]
        last = lax.slice_in_dim(shard, length - width, length, axis=dim)
        initial = lax.slice_in_dim(shard, 0, width, axis=dim)
        before = lax.ppermute(last, axis, up)
        after = lax.ppermute(initial, axis, down)
        shard = jnp.concatenate([before, shard, after], axis=dim)
    return shard


def unpack(flat_vec):
    layout = [
        (9 * CH, CH),
        (9 * CH, CH),
        (CH, 3 * CH),
        (CH, CH),
        (9 * CH, CH2),
        (TEMB, 2 * CH),
        (CLASSES + 1, TEMB),
        (6, CH),
    ]
    pieces = []
    offset = 0
    for rows_n, cols_n in layout:
        pieces.append(flat_vec[offset : offset + rows_n * cols_n].reshape(rows_n, cols_n))
        offset += rows_n * cols_n
    return (pieces, offset)


def time_vector(level_ids):
    half_width = TEMB // 2
    frequency = jnp.exp(-math.log(10000.0) * jnp.arange(half_width, dtype=jnp.float32) / half_width)
    angles = level_ids.astype(jnp.float32)[..., None] * (1000.0 / LEVELS) * frequency
    return jnp.concatenate([jnp.cos(angles), jnp.sin(angles)], -1)


def silu_slope(values):
    sigmoid = jax.nn.sigmoid(values)
    return sigmoid * (1.0 + values * (1.0 - sigmoid))


def pix_sums(pair_sums):
    return lax.psum((pair_sums[0], pair_sums[1]), "pix")


def group_forward(values, pixels_all):
    grouped = values.reshape(values.shape[0], values.shape[1], GROUPS, -1)
    totals = pix_sums((jnp.sum(grouped, (1, 3)), jnp.sum(grouped * grouped, (1, 3))))
    per_group = pixels_all * grouped.shape[3]
    center = totals[0] / per_group
    spread = totals[1] / per_group - center * center
    inverse = lax.rsqrt(spread + EPS_NORM)
    normed = (grouped - center[:, None, :, None]) * inverse[:, None, :, None]
    return (normed.reshape(values.shape), inverse)


def group_backward(grad_normed, normed, inverse, pixels_all):
    grad_grouped = grad_normed.reshape(normed.shape[0], normed.shape[1], GROUPS, -1)
    val_grouped = normed.reshape(grad_grouped.shape)
    totals = pix_sums((jnp.sum(grad_grouped, (1, 3)), jnp.sum(grad_grouped * val_grouped, (1, 3))))
    per_group = pixels_all * grad_grouped.shape[3]
    result = (
        grad_grouped
        - (totals[0] / per_group)[:, None, :, None]
        - val_grouped * (totals[1] / per_group)[:, None, :, None]
    )
    return (result * inverse[:, None, :, None]).reshape(normed.shape)


def columns_of(values, stride):
    rows_out = values.shape[1] // stride
    cols_out = values.shape[2] // stride
    span_rows = stride * (rows_out - 1) + 1
    span_cols = stride * (cols_out - 1) + 1
    padded = extended(values, (("pix", 1),), 1)
    padded = jnp.pad(padded, ((0, 0), (0, 0), (1, 1), (0, 0)))
    return jnp.concatenate(
        [
            padded[
                :, row_off : row_off + span_rows : stride, col_off : col_off + span_cols : stride, :
            ]
            for row_off in range(3)
            for col_off in range(3)
        ],
        -1,
    )


def conv_forward(values, weight, rows_in, stride):
    n_img, pixels_in, in_chan = values.shape
    columns = columns_of(values.reshape(n_img, rows_in, -1, in_chan), stride)
    result = jnp.dot(columns.reshape(-1, 9 * in_chan), weight, preferred_element_type=jnp.float32)
    return (result.reshape(n_img, -1, weight.shape[1]), columns)


def conv_back(columns, grad_low, weight, rows_in, stride):
    n_img, pix_out, out_chan = grad_low.shape
    in_chan = weight.shape[0] // 9
    d_weight = jnp.einsum(
        "rk,rc->kc",
        columns.reshape(-1, 9 * in_chan),
        grad_low.reshape(-1, out_chan),
        preferred_element_type=jnp.float32,
    )
    flipped = (
        weight.reshape(3, 3, in_chan, out_chan)[::-1, ::-1]
        .transpose(0, 1, 3, 2)
        .reshape(9 * out_chan, in_chan)
    )
    rows_out = rows_in // stride
    grid_grad = grad_low.reshape(n_img, rows_out, pix_out // rows_out, out_chan)
    if stride > 1:
        grid_grad = jnp.pad(
            grid_grad[:, :, None, :, None, :],
            ((0, 0), (0, 0), (0, stride - 1), (0, 0), (0, stride - 1), (0, 0)),
        )
        grid_grad = grid_grad.reshape(n_img, rows_in, -1, out_chan)
    grad_columns = columns_of(grid_grad, 1)
    grad_input = jnp.dot(
        grad_columns.reshape(-1, 9 * out_chan), flipped, preferred_element_type=jnp.float32
    )
    return (d_weight, grad_input.reshape(n_img, -1, in_chan))


def res_forward(values, gain_rows, scale, shift, w_first, w_second, rows_in, pixels_all):
    normed_a, inverse_a = group_forward(values, pixels_all)
    pre_a = normed_a * gain_rows[0] + gain_rows[1]
    act_a = jax.nn.silu(pre_a).astype(jnp.bfloat16)
    inner, columns_a = conv_forward(act_a, w_first, rows_in, 1)
    normed_b, inverse_b = group_forward(inner, pixels_all)
    affine_b = normed_b * gain_rows[2] + gain_rows[3]
    pre_b = affine_b * (1.0 + scale) + shift
    second = jax.nn.silu(pre_b).astype(jnp.bfloat16)
    branch, columns_b = conv_forward(second, w_second, rows_in, 1)
    kept_state = (
        normed_a,
        inverse_a,
        pre_a,
        columns_a,
        normed_b,
        inverse_b,
        affine_b,
        pre_b,
        columns_b,
    )
    return (values + branch, kept_state)


def res_back(grad_result, kept_state, gain_rows, scale, w_first, w_second, rows_in, pixels_all):
    normed_a, inverse_a, pre_a, columns_a, normed_b, inverse_b, affine_b, pre_b, columns_b = (
        kept_state
    )
    d_w_second, grad_second = conv_back(
        columns_b, grad_result.astype(jnp.bfloat16), w_second, rows_in, 1
    )
    grad_pre_b = grad_second * silu_slope(pre_b)
    d_scale = jnp.sum(grad_pre_b * affine_b, 1)
    d_shift = jnp.sum(grad_pre_b, 1)
    grad_affine = grad_pre_b * (1.0 + scale)
    d_gain_b = jnp.sum(grad_affine * normed_b, (0, 1))
    d_bias_b = jnp.sum(grad_affine, (0, 1))
    grad_inner = group_backward(grad_affine * gain_rows[2], normed_b, inverse_b, pixels_all).astype(
        jnp.bfloat16
    )
    d_w_first, grad_act = conv_back(columns_a, grad_inner, w_first, rows_in, 1)
    grad_pre_a = grad_act * silu_slope(pre_a)
    d_gain_a = jnp.sum(grad_pre_a * normed_a, (0, 1))
    d_bias_a = jnp.sum(grad_pre_a, (0, 1))
    grad_values = None
    d_gains = jnp.stack([d_gain_a, d_bias_a, d_gain_b, d_bias_b])
    return (d_w_first, d_w_second, d_gains, d_scale, d_shift, grad_values)


def to_heads(values):
    return lax.all_to_all(values, "pix", split_axis=2, concat_axis=1, tiled=True)


def to_pixels(values):
    return lax.all_to_all(values, "pix", split_axis=1, concat_axis=2, tiled=True)


def flat_heads(values):
    return values.reshape(-1, values.shape[2], values.shape[3])


def attend(queries, keys, values):
    root_dim = math.sqrt(queries.shape[-1])

    def single(bundle):
        q_one, k_one, v_one = bundle
        scores = (
            jnp.einsum("qd,kd->qk", q_one, k_one, preferred_element_type=jnp.float32) / root_dim
        )
        row_peak = jnp.max(scores, -1, keepdims=True)
        exp_scores = jnp.exp(scores - row_peak)
        sum_exp = jnp.sum(exp_scores, -1, keepdims=True)
        probabilities = (exp_scores / sum_exp).astype(jnp.bfloat16)
        attended = jnp.einsum("qk,kd->qd", probabilities, v_one, preferred_element_type=jnp.float32)
        return (attended.astype(jnp.bfloat16), row_peak + jnp.log(sum_exp))

    attended, log_total = lax.map(
        single, (flat_heads(queries), flat_heads(keys), flat_heads(values))
    )
    return (attended.reshape(queries.shape), log_total)


def attend_back(queries, keys, values, log_total, grad_out):
    root_dim = math.sqrt(queries.shape[-1])

    def single(bundle):
        q_one, k_one, v_one, lse_one, g_one = bundle
        scores = (
            jnp.einsum("qd,kd->qk", q_one, k_one, preferred_element_type=jnp.float32) / root_dim
        )
        probabilities = jnp.exp(scores - lse_one)
        grad_v = jnp.einsum(
            "qk,qd->kd",
            probabilities.astype(jnp.bfloat16),
            g_one,
            preferred_element_type=jnp.float32,
        )
        grad_p = jnp.einsum("qd,kd->qk", g_one, v_one, preferred_element_type=jnp.float32)
        inner_sum = jnp.sum(probabilities * grad_p, -1, keepdims=True)
        grad_s = (probabilities * (grad_p - inner_sum)).astype(jnp.bfloat16)
        grad_q = (
            jnp.einsum("qk,kd->qd", grad_s, k_one, preferred_element_type=jnp.float32) / root_dim
        )
        grad_k = (
            jnp.einsum("qk,qd->kd", grad_s, q_one, preferred_element_type=jnp.float32) / root_dim
        )
        return (grad_q, grad_k, grad_v)

    grad_q, grad_k, grad_v = lax.map(
        single,
        (
            flat_heads(queries),
            flat_heads(keys),
            flat_heads(values),
            log_total,
            flat_heads(grad_out),
        ),
    )
    return (grad_q.reshape(queries.shape), grad_k.reshape(keys.shape), grad_v.reshape(values.shape))


def local(
    images,
    target,
    clean_images,
    levels,
    labels,
    null_mask,
    vgg_proj,
    lpips_lin,
    master,
    first_moment,
    second_moment,
):
    gathered = lax.all_gather(master.astype(jnp.bfloat16), ("batch", "pix"), axis=0, tiled=True)
    pieces, used_len = unpack(gathered)
    w_one, w_two, w_qkv, w_proj, w_down, w_emb, class_table, gains_low = pieces
    gains_one = gains_low.astype(jnp.float32)
    n_img, rows_local, cols_local, channels = images.shape
    wide_channels = w_down.shape[1]
    pix_count = lax.axis_size("pix")
    batch_count = lax.axis_size("batch")
    pixels_here = rows_local * cols_local
    pixels_all = pixels_here * pix_count
    pixels_all_two = pixels_all // 4
    images_all = n_img * batch_count
    row_index = jnp.where(null_mask == 1, class_table.shape[0] - 1, labels)
    one_hot = (
        row_index[:, None] == jnp.arange(class_table.shape[0], dtype=jnp.int32)[None, :]
    ).astype(jnp.float32)
    pre_embed = time_vector(levels) + jnp.dot(
        one_hot, class_table.astype(jnp.float32), precision=precise
    )
    embedded = jax.nn.silu(pre_embed)
    w_emb_wide = w_emb.astype(jnp.float32)
    scale_shift = jnp.dot(embedded, w_emb_wide, precision=precise)
    scale_one = scale_shift[:, None, :channels]
    shift_one = scale_shift[:, None, channels:]
    flat_in = images.astype(jnp.float32).reshape(n_img, pixels_here, channels)
    middle, kept_one = res_forward(
        flat_in, gains_one, scale_one, shift_one, w_one, w_two, rows_local, pixels_all
    )
    normed_three, inverse_three = group_forward(middle, pixels_all)
    attn_in = (normed_three * gains_one[4] + gains_one[5]).astype(jnp.bfloat16)
    triples = jnp.dot(attn_in.reshape(-1, channels), w_qkv, preferred_element_type=jnp.float32)
    triples = triples.astype(jnp.bfloat16).reshape(n_img, pixels_here, 3 * channels)
    spread_heads = to_heads(triples)
    local_heads = spread_heads.shape[2] // (3 * HEAD)
    split_heads = spread_heads.reshape(n_img, -1, local_heads, 3, HEAD).transpose(3, 0, 2, 1, 4)
    queries, keys, values = (split_heads[0], split_heads[1], split_heads[2])
    attended, log_total = attend(queries, keys, values)
    attended_px = to_pixels(attended.transpose(0, 2, 1, 3).reshape(n_img, -1, local_heads * HEAD))
    projected = jnp.dot(
        attended_px.reshape(-1, channels), w_proj, preferred_element_type=jnp.float32
    )
    output = middle + projected.reshape(n_img, pixels_here, channels)
    final_out, columns_down = conv_forward(output.astype(jnp.bfloat16), w_down, rows_local, 2)
    pixels_two = final_out.shape[1]
    feat_width = vgg_proj.shape[1]
    online_feat = jnp.dot(
        final_out.astype(jnp.bfloat16).reshape(-1, wide_channels),
        vgg_proj,
        preferred_element_type=jnp.float32,
    )
    online_feat = online_feat.reshape(n_img, pixels_two, feat_width)
    target_feat = jnp.dot(
        target.reshape(-1, wide_channels), vgg_proj, preferred_element_type=jnp.float32
    )
    target_feat = target_feat.reshape(n_img, pixels_two, feat_width)
    target_unit = target_feat * lax.rsqrt(
        jnp.mean(target_feat * target_feat, -1, keepdims=True) + EPS_FEAT
    )
    clean_wide = clean_images.astype(jnp.float32).reshape(n_img, pixels_two, wide_channels)

    def loss_terms(feature, out_value):
        unit = feature * lax.rsqrt(jnp.mean(feature * feature, -1, keepdims=True) + EPS_FEAT)
        consist = jnp.sum(lpips_lin * (unit - target_unit) ** 2, (1, 2)) / (
            feat_width * pixels_all_two
        )
        denoise = jnp.sum((out_value - clean_wide) ** 2, (1, 2)) / (pixels_all_two * wide_channels)
        return (consist, denoise)

    (consist, denoise), pullback = jax.vjp(loss_terms, online_feat, final_out)
    level_hot = (levels[:, None] == jnp.arange(LEVELS, dtype=jnp.int32)[None, :]).astype(
        jnp.float32
    )
    level_pair = lax.psum(
        (jnp.sum(consist[:, None] * level_hot, 0), jnp.sum(level_hot / pix_count, 0)),
        ("batch", "pix"),
    )
    zero_count = level_pair[1][0]
    is_zero = (levels == 0).astype(jnp.float32)
    grad_feat, grad_out = pullback(
        (jnp.full_like(consist, 1.0 / images_all), is_zero / jnp.maximum(zero_count, 1.0))
    )
    grad_feat_low = grad_feat.astype(jnp.bfloat16).reshape(-1, feat_width)
    grad_final = grad_out + jnp.einsum(
        "rf,cf->rc", grad_feat_low, vgg_proj, preferred_element_type=jnp.float32
    ).reshape(n_img, pixels_two, wide_channels)
    d_w_down, grad_output = conv_back(
        columns_down, grad_final.astype(jnp.bfloat16), w_down, rows_local, 2
    )
    grad_proj = grad_output.astype(jnp.bfloat16).reshape(-1, channels)
    d_w_proj = jnp.einsum(
        "rc,rd->cd",
        attended_px.reshape(-1, channels),
        grad_proj,
        preferred_element_type=jnp.float32,
    )
    grad_att_px = jnp.einsum("rd,cd->rc", grad_proj, w_proj, preferred_element_type=jnp.float32)
    grad_att_px = grad_att_px.astype(jnp.bfloat16).reshape(n_img, pixels_here, channels)
    grad_heads = to_heads(grad_att_px)
    grad_split = grad_heads.reshape(n_img, -1, local_heads, HEAD).transpose(0, 2, 1, 3)
    grad_q, grad_k, grad_v = attend_back(queries, keys, values, log_total, grad_split)
    grad_triples = jnp.stack([grad_q, grad_k, grad_v], 3).transpose(0, 2, 1, 3, 4)
    grad_triples = grad_triples.reshape(n_img, -1, local_heads * 3 * HEAD).astype(jnp.bfloat16)
    grad_triples = to_pixels(grad_triples)
    grad_rows = grad_triples.reshape(-1, 3 * channels)
    d_w_qkv = jnp.einsum(
        "rc,rd->cd", attn_in.reshape(-1, channels), grad_rows, preferred_element_type=jnp.float32
    )
    grad_attn_in = jnp.einsum(
        "rd,cd->rc", grad_rows, w_qkv, preferred_element_type=jnp.float32
    ).reshape(n_img, pixels_here, channels)
    d_gain_three = jnp.sum(grad_attn_in * normed_three, (0, 1))
    d_bias_three = jnp.sum(grad_attn_in, (0, 1))
    grad_middle = grad_output + group_backward(
        grad_attn_in * gains_one[4], normed_three, inverse_three, pixels_all
    )
    d_w_one, d_w_two, d_gains_one, d_scale_one, d_shift_one, unused_grad = res_back(
        grad_middle, kept_one, gains_one, scale_one, w_one, w_two, rows_local, pixels_all
    )
    grad_scale_shift = jnp.concatenate([d_scale_one, d_shift_one], 1)
    d_w_emb = jnp.dot(embedded.T, grad_scale_shift, precision=precise)
    grad_embedded = jnp.dot(grad_scale_shift, w_emb_wide.T, precision=precise)
    d_table = jnp.dot(one_hot.T, grad_embedded * silu_slope(pre_embed), precision=precise)
    d_norms_one = jnp.concatenate([d_gains_one, jnp.stack([d_gain_three, d_bias_three])], 0)
    flat_grad = jnp.concatenate(
        [
            d_w_one.ravel(),
            d_w_two.ravel(),
            d_w_qkv.ravel(),
            d_w_proj.ravel(),
            d_w_down.ravel(),
            d_w_emb.ravel(),
            d_table.ravel(),
            d_norms_one.ravel(),
            jnp.zeros((gathered.shape[0] - used_len,), jnp.float32),
        ]
    )
    own_grad = lax.psum_scatter(flat_grad, ("batch", "pix"), scatter_dimension=0, tiled=True)
    norm_before = jnp.sqrt(lax.psum(jnp.sum(own_grad * own_grad), ("batch", "pix")))
    clipped = own_grad * jnp.minimum(1.0, CLIP / norm_before)
    new_first = BETA_ONE * first_moment + (1.0 - BETA_ONE) * clipped
    new_second = BETA_TWO * second_moment + (1.0 - BETA_TWO) * clipped * clipped
    fixed_first = new_first / (1.0 - BETA_ONE**STEP)
    fixed_second = new_second / (1.0 - BETA_TWO**STEP)
    new_master = master - RATE * (
        fixed_first / (jnp.sqrt(fixed_second) + EPS_ADAM) + DECAY * master
    )
    level_sums = jnp.stack([level_pair[0], level_pair[1]])
    return (
        new_master,
        new_first,
        new_second,
        new_master.astype(jnp.bfloat16),
        norm_before,
        level_sums,
    )


MESH = pl.DeviceIdType.MESH
ROWS=537; BLK=560; HALF=288
PX=512
R_ONE,R_TWO,R_QKV,R_PROJ,R_DOWN,R_EMB,R_TAB,R_GAIN,R_END=0,3456,6912,8064,8448,13632,15168,17170,17184
f32=jnp.float32; bf=jnp.bfloat16
class Comm:
    def __init__(self): self.sent=[]
    def go(self, cond, src, dst, ssem, rsem, b, p):
        c = pltpu.make_async_remote_copy(src_ref=src,dst_ref=dst,send_sem=ssem,recv_sem=rsem,device_id=(b,p),device_id_type=MESH)
        if cond is None: c.start()
        else: pl.when(cond)(lambda: c.start())
        self.sent.append((cond,c))
    def drain(self):
        for cond,c in self.sent:
            if cond is None: c.wait_send()
            else: pl.when(cond)(lambda c=c: c.wait_send())
        self.sent=[]

def place():
    b=lax.axis_index("batch"); p=lax.axis_index("pix")
    core=lax.rem(b,2); y=lax.rem(lax.div(b,2),2); z=lax.div(b,4)
    return b,p,core,y,z

def base_of(s): return 16*((ROWS*s)//16)
def dg(a,b,ca,cb): return lax.dot_general(a,b,(((ca,),(cb,)),((),())),preferred_element_type=f32)
def nn(a,b): return dg(a,b,1,0)
def nt(a,b): return dg(a,b,1,1)
def tn(a,b): return dg(a,b,0,0)
def split3(v):
    hi=v.astype(bf); r=v-hi.astype(f32); mid=r.astype(bf); lo=(r-mid.astype(f32)).astype(bf)
    return hi,mid,lo
def exact(v,w,dot):
    hi,mid,lo=split3(v)
    return dot(hi,w)+dot(mid,w)+dot(lo,w)
def sigmoid(v): return 1.0/(1.0+jnp.exp(-v))
def silu(v): return v*sigmoid(v)
def slope(v):
    s=sigmoid(v)
    return s*(1.0+v*(1.0-s))
def cloop(n,chunk,body,init):
    return lax.fori_loop(0,n//chunk,lambda i,c: body(pl.multiple_of(i*chunk,chunk),c),init)
def col8(v): return jnp.sum(v.reshape(-1,8,v.shape[-1]),axis=0)
Z8=lambda: jnp.zeros((8,CH),f32)
class Blocks:
    def __init__(self,ref,n): self.ref=ref; self.n=n
def at_block(ref,j,sl):
    if isinstance(ref,Blocks): return ref.ref,(pl.ds(ref.n*j+sl.start,sl.size,stride=sl.stride),slice(None))
    return ref,(j,sl,slice(None))
def ld(ref,sl):
    out=[]
    for j in range(ref.ref.shape[0]//ref.n if isinstance(ref,Blocks) else ref.shape[0]):
        r,k=at_block(ref,j,sl)
        out.append(r[k])
    return jnp.concatenate(out,1)
def put3(ref,sl,v):
    for j in range(v.shape[1]//128):
        r,k=at_block(ref,j,sl)
        r[k]=v[:,128*j:128*j+128]
def every(start,n,step): return pl.ds(start,n,stride=step)
def row(v): return jnp.sum(v,axis=0,keepdims=True)


LAST=25
def step_kernel(images_all,
    mast,img,tgt,cln,vgg,lin,tvec,rowid,level,gm,
    flat_ref,all_ref,g_ref,
    wv,tails,cvt,cvt2,wd,wee,weo,wqT,x3a,x3b,z3,inner,middle,gout,gsec,ain,trT,dtrT,attT,xd,lse,dattT,ssend,srecv,hsend,hrecv,himg,dzs,dzr,geo,oth,wsem,tsem,xs,xr,total,blk,own_sem,azs,azr,axs,axr,ays,ayr,adas,adar,adbs,adbr,ass,asr,pack_ref,lpk,ppk,red1,red2,tile,lps,lpr,pps,ppr,n1s,n1r,n2s,n2r,sibr,rb,rx,ry,zu,zd,s1s,s1r,das,dar,dbs,dbr,rxs,rxr,rys,ryr,zs,zur,zdr,acc,gtile,gls,glr,gps,gpr,rba,a2s,a2r):
    b,p,core,y,z=place()
    q=1-p; xn=q; s=b*2+p
    pf=p.astype(f32); qf=1.0-pf
    yn=b+2-4*y; sib=b+1-2*core; oc=1-core
    up_ok=z<3; dn_ok=z>0
    top=z==3
    mine=(y*2+core)*2+p
    cvt3=Blocks(cvt,1536)
    mcopy=pltpu.make_async_copy(mast,cvt.at[pl.ds(0,1611)],own_sem)
    mcopy.start()
    barrier=pltpu.get_barrier_semaphore()
    plane=[]
    for dy in range(2):
        for dc in range(2):
            for dp in range(2):
                if dy+dc+dp: plane.append((4*dy+2*dc+dp,z*4+lax.rem(y+dy,2)*2+lax.rem(core+dc,2),lax.rem(p+dp,2)))
    line=[(k,lax.rem(z+k,4)) for k in range(1,4)]
    def sig(bb,pp): pl.semaphore_signal(barrier,inc=1,device_id=(bb,pp),device_id_type=MESH)
    for _,bb,pp in plane: sig(bb,pp)
    for _,zz in line: sig(b+4*(zz-z),p)
    def when(ok,f):
        if ok is None: f()
        else: pl.when(ok)(f)
    def AND(*c):
        r=None
        for k in c:
            if k is not None: r=k if r is None else r&k
        return r
    def wait_in(ref,sem):
        pltpu.make_async_remote_copy(src_ref=ref,dst_ref=ref,send_sem=sem,recv_sem=sem,device_id=(b,xn),device_id_type=MESH).wait_recv()
    def slot(zz,yy,pp,cc=core): return ((zz*2+yy)*2+cc)*2+pp
    A=pl.ds(0,HALF); B=pl.ds(HALF,BLK-HALF)
    cm=Comm()
    shift=lax.rem(9*s,16)
    total[ROWS-1:BLK]=jnp.zeros((BLK-ROWS+1,CH),f32)
    mcopy.wait()
    for j in range(3): total[0:ROWS,128*j:128*j+128]=cvt[pl.ds(j,ROWS,stride=3),:]
    at=lax.broadcasted_iota(jnp.int32,(BLK,CH),0)
    blk[...]=jnp.where(at==BLK-4,(level[...]==0).astype(f32),pltpu.roll(total[...],shift,0)).astype(bf)
    own=pltpu.make_async_copy(blk,g_ref.at[s],own_sem)
    own.start()
    pl.semaphore_wait(barrier,10)
    def valid(zz): return (zz>=0)&(zz<4)
    def pick(c0,c1,c2,c3): return jnp.where(z==0,c0,jnp.where(z==1,c1,jnp.where(z==2,c2,c3)))
    hs=(A,B)
    ends=(z==0)|(z==3); is1=z==1; is2=z==2; inner_z=jnp.logical_not(ends)
    f0=pick(0,0,3,3); f1=3-f0
    def z_send(ok,zz,h,d,src=None):
        g=g_ref.at[slot(zz,y,p),hs[h]]
        cm.go(ok,g if src is None else src,g,azs.at[zz,h,(1-d)//2],azr.at[zz,h],b+4*d,p)
    def xy_send(ok,zz,h,src=None):
        g=g_ref.at[slot(zz,y,p),hs[h]]
        cm.go(ok,g if src is None else src,g,axs.at[zz,h],axr.at[zz,h],b,xn)
        cm.go(ok,g if src is None else src,g,ays.at[zz,h],ayr.at[zz,h],yn,p)
    def sib_send(ok,zz,yy,pp,h,src=None):
        g=g_ref.at[slot(zz,yy,pp),hs[h]]
        cm.go(ok,g if src is None else src,g,ass.at[zz,yy,pp,h],asr.at[zz,yy,pp,h],sib,p)
    def own_sends():
        for h in range(2):
            src=blk.at[hs[h]]
            z_send(z==0,z,h,1,src)
            z_send(z==3,z,h,-1,src)
            sib_send(None,z,y,p,h,src)
    def own_xy():
        for h in range(2): xy_send(z!=1,z,h,blk.at[hs[h]])
    four=((1-y,xn),(y,xn),(1-y,p),(y,p))
    def two_send(ok,i,d):
        yy,pp=four[i]
        for h in range(2):
            g=g_ref.at[slot(2,yy,pp),hs[h]]
            cm.go(ok,g,g,a2s.at[yy,pp,h,(1-d)//2],a2r.at[yy,pp,h],b+4*d,p)
    def two_in(i,ok):
        yy,pp=four[i]
        for h in range(2):
            g=g_ref.at[slot(2,yy,pp),hs[h]]
            when(ok,lambda: wait_in(g,a2r.at[yy,pp,h]))
            cm.go(ok&(z==1),g,g,a2s.at[yy,pp,h,1],a2r.at[yy,pp,h],b-4,p)
            sib_send(ok,2,yy,pp,h)
    def two_diag():
        sd=slot(2,1-y,xn)
        def f():
            wait_in(g_ref.at[sd,A],adar.at[2])
            wait_in(g_ref.at[sd,B],adbr.at[2])
        when(z==2,f)
        for h in range(2): sib_send(z==2,2,1-y,xn,h)
    def arrive(f,h):
        ok=f!=z
        when(ok,lambda: wait_in(g_ref.at[slot(f,y,p),hs[h]],azr.at[f,h]))
        z_send(ok&(f==0)&up_ok,f,h,1)
        z_send(ok&(f==3)&dn_ok,f,h,-1)
        xy_send(ok,f,h)
        sib_send(ok,f,y,p,h)
    def xy_arrive(ok,f,h):
        sx=slot(f,y,xn); sy=slot(f,1-y,p)
        when(ok,lambda: wait_in(g_ref.at[sx,hs[h]],axr.at[f,h]))
        if h==0: cm.go(ok,g_ref.at[sx,A],g_ref.at[sx,A],adas.at[f],adar.at[f],yn,p)
        sib_send(ok,f,y,xn,h)
        when(ok,lambda: wait_in(g_ref.at[sy,hs[h]],ayr.at[f,h]))
        if h==1: cm.go(ok,g_ref.at[sy,B],g_ref.at[sy,B],adbs.at[f],adbr.at[f],b,xn)
        sib_send(ok,f,1-y,p,h)
    def later_sends():
        for h in range(2):
            src=blk.at[hs[h]]
            z_send(z==1,z,h,1,src)
            z_send(z==1,z,h,-1,src)
    def one_in(h,ok):
        when(ok,lambda: wait_in(g_ref.at[slot(1,y,p),hs[h]],azr.at[1,h]))
        z_send(ok&is2,1,h,1)
        sib_send(ok,1,y,p,h)
    def load(sl): return (pltpu.make_async_copy(g_ref.at[sl,pl.ds(0,528)],wv.at[pl.ds(pl.multiple_of(16*lax.div(ROWS*sl,16),16),528)],wsem.at[sl]),
                          pltpu.make_async_copy(g_ref.at[sl,pl.ds(528,32)],tails.at[sl],tsem.at[sl]))
    def d_arrive(zz):
        sd=slot(zz,1-y,xn)
        wait_in(g_ref.at[sd,A],adar.at[zz])
        sib_send(None,zz,1-y,xn,0)
        wait_in(g_ref.at[sd,B],adbr.at[zz])
        sib_send(None,zz,1-y,xn,1)
        for yy in range(2):
            for pp in range(2):
                for c in load(slot(zz,yy,pp)): c.start()
    def sib_arrive(zz):
        for yy in range(2):
            for pp in range(2):
                sl=slot(zz,yy,pp,oc)
                for h in range(2): wait_in(g_ref.at[sl,hs[h]],asr.at[zz,yy,pp,h])
                for c in load(sl): c.start()
    has_gains=s==31
    gain_line=(y==1)&(core==1)&(p==1)
    def gain_sends():
        for k,zz in line: cm.go(has_gains,blk.at[pl.ds(528,16)],gtile,gls.at[k],glr,b+4*(zz-z),p)
    def gain_pass():
        pl.when(has_gains)(lambda: gtile.__setitem__(Ellipsis,blk[528:544]))
        pl.when(gain_line&jnp.logical_not(has_gains))(lambda: wait_in(gtile,glr))
        for d,bb,pp in plane: cm.go(gain_line,gtile,gtile,gps.at[d],gpr,bb,pp)
    def gain_wait():
        pl.when(jnp.logical_not(gain_line))(lambda: wait_in(gtile,gpr))
    seen=[]
    def take(shards):
        for k in shards:
            for c in load(k): c.wait()
            lo=base_of(k)
            if k<31 and base_of(k+1)-lo==544 or k==31: wv[lo+528:lo+544]=tails[k,0:16]
            seen.append(k)
        for k in range(1,32):
            if k in seen and k-1 in seen and (k in shards or k-1 in shards):
                off=base_of(k)-base_of(k-1)-528
                t=tails[k-1,off:off+16].astype(f32)
                if off: t=jnp.where(lax.broadcasted_iota(jnp.int32,(16,CH),0)<8,t,0.0)
                lo=base_of(k)
                wv[lo:lo+16]=(wv[lo:lo+16].astype(f32)+t).astype(bf)
    def rows(u,yy,pp,cc=core):
        at=pl.ds(pl.multiple_of(16*lax.div(ROWS*slot(u,yy,pp,cc),16),16),BLK)
        return wd.at[at,pl.ds(0,CH)] if u==0 else wv.at[at]
    def need(u,yy,pp,cc=core): return None if u<3 else slot(u,yy,pp,cc)<=LAST
    def sibsend(u):
        for yy,pp in four:
            cm.go(need(u,yy,pp,oc),rows(u,yy,pp,oc),sibr.at[4*u+2*yy+pp],s1s.at[u,yy,pp],s1r.at[u,yy,pp],sib,p)
    def both(u,yy,pp,lo,n):
        a=pl.multiple_of(16*lax.div(ROWS*slot(u,yy,pp),16)+lo,16)
        mine_=wd[pl.ds(a,n),0:CH] if u==0 else wv[pl.ds(a,n)]
        return mine_.astype(f32)+sibr[4*u+2*yy+pp,lo:lo+n].astype(f32)
    HA=(0,HALF); HB=(HALF,BLK-HALF)
    def sib_in(u,yy,pp): wait_in(sibr.at[4*u+2*yy+pp],s1r.at[u,yy,pp])
    def keep(u,yy,pp,half,more=None):
        t=both(u,yy,pp,*half)
        if more is not None: t=t+more.astype(f32)
        sibr[4*u+2*yy+pp,half[0]:half[0]+half[1]]=t.astype(bf)
    def diag(u):
        yy,pp=1-y,xn
        c=need(u,yy,pp)
        def f():
            sib_in(u,yy,pp)
            keep(u,yy,pp,HA); keep(u,yy,pp,HB)
        when(c,f)
        src=sibr.at[4*u+2*yy+pp]
        if u==0: cm.go(c,src.at[A],rba.at[u],das.at[u],dar.at[u],b,xn)
        else: cm.go(c,src.at[A],rba.at[u],das.at[u],dar.at[u],yn,p)
        cm.go(c,src.at[B],rb.at[u],dbs.at[u],dbr.at[u],yn,p)
    def ysend(u):
        c=need(u,1-y,p)
        def f():
            sib_in(u,1-y,p)
            keep(u,1-y,p,HA); keep(u,1-y,p,HB)
        when(c,f)
        for h in range(2): cm.go(c,sibr.at[4*u+2*(1-y)+p,hs[h]],ry.at[u,hs[h]],rys.at[u,h],ryr.at[u,h],yn,p)
    def xsend(u):
        c=need(u,y,xn)
        def f():
            sib_in(u,y,xn)
            wait_in(rba.at[u],dar.at[u])
            keep(u,y,xn,HA,rba[u])
        when(c,f)
        cm.go(c,sibr.at[4*u+2*y+xn,A],rx.at[u,A],rxs.at[u,0],rxr.at[u,0],b,xn)
        def f2():
            wait_in(rb.at[u],dbr.at[u])
            keep(u,y,xn,HB,rb[u])
        when(c,f2)
        cm.go(c,sibr.at[4*u+2*y+xn,B],rx.at[u,B],rxs.at[u,1],rxr.at[u,1],b,xn)
    def first_halves(u):
        sib_in(u,y,xn)
        keep(u,y,xn,HA)
        cm.go(None,sibr.at[4*u+2*y+xn,A],rx.at[u,A],rxs.at[u,0],rxr.at[u,0],b,xn)
        sib_in(u,1-y,p)
        keep(u,1-y,p,HB)
        cm.go(None,sibr.at[4*u+2*(1-y)+p,B],ry.at[u,B],rys.at[u,1],ryr.at[u,1],yn,p)
    def second_halves(u):
        wait_in(rba.at[u],dar.at[u])
        keep(u,1-y,p,HA,rba[u])
        cm.go(None,sibr.at[4*u+2*(1-y)+p,A],ry.at[u,A],rys.at[u,0],ryr.at[u,0],yn,p)
        wait_in(rb.at[u],dbr.at[u])
        keep(u,y,xn,HB,rb[u])
        cm.go(None,sibr.at[4*u+2*y+xn,B],rx.at[u,B],rxs.at[u,1],rxr.at[u,1],b,xn)
    def chunks(u): return ((0,144,0),(144,144,0),(288,144,1),(432,128,1)) if u==0 else ((0,HALF,0),(HALF,BLK-HALF,1))
    def xy_in(u,h):
        wait_in(rx.at[u,hs[h]],rxr.at[u,h])
        wait_in(ry.at[u,hs[h]],ryr.at[u,h])
    def zstep(u,i):
        for d in (1,-1):
            at_z=i if d==1 else 3-i
            if not (at_z<u if d==1 else at_z>u): continue
            c=AND(need(u,y,p),z==at_z)
            buf,bsem=(zu.at[u-1],zur) if d==1 else (zd.at[u],zdr)
            own_at=4*u+2*y+p
            def first(): sib_in(u,y,p)
            when(c,first)
            seen_h=set()
            for k,(lo,n,h) in enumerate(chunks(u)):
                def f():
                    if h not in seen_h: xy_in(u,h)
                    t=both(u,y,p,lo,n)+rx[u,lo:lo+n].astype(f32)+ry[u,lo:lo+n].astype(f32)
                    if i>0:
                        wait_in(buf.at[pl.ds(lo,n)],bsem.at[u,k])
                        t=t+buf[lo:lo+n].astype(f32)
                    sibr[own_at,lo:lo+n]=t.astype(bf)
                when(c,f)
                seen_h.add(h)
                cm.go(c,sibr.at[own_at,pl.ds(lo,n)],buf.at[pl.ds(lo,n)],zs.at[u,k],bsem.at[u,k],b+4*d,p)
    def zend(u):
        def f():
            sib_in(u,y,p)
            done=set()
            for k,(lo,n,h) in enumerate(chunks(u)):
                if h not in done: xy_in(u,h); done.add(h)
                t=both(u,y,p,lo,n)+rx[u,lo:lo+n].astype(f32)+ry[u,lo:lo+n].astype(f32)
                if u>0:
                    wait_in(zu.at[u-1,pl.ds(lo,n)],zur.at[u,k])
                    t=t+zu[u-1,lo:lo+n].astype(f32)
                if u<3:
                    wait_in(zd.at[u,pl.ds(lo,n)],zdr.at[u,k])
                    t=t+zd[u,lo:lo+n].astype(f32)
                total[lo:lo+n]=t
        when(AND(need(u,y,p),z==u),f)
    state={"k":0}
    def xchg(src,dst,dst_like=None):
        k=state["k"]; state["k"]=k+1
        c=pltpu.make_async_remote_copy(src_ref=src,dst_ref=dst,send_sem=xs.at[k],recv_sem=xr.at[k],device_id=(b,q),device_id_type=MESH)
        c.start()
        return c
    edge=pl.ds(pl.multiple_of(q*480,32),32)
    gain_sends()
    own_sends()
    gain_pass()
    own_xy()
    c_img=xchg(img.at[edge],himg)
    def gsum(v): return exact(v,gm[...],nn)
    def swap_sums(k,s1,s2):
        ssend[k]=jnp.concatenate([s1,s2,jnp.zeros((6,CH),f32)],0)
        return xchg(ssend.at[k],srecv.at[k])
    def total_sums(k):
        t=gsum(ssend[k]+srecv[k])*(1.0/(12*2*PX))
        return t[0:1],t[1:2]
    def norm_of(t):
        mean,sq=t
        return mean,lax.rsqrt(sq-mean*mean+EPS_NORM)
    def fill3(dst,at,a):
        col=lax.broadcasted_iota(jnp.int32,a.shape,0)&31
        n=a.shape[0]
        dst[pl.ds(at,n),CH:2*CH]=a.astype(bf)
        dst[pl.ds(at,n),0:CH]=jnp.where(col==0,0.0,pltpu.roll(a,1,0)).astype(bf)
        dst[pl.ds(at,n),2*CH:3*CH]=jnp.where(col==31,0.0,pltpu.roll(a,n-1,0)).astype(bf)
    def fill_edges(dst,h):
        fill3(dst,0,h*pf); fill3(dst,544,h*qf)
    def conv_to(dst,x3,wrow,add=None):
        for dr in range(3):
            d=nn(x3[32*dr:32*dr+PX],wv[wrow+1152*dr:wrow+1152*dr+1152])
            if dr==0: dst[...]=d if add is None else add()+d
            else: dst[...]+=d
    def conv_dx(dst,wrow):
        first=True
        for dr in range(3):
            for dc in range(3):
                d=nt(z3[32*(2-dr):32*(2-dr)+PX,CH*(2-dc):CH*(2-dc)+CH],wv[wrow+CH*(3*dr+dc):wrow+CH*(3*dr+dc)+CH])
                if first: dst[...]=d
                else: dst[...]+=d
                first=False
    def st(i,c):
        v=img[pl.ds(i,64)].astype(f32)
        return c[0]+col8(v),c[1]+col8(v*v)
    a1,a2=cloop(PX,64,st,(Z8(),Z8()))
    c=swap_sums(0,row(a1),row(a2))
    arrive(f0,0)
    gain_wait()
    g6=gtile[...].astype(f32)
    g1,b1,g2,b2,g3,b3=[g6[2+i:3+i] for i in range(6)]
    c.wait()
    mean1,inv1=norm_of(total_sums(0))
    def act_of(v): return silu((v-mean1)*inv1*g1+b1)
    arrive(f0,1)
    def fa(i,_):
        fill3(x3a,pl.multiple_of(i+32,32),act_of(img[pl.ds(i,64)].astype(f32)))
        return 0
    cloop(PX,64,fa,0)
    c_img.wait()
    fill_edges(x3a,act_of(himg[...].astype(f32)))
    own.wait()
    xy_arrive(is2,2,0)
    xy_arrive(is2,2,1)
    xy_arrive(ends,f0,0)
    xy_arrive(ends,f0,1)
    arrive(f1,0)
    xy_arrive(inner_z,f0,0)
    arrive(f1,1)
    later_sends()
    two_send(is2,3,-1)
    two_send(is2,1,-1); two_send(is2,2,-1)
    xy_arrive(inner_z,f0,1)
    one_in(0,is2)
    one_in(1,is2)
    for i in (3,1,2): two_send(is2,i,1)
    two_diag()
    two_send(is2,0,-1); two_send(is2,0,1)
    d_arrive(f0)
    xy_arrive(None,f1,0)
    xy_arrive(None,f1,1)
    d_arrive(f1)
    sib_arrive(f0)
    one_in(0,ends)
    one_in(1,ends)
    for h in range(2): xy_send(None,1,h)
    sib_arrive(f1)
    two_in(3,is1)
    take(range(24,32)); take(range(0,8))
    conv_to(inner,x3a,R_ONE)
    xy_arrive(None,1,0)
    def st2(i,c):
        v=inner[pl.ds(i,64)]
        return c[0]+col8(v),c[1]+col8(v*v)
    a1,a2=cloop(PX,64,st2,(Z8(),Z8()))
    c1=swap_sums(1,row(a1),row(a2))
    c2=xchg(inner.at[edge],hrecv.at[0])
    ids=rowid[...]
    pre=[]
    tcol=lax.broadcasted_iota(jnp.int32,(16,R_END-R_TAB),1)
    for h in range(2):
        hot=(tcol==2*ids+h).astype(f32).astype(bf)
        pre.append(nn(hot,wv[R_TAB:R_END])[0:1]+tvec[:,CH*h:CH*h+CH])
    emb=[silu(v) for v in pre]
    put3(cvt3,pl.ds(0,1536),wv[R_EMB:R_TAB].astype(f32))
    wee[...]=ld(cvt3,every(0,768,2)).astype(bf)
    weo[...]=ld(cvt3,every(1,768,2)).astype(bf)
    def emb_dot(w):
        r=None
        for h in range(2):
            e=jnp.broadcast_to(emb[h],(16,CH))
            d=exact(e,w[CH*h:CH*h+CH],nn)[0:1]
            r=d if r is None else r+d
        return r
    sc1=1.0+emb_dot(wee); sh=emb_dot(weo)
    xy_arrive(None,1,1)
    c1.wait()
    mean2,inv2=norm_of(total_sums(1))
    def pre_b(v):
        n=(v-mean2)*inv2
        af=n*g2+b2
        return n,af,af*sc1+sh
    def fb(i,_):
        fill3(x3b,pl.multiple_of(i+32,32),silu(pre_b(inner[pl.ds(i,64)])[2]))
        return 0
    cloop(PX,64,fb,0)
    c2.wait()
    fill_edges(x3b,silu(pre_b(hrecv[0])[2]))
    two_in(1,is1)
    two_in(2,is1)
    d_arrive(1)
    sib_arrive(1)
    take(range(8,16))
    conv_to(middle,x3b,R_TWO,lambda: img[...].astype(f32))
    def st3(i,c):
        v=middle[pl.ds(i,64)]
        return c[0]+col8(v),c[1]+col8(v*v)
    a1,a2=cloop(PX,64,st3,(Z8(),Z8()))
    c1=swap_sums(2,row(a1),row(a2))
    put3(cvt3,pl.ds(0,1152),wv[R_QKV:R_PROJ].astype(f32))
    for j in range(3):
        wqT[CH*j:CH*j+CH]=ld(cvt3,every(j,CH,3)).T.astype(bf)
    c1.wait()
    mean3,inv3=norm_of(total_sums(2))
    def fc(i,_):
        n=(middle[pl.ds(i,64)]-mean3)*inv3
        ain[pl.ds(i,64)]=(n*g3+b3).astype(bf)
        return 0
    cloop(PX,64,fc,0)
    c1=xchg(ain.at[pl.ds(0,PX)],ain.at[pl.ds(PX,PX)])
    def triples(a):
        t=nt(wqT[...],a)
        is_q=lax.rem(lax.broadcasted_iota(jnp.int32,t.shape,0),192)<64
        return jnp.where(is_q,t*0.125,t).astype(bf)
    trT[:,0:PX]=triples(ain[0:PX])
    two_in(0,is1)
    def head_rows(h):
        r0=pl.multiple_of(h*192,64)
        return r0,pl.multiple_of(r0+64,64),pl.multiple_of(r0+128,64)
    def fh1(h,_):
        r0,r1,r2=head_rows(h)
        sco=nn(trT[pl.ds(r1,64),0:PX].T,trT[pl.ds(r0,64),0:PX])
        m=jnp.max(sco,0,keepdims=True)
        e=jnp.exp(sco-m)
        lse[h,0:1]=m
        lse[h,1:2]=jnp.sum(e,0,keepdims=True)
        acc[h]=nn(trT[pl.ds(r2,64),0:PX],e.astype(bf))
        return 0
    lax.fori_loop(0,6,fh1,0)
    c1.wait()
    trT[:,PX:2*PX]=triples(ain[PX:2*PX])
    def fh(h,_):
        r0,r1,r2=head_rows(h)
        sco=nn(trT[pl.ds(r1,64),PX:2*PX].T,trT[pl.ds(r0,64),0:PX])
        m0=lse[h,0:1]
        m=jnp.maximum(m0,jnp.max(sco,0,keepdims=True))
        e=jnp.exp(sco-m)
        a=jnp.exp(m0-m)
        l=lse[h,1:2]*a+jnp.sum(e,0,keepdims=True)
        o=acc[h]*a+nn(trT[pl.ds(r2,64),PX:2*PX],e.astype(bf))
        attT[pl.ds(pl.multiple_of(h*64,64),64),:]=(o*(1.0/l)).astype(bf)
        lse[h,0:1]=m+jnp.log(l)
        return 0
    lax.fori_loop(0,6,fh,0)
    put3(gout,pl.ds(0,PX),middle[...]+tn(attT[...],wv[R_PROJ:R_DOWN]))
    hsend[0]=ld(gout,edge).astype(bf)
    c1=xchg(hsend.at[0],oth.at[0])
    for i in (3,1,2,0): two_in(i,ends)
    for yy in range(2):
        for pp in range(2):
            for k in load(slot(2,yy,pp)): k.start()
    sib_arrive(2)
    take(range(16,24))
    for off in range(9):
        put3(cvt3,pl.ds(0,576),wv[R_DOWN+576*off:R_DOWN+576*off+576].astype(f32))
        v0,v1,v2=[ld(cvt3,every(i,192,3)) for i in range(3)]
        put3(cvt2,every(0,192,2),jnp.concatenate([v0,v1[:,0:256]],1))
        w=jnp.concatenate([v1[:,128:384],v2],1)
        w=pltpu.roll(w,w.shape[1]-64,1)
        put3(cvt2,every(1,192,2),w)
        wd[CH*off:CH*off+CH]=ld(cvt2,pl.ds(0,CH))[:,0:576].astype(bf)
    def parts(ref,n):
        e=ld(ref,every(0,n//2,2)); o=ld(ref,every(1,n//2,2))
        col=lax.broadcasted_iota(jnp.int32,o.shape,0)&15
        return jnp.where(col==0,0.0,pltpu.roll(o,1,0)).astype(bf),e.astype(bf),o.astype(bf)
    for dc,v in enumerate(parts(gout,PX)):
        v=v.reshape(8,32,CH)
        even=v[:,0:16].reshape(128,CH); odd=v[:,16:32].reshape(128,CH)
        xd[:,CH*(3+dc):CH*(3+dc)+CH]=even
        xd[:,CH*(6+dc):CH*(6+dc)+CH]=odd
        xd[16:128,CH*dc:CH*dc+CH]=odd[0:112]
    c1.wait()
    put3(geo,pl.ds(0,32),oth[0].astype(f32)*pf)
    for dc,v in enumerate(parts(geo,32)):
        xd[0:16,CH*dc:CH*dc+CH]=v
    fin=nn(xd[...],wd[0:9*CH])
    feat=nn(fin.astype(bf),vgg[...]); tf=nn(tgt[...],vgg[...])
    ir=lax.rsqrt(jnp.mean(feat*feat,-1,keepdims=True)+EPS_FEAT)
    unit=feat*ir
    diff=unit-tf*lax.rsqrt(jnp.mean(tf*tf,-1,keepdims=True)+EPS_FEAT)
    wl=lin[...]*diff
    consist=jnp.sum(row(wl*diff),1,keepdims=True)*(1.0/(256*256))
    du=wl*(2.0/(256*256*images_all))
    dfeat=(ir*(du-unit*jnp.mean(du*unit,-1,keepdims=True))).astype(bf)
    zc=jnp.zeros((16,128),f32)
    for t_ in range(0,32,2): zc=zc+tails[t_,16:32,0:128].astype(f32)
    zc=zc[12:13,0:1]
    seed=(level[...]==0).astype(f32)/jnp.maximum(zc,1.0)*(2.0/(256*CH2))
    gfin=nt(dfeat,vgg[...])+seed*(fin-cln[...].astype(f32))
    dz=gfin.astype(bf)
    dzs[...]=dz[0:16]
    c1=xchg(dzs,dzr)
    for off in range(9):
        dw=tn(xd[:,CH*off:CH*off+CH],dz)
        put3(cvt2,pl.ds(0,CH),jnp.concatenate([dw,jnp.zeros((CH,64),f32)],1))
        e=ld(cvt2,every(0,192,2)); o_=pltpu.roll(ld(cvt2,every(1,192,2)),64,1)
        lane=lax.broadcasted_iota(jnp.int32,(192,128),1)
        put3(cvt3,every(0,192,3),e[:,0:384])
        put3(cvt3,every(1,192,3),jnp.concatenate([e[:,384:512],jnp.where(lane<64,e[:,512:640],o_[:,0:128]),o_[:,128:256]],1))
        put3(cvt3,every(2,192,3),o_[:,256:640])
        wv[R_DOWN+576*off:R_DOWN+576*off+576]=ld(cvt3,pl.ds(0,576)).astype(bf)
    sibsend(2); sibsend(3)
    c1.wait()
    z32=dz.astype(f32)
    down=jnp.concatenate([z32[16:128],dzr[...].astype(f32)*qf],0)
    def left(v):
        col=lax.broadcasted_iota(jnp.int32,v.shape,0)&15
        return jnp.where(col==15,0.0,pltpu.roll(v,127,0)).astype(bf)
    s00,s01,s10,s11=dz,left(z32),down.astype(bf),left(down)
    W=lambda a,c: wd[CH*(3*a+c):CH*(3*a+c)+CH]
    def put(a,c,v):
        for i in range(8):
            put3(gout,every((2*i+a)*32+c,16,2),v[16*i:16*i+16])
    put(0,0,nt(s00,W(1,1)))
    put(0,1,nt(s00,W(1,2))+nt(s01,W(1,0)))
    put(1,0,nt(s00,W(2,1))+nt(s10,W(0,1)))
    put(1,1,nt(s00,W(2,2))+nt(s01,W(2,0))+nt(s10,W(0,2))+nt(s11,W(0,0)))
    diag(2); diag(3); ysend(2); ysend(3)
    gp=ld(gout,pl.ds(0,PX)).astype(bf)
    dattT[...]=nt(wv[R_PROJ:R_DOWN],gp).astype(bf)
    wv[R_PROJ:R_DOWN]=nn(attT[...],gp).astype(bf)
    def bh_part(h,at):
        r0,r1,r2=head_rows(h)
        ra_=pl.ds(pl.multiple_of(h*64,64),64)
        qT=trT[pl.ds(r0,64),0:PX]
        kT=trT[pl.ds(r1,64),at:at+PX]
        gT=dattT[ra_,:]
        pr=jnp.exp(nn(kT.T,qT)-lse[h,0:1])
        de=jnp.sum(gT.astype(f32)*attT[ra_,:].astype(f32),0,keepdims=True)
        ds=(pr*(nn(trT[pl.ds(r2,64),at:at+PX].T,gT)-de)).astype(bf)
        dtrT[pl.ds(r1,64),at:at+PX]=nt(qT,ds).astype(bf)
        dtrT[pl.ds(r2,64),at:at+PX]=nt(gT,pr.astype(bf)).astype(bf)
        return r0,nn(kT,ds)*0.125
    def bh(h,_):
        r0,dqT=bh_part(h,PX)
        acc[h]=dqT
        dtrT[pl.ds(r0,64),PX:2*PX]=jnp.zeros((64,PX),bf)
        return 0
    lax.fori_loop(0,6,bh,0)
    oth[1:17]=tn(dtrT[:,PX:2*PX],wqT[...]).astype(bf).reshape(16,32,CH)
    c1=xchg(oth.at[pl.ds(1,16)],oth.at[pl.ds(17,16)])
    def bh2(h,_):
        r0,dqT=bh_part(h,0)
        dtrT[pl.ds(r0,64),0:PX]=(acc[h]+dqT).astype(bf)
        return 0
    lax.fori_loop(0,6,bh2,0)
    gsec[...]=tn(dtrT[:,0:PX],wqT[...])
    dq=nt(ain[...].T,dtrT[...])
    for j in range(3):
        put3(cvt3,every(j,CH,3),dq[:,CH*j:CH*j+CH])
    wv[R_QKV:R_PROJ]=ld(cvt3,pl.ds(0,1152)).astype(bf)
    c1.wait()
    def n3_of(i): return (middle[pl.ds(i,64)]-mean3)*inv3
    def s3(i,c):
        j=pl.multiple_of(17+lax.div(i,32),1)
        v=gsec[pl.ds(i,64)]+oth[pl.ds(j,2)].reshape(64,CH).astype(f32)
        gsec[pl.ds(i,64)]=v
        return c[0]+col8(v),c[1]+col8(v*n3_of(i))
    a1,a2=cloop(PX,64,s3,(Z8(),Z8()))
    db3,dg3=row(a1),row(a2)
    c1=swap_sums(3,db3*g3,dg3*g3)
    c1.wait()
    m1,m2=total_sums(3)
    def f3(i,_):
        v=ld(gout,pl.ds(i,64))+inv3*(gsec[pl.ds(i,64)]*g3-m1-n3_of(i)*m2)
        fill3(z3,pl.multiple_of(i+32,32),v)
        return 0
    cloop(PX,64,f3,0)
    zedge=pl.ds(pl.multiple_of(q*480+32,32),32)
    hsend[1]=z3[zedge,CH:2*CH]
    c1=xchg(hsend.at[1],oth.at[33])
    c1.wait()
    fill_edges(z3,oth[33].astype(f32))
    xsend(2)
    conv_dx(gsec,R_TWO)
    for dr in range(3):
        d=tn(x3b[32*dr:32*dr+PX],z3[32:32+PX,CH:2*CH]).astype(bf)
        wv[R_TWO+1152*dr:R_TWO+1152*dr+1152]=d
        if dr==0: wd[R_TWO:4304,0:CH]=d[0:4304-R_TWO]
    sibsend(1)
    def s2(i,c):
        n,af,pb=pre_b(inner[pl.ds(i,64)])
        gpre=gsec[pl.ds(i,64)]*slope(pb)
        gaff=gpre*sc1
        gsec[pl.ds(i,64)]=gaff
        return c[0]+col8(gpre*af),c[1]+col8(gpre),c[2]+col8(gaff*n),c[3]+col8(gaff)
    a1,a2,a3,a4=cloop(PX,64,s2,(Z8(),Z8(),Z8(),Z8()))
    dsc,dsh,dg2,db2=row(a1),row(a2),row(a3),row(a4)
    c1=swap_sums(4,db2*g2,dg2*g2)
    diag(1); ysend(1)
    c1.wait()
    m1,m2=total_sums(4)
    def f2(i,_):
        n=(inner[pl.ds(i,64)]-mean2)*inv2
        fill3(z3,pl.multiple_of(i+32,32),inv2*(gsec[pl.ds(i,64)]*g2-m1-n*m2))
        return 0
    cloop(PX,64,f2,0)
    hsend[2]=z3[zedge,CH:2*CH]
    c1=xchg(hsend.at[2],oth.at[34])
    for dr in range(3):
        wd[1152*dr:1152*dr+1152,0:CH]=tn(x3a[32*dr:32*dr+PX],z3[32:32+PX,CH:2*CH]).astype(bf)
    sibsend(0)
    c1.wait()
    fill_edges(z3,oth[34].astype(f32))
    xsend(3); xsend(1)
    zstep(2,0)
    conv_dx(gsec,R_ONE)
    diag(0)
    first_halves(0)
    def s1(i,c):
        n=(img[pl.ds(i,64)].astype(f32)-mean1)*inv1
        gpre=gsec[pl.ds(i,64)]*slope(n*g1+b1)
        return c[0]+col8(gpre*n),c[1]+col8(gpre)
    a1,a2=cloop(PX,64,s1,(Z8(),Z8()))
    zstep(3,0)
    ge=[]
    for h in range(2):
        d=exact(jnp.broadcast_to(dsc,(16,CH)),wee[CH*h:CH*h+CH],nt)+exact(jnp.broadcast_to(dsh,(16,CH)),weo[CH*h:CH*h+CH],nt)
        ge.append(d[0:1]*slope(pre[h]))
    hot_level=(lax.broadcasted_iota(jnp.int32,(1,CH),1)==level[...]).astype(f32)
    pack_ref[...]=jnp.concatenate([row(a1),row(a2),dg2,db2,dg3,db3,dsc,dsh,ge[0],ge[1],emb[0],emb[1],consist*hot_level,jnp.broadcast_to(ids.astype(f32),(1,CH)),0.5*hot_level,jnp.zeros((1,CH),f32)],0)
    low=jnp.logical_not(top)
    cm.go(low,pack_ref,lpk.at[z],lps,lpr.at[z],b+4*(3-z),p)
    zstep(1,0)
    second_halves(0)
    zstep(2,1)
    zstep(3,1)
    zstep(1,1)
    zstep(3,2)
    zstep(0,0)
    zend(3)
    def packs_line():
        pl.when(jnp.logical_not(slot(z,y,p)<=LAST))(lambda: total.__setitem__(Ellipsis,jnp.zeros(total.shape,f32)))
        lpk[3]=pack_ref[...]
        for zz in range(3): wait_in(lpk.at[zz],lpr.at[zz])
    pl.when(top)(packs_line)
    for d,bb,pp in plane:
        cm.go(top,lpk,ppk.at[mine],pps.at[d],ppr.at[mine],bb,pp)
    def packs_plane():
        ppk[mine]=lpk[...]
        for d,bb,pp in plane:
            o=(lax.rem(lax.div(bb,2),2)*2+lax.rem(bb,2))*2+pp
            wait_in(ppk.at[o],ppr.at[o])
        a_s=16*lax.div(ROWS*s,16)
        rows_at=lambda k: ppk[:,:,k,:].reshape(32,384)
        zero=jnp.zeros((64,384),f32)
        for h in range(2):
            e=rows_at(10+h)
            t=jnp.concatenate([e,e,zero],0).T
            cvt[pl.ds(BLK+768*h,384,stride=2),:]=t
            cvt[pl.ds(BLK+768*h+1,384,stride=2),:]=t
        r=a_s+lax.broadcasted_iota(jnp.int32,(BLK,128),0)
        l=lax.broadcasted_iota(jnp.int32,(BLK,128),1)
        inside=(r>=R_EMB)&(r<R_TAB)
        start=pl.multiple_of(jnp.clip(a_s-R_EMB+BLK,0,BLK+1536),16)
        lf=jnp.where(inside&(((r&1)==1)==(l>=32))&(l<64),cvt[pl.ds(start,BLK),:],0.0)
        ids=rows_at(13)[:,0:128].astype(jnp.int32)
        ids=jnp.concatenate([ids]*4,0).astype(f32).T[0:1].astype(jnp.int32)
        hot=(r-R_TAB==2*ids+(l>=96).astype(jnp.int32))&(l>=64)&(r>=R_TAB)
        lf=jnp.where(hot,1.0,lf)
        rg=jnp.concatenate([rows_at(6),rows_at(7),rows_at(8),rows_at(9)],0)
        gains=[jnp.sum(rows_at(k),0,keepdims=True) for k in range(6)]
        hi=lax.Precision.HIGHEST
        add=lax.dot_general(lf,rg,(((1,),(0,)),((),())),precision=hi,preferred_element_type=f32)
        for k in range(6): add=add+jnp.where(r[:,0:1]-R_GAIN==k,gains[k],0.0)
        rr=a_s+lax.broadcasted_iota(jnp.int32,(BLK,384),0)
        total[...]=jnp.where(rr<R_EMB,total[...],add)
    pl.when(top)(packs_plane)
    zstep(0,1); zstep(0,2)
    zend(1); zend(2)
    zend(0)
    shift=lax.rem(9*s,16)
    tr_=lax.broadcasted_iota(jnp.int32,(BLK,1),0)
    t=jnp.where((tr_>=shift)&(tr_<shift+ROWS),total[...],0.0)
    sq=jnp.sum(jnp.sum(t*t,0,keepdims=True),1,keepdims=True)
    tile[...]=jnp.concatenate([jnp.broadcast_to(sq,(1,128)),pack_ref[12:13,0:128],pack_ref[14:15,0:128],jnp.zeros((5,128),f32)],0)
    red1[mine]=tile[...]
    for d,bb,pp in plane: cm.go(None,tile,red1.at[mine],n1s.at[d],n1r.at[mine],bb,pp)
    t=pltpu.roll(total[...],lax.rem(BLK-shift,BLK),0)[0:ROWS]
    for j in range(3): cvt[pl.ds(j,ROWS,stride=3),:]=t[:,128*j:128*j+128]
    fcopy=pltpu.make_async_copy(cvt.at[pl.ds(0,1611)],flat_ref,own_sem)
    fcopy.start()
    for d,bb,pp in plane:
        o=(lax.rem(lax.div(bb,2),2)*2+lax.rem(bb,2))*2+pp
        wait_in(red1.at[o],n1r.at[o])
    v=red1[0]
    for k in range(1,8): v=v+red1[k]
    red2[z]=v
    for k,zz in line: cm.go(None,red2.at[z],red2.at[z],n2s.at[k],n2r.at[z],b+4*(zz-z),p)
    for k,zz in line: wait_in(red2.at[zz],n2r.at[zz])
    all_ref[...]=red2[0]+red2[1]+red2[2]+red2[3]
    cm.drain()
    fcopy.wait()

def step(images_all,mast,img,tgt,cln,vgg,lin,tvec,rowid,level,gm):
    D=pltpu.SemaphoreType.DMA
    V=lambda *s: pltpu.VMEM(s,bf)
    F=lambda *s: pltpu.VMEM(s,f32)
    vm=pl.BlockSpec(memory_space=pltpu.VMEM)
    return pl.pallas_call(functools.partial(step_kernel,images_all),
        out_shape=(jax.ShapeDtypeStruct((1611,128),f32),jax.ShapeDtypeStruct((8,128),f32),jax.ShapeDtypeStruct((32,BLK,CH),bf)),
        in_specs=[pl.BlockSpec(memory_space=pl.ANY)]+[vm]*9,
        out_specs=(pl.BlockSpec(memory_space=pl.ANY),vm,pl.BlockSpec(memory_space=pl.ANY)),
        scratch_shapes=[V(17184,CH),V(32,32,CH),F(4608,128),F(5,CH,128),V(4304,CH2),V(768,CH),V(768,CH),V(1152,CH),V(576,1152),V(576,1152),V(576,1152),F(PX,CH),F(PX,CH),F(3,PX,128),F(PX,CH),V(1024,CH),V(1152,1024),V(1152,1024),V(CH,PX),V(128,3456),F(6,8,PX),V(CH,PX),F(5,8,CH),F(5,8,CH),V(3,32,CH),F(1,32,CH),V(32,CH),V(16,CH2),V(16,CH2),F(3,32,128),V(35,32,CH),D((32,)),D((32,)),D((16,)),D((16,)),F(BLK,CH),V(BLK,CH),D,D((4,2,2)),D((4,2)),D((4,2)),D((4,2)),D((4,2)),D((4,2)),D((4,)),D((4,)),D((4,)),D((4,)),D((4,2,2,2)),D((4,2,2,2)),F(16,CH),F(4,16,CH),F(8,4,16,CH),F(8,8,128),F(4,8,128),F(8,128),D,D((4,)),D((8,)),D((8,)),D((8,)),D((8,)),D((4,)),D((4,)),V(14,BLK,CH),V(4,BLK-HALF,CH),V(4,BLK,CH),V(4,BLK,CH),V(3,BLK,CH),V(3,BLK,CH),D((4,2,2)),D((4,2,2)),D((4,)),D((4,)),D((4,)),D((4,)),D((4,2)),D((4,2)),D((4,2)),D((4,2)),D((4,4)),D((4,4)),D((4,4)),F(6,64,PX),V(16,CH),D((4,)),D,D((8,)),D,V(4,HALF,CH),D((2,2,2,2)),D((2,2,2))],
        compiler_params=pltpu.CompilerParams(collective_id=0,has_side_effects=True,vmem_limit_bytes=63<<20),
        name="train_step",
    )(mast,img,tgt,cln,vgg,lin,tvec,rowid,level,gm)


def fast(images, target, clean_images, levels, labels, null_mask, vgg_proj, lpips_lin, master, first_moment, second_moment):
    row_index = jnp.where(null_mask == 1, CLASSES, labels).reshape(1, 1)
    tvec = time_vector(levels)
    lane = jnp.arange(CH, dtype=jnp.int32) // 12
    gm = (lane[:, None] == lane[None, :]).astype(jnp.bfloat16)
    own_grad, sums, _ = step(
        16,
        master.reshape(1611, 128),
        images.reshape(PX, CH),
        target.reshape(128, CH2),
        clean_images.reshape(128, CH2),
        vgg_proj,
        lpips_lin.reshape(1, 256),
        tvec,
        row_index,
        levels.reshape(1, 1),
        gm,
    )
    own_grad = own_grad.reshape(-1)
    level_sums = sums[1:3, :LEVELS]
    norm_before = jnp.sqrt(sums[0, 0])
    clipped = own_grad * jnp.minimum(1.0, CLIP / norm_before)
    new_first = BETA_ONE * first_moment + (1.0 - BETA_ONE) * clipped
    new_second = BETA_TWO * second_moment + (1.0 - BETA_TWO) * clipped * clipped
    fixed_first = new_first / (1.0 - BETA_ONE**STEP)
    fixed_second = new_second / (1.0 - BETA_TWO**STEP)
    new_master = master - RATE * (fixed_first / (jnp.sqrt(fixed_second) + EPS_ADAM) + DECAY * master)
    return (new_master, new_first, new_second, new_master.astype(jnp.bfloat16), norm_before, level_sums)


def solution(mesh):
    small = mesh.shape["batch"] == 16 and mesh.shape["pix"] == 2
    return jax.shard_map(
        fast if small else local,
        mesh=mesh,
        in_specs=(
            P("batch", "pix", None, None),
            P("batch", "pix", None, None),
            P("batch", "pix", None, None),
            P("batch"),
            P("batch"),
            P("batch"),
            P(),
            P(),
            P(("batch", "pix")),
            P(("batch", "pix")),
            P(("batch", "pix")),
        ),
        out_specs=(
            P(("batch", "pix")),
            P(("batch", "pix")),
            P(("batch", "pix")),
            P(("batch", "pix")),
            P(),
            P(),
        ),
        check_vma=False,
    )
```

```python
import functools
import math

import jax
import jax.numpy as jnp
from jax import lax
from jax.experimental import pallas as pl
from jax.experimental.pallas import tpu as pltpu
from jax.sharding import PartitionSpec as P

CH = 384
CH2 = 576
GROUPS = 32
HEAD = 64
TEMB = 768
CLASSES = 1000
LEVELS = 40
STEP = 10


EPS_NORM = 1e-05
EPS_FEAT = 1e-06
BETA_ONE = 0.9
BETA_TWO = 0.999
EPS_ADAM = 1e-08
RATE = 0.02
DECAY = 0.01
CLIP = 0.01
precise = lax.Precision.HIGHEST


def extended(shard, sides, width):
    for axis, dim in sides:
        size, length = (lax.axis_size(axis), shard.shape[dim])
        up = [(i, (i + 1) % size) for i in range(size - 1)]
        down = [(j, i) for i, j in up]
        last = lax.slice_in_dim(shard, length - width, length, axis=dim)
        initial = lax.slice_in_dim(shard, 0, width, axis=dim)
        before = lax.ppermute(last, axis, up)
        after = lax.ppermute(initial, axis, down)
        shard = jnp.concatenate([before, shard, after], axis=dim)
    return shard


def unpack(flat_vec):
    layout = [
        (9 * CH, CH),
        (9 * CH, CH),
        (CH, 3 * CH),
        (CH, CH),
        (9 * CH, CH2),
        (TEMB, 2 * CH),
        (CLASSES + 1, TEMB),
        (6, CH),
    ]
    pieces = []
    offset = 0
    for rows_n, cols_n in layout:
        pieces.append(flat_vec[offset : offset + rows_n * cols_n].reshape(rows_n, cols_n))
        offset += rows_n * cols_n
    return (pieces, offset)


def time_vector(level_ids):
    half_width = TEMB // 2
    frequency = jnp.exp(-math.log(10000.0) * jnp.arange(half_width, dtype=jnp.float32) / half_width)
    angles = level_ids.astype(jnp.float32)[..., None] * (1000.0 / LEVELS) * frequency
    return jnp.concatenate([jnp.cos(angles), jnp.sin(angles)], -1)


def silu_slope(values):
    sigmoid = jax.nn.sigmoid(values)
    return sigmoid * (1.0 + values * (1.0 - sigmoid))


def pix_sums(pair_sums):
    return lax.psum((pair_sums[0], pair_sums[1]), "pix")


def group_forward(values, pixels_all):
    grouped = values.reshape(values.shape[0], values.shape[1], GROUPS, -1)
    totals = pix_sums((jnp.sum(grouped, (1, 3)), jnp.sum(grouped * grouped, (1, 3))))
    per_group = pixels_all * grouped.shape[3]
    center = totals[0] / per_group
    spread = totals[1] / per_group - center * center
    inverse = lax.rsqrt(spread + EPS_NORM)
    normed = (grouped - center[:, None, :, None]) * inverse[:, None, :, None]
    return (normed.reshape(values.shape), inverse)


def group_backward(grad_normed, normed, inverse, pixels_all):
    grad_grouped = grad_normed.reshape(normed.shape[0], normed.shape[1], GROUPS, -1)
    val_grouped = normed.reshape(grad_grouped.shape)
    totals = pix_sums((jnp.sum(grad_grouped, (1, 3)), jnp.sum(grad_grouped * val_grouped, (1, 3))))
    per_group = pixels_all * grad_grouped.shape[3]
    result = (
        grad_grouped
        - (totals[0] / per_group)[:, None, :, None]
        - val_grouped * (totals[1] / per_group)[:, None, :, None]
    )
    return (result * inverse[:, None, :, None]).reshape(normed.shape)


def columns_of(values, stride):
    rows_out = values.shape[1] // stride
    cols_out = values.shape[2] // stride
    span_rows = stride * (rows_out - 1) + 1
    span_cols = stride * (cols_out - 1) + 1
    padded = extended(values, (("pix", 1),), 1)
    padded = jnp.pad(padded, ((0, 0), (0, 0), (1, 1), (0, 0)))
    return jnp.concatenate(
        [
            padded[
                :, row_off : row_off + span_rows : stride, col_off : col_off + span_cols : stride, :
            ]
            for row_off in range(3)
            for col_off in range(3)
        ],
        -1,
    )


def conv_forward(values, weight, rows_in, stride):
    n_img, pixels_in, in_chan = values.shape
    columns = columns_of(values.reshape(n_img, rows_in, -1, in_chan), stride)
    result = jnp.dot(columns.reshape(-1, 9 * in_chan), weight, preferred_element_type=jnp.float32)
    return (result.reshape(n_img, -1, weight.shape[1]), columns)


def conv_back(columns, grad_low, weight, rows_in, stride):
    n_img, pix_out, out_chan = grad_low.shape
    in_chan = weight.shape[0] // 9
    d_weight = jnp.einsum(
        "rk,rc->kc",
        columns.reshape(-1, 9 * in_chan),
        grad_low.reshape(-1, out_chan),
        preferred_element_type=jnp.float32,
    )
    flipped = (
        weight.reshape(3, 3, in_chan, out_chan)[::-1, ::-1]
        .transpose(0, 1, 3, 2)
        .reshape(9 * out_chan, in_chan)
    )
    rows_out = rows_in // stride
    grid_grad = grad_low.reshape(n_img, rows_out, pix_out // rows_out, out_chan)
    if stride > 1:
        grid_grad = jnp.pad(
            grid_grad[:, :, None, :, None, :],
            ((0, 0), (0, 0), (0, stride - 1), (0, 0), (0, stride - 1), (0, 0)),
        )
        grid_grad = grid_grad.reshape(n_img, rows_in, -1, out_chan)
    grad_columns = columns_of(grid_grad, 1)
    grad_input = jnp.dot(
        grad_columns.reshape(-1, 9 * out_chan), flipped, preferred_element_type=jnp.float32
    )
    return (d_weight, grad_input.reshape(n_img, -1, in_chan))


def res_forward(values, gain_rows, scale, shift, w_first, w_second, rows_in, pixels_all):
    normed_a, inverse_a = group_forward(values, pixels_all)
    pre_a = normed_a * gain_rows[0] + gain_rows[1]
    act_a = jax.nn.silu(pre_a).astype(jnp.bfloat16)
    inner, columns_a = conv_forward(act_a, w_first, rows_in, 1)
    normed_b, inverse_b = group_forward(inner, pixels_all)
    affine_b = normed_b * gain_rows[2] + gain_rows[3]
    pre_b = affine_b * (1.0 + scale) + shift
    second = jax.nn.silu(pre_b).astype(jnp.bfloat16)
    branch, columns_b = conv_forward(second, w_second, rows_in, 1)
    kept_state = (
        normed_a,
        inverse_a,
        pre_a,
        columns_a,
        normed_b,
        inverse_b,
        affine_b,
        pre_b,
        columns_b,
    )
    return (values + branch, kept_state)


def res_back(grad_result, kept_state, gain_rows, scale, w_first, w_second, rows_in, pixels_all):
    normed_a, inverse_a, pre_a, columns_a, normed_b, inverse_b, affine_b, pre_b, columns_b = (
        kept_state
    )
    d_w_second, grad_second = conv_back(
        columns_b, grad_result.astype(jnp.bfloat16), w_second, rows_in, 1
    )
    grad_pre_b = grad_second * silu_slope(pre_b)
    d_scale = jnp.sum(grad_pre_b * affine_b, 1)
    d_shift = jnp.sum(grad_pre_b, 1)
    grad_affine = grad_pre_b * (1.0 + scale)
    d_gain_b = jnp.sum(grad_affine * normed_b, (0, 1))
    d_bias_b = jnp.sum(grad_affine, (0, 1))
    grad_inner = group_backward(grad_affine * gain_rows[2], normed_b, inverse_b, pixels_all).astype(
        jnp.bfloat16
    )
    d_w_first, grad_act = conv_back(columns_a, grad_inner, w_first, rows_in, 1)
    grad_pre_a = grad_act * silu_slope(pre_a)
    d_gain_a = jnp.sum(grad_pre_a * normed_a, (0, 1))
    d_bias_a = jnp.sum(grad_pre_a, (0, 1))
    grad_values = None
    d_gains = jnp.stack([d_gain_a, d_bias_a, d_gain_b, d_bias_b])
    return (d_w_first, d_w_second, d_gains, d_scale, d_shift, grad_values)


def to_heads(values):
    return lax.all_to_all(values, "pix", split_axis=2, concat_axis=1, tiled=True)


def to_pixels(values):
    return lax.all_to_all(values, "pix", split_axis=1, concat_axis=2, tiled=True)


def flat_heads(values):
    return values.reshape(-1, values.shape[2], values.shape[3])


def attend(queries, keys, values):
    root_dim = math.sqrt(queries.shape[-1])

    def single(bundle):
        q_one, k_one, v_one = bundle
        scores = (
            jnp.einsum("qd,kd->qk", q_one, k_one, preferred_element_type=jnp.float32) / root_dim
        )
        row_peak = jnp.max(scores, -1, keepdims=True)
        exp_scores = jnp.exp(scores - row_peak)
        sum_exp = jnp.sum(exp_scores, -1, keepdims=True)
        probabilities = (exp_scores / sum_exp).astype(jnp.bfloat16)
        attended = jnp.einsum("qk,kd->qd", probabilities, v_one, preferred_element_type=jnp.float32)
        return (attended.astype(jnp.bfloat16), row_peak + jnp.log(sum_exp))

    attended, log_total = lax.map(
        single, (flat_heads(queries), flat_heads(keys), flat_heads(values))
    )
    return (attended.reshape(queries.shape), log_total)


def attend_back(queries, keys, values, log_total, grad_out):
    root_dim = math.sqrt(queries.shape[-1])

    def single(bundle):
        q_one, k_one, v_one, lse_one, g_one = bundle
        scores = (
            jnp.einsum("qd,kd->qk", q_one, k_one, preferred_element_type=jnp.float32) / root_dim
        )
        probabilities = jnp.exp(scores - lse_one)
        grad_v = jnp.einsum(
            "qk,qd->kd",
            probabilities.astype(jnp.bfloat16),
            g_one,
            preferred_element_type=jnp.float32,
        )
        grad_p = jnp.einsum("qd,kd->qk", g_one, v_one, preferred_element_type=jnp.float32)
        inner_sum = jnp.sum(probabilities * grad_p, -1, keepdims=True)
        grad_s = (probabilities * (grad_p - inner_sum)).astype(jnp.bfloat16)
        grad_q = (
            jnp.einsum("qk,kd->qd", grad_s, k_one, preferred_element_type=jnp.float32) / root_dim
        )
        grad_k = (
            jnp.einsum("qk,qd->kd", grad_s, q_one, preferred_element_type=jnp.float32) / root_dim
        )
        return (grad_q, grad_k, grad_v)

    grad_q, grad_k, grad_v = lax.map(
        single,
        (
            flat_heads(queries),
            flat_heads(keys),
            flat_heads(values),
            log_total,
            flat_heads(grad_out),
        ),
    )
    return (grad_q.reshape(queries.shape), grad_k.reshape(keys.shape), grad_v.reshape(values.shape))


def local(
    images,
    target,
    clean_images,
    levels,
    labels,
    null_mask,
    vgg_proj,
    lpips_lin,
    master,
    first_moment,
    second_moment,
):
    gathered = lax.all_gather(master.astype(jnp.bfloat16), ("batch", "pix"), axis=0, tiled=True)
    pieces, used_len = unpack(gathered)
    w_one, w_two, w_qkv, w_proj, w_down, w_emb, class_table, gains_low = pieces
    gains_one = gains_low.astype(jnp.float32)
    n_img, rows_local, cols_local, channels = images.shape
    wide_channels = w_down.shape[1]
    pix_count = lax.axis_size("pix")
    batch_count = lax.axis_size("batch")
    pixels_here = rows_local * cols_local
    pixels_all = pixels_here * pix_count
    pixels_all_two = pixels_all // 4
    images_all = n_img * batch_count
    row_index = jnp.where(null_mask == 1, class_table.shape[0] - 1, labels)
    one_hot = (
        row_index[:, None] == jnp.arange(class_table.shape[0], dtype=jnp.int32)[None, :]
    ).astype(jnp.float32)
    pre_embed = time_vector(levels) + jnp.dot(
        one_hot, class_table.astype(jnp.float32), precision=precise
    )
    embedded = jax.nn.silu(pre_embed)
    w_emb_wide = w_emb.astype(jnp.float32)
    scale_shift = jnp.dot(embedded, w_emb_wide, precision=precise)
    scale_one = scale_shift[:, None, :channels]
    shift_one = scale_shift[:, None, channels:]
    flat_in = images.astype(jnp.float32).reshape(n_img, pixels_here, channels)
    middle, kept_one = res_forward(
        flat_in, gains_one, scale_one, shift_one, w_one, w_two, rows_local, pixels_all
    )
    normed_three, inverse_three = group_forward(middle, pixels_all)
    attn_in = (normed_three * gains_one[4] + gains_one[5]).astype(jnp.bfloat16)
    triples = jnp.dot(attn_in.reshape(-1, channels), w_qkv, preferred_element_type=jnp.float32)
    triples = triples.astype(jnp.bfloat16).reshape(n_img, pixels_here, 3 * channels)
    spread_heads = to_heads(triples)
    local_heads = spread_heads.shape[2] // (3 * HEAD)
    split_heads = spread_heads.reshape(n_img, -1, local_heads, 3, HEAD).transpose(3, 0, 2, 1, 4)
    queries, keys, values = (split_heads[0], split_heads[1], split_heads[2])
    attended, log_total = attend(queries, keys, values)
    attended_px = to_pixels(attended.transpose(0, 2, 1, 3).reshape(n_img, -1, local_heads * HEAD))
    projected = jnp.dot(
        attended_px.reshape(-1, channels), w_proj, preferred_element_type=jnp.float32
    )
    output = middle + projected.reshape(n_img, pixels_here, channels)
    final_out, columns_down = conv_forward(output.astype(jnp.bfloat16), w_down, rows_local, 2)
    pixels_two = final_out.shape[1]
    feat_width = vgg_proj.shape[1]
    online_feat = jnp.dot(
        final_out.astype(jnp.bfloat16).reshape(-1, wide_channels),
        vgg_proj,
        preferred_element_type=jnp.float32,
    )
    online_feat = online_feat.reshape(n_img, pixels_two, feat_width)
    target_feat = jnp.dot(
        target.reshape(-1, wide_channels), vgg_proj, preferred_element_type=jnp.float32
    )
    target_feat = target_feat.reshape(n_img, pixels_two, feat_width)
    target_unit = target_feat * lax.rsqrt(
        jnp.mean(target_feat * target_feat, -1, keepdims=True) + EPS_FEAT
    )
    clean_wide = clean_images.astype(jnp.float32).reshape(n_img, pixels_two, wide_channels)

    def loss_terms(feature, out_value):
        unit = feature * lax.rsqrt(jnp.mean(feature * feature, -1, keepdims=True) + EPS_FEAT)
        consist = jnp.sum(lpips_lin * (unit - target_unit) ** 2, (1, 2)) / (
            feat_width * pixels_all_two
        )
        denoise = jnp.sum((out_value - clean_wide) ** 2, (1, 2)) / (pixels_all_two * wide_channels)
        return (consist, denoise)

    (consist, denoise), pullback = jax.vjp(loss_terms, online_feat, final_out)
    level_hot = (levels[:, None] == jnp.arange(LEVELS, dtype=jnp.int32)[None, :]).astype(
        jnp.float32
    )
    level_pair = lax.psum(
        (jnp.sum(consist[:, None] * level_hot, 0), jnp.sum(level_hot / pix_count, 0)),
        ("batch", "pix"),
    )
    zero_count = level_pair[1][0]
    is_zero = (levels == 0).astype(jnp.float32)
    grad_feat, grad_out = pullback(
        (jnp.full_like(consist, 1.0 / images_all), is_zero / jnp.maximum(zero_count, 1.0))
    )
    grad_feat_low = grad_feat.astype(jnp.bfloat16).reshape(-1, feat_width)
    grad_final = grad_out + jnp.einsum(
        "rf,cf->rc", grad_feat_low, vgg_proj, preferred_element_type=jnp.float32
    ).reshape(n_img, pixels_two, wide_channels)
    d_w_down, grad_output = conv_back(
        columns_down, grad_final.astype(jnp.bfloat16), w_down, rows_local, 2
    )
    grad_proj = grad_output.astype(jnp.bfloat16).reshape(-1, channels)
    d_w_proj = jnp.einsum(
        "rc,rd->cd",
        attended_px.reshape(-1, channels),
        grad_proj,
        preferred_element_type=jnp.float32,
    )
    grad_att_px = jnp.einsum("rd,cd->rc", grad_proj, w_proj, preferred_element_type=jnp.float32)
    grad_att_px = grad_att_px.astype(jnp.bfloat16).reshape(n_img, pixels_here, channels)
    grad_heads = to_heads(grad_att_px)
    grad_split = grad_heads.reshape(n_img, -1, local_heads, HEAD).transpose(0, 2, 1, 3)
    grad_q, grad_k, grad_v = attend_back(queries, keys, values, log_total, grad_split)
    grad_triples = jnp.stack([grad_q, grad_k, grad_v], 3).transpose(0, 2, 1, 3, 4)
    grad_triples = grad_triples.reshape(n_img, -1, local_heads * 3 * HEAD).astype(jnp.bfloat16)
    grad_triples = to_pixels(grad_triples)
    grad_rows = grad_triples.reshape(-1, 3 * channels)
    d_w_qkv = jnp.einsum(
        "rc,rd->cd", attn_in.reshape(-1, channels), grad_rows, preferred_element_type=jnp.float32
    )
    grad_attn_in = jnp.einsum(
        "rd,cd->rc", grad_rows, w_qkv, preferred_element_type=jnp.float32
    ).reshape(n_img, pixels_here, channels)
    d_gain_three = jnp.sum(grad_attn_in * normed_three, (0, 1))
    d_bias_three = jnp.sum(grad_attn_in, (0, 1))
    grad_middle = grad_output + group_backward(
        grad_attn_in * gains_one[4], normed_three, inverse_three, pixels_all
    )
    d_w_one, d_w_two, d_gains_one, d_scale_one, d_shift_one, unused_grad = res_back(
        grad_middle, kept_one, gains_one, scale_one, w_one, w_two, rows_local, pixels_all
    )
    grad_scale_shift = jnp.concatenate([d_scale_one, d_shift_one], 1)
    d_w_emb = jnp.dot(embedded.T, grad_scale_shift, precision=precise)
    grad_embedded = jnp.dot(grad_scale_shift, w_emb_wide.T, precision=precise)
    d_table = jnp.dot(one_hot.T, grad_embedded * silu_slope(pre_embed), precision=precise)
    d_norms_one = jnp.concatenate([d_gains_one, jnp.stack([d_gain_three, d_bias_three])], 0)
    flat_grad = jnp.concatenate(
        [
            d_w_one.ravel(),
            d_w_two.ravel(),
            d_w_qkv.ravel(),
            d_w_proj.ravel(),
            d_w_down.ravel(),
            d_w_emb.ravel(),
            d_table.ravel(),
            d_norms_one.ravel(),
            jnp.zeros((gathered.shape[0] - used_len,), jnp.float32),
        ]
    )
    own_grad = lax.psum_scatter(flat_grad, ("batch", "pix"), scatter_dimension=0, tiled=True)
    norm_before = jnp.sqrt(lax.psum(jnp.sum(own_grad * own_grad), ("batch", "pix")))
    clipped = own_grad * jnp.minimum(1.0, CLIP / norm_before)
    new_first = BETA_ONE * first_moment + (1.0 - BETA_ONE) * clipped
    new_second = BETA_TWO * second_moment + (1.0 - BETA_TWO) * clipped * clipped
    fixed_first = new_first / (1.0 - BETA_ONE**STEP)
    fixed_second = new_second / (1.0 - BETA_TWO**STEP)
    new_master = master - RATE * (
        fixed_first / (jnp.sqrt(fixed_second) + EPS_ADAM) + DECAY * master
    )
    level_sums = jnp.stack([level_pair[0], level_pair[1]])
    return (
        new_master,
        new_first,
        new_second,
        new_master.astype(jnp.bfloat16),
        norm_before,
        level_sums,
    )


MESH = pl.DeviceIdType.MESH
ROWS=537; BLK=560; HALF=288
PX=512
R_ONE,R_TWO,R_QKV,R_PROJ,R_DOWN,R_EMB,R_TAB,R_GAIN,R_END=0,3456,6912,8064,8448,13632,15168,17170,17184
f32=jnp.float32; bf=jnp.bfloat16
class Comm:
    def __init__(self): self.sent=[]
    def go(self, cond, src, dst, ssem, rsem, b, p):
        c = pltpu.make_async_remote_copy(src_ref=src,dst_ref=dst,send_sem=ssem,recv_sem=rsem,device_id=(b,p),device_id_type=MESH)
        if cond is None: c.start()
        else: pl.when(cond)(lambda: c.start())
        self.sent.append((cond,c))
    def drain(self):
        for cond,c in self.sent:
            if cond is None: c.wait_send()
            else: pl.when(cond)(lambda c=c: c.wait_send())
        self.sent=[]

def place():
    b=lax.axis_index("batch"); p=lax.axis_index("pix")
    core=lax.rem(b,2); y=lax.rem(lax.div(b,2),2); z=lax.div(b,4)
    return b,p,core,y,z

def base_of(s): return 16*((ROWS*s)//16)
def dg(a,b,ca,cb): return lax.dot_general(a,b,(((ca,),(cb,)),((),())),preferred_element_type=f32)
def nn(a,b): return dg(a,b,1,0)
def nt(a,b): return dg(a,b,1,1)
def tn(a,b): return dg(a,b,0,0)
def split3(v):
    hi=v.astype(bf); r=v-hi.astype(f32); mid=r.astype(bf); lo=(r-mid.astype(f32)).astype(bf)
    return hi,mid,lo
def exact(v,w,dot):
    hi,mid,lo=split3(v)
    return dot(hi,w)+dot(mid,w)+dot(lo,w)
def sigmoid(v): return 1.0/(1.0+jnp.exp(-v))
def silu(v): return v*sigmoid(v)
def slope(v):
    s=sigmoid(v)
    return s*(1.0+v*(1.0-s))
def cloop(n,chunk,body,init):
    return lax.fori_loop(0,n//chunk,lambda i,c: body(pl.multiple_of(i*chunk,chunk),c),init)
def col8(v): return jnp.sum(v.reshape(-1,8,v.shape[-1]),axis=0)
Z8=lambda: jnp.zeros((8,CH),f32)
class Blocks:
    def __init__(self,ref,n): self.ref=ref; self.n=n
def at_block(ref,j,sl):
    if isinstance(ref,Blocks): return ref.ref,(pl.ds(ref.n*j+sl.start,sl.size,stride=sl.stride),slice(None))
    return ref,(j,sl,slice(None))
def ld(ref,sl):
    out=[]
    for j in range(ref.ref.shape[0]//ref.n if isinstance(ref,Blocks) else ref.shape[0]):
        r,k=at_block(ref,j,sl)
        out.append(r[k])
    return jnp.concatenate(out,1)
def put3(ref,sl,v):
    for j in range(v.shape[1]//128):
        r,k=at_block(ref,j,sl)
        r[k]=v[:,128*j:128*j+128]
def every(start,n,step): return pl.ds(start,n,stride=step)
def row(v): return jnp.sum(v,axis=0,keepdims=True)


LAST=25
def step_kernel(images_all,
    mast,img,tgt,cln,vgg,lin,tvec,rowid,level,gm,
    flat_ref,all_ref,g_ref,
    wv,tails,cvt,cvt2,wd,wee,weo,wqT,x3a,x3b,z3,inner,middle,gout,gsec,ain,trT,dtrT,attT,xd,lse,dattT,ssend,srecv,hsend,hrecv,himg,dzs,dzr,geo,oth,wsem,tsem,xs,xr,total,blk,own_sem,azs,azr,axs,axr,ays,ayr,adar,adbr,ass,asr,pack_ref,lpk,ppk,red1,red2,tile,lps,lpr,pps,ppr,n1s,n1r,n2s,n2r,sibr,rb,rx,ry,zu,zd,s1s,s1r,dar,dbr,rxs,rxr,rys,ryr,zs,zur,zdr,acc,gtile,gls,glr,gps,gpr,rba,a2s,a2r,ads,ds_,hmid,esend,erecv):
    b,p,core,y,z=place()
    q=1-p; xn=q; s=b*2+p
    pf=p.astype(f32); qf=1.0-pf
    yn=b+2-4*y; sib=b+1-2*core; oc=1-core
    up_ok=z<3; dn_ok=z>0
    top=z==3
    mine=(y*2+core)*2+p
    cvt3=Blocks(cvt,1536)
    mcopy=pltpu.make_async_copy(mast,cvt.at[pl.ds(0,1611)],own_sem)
    mcopy.start()
    barrier=pltpu.get_barrier_semaphore()
    plane=[]
    for dy in range(2):
        for dc in range(2):
            for dp in range(2):
                if dy+dc+dp: plane.append((4*dy+2*dc+dp,z*4+lax.rem(y+dy,2)*2+lax.rem(core+dc,2),lax.rem(p+dp,2)))
    line=[(k,lax.rem(z+k,4)) for k in range(1,4)]
    def sig(bb,pp): pl.semaphore_signal(barrier,inc=1,device_id=(bb,pp),device_id_type=MESH)
    for _,bb,pp in plane: sig(bb,pp)
    for _,zz in line: sig(b+4*(zz-z),p)
    def when(ok,f):
        if ok is None: f()
        else: pl.when(ok)(f)
    def AND(*c):
        r=None
        for k in c:
            if k is not None: r=k if r is None else r&k
        return r
    def wait_in(ref,sem):
        pltpu.make_async_remote_copy(src_ref=ref,dst_ref=ref,send_sem=sem,recv_sem=sem,device_id=(b,xn),device_id_type=MESH).wait_recv()
    def slot(zz,yy,pp,cc=core): return ((zz*2+yy)*2+cc)*2+pp
    A=pl.ds(0,HALF); B=pl.ds(HALF,BLK-HALF)
    cm=Comm()
    shift=lax.rem(9*s,16)
    total[ROWS-1:BLK]=jnp.zeros((BLK-ROWS+1,CH),f32)
    mcopy.wait()
    for j in range(3): total[0:ROWS,128*j:128*j+128]=cvt[pl.ds(j,ROWS,stride=3),:]
    at=lax.broadcasted_iota(jnp.int32,(BLK,CH),0)
    blk[...]=jnp.where(at==BLK-4,(level[...]==0).astype(f32),pltpu.roll(total[...],shift,0)).astype(bf)
    own=pltpu.make_async_copy(blk,g_ref.at[s],own_sem)
    own.start()
    pl.semaphore_wait(barrier,10)
    def valid(zz): return (zz>=0)&(zz<4)
    def pick(c0,c1,c2,c3): return jnp.where(z==0,c0,jnp.where(z==1,c1,jnp.where(z==2,c2,c3)))
    hs=(A,B)
    ends=(z==0)|(z==3); is1=z==1; is2=z==2; inner_z=jnp.logical_not(ends)
    def z_send(ok,zz,h,d,src=None):
        g=g_ref.at[slot(zz,y,p),hs[h]]
        cm.go(ok,g if src is None else src,g,azs.at[zz,(1-d)//2],azr.at[zz,h],b+4*d,p)
    def xy_send(ok,zz,h,src=None):
        g=g_ref.at[slot(zz,y,p),hs[h]]
        cm.go(ok,g if src is None else src,g,axs.at[zz],axr.at[zz,h],b,xn)
        cm.go(ok,g if src is None else src,g,ays.at[zz],ayr.at[zz,h],yn,p)
    def sib_send(ok,zz,yy,pp,h,src=None):
        g=g_ref.at[slot(zz,yy,pp),hs[h]]
        cm.go(ok,g if src is None else src,g,ass.at[zz],asr.at[zz],sib,p)
    def own_sends():
        for h in range(2):
            src=blk.at[hs[h]]
            z_send(z==0,z,h,1,src)
            z_send(z==3,z,h,-1,src)
            sib_send(None,z,y,p,h,src)
    def own_xy():
        for h in range(2): xy_send(z!=1,z,h,blk.at[hs[h]])
    four=((1-y,xn),(y,xn),(1-y,p),(y,p))
    def two_send(ok,i,d):
        yy,pp=four[i]
        for h in range(2):
            g=g_ref.at[slot(2,yy,pp),hs[h]]
            cm.go(ok,g,g,a2s.at[(1-d)//2],a2r.at[yy,pp,h],b+4*d,p)
    def two_in(i,ok):
        yy,pp=four[i]
        for h in range(2):
            g=g_ref.at[slot(2,yy,pp),hs[h]]
            when(ok,lambda: wait_in(g,a2r.at[yy,pp,h]))
            cm.go(ok&(z==1),g,g,a2s.at[1],a2r.at[yy,pp,h],b-4,p)
            sib_send(ok,2,yy,pp,h)
    def two_diag():
        sd=slot(2,1-y,xn)
        def f():
            wait_in(g_ref.at[sd,A],adar.at[2])
            wait_in(g_ref.at[sd,B],adbr.at[2])
        when(z==2,f)
        for h in range(2): sib_send(z==2,2,1-y,xn,h)
    def arrive0(h):
        ok=z!=0
        when(ok,lambda: wait_in(g_ref.at[slot(0,y,p),hs[h]],azr.at[0,h]))
        z_send(ok&up_ok,0,h,1)
        xy_send(ok,0,h)
        sib_send(ok,0,y,p,h)
    def arrive3(h,ok):
        when(ok,lambda: wait_in(g_ref.at[slot(3,y,p),hs[h]],azr.at[3,h]))
        z_send(ok&dn_ok,3,h,-1)
        sib_send(ok,3,y,p,h)
    def xy_arrive(ok,f,h):
        sx=slot(f,y,xn); sy=slot(f,1-y,p)
        when(ok,lambda: wait_in(g_ref.at[sx,hs[h]],axr.at[f,h]))
        if h==0: cm.go(ok,g_ref.at[sx,A],g_ref.at[sx,A],ads.at[f],adar.at[f],yn,p)
        sib_send(ok,f,y,xn,h)
        when(ok,lambda: wait_in(g_ref.at[sy,hs[h]],ayr.at[f,h]))
        if h==1: cm.go(ok,g_ref.at[sy,B],g_ref.at[sy,B],ads.at[f],adbr.at[f],b,xn)
        sib_send(ok,f,1-y,p,h)
    def later_sends():
        for h in range(2):
            src=blk.at[hs[h]]
            z_send(z==1,z,h,1,src)
            z_send(z==1,z,h,-1,src)
    def one_in(h,ok):
        when(ok,lambda: wait_in(g_ref.at[slot(1,y,p),hs[h]],azr.at[1,h]))
        z_send(ok&is2,1,h,1)
        sib_send(ok,1,y,p,h)
    def load(sl): return (pltpu.make_async_copy(g_ref.at[sl,pl.ds(0,528)],wv.at[pl.ds(pl.multiple_of(16*lax.div(ROWS*sl,16),16),528)],wsem.at[lax.div(sl,8)]),
                          pltpu.make_async_copy(g_ref.at[sl,pl.ds(528,32)],tails.at[sl],tsem.at[lax.div(sl,8)]))
    def d_arrive(zz):
        sd=slot(zz,1-y,xn)
        wait_in(g_ref.at[sd,A],adar.at[zz])
        sib_send(None,zz,1-y,xn,0)
        wait_in(g_ref.at[sd,B],adbr.at[zz])
        sib_send(None,zz,1-y,xn,1)
        for yy in range(2):
            for pp in range(2):
                for c in load(slot(zz,yy,pp)): c.start()
    def sib_arrive(zz):
        wait_in(g_ref.at[pl.ds(0,4)],asr.at[zz])
        for yy in range(2):
            for pp in range(2):
                sl=slot(zz,yy,pp,oc)
                for c in load(sl): c.start()
    has_gains=s==31
    gain_line=(y==1)&(core==1)&(p==1)
    def gain_sends():
        for k,zz in line: cm.go(has_gains,blk.at[pl.ds(528,16)],gtile,gls,glr,b+4*(zz-z),p)
    def gain_pass():
        pl.when(has_gains)(lambda: gtile.__setitem__(Ellipsis,blk[528:544]))
        pl.when(gain_line&jnp.logical_not(has_gains))(lambda: wait_in(gtile,glr))
        for d,bb,pp in plane: cm.go(gain_line,gtile,gtile,gps,gpr,bb,pp)
    def gain_wait():
        pl.when(jnp.logical_not(gain_line))(lambda: wait_in(gtile,gpr))
    seen=[]
    def take(shards):
        pltpu.make_async_copy(wv.at[pl.ds(0,8*528)],wv.at[pl.ds(0,8*528)],wsem.at[shards[0]//8]).wait()
        pltpu.make_async_copy(tails.at[pl.ds(0,8)],tails.at[pl.ds(0,8)],tsem.at[shards[0]//8]).wait()
        for k in shards:
            lo=base_of(k)
            if k<31 and base_of(k+1)-lo==544 or k==31: wv[lo+528:lo+544]=tails[k,0:16]
            seen.append(k)
        for k in range(1,32):
            if k in seen and k-1 in seen and (k in shards or k-1 in shards):
                off=base_of(k)-base_of(k-1)-528
                t=tails[k-1,off:off+16].astype(f32)
                if off: t=jnp.where(lax.broadcasted_iota(jnp.int32,(16,CH),0)<8,t,0.0)
                lo=base_of(k)
                wv[lo:lo+16]=(wv[lo:lo+16].astype(f32)+t).astype(bf)
    def rows(u,yy,pp,cc=core):
        at=pl.ds(pl.multiple_of(16*lax.div(ROWS*slot(u,yy,pp,cc),16),16),BLK)
        return wd.at[at,pl.ds(0,CH)] if u==0 else wv.at[at]
    def need(u,yy,pp,cc=core): return None if u<3 else slot(u,yy,pp,cc)<=LAST
    def sibsend(u):
        for yy,pp in four:
            cm.go(need(u,yy,pp,oc),rows(u,yy,pp,oc),sibr.at[4*u+2*yy+pp],s1s.at[u],s1r.at[u,yy,pp],sib,p)
    def both(u,yy,pp,lo,n):
        a=pl.multiple_of(16*lax.div(ROWS*slot(u,yy,pp),16)+lo,16)
        mine_=wd[pl.ds(a,n),0:CH] if u==0 else wv[pl.ds(a,n)]
        return mine_.astype(f32)+sibr[4*u+2*yy+pp,lo:lo+n].astype(f32)
    HA=(0,HALF); HB=(HALF,BLK-HALF)
    def sib_in(u,yy,pp): wait_in(sibr.at[4*u+2*yy+pp],s1r.at[u,yy,pp])
    def keep(u,yy,pp,half,more=None):
        t=both(u,yy,pp,*half)
        if more is not None: t=t+more.astype(f32)
        sibr[4*u+2*yy+pp,half[0]:half[0]+half[1]]=t.astype(bf)
    def diag(u):
        yy,pp=1-y,xn
        c=need(u,yy,pp)
        def f():
            sib_in(u,yy,pp)
            keep(u,yy,pp,HA); keep(u,yy,pp,HB)
        when(c,f)
        src=sibr.at[4*u+2*yy+pp]
        if u<2: cm.go(c,src.at[A],rba.at[u],ds_.at[u],dar.at[u],b,xn)
        else: cm.go(c,src.at[A],rba.at[u],ds_.at[u],dar.at[u],yn,p)
        cm.go(c,src.at[B],rb.at[u],ds_.at[u],dbr.at[u],yn,p)
    def ysend(u):
        c=need(u,1-y,p)
        def f():
            sib_in(u,1-y,p)
            keep(u,1-y,p,HA); keep(u,1-y,p,HB)
        when(c,f)
        for h in range(2): cm.go(c,sibr.at[4*u+2*(1-y)+p,hs[h]],ry.at[u,hs[h]],rys.at[u],ryr.at[u,h],yn,p)
    def xsend(u):
        c=need(u,y,xn)
        def f():
            sib_in(u,y,xn)
            wait_in(rba.at[u],dar.at[u])
            keep(u,y,xn,HA,rba[u])
        when(c,f)
        cm.go(c,sibr.at[4*u+2*y+xn,A],rx.at[u,A],rxs.at[u],rxr.at[u,0],b,xn)
        def f2():
            wait_in(rb.at[u],dbr.at[u])
            keep(u,y,xn,HB,rb[u])
        when(c,f2)
        cm.go(c,sibr.at[4*u+2*y+xn,B],rx.at[u,B],rxs.at[u],rxr.at[u,1],b,xn)
    def first_halves(u):
        sib_in(u,y,xn)
        keep(u,y,xn,HA)
        cm.go(None,sibr.at[4*u+2*y+xn,A],rx.at[u,A],rxs.at[u],rxr.at[u,0],b,xn)
        sib_in(u,1-y,p)
        keep(u,1-y,p,HB)
        cm.go(None,sibr.at[4*u+2*(1-y)+p,B],ry.at[u,B],rys.at[u],ryr.at[u,1],yn,p)
    def second_halves(u):
        wait_in(rba.at[u],dar.at[u])
        keep(u,1-y,p,HA,rba[u])
        cm.go(None,sibr.at[4*u+2*(1-y)+p,A],ry.at[u,A],rys.at[u],ryr.at[u,0],yn,p)
        wait_in(rb.at[u],dbr.at[u])
        keep(u,y,xn,HB,rb[u])
        cm.go(None,sibr.at[4*u+2*y+xn,B],rx.at[u,B],rxs.at[u],rxr.at[u,1],b,xn)
    def chunks(u): return ((0,80,0),(80,80,0),(160,64,0),(224,64,0),(288,80,1),(368,64,1),(432,64,1),(496,64,1)) if u==0 else ((0,HALF,0),(HALF,BLK-HALF,1))
    def zur_at(u,k): return zur.at[2*(u-1)+k]
    def zdr_at(u,k): return zdr.at[k if u==0 else 8+2*(u-1)+k]
    def xy_in(u,h):
        wait_in(rx.at[u,hs[h]],rxr.at[u,h])
        wait_in(ry.at[u,hs[h]],ryr.at[u,h])
    def zstep(u,i):
        for d in (1,-1):
            at_z=i if d==1 else 3-i
            if not (at_z<u if d==1 else at_z>u): continue
            c=AND(need(u,y,p),z==at_z)
            buf,bsem=(zu.at[u-1],zur_at) if d==1 else (zd.at[u],zdr_at)
            own_at=4*u+2*y+p
            def first(): sib_in(u,y,p)
            when(c,first)
            seen_h=set()
            for k,(lo,n,h) in enumerate(chunks(u)):
                def f():
                    if h not in seen_h: xy_in(u,h)
                    t=both(u,y,p,lo,n)+rx[u,lo:lo+n].astype(f32)+ry[u,lo:lo+n].astype(f32)
                    if i>0:
                        wait_in(buf.at[pl.ds(lo,n)],bsem(u,k))
                        t=t+buf[lo:lo+n].astype(f32)
                    sibr[own_at,lo:lo+n]=t.astype(bf)
                when(c,f)
                seen_h.add(h)
                cm.go(c,sibr.at[own_at,pl.ds(lo,n)],buf.at[pl.ds(lo,n)],zs.at[u],bsem(u,k),b+4*d,p)
    def zend(u):
        def f():
            sib_in(u,y,p)
            done=set()
            for k,(lo,n,h) in enumerate(chunks(u)):
                if h not in done: xy_in(u,h); done.add(h)
                t=both(u,y,p,lo,n)+rx[u,lo:lo+n].astype(f32)+ry[u,lo:lo+n].astype(f32)
                if u>0:
                    wait_in(zu.at[u-1,pl.ds(lo,n)],zur_at(u,k))
                    t=t+zu[u-1,lo:lo+n].astype(f32)
                if u<3:
                    wait_in(zd.at[u,pl.ds(lo,n)],zdr_at(u,k))
                    t=t+zd[u,lo:lo+n].astype(f32)
                if u==3:
                    rr=16*lax.div(ROWS*s,16)+lo+lax.broadcasted_iota(jnp.int32,(n,CH),0)
                    t=jnp.where(rr<R_EMB,t,total[lo:lo+n])
                total[lo:lo+n]=t
        when(AND(need(u,y,p),z==u),f)
    state={"k":0}
    def xchg(src,dst,dst_like=None):
        k=state["k"]; state["k"]=k+1
        c=pltpu.make_async_remote_copy(src_ref=src,dst_ref=dst,send_sem=xs.at[k],recv_sem=xr.at[k],device_id=(b,q),device_id_type=MESH)
        c.start()
        return c
    edge=pl.ds(pl.multiple_of(q*480,32),32)
    gain_sends()
    c_img=xchg(img.at[edge],himg)
    def gsum(v): return exact(v,gm[...],nn)
    def swap_sums(k,s1,s2):
        ssend[k]=jnp.concatenate([s1,s2,jnp.zeros((6,CH),f32)],0)
        return xchg(ssend.at[k],srecv.at[k])
    def total_sums(k):
        t=gsum(ssend[k]+srecv[k])*(1.0/(12*2*PX))
        return t[0:1],t[1:2]
    def norm_of(t):
        mean,sq=t
        return mean,lax.rsqrt(sq-mean*mean+EPS_NORM)
    def fill3(dst,at,a):
        col=lax.broadcasted_iota(jnp.int32,a.shape,0)&31
        n=a.shape[0]
        dst[pl.ds(at,n),CH:2*CH]=a.astype(bf)
        dst[pl.ds(at,n),0:CH]=jnp.where(col==0,0.0,pltpu.roll(a,1,0)).astype(bf)
        dst[pl.ds(at,n),2*CH:3*CH]=jnp.where(col==31,0.0,pltpu.roll(a,n-1,0)).astype(bf)
    def fill_edges(dst,h):
        fill3(dst,0,h*pf); fill3(dst,544,h*qf)
    def conv_to(dst,x3,wrow,add=None):
        for dr in range(3):
            d=nn(x3[32*dr:32*dr+PX],wv[wrow+1152*dr:wrow+1152*dr+1152])
            if dr==0: dst[...]=d if add is None else add()+d
            else: dst[...]+=d
    def conv_dx(dst,wrow):
        first=True
        for dr in range(3):
            for dc in range(3):
                d=nt(z3[32*(2-dr):32*(2-dr)+PX,CH*(2-dc):CH*(2-dc)+CH],wv[wrow+CH*(3*dr+dc):wrow+CH*(3*dr+dc)+CH])
                if first: dst[...]=d
                else: dst[...]+=d
                first=False
    def st(i,c):
        v=img[pl.ds(i,64)].astype(f32)
        return c[0]+col8(v),c[1]+col8(v*v)
    a1,a2=cloop(PX,64,st,(Z8(),Z8()))
    c=swap_sums(0,row(a1),row(a2))
    own_sends()
    gain_pass()
    own_xy()
    gain_wait()
    g6=gtile[...].astype(f32)
    g1,b1,g2,b2,g3,b3=[g6[2+i:3+i] for i in range(6)]
    c.wait()
    mean1,inv1=norm_of(total_sums(0))
    def act_of(v): return silu((v-mean1)*inv1*g1+b1)
    arrive3(0,is2)
    arrive3(1,is2)
    def fa(i,_):
        fill3(x3a,pl.multiple_of(i+32,32),act_of(img[pl.ds(i,64)].astype(f32)))
        return 0
    cloop(PX,64,fa,0)
    c_img.wait()
    fill_edges(x3a,act_of(himg[...].astype(f32)))
    own.wait()
    xy_arrive(z==3,3,0)
    xy_arrive(z==3,3,1)
    arrive0(0)
    xy_arrive(is2,2,0)
    arrive0(1)
    xy_arrive(is2,2,1)
    arrive3(0,is1)
    arrive3(1,is1)
    later_sends()
    two_send(is2,3,-1)
    two_send(is2,1,-1); two_send(is2,2,-1)
    xy_arrive(None,0,0)
    one_in(0,is2)
    one_in(1,is2)
    xy_arrive(None,0,1)
    for h in range(2): xy_send(inner_z,3,h)
    for h in range(2): one_in(h,top)
    for h in range(2): xy_send(top,1,h)
    for i in (3,1,2): two_send(is2,i,1)
    two_diag()
    two_send(is2,0,-1); two_send(is2,0,1)
    d_arrive(0)
    sib_arrive(0)
    take(range(0,8))
    conv_to(inner,x3a,R_ONE)
    def st2(i,c):
        v=inner[pl.ds(i,64)]
        return c[0]+col8(v),c[1]+col8(v*v)
    a1,a2=cloop(PX,64,st2,(Z8(),Z8()))
    c1=swap_sums(1,row(a1),row(a2))
    c2=xchg(inner.at[edge],hrecv.at[0])
    two_in(3,is1)
    arrive3(0,z==0)
    arrive3(1,z==0)
    for h in range(2): xy_send(z==0,3,h)
    xy_arrive(z!=3,3,0)
    xy_arrive(z!=3,3,1)
    for h in range(2): one_in(h,z==0)
    for h in range(2): xy_send(z!=3,1,h)
    d_arrive(3)
    sib_arrive(3)
    two_in(1,is1)
    take(range(24,32))
    ids=rowid[...]
    pre=[]
    tcol=lax.broadcasted_iota(jnp.int32,(16,R_END-R_TAB),1)
    for h in range(2):
        hot=(tcol==2*ids+h).astype(f32).astype(bf)
        pre.append(nn(hot,wv[R_TAB:R_END])[0:1]+tvec[:,CH*h:CH*h+CH])
    emb=[silu(v) for v in pre]
    put3(cvt3,pl.ds(0,1536),wv[R_EMB:R_TAB].astype(f32))
    wee[...]=ld(cvt3,every(0,768,2)).astype(bf)
    weo[...]=ld(cvt3,every(1,768,2)).astype(bf)
    def emb_dot(w):
        r=None
        for h in range(2):
            e=jnp.broadcast_to(emb[h],(16,CH))
            d=exact(e,w[CH*h:CH*h+CH],nn)[0:1]
            r=d if r is None else r+d
        return r
    sc1=1.0+emb_dot(wee); sh=emb_dot(weo)
    c1.wait()
    xy_arrive(None,1,0)
    mean2,inv2=norm_of(total_sums(1))
    def pre_b(v):
        n=(v-mean2)*inv2
        af=n*g2+b2
        return n,af,af*sc1+sh
    def fb(i,_):
        fill3(x3b,pl.multiple_of(i+32,32),silu(pre_b(inner[pl.ds(i,64)])[2]))
        return 0
    cloop(PX,64,fb,0)
    c2.wait()
    fill_edges(x3b,silu(pre_b(hrecv[0])[2]))
    xy_arrive(None,1,1)
    two_in(2,is1)
    d_arrive(1)
    sib_arrive(1)
    two_in(0,is1)
    take(range(8,16))
    conv_to(middle,x3b,R_TWO,lambda: img[...].astype(f32))
    def st3(i,c):
        v=middle[pl.ds(i,64)]
        return c[0]+col8(v),c[1]+col8(v*v)
    a1,a2=cloop(PX,64,st3,(Z8(),Z8()))
    c1=swap_sums(2,row(a1),row(a2))
    put3(cvt3,pl.ds(0,1152),wv[R_QKV:R_PROJ].astype(f32))
    for j in range(3):
        wqT[CH*j:CH*j+CH]=ld(cvt3,every(j,CH,3)).T.astype(bf)
    c1.wait()
    mean3,inv3=norm_of(total_sums(2))
    def fc(i,_):
        n=(middle[pl.ds(i,64)]-mean3)*inv3
        ain[pl.ds(i,64)]=(n*g3+b3).astype(bf)
        return 0
    cloop(PX,64,fc,0)
    c_in=xchg(ain.at[pl.ds(0,PX)],ain.at[pl.ds(PX,PX)])
    c_mid=xchg(middle.at[edge],hmid)
    def triples(a):
        t=nt(wqT[...],a)
        is_q=lax.rem(lax.broadcasted_iota(jnp.int32,t.shape,0),192)<64
        return jnp.where(is_q,t*0.125,t).astype(bf)
    trT[:,0:PX]=triples(ain[0:PX])
    def head_rows(h):
        r0=pl.multiple_of(h*192,64)
        return r0,pl.multiple_of(r0+64,64),pl.multiple_of(r0+128,64)
    def fh1(h,_):
        r0,r1,r2=head_rows(h)
        sco=nn(trT[pl.ds(r1,64),0:PX].T,trT[pl.ds(r0,64),0:PX])
        m=jnp.max(sco,0,keepdims=True)
        e=jnp.exp(sco-m)
        lse[h,0:1]=m
        lse[h,1:2]=jnp.sum(e,0,keepdims=True)
        acc[h]=nn(trT[pl.ds(r2,64),0:PX],e.astype(bf))
        return 0
    lax.fori_loop(0,6,fh1,0)
    for i in (3,1,2): two_in(i,ends)
    c_in.wait()
    trT[:,PX:2*PX]=triples(ain[PX:2*PX])
    def fh(h,_):
        r0,r1,r2=head_rows(h)
        sco=nn(trT[pl.ds(r1,64),PX:2*PX].T,trT[pl.ds(r0,64),0:PX])
        m0=lse[h,0:1]
        m=jnp.maximum(m0,jnp.max(sco,0,keepdims=True))
        e=jnp.exp(sco-m)
        a=jnp.exp(m0-m)
        l=lse[h,1:2]*a+jnp.sum(e,0,keepdims=True)
        o=acc[h]*a+nn(trT[pl.ds(r2,64),PX:2*PX],e.astype(bf))
        attT[pl.ds(pl.multiple_of(h*64,64),64),:]=(o*(1.0/l)).astype(bf)
        lse[h,0:1]=m+jnp.log(l)
        return 0
    lax.fori_loop(0,6,fh,0)
    put3(gout,pl.ds(0,PX),middle[...]+tn(attT[...],wv[R_PROJ:R_DOWN]))
    hsend[0]=ld(gout,edge).astype(bf)
    c1=xchg(hsend.at[0],oth.at[0])
    two_in(0,ends)
    for yy in range(2):
        for pp in range(2):
            for k in load(slot(2,yy,pp)): k.start()
    sib_arrive(2)
    take(range(16,24))
    for off in range(9):
        put3(cvt3,pl.ds(0,576),wv[R_DOWN+576*off:R_DOWN+576*off+576].astype(f32))
        v0,v1,v2=[ld(cvt3,every(i,192,3)) for i in range(3)]
        put3(cvt2,every(0,192,2),jnp.concatenate([v0,v1[:,0:256]],1))
        w=jnp.concatenate([v1[:,128:384],v2],1)
        w=pltpu.roll(w,w.shape[1]-64,1)
        put3(cvt2,every(1,192,2),w)
        wd[CH*off:CH*off+CH]=ld(cvt2,pl.ds(0,CH))[:,0:576].astype(bf)
    def parts(ref,n):
        e=ld(ref,every(0,n//2,2)); o=ld(ref,every(1,n//2,2))
        col=lax.broadcasted_iota(jnp.int32,o.shape,0)&15
        return jnp.where(col==0,0.0,pltpu.roll(o,1,0)).astype(bf),e.astype(bf),o.astype(bf)
    for dc,v in enumerate(parts(gout,PX)):
        v=v.reshape(8,32,CH)
        even=v[:,0:16].reshape(128,CH); odd=v[:,16:32].reshape(128,CH)
        xd[:,CH*(3+dc):CH*(3+dc)+CH]=even
        xd[:,CH*(6+dc):CH*(6+dc)+CH]=odd
        xd[16:128,CH*dc:CH*dc+CH]=odd[0:112]
    c1.wait()
    put3(geo,pl.ds(0,32),oth[0].astype(f32)*pf)
    for dc,v in enumerate(parts(geo,32)):
        xd[0:16,CH*dc:CH*dc+CH]=v
    fin=nn(xd[...],wd[0:9*CH])
    feat=nn(fin.astype(bf),vgg[...]); tf=nn(tgt[...],vgg[...])
    ir=lax.rsqrt(jnp.mean(feat*feat,-1,keepdims=True)+EPS_FEAT)
    unit=feat*ir
    diff=unit-tf*lax.rsqrt(jnp.mean(tf*tf,-1,keepdims=True)+EPS_FEAT)
    wl=lin[...]*diff
    consist=jnp.sum(row(wl*diff),1,keepdims=True)*(1.0/(256*256))
    du=wl*(2.0/(256*256*images_all))
    dfeat=(ir*(du-unit*jnp.mean(du*unit,-1,keepdims=True))).astype(bf)
    zc=jnp.zeros((16,128),f32)
    for t_ in range(0,32,2): zc=zc+tails[t_,16:32,0:128].astype(f32)
    zc=zc[12:13,0:1]
    seed=(level[...]==0).astype(f32)/jnp.maximum(zc,1.0)*(2.0/(256*CH2))
    gfin=nt(dfeat,vgg[...])+seed*(fin-cln[...].astype(f32))
    dz=gfin.astype(bf)
    dzs[...]=dz[0:16]
    c1=xchg(dzs,dzr)
    for off in range(9):
        dw=tn(xd[:,CH*off:CH*off+CH],dz)
        put3(cvt2,pl.ds(0,CH),jnp.concatenate([dw,jnp.zeros((CH,64),f32)],1))
        e=ld(cvt2,every(0,192,2)); o_=pltpu.roll(ld(cvt2,every(1,192,2)),64,1)
        lane=lax.broadcasted_iota(jnp.int32,(192,128),1)
        put3(cvt3,every(0,192,3),e[:,0:384])
        put3(cvt3,every(1,192,3),jnp.concatenate([e[:,384:512],jnp.where(lane<64,e[:,512:640],o_[:,0:128]),o_[:,128:256]],1))
        put3(cvt3,every(2,192,3),o_[:,256:640])
        wv[R_DOWN+576*off:R_DOWN+576*off+576]=ld(cvt3,pl.ds(0,576)).astype(bf)
    sibsend(2); sibsend(3)
    c1.wait()
    z32=dz.astype(f32)
    down=jnp.concatenate([z32[16:128],dzr[...].astype(f32)*qf],0)
    def left(v):
        col=lax.broadcasted_iota(jnp.int32,v.shape,0)&15
        return jnp.where(col==15,0.0,pltpu.roll(v,127,0)).astype(bf)
    s00,s01,s10,s11=dz,left(z32),down.astype(bf),left(down)
    W=lambda a,c: wd[CH*(3*a+c):CH*(3*a+c)+CH]
    def put(a,c,v):
        for i in range(8):
            put3(gout,every((2*i+a)*32+c,16,2),v[16*i:16*i+16])
    put(0,0,nt(s00,W(1,1)))
    put(0,1,nt(s00,W(1,2))+nt(s01,W(1,0)))
    put(1,0,nt(s00,W(2,1))+nt(s10,W(0,1)))
    put(1,1,nt(s00,W(2,2))+nt(s01,W(2,0))+nt(s10,W(0,2))+nt(s11,W(0,0)))
    diag(2); diag(3); ysend(2); ysend(3)
    gp=ld(gout,pl.ds(0,PX)).astype(bf)
    dattT[...]=nt(wv[R_PROJ:R_DOWN],gp).astype(bf)
    wv[R_PROJ:R_DOWN]=nn(attT[...],gp).astype(bf)
    def bh_part(h,at):
        r0,r1,r2=head_rows(h)
        ra_=pl.ds(pl.multiple_of(h*64,64),64)
        qT=trT[pl.ds(r0,64),0:PX]
        kT=trT[pl.ds(r1,64),at:at+PX]
        gT=dattT[ra_,:]
        pr=jnp.exp(nn(kT.T,qT)-lse[h,0:1])
        de=jnp.sum(gT.astype(f32)*attT[ra_,:].astype(f32),0,keepdims=True)
        ds=(pr*(nn(trT[pl.ds(r2,64),at:at+PX].T,gT)-de)).astype(bf)
        dtrT[pl.ds(r1,64),at:at+PX]=nt(qT,ds).astype(bf)
        dtrT[pl.ds(r2,64),at:at+PX]=nt(gT,pr.astype(bf)).astype(bf)
        return r0,nn(kT,ds)*0.125
    def bh(h,_):
        r0,dqT=bh_part(h,PX)
        acc[h]=dqT
        dtrT[pl.ds(r0,64),PX:2*PX]=jnp.zeros((64,PX),bf)
        return 0
    lax.fori_loop(0,6,bh,0)
    oth[1:17]=tn(dtrT[:,PX:2*PX],wqT[...]).astype(bf).reshape(16,32,CH)
    c1=xchg(oth.at[pl.ds(1,16)],oth.at[pl.ds(17,16)])
    def bh2(h,_):
        r0,dqT=bh_part(h,0)
        dtrT[pl.ds(r0,64),0:PX]=(acc[h]+dqT).astype(bf)
        return 0
    lax.fori_loop(0,6,bh2,0)
    gsec[...]=tn(dtrT[:,0:PX],wqT[...])
    dq=nt(ain[...].T,dtrT[...])
    for j in range(3):
        put3(cvt3,every(j,CH,3),dq[:,CH*j:CH*j+CH])
    wv[R_QKV:R_PROJ]=ld(cvt3,pl.ds(0,1152)).astype(bf)
    c1.wait()
    def n3_of(i): return (middle[pl.ds(i,64)]-mean3)*inv3
    def s3(i,c):
        j=pl.multiple_of(17+lax.div(i,32),1)
        v=gsec[pl.ds(i,64)]+oth[pl.ds(j,2)].reshape(64,CH).astype(f32)
        gsec[pl.ds(i,64)]=v
        return c[0]+col8(v),c[1]+col8(v*n3_of(i))
    a1,a2=cloop(PX,64,s3,(Z8(),Z8()))
    db3,dg3=row(a1),row(a2)
    c1=swap_sums(3,db3*g3,dg3*g3)
    esend[0]=ld(gout,edge)+inv3*(gsec[edge]*g3)
    c2=xchg(esend.at[0],erecv.at[0])
    xsend(2)
    c1.wait()
    m1,m2=total_sums(3)
    def f3(i,_):
        v=ld(gout,pl.ds(i,64))+inv3*(gsec[pl.ds(i,64)]*g3-m1-n3_of(i)*m2)
        fill3(z3,pl.multiple_of(i+32,32),v)
        return 0
    cloop(PX,64,f3,0)
    c_mid.wait()
    c2.wait()
    fill_edges(z3,erecv[0]-inv3*(m1+(hmid[...]-mean3)*inv3*m2))
    conv_dx(gsec,R_TWO)
    for dr in range(3):
        d=tn(x3b[32*dr:32*dr+PX],z3[32:32+PX,CH:2*CH]).astype(bf)
        wv[R_TWO+1152*dr:R_TWO+1152*dr+1152]=d
        if dr==0: wd[R_TWO:4304,0:CH]=d[0:4304-R_TWO]
    sibsend(1)
    def s2(i,c):
        n,af,pb=pre_b(inner[pl.ds(i,64)])
        gpre=gsec[pl.ds(i,64)]*slope(pb)
        gaff=gpre*sc1
        gsec[pl.ds(i,64)]=gaff
        return c[0]+col8(gpre*af),c[1]+col8(gpre),c[2]+col8(gaff*n),c[3]+col8(gaff)
    a1,a2,a3,a4=cloop(PX,64,s2,(Z8(),Z8(),Z8(),Z8()))
    dsc,dsh,dg2,db2=row(a1),row(a2),row(a3),row(a4)
    c1=swap_sums(4,db2*g2,dg2*g2)
    esend[1]=gsec[edge]*g2
    c2=xchg(esend.at[1],erecv.at[1])
    diag(1)
    first_halves(1)
    c1.wait()
    m1,m2=total_sums(4)
    def f2(i,_):
        n=(inner[pl.ds(i,64)]-mean2)*inv2
        fill3(z3,pl.multiple_of(i+32,32),inv2*(gsec[pl.ds(i,64)]*g2-m1-n*m2))
        return 0
    cloop(PX,64,f2,0)
    c2.wait()
    fill_edges(z3,inv2*(erecv[1]-m1-(hrecv[0]-mean2)*inv2*m2))
    for dr in range(3):
        wd[1152*dr:1152*dr+1152,0:CH]=tn(x3a[32*dr:32*dr+PX],z3[32:32+PX,CH:2*CH]).astype(bf)
    sibsend(0)
    second_halves(1)
    zstep(2,0)
    conv_dx(gsec,R_ONE)
    diag(0)
    first_halves(0)
    def s1(i,c):
        n=(img[pl.ds(i,64)].astype(f32)-mean1)*inv1
        gpre=gsec[pl.ds(i,64)]*slope(n*g1+b1)
        return c[0]+col8(gpre*n),c[1]+col8(gpre)
    a1,a2=cloop(PX,64,s1,(Z8(),Z8()))
    ge=[]
    for h in range(2):
        d=exact(jnp.broadcast_to(dsc,(16,CH)),wee[CH*h:CH*h+CH],nt)+exact(jnp.broadcast_to(dsh,(16,CH)),weo[CH*h:CH*h+CH],nt)
        ge.append(d[0:1]*slope(pre[h]))
    hot_level=(lax.broadcasted_iota(jnp.int32,(1,CH),1)==level[...]).astype(f32)
    pack_ref[...]=jnp.concatenate([row(a1),row(a2),dg2,db2,dg3,db3,dsc,dsh,ge[0],ge[1],emb[0],emb[1],consist*hot_level,jnp.broadcast_to(ids.astype(f32),(1,CH)),0.5*hot_level,jnp.zeros((1,CH),f32)],0)
    low=jnp.logical_not(top)
    cm.go(low,pack_ref,lpk.at[z],lps,lpr,b+4*(3-z),p)
    zstep(1,0)
    second_halves(0)
    xsend(3)
    zstep(2,1)
    zstep(3,0)
    zstep(1,1)
    zstep(0,0)
    zstep(3,1)
    zstep(0,1)
    zstep(3,2)
    def packs_line():
        lpk[3]=pack_ref[...]
        wait_in(lpk.at[pl.ds(0,3)],lpr)
    pl.when(top)(packs_line)
    for d,bb,pp in plane:
        cm.go(top,lpk,ppk.at[mine],pps,ppr,bb,pp)
    def packs_plane():
        ppk[mine]=lpk[...]
        wait_in(ppk.at[pl.ds(0,7)],ppr)
        a_s=16*lax.div(ROWS*s,16)
        rows_at=lambda k: ppk[:,:,k,:].reshape(32,384)
        zero=jnp.zeros((64,384),f32)
        for h in range(2):
            e=rows_at(10+h)
            t=jnp.concatenate([e,e,zero],0).T
            cvt[pl.ds(BLK+768*h,384,stride=2),:]=t
            cvt[pl.ds(BLK+768*h+1,384,stride=2),:]=t
        r=a_s+lax.broadcasted_iota(jnp.int32,(BLK,128),0)
        l=lax.broadcasted_iota(jnp.int32,(BLK,128),1)
        inside=(r>=R_EMB)&(r<R_TAB)
        start=pl.multiple_of(jnp.clip(a_s-R_EMB+BLK,0,BLK+1536),16)
        lf=jnp.where(inside&(((r&1)==1)==(l>=32))&(l<64),cvt[pl.ds(start,BLK),:],0.0)
        ids=rows_at(13)[:,0:128].astype(jnp.int32)
        ids=jnp.concatenate([ids]*4,0).astype(f32).T[0:1].astype(jnp.int32)
        hot=(r-R_TAB==2*ids+(l>=96).astype(jnp.int32))&(l>=64)&(r>=R_TAB)
        lf=jnp.where(hot,1.0,lf)
        rg=jnp.concatenate([rows_at(6),rows_at(7),rows_at(8),rows_at(9)],0)
        gains=[jnp.sum(rows_at(k),0,keepdims=True) for k in range(6)]
        hi=lax.Precision.HIGHEST
        add=lax.dot_general(lf,rg,(((1,),(0,)),((),())),precision=hi,preferred_element_type=f32)
        for k in range(6): add=add+jnp.where(r[:,0:1]-R_GAIN==k,gains[k],0.0)
        rr=a_s+lax.broadcasted_iota(jnp.int32,(BLK,384),0)
        total[...]=jnp.where(rr<R_EMB,0.0,add)
    pl.when(top)(packs_plane)
    zstep(0,2)
    zend(1); zend(2); zend(3)
    zend(0)
    shift=lax.rem(9*s,16)
    tr_=lax.broadcasted_iota(jnp.int32,(BLK,1),0)
    t=jnp.where((tr_>=shift)&(tr_<shift+ROWS),total[...],0.0)
    sq=jnp.sum(jnp.sum(t*t,0,keepdims=True),1,keepdims=True)
    tile[...]=jnp.concatenate([jnp.broadcast_to(sq,(1,128)),pack_ref[12:13,0:128],pack_ref[14:15,0:128],jnp.zeros((5,128),f32)],0)
    red1[mine]=tile[...]
    for d,bb,pp in plane: cm.go(None,tile,red1.at[mine],n1s,n1r,bb,pp)
    t=pltpu.roll(total[...],lax.rem(BLK-shift,BLK),0)[0:ROWS]
    for j in range(3): cvt[pl.ds(j,ROWS,stride=3),:]=t[:,128*j:128*j+128]
    fcopy=pltpu.make_async_copy(cvt.at[pl.ds(0,1611)],flat_ref,own_sem)
    fcopy.start()
    wait_in(red1.at[pl.ds(0,7)],n1r)
    v=red1[0]
    for k in range(1,8): v=v+red1[k]
    red2[z]=v
    for k,zz in line: cm.go(None,red2.at[z],red2.at[z],n2s,n2r,b+4*(zz-z),p)
    wait_in(red2.at[pl.ds(0,3)],n2r)
    all_ref[...]=red2[0]+red2[1]+red2[2]+red2[3]
    def sent(ok,ref,sem):
        when(ok,lambda: pltpu.make_async_copy(ref,ref,sem).wait())
    block=sibr.at[0]
    for zz in range(4):
        sent(None if zz!=2 else is2,block,axs.at[zz])
        sent(None if zz!=2 else is2,block,ays.at[zz])
        sent(None if zz!=2 else is2,block,ads.at[zz])
        sent(None,sibr.at[pl.ds(0,4)],ass.at[zz])
        if zz<3:
            sent(None,sibr.at[pl.ds(0,4)],s1s.at[zz])
        else:
            sent(core==1,sibr.at[pl.ds(0,2)],s1s.at[zz])
        sent(need(zz,1-y,xn),block,ds_.at[zz])
        sent(need(zz,y,xn),block,rxs.at[zz])
        sent(need(zz,1-y,p),block,rys.at[zz])
        sent(AND(need(zz,y,p),z!=zz),block,zs.at[zz])
    sent(z<3,block,azs.at[0,0])
    sent(z>0,block,azs.at[3,1])
    sent(is1|is2,block,azs.at[1,0])
    sent(is1,block,azs.at[1,1])
    sent(is2,sibr.at[pl.ds(0,4)],a2s.at[0])
    sent(is1|is2,sibr.at[pl.ds(0,4)],a2s.at[1])
    sent(has_gains,blk.at[pl.ds(0,48)],gls)
    sent(gain_line,blk.at[pl.ds(0,112)],gps)
    sent(low,pack_ref,lps)
    sent(top,ppk.at[pl.ds(0,7)],pps)
    sent(None,red1.at[pl.ds(0,7)],n1s)
    sent(None,red2.at[pl.ds(0,3)],n2s)
    fcopy.wait()

def step(images_all,mast,img,tgt,cln,vgg,lin,tvec,rowid,level,gm):
    D=pltpu.SemaphoreType.DMA
    V=lambda *s: pltpu.VMEM(s,bf)
    F=lambda *s: pltpu.VMEM(s,f32)
    vm=pl.BlockSpec(memory_space=pltpu.VMEM)
    return pl.pallas_call(functools.partial(step_kernel,images_all),
        out_shape=(jax.ShapeDtypeStruct((1611,128),f32),jax.ShapeDtypeStruct((8,128),f32),jax.ShapeDtypeStruct((32,BLK,CH),bf)),
        in_specs=[pl.BlockSpec(memory_space=pl.ANY)]+[vm]*9,
        out_specs=(pl.BlockSpec(memory_space=pl.ANY),vm,pl.BlockSpec(memory_space=pl.ANY)),
        scratch_shapes=[V(17184,CH),V(32,32,CH),F(4608,128),F(5,CH,128),V(4304,CH2),V(768,CH),V(768,CH),V(1152,CH),V(576,1152),V(576,1152),V(576,1152),F(PX,CH),F(PX,CH),F(3,PX,128),F(PX,CH),V(1024,CH),V(1152,1024),V(1152,1024),V(CH,PX),V(128,3456),F(6,8,PX),V(CH,PX),F(5,8,CH),F(5,8,CH),V(1,32,CH),F(1,32,CH),V(32,CH),V(16,CH2),V(16,CH2),F(3,32,128),V(33,32,CH),D((4,)),D((4,)),D((15,)),D((15,)),F(BLK,CH),V(BLK,CH),D,D((4,2)),D((4,2)),D((4,)),D((4,2)),D((4,)),D((4,2)),D((4,)),D((4,)),D((4,)),D((4,)),F(16,CH),F(4,16,CH),F(8,4,16,CH),F(8,8,128),F(4,8,128),F(8,128),D,D,D,D,D,D,D,D,V(14,BLK,CH),V(4,BLK-HALF,CH),V(4,BLK,CH),V(4,BLK,CH),V(3,BLK,CH),V(3,BLK,CH),D((4,)),D((4,2,2)),D((4,)),D((4,)),D((4,)),D((4,2)),D((4,)),D((4,2)),D((4,)),D((6,)),D((12,)),F(6,64,PX),V(16,CH),D,D,D,D,V(4,HALF,CH),D((2,)),D((2,2,2)),D((4,)),D((4,)),F(32,CH),F(2,32,CH),F(2,32,CH)],
        compiler_params=pltpu.CompilerParams(collective_id=0,has_side_effects=True,vmem_limit_bytes=63<<20),
        name="train_step",
    )(mast,img,tgt,cln,vgg,lin,tvec,rowid,level,gm)


def fast(images, target, clean_images, levels, labels, null_mask, vgg_proj, lpips_lin, master, first_moment, second_moment):
    row_index = jnp.where(null_mask == 1, CLASSES, labels).reshape(1, 1)
    tvec = time_vector(levels)
    lane = jnp.arange(CH, dtype=jnp.int32) // 12
    gm = (lane[:, None] == lane[None, :]).astype(jnp.bfloat16)
    own_grad, sums, _ = step(
        16,
        master.reshape(1611, 128),
        images.reshape(PX, CH),
        target.reshape(128, CH2),
        clean_images.reshape(128, CH2),
        vgg_proj,
        lpips_lin.reshape(1, 256),
        tvec,
        row_index,
        levels.reshape(1, 1),
        gm,
    )
    own_grad = own_grad.reshape(-1)
    level_sums = sums[1:3, :LEVELS]
    norm_before = jnp.sqrt(sums[0, 0])
    clipped = own_grad * jnp.minimum(1.0, CLIP / norm_before)
    new_first = BETA_ONE * first_moment + (1.0 - BETA_ONE) * clipped
    new_second = BETA_TWO * second_moment + (1.0 - BETA_TWO) * clipped * clipped
    fixed_first = new_first / (1.0 - BETA_ONE**STEP)
    fixed_second = new_second / (1.0 - BETA_TWO**STEP)
    new_master = master - RATE * (fixed_first / (jnp.sqrt(fixed_second) + EPS_ADAM) + DECAY * master)
    return (new_master, new_first, new_second, new_master.astype(jnp.bfloat16), norm_before, level_sums)


def solution(mesh):
    small = mesh.shape["batch"] == 16 and mesh.shape["pix"] == 2
    return jax.shard_map(
        fast if small else local,
        mesh=mesh,
        in_specs=(
            P("batch", "pix", None, None),
            P("batch", "pix", None, None),
            P("batch", "pix", None, None),
            P("batch"),
            P("batch"),
            P("batch"),
            P(),
            P(),
            P(("batch", "pix")),
            P(("batch", "pix")),
            P(("batch", "pix")),
        ),
        out_specs=(
            P(("batch", "pix")),
            P(("batch", "pix")),
            P(("batch", "pix")),
            P(("batch", "pix")),
            P(),
            P(),
        ),
        check_vma=False,
    )
```

```python
import functools
import math

import jax
import jax.numpy as jnp
from jax import lax
from jax.experimental import pallas as pl
from jax.experimental.pallas import tpu as pltpu
from jax.sharding import PartitionSpec as P

CH = 384
CH2 = 576
GROUPS = 32
HEAD = 64
TEMB = 768
CLASSES = 1000
LEVELS = 40
STEP = 10


EPS_NORM = 1e-05
EPS_FEAT = 1e-06
BETA_ONE = 0.9
BETA_TWO = 0.999
EPS_ADAM = 1e-08
RATE = 0.02
DECAY = 0.01
CLIP = 0.01
precise = lax.Precision.HIGHEST


def extended(shard, sides, width):
    for axis, dim in sides:
        size, length = (lax.axis_size(axis), shard.shape[dim])
        up = [(i, (i + 1) % size) for i in range(size - 1)]
        down = [(j, i) for i, j in up]
        last = lax.slice_in_dim(shard, length - width, length, axis=dim)
        initial = lax.slice_in_dim(shard, 0, width, axis=dim)
        before = lax.ppermute(last, axis, up)
        after = lax.ppermute(initial, axis, down)
        shard = jnp.concatenate([before, shard, after], axis=dim)
    return shard


def unpack(flat_vec):
    layout = [
        (9 * CH, CH),
        (9 * CH, CH),
        (CH, 3 * CH),
        (CH, CH),
        (9 * CH, CH2),
        (TEMB, 2 * CH),
        (CLASSES + 1, TEMB),
        (6, CH),
    ]
    pieces = []
    offset = 0
    for rows_n, cols_n in layout:
        pieces.append(flat_vec[offset : offset + rows_n * cols_n].reshape(rows_n, cols_n))
        offset += rows_n * cols_n
    return (pieces, offset)


def time_vector(level_ids):
    half_width = TEMB // 2
    frequency = jnp.exp(-math.log(10000.0) * jnp.arange(half_width, dtype=jnp.float32) / half_width)
    angles = level_ids.astype(jnp.float32)[..., None] * (1000.0 / LEVELS) * frequency
    return jnp.concatenate([jnp.cos(angles), jnp.sin(angles)], -1)


def silu_slope(values):
    sigmoid = jax.nn.sigmoid(values)
    return sigmoid * (1.0 + values * (1.0 - sigmoid))


def pix_sums(pair_sums):
    return lax.psum((pair_sums[0], pair_sums[1]), "pix")


def group_forward(values, pixels_all):
    grouped = values.reshape(values.shape[0], values.shape[1], GROUPS, -1)
    totals = pix_sums((jnp.sum(grouped, (1, 3)), jnp.sum(grouped * grouped, (1, 3))))
    per_group = pixels_all * grouped.shape[3]
    center = totals[0] / per_group
    spread = totals[1] / per_group - center * center
    inverse = lax.rsqrt(spread + EPS_NORM)
    normed = (grouped - center[:, None, :, None]) * inverse[:, None, :, None]
    return (normed.reshape(values.shape), inverse)


def group_backward(grad_normed, normed, inverse, pixels_all):
    grad_grouped = grad_normed.reshape(normed.shape[0], normed.shape[1], GROUPS, -1)
    val_grouped = normed.reshape(grad_grouped.shape)
    totals = pix_sums((jnp.sum(grad_grouped, (1, 3)), jnp.sum(grad_grouped * val_grouped, (1, 3))))
    per_group = pixels_all * grad_grouped.shape[3]
    result = (
        grad_grouped
        - (totals[0] / per_group)[:, None, :, None]
        - val_grouped * (totals[1] / per_group)[:, None, :, None]
    )
    return (result * inverse[:, None, :, None]).reshape(normed.shape)


def columns_of(values, stride):
    rows_out = values.shape[1] // stride
    cols_out = values.shape[2] // stride
    span_rows = stride * (rows_out - 1) + 1
    span_cols = stride * (cols_out - 1) + 1
    padded = extended(values, (("pix", 1),), 1)
    padded = jnp.pad(padded, ((0, 0), (0, 0), (1, 1), (0, 0)))
    return jnp.concatenate(
        [
            padded[
                :, row_off : row_off + span_rows : stride, col_off : col_off + span_cols : stride, :
            ]
            for row_off in range(3)
            for col_off in range(3)
        ],
        -1,
    )


def conv_forward(values, weight, rows_in, stride):
    n_img, pixels_in, in_chan = values.shape
    columns = columns_of(values.reshape(n_img, rows_in, -1, in_chan), stride)
    result = jnp.dot(columns.reshape(-1, 9 * in_chan), weight, preferred_element_type=jnp.float32)
    return (result.reshape(n_img, -1, weight.shape[1]), columns)


def conv_back(columns, grad_low, weight, rows_in, stride):
    n_img, pix_out, out_chan = grad_low.shape
    in_chan = weight.shape[0] // 9
    d_weight = jnp.einsum(
        "rk,rc->kc",
        columns.reshape(-1, 9 * in_chan),
        grad_low.reshape(-1, out_chan),
        preferred_element_type=jnp.float32,
    )
    flipped = (
        weight.reshape(3, 3, in_chan, out_chan)[::-1, ::-1]
        .transpose(0, 1, 3, 2)
        .reshape(9 * out_chan, in_chan)
    )
    rows_out = rows_in // stride
    grid_grad = grad_low.reshape(n_img, rows_out, pix_out // rows_out, out_chan)
    if stride > 1:
        grid_grad = jnp.pad(
            grid_grad[:, :, None, :, None, :],
            ((0, 0), (0, 0), (0, stride - 1), (0, 0), (0, stride - 1), (0, 0)),
        )
        grid_grad = grid_grad.reshape(n_img, rows_in, -1, out_chan)
    grad_columns = columns_of(grid_grad, 1)
    grad_input = jnp.dot(
        grad_columns.reshape(-1, 9 * out_chan), flipped, preferred_element_type=jnp.float32
    )
    return (d_weight, grad_input.reshape(n_img, -1, in_chan))


def res_forward(values, gain_rows, scale, shift, w_first, w_second, rows_in, pixels_all):
    normed_a, inverse_a = group_forward(values, pixels_all)
    pre_a = normed_a * gain_rows[0] + gain_rows[1]
    act_a = jax.nn.silu(pre_a).astype(jnp.bfloat16)
    inner, columns_a = conv_forward(act_a, w_first, rows_in, 1)
    normed_b, inverse_b = group_forward(inner, pixels_all)
    affine_b = normed_b * gain_rows[2] + gain_rows[3]
    pre_b = affine_b * (1.0 + scale) + shift
    second = jax.nn.silu(pre_b).astype(jnp.bfloat16)
    branch, columns_b = conv_forward(second, w_second, rows_in, 1)
    kept_state = (
        normed_a,
        inverse_a,
        pre_a,
        columns_a,
        normed_b,
        inverse_b,
        affine_b,
        pre_b,
        columns_b,
    )
    return (values + branch, kept_state)


def res_back(grad_result, kept_state, gain_rows, scale, w_first, w_second, rows_in, pixels_all):
    normed_a, inverse_a, pre_a, columns_a, normed_b, inverse_b, affine_b, pre_b, columns_b = (
        kept_state
    )
    d_w_second, grad_second = conv_back(
        columns_b, grad_result.astype(jnp.bfloat16), w_second, rows_in, 1
    )
    grad_pre_b = grad_second * silu_slope(pre_b)
    d_scale = jnp.sum(grad_pre_b * affine_b, 1)
    d_shift = jnp.sum(grad_pre_b, 1)
    grad_affine = grad_pre_b * (1.0 + scale)
    d_gain_b = jnp.sum(grad_affine * normed_b, (0, 1))
    d_bias_b = jnp.sum(grad_affine, (0, 1))
    grad_inner = group_backward(grad_affine * gain_rows[2], normed_b, inverse_b, pixels_all).astype(
        jnp.bfloat16
    )
    d_w_first, grad_act = conv_back(columns_a, grad_inner, w_first, rows_in, 1)
    grad_pre_a = grad_act * silu_slope(pre_a)
    d_gain_a = jnp.sum(grad_pre_a * normed_a, (0, 1))
    d_bias_a = jnp.sum(grad_pre_a, (0, 1))
    grad_values = None
    d_gains = jnp.stack([d_gain_a, d_bias_a, d_gain_b, d_bias_b])
    return (d_w_first, d_w_second, d_gains, d_scale, d_shift, grad_values)


def to_heads(values):
    return lax.all_to_all(values, "pix", split_axis=2, concat_axis=1, tiled=True)


def to_pixels(values):
    return lax.all_to_all(values, "pix", split_axis=1, concat_axis=2, tiled=True)


def flat_heads(values):
    return values.reshape(-1, values.shape[2], values.shape[3])


def attend(queries, keys, values):
    root_dim = math.sqrt(queries.shape[-1])

    def single(bundle):
        q_one, k_one, v_one = bundle
        scores = (
            jnp.einsum("qd,kd->qk", q_one, k_one, preferred_element_type=jnp.float32) / root_dim
        )
        row_peak = jnp.max(scores, -1, keepdims=True)
        exp_scores = jnp.exp(scores - row_peak)
        sum_exp = jnp.sum(exp_scores, -1, keepdims=True)
        probabilities = (exp_scores / sum_exp).astype(jnp.bfloat16)
        attended = jnp.einsum("qk,kd->qd", probabilities, v_one, preferred_element_type=jnp.float32)
        return (attended.astype(jnp.bfloat16), row_peak + jnp.log(sum_exp))

    attended, log_total = lax.map(
        single, (flat_heads(queries), flat_heads(keys), flat_heads(values))
    )
    return (attended.reshape(queries.shape), log_total)


def attend_back(queries, keys, values, log_total, grad_out):
    root_dim = math.sqrt(queries.shape[-1])

    def single(bundle):
        q_one, k_one, v_one, lse_one, g_one = bundle
        scores = (
            jnp.einsum("qd,kd->qk", q_one, k_one, preferred_element_type=jnp.float32) / root_dim
        )
        probabilities = jnp.exp(scores - lse_one)
        grad_v = jnp.einsum(
            "qk,qd->kd",
            probabilities.astype(jnp.bfloat16),
            g_one,
            preferred_element_type=jnp.float32,
        )
        grad_p = jnp.einsum("qd,kd->qk", g_one, v_one, preferred_element_type=jnp.float32)
        inner_sum = jnp.sum(probabilities * grad_p, -1, keepdims=True)
        grad_s = (probabilities * (grad_p - inner_sum)).astype(jnp.bfloat16)
        grad_q = (
            jnp.einsum("qk,kd->qd", grad_s, k_one, preferred_element_type=jnp.float32) / root_dim
        )
        grad_k = (
            jnp.einsum("qk,qd->kd", grad_s, q_one, preferred_element_type=jnp.float32) / root_dim
        )
        return (grad_q, grad_k, grad_v)

    grad_q, grad_k, grad_v = lax.map(
        single,
        (
            flat_heads(queries),
            flat_heads(keys),
            flat_heads(values),
            log_total,
            flat_heads(grad_out),
        ),
    )
    return (grad_q.reshape(queries.shape), grad_k.reshape(keys.shape), grad_v.reshape(values.shape))


def local(
    images,
    target,
    clean_images,
    levels,
    labels,
    null_mask,
    vgg_proj,
    lpips_lin,
    master,
    first_moment,
    second_moment,
):
    gathered = lax.all_gather(master.astype(jnp.bfloat16), ("batch", "pix"), axis=0, tiled=True)
    pieces, used_len = unpack(gathered)
    w_one, w_two, w_qkv, w_proj, w_down, w_emb, class_table, gains_low = pieces
    gains_one = gains_low.astype(jnp.float32)
    n_img, rows_local, cols_local, channels = images.shape
    wide_channels = w_down.shape[1]
    pix_count = lax.axis_size("pix")
    batch_count = lax.axis_size("batch")
    pixels_here = rows_local * cols_local
    pixels_all = pixels_here * pix_count
    pixels_all_two = pixels_all // 4
    images_all = n_img * batch_count
    row_index = jnp.where(null_mask == 1, class_table.shape[0] - 1, labels)
    one_hot = (
        row_index[:, None] == jnp.arange(class_table.shape[0], dtype=jnp.int32)[None, :]
    ).astype(jnp.float32)
    pre_embed = time_vector(levels) + jnp.dot(
        one_hot, class_table.astype(jnp.float32), precision=precise
    )
    embedded = jax.nn.silu(pre_embed)
    w_emb_wide = w_emb.astype(jnp.float32)
    scale_shift = jnp.dot(embedded, w_emb_wide, precision=precise)
    scale_one = scale_shift[:, None, :channels]
    shift_one = scale_shift[:, None, channels:]
    flat_in = images.astype(jnp.float32).reshape(n_img, pixels_here, channels)
    middle, kept_one = res_forward(
        flat_in, gains_one, scale_one, shift_one, w_one, w_two, rows_local, pixels_all
    )
    normed_three, inverse_three = group_forward(middle, pixels_all)
    attn_in = (normed_three * gains_one[4] + gains_one[5]).astype(jnp.bfloat16)
    triples = jnp.dot(attn_in.reshape(-1, channels), w_qkv, preferred_element_type=jnp.float32)
    triples = triples.astype(jnp.bfloat16).reshape(n_img, pixels_here, 3 * channels)
    spread_heads = to_heads(triples)
    local_heads = spread_heads.shape[2] // (3 * HEAD)
    split_heads = spread_heads.reshape(n_img, -1, local_heads, 3, HEAD).transpose(3, 0, 2, 1, 4)
    queries, keys, values = (split_heads[0], split_heads[1], split_heads[2])
    attended, log_total = attend(queries, keys, values)
    attended_px = to_pixels(attended.transpose(0, 2, 1, 3).reshape(n_img, -1, local_heads * HEAD))
    projected = jnp.dot(
        attended_px.reshape(-1, channels), w_proj, preferred_element_type=jnp.float32
    )
    output = middle + projected.reshape(n_img, pixels_here, channels)
    final_out, columns_down = conv_forward(output.astype(jnp.bfloat16), w_down, rows_local, 2)
    pixels_two = final_out.shape[1]
    feat_width = vgg_proj.shape[1]
    online_feat = jnp.dot(
        final_out.astype(jnp.bfloat16).reshape(-1, wide_channels),
        vgg_proj,
        preferred_element_type=jnp.float32,
    )
    online_feat = online_feat.reshape(n_img, pixels_two, feat_width)
    target_feat = jnp.dot(
        target.reshape(-1, wide_channels), vgg_proj, preferred_element_type=jnp.float32
    )
    target_feat = target_feat.reshape(n_img, pixels_two, feat_width)
    target_unit = target_feat * lax.rsqrt(
        jnp.mean(target_feat * target_feat, -1, keepdims=True) + EPS_FEAT
    )
    clean_wide = clean_images.astype(jnp.float32).reshape(n_img, pixels_two, wide_channels)

    def loss_terms(feature, out_value):
        unit = feature * lax.rsqrt(jnp.mean(feature * feature, -1, keepdims=True) + EPS_FEAT)
        consist = jnp.sum(lpips_lin * (unit - target_unit) ** 2, (1, 2)) / (
            feat_width * pixels_all_two
        )
        denoise = jnp.sum((out_value - clean_wide) ** 2, (1, 2)) / (pixels_all_two * wide_channels)
        return (consist, denoise)

    (consist, denoise), pullback = jax.vjp(loss_terms, online_feat, final_out)
    level_hot = (levels[:, None] == jnp.arange(LEVELS, dtype=jnp.int32)[None, :]).astype(
        jnp.float32
    )
    level_pair = lax.psum(
        (jnp.sum(consist[:, None] * level_hot, 0), jnp.sum(level_hot / pix_count, 0)),
        ("batch", "pix"),
    )
    zero_count = level_pair[1][0]
    is_zero = (levels == 0).astype(jnp.float32)
    grad_feat, grad_out = pullback(
        (jnp.full_like(consist, 1.0 / images_all), is_zero / jnp.maximum(zero_count, 1.0))
    )
    grad_feat_low = grad_feat.astype(jnp.bfloat16).reshape(-1, feat_width)
    grad_final = grad_out + jnp.einsum(
        "rf,cf->rc", grad_feat_low, vgg_proj, preferred_element_type=jnp.float32
    ).reshape(n_img, pixels_two, wide_channels)
    d_w_down, grad_output = conv_back(
        columns_down, grad_final.astype(jnp.bfloat16), w_down, rows_local, 2
    )
    grad_proj = grad_output.astype(jnp.bfloat16).reshape(-1, channels)
    d_w_proj = jnp.einsum(
        "rc,rd->cd",
        attended_px.reshape(-1, channels),
        grad_proj,
        preferred_element_type=jnp.float32,
    )
    grad_att_px = jnp.einsum("rd,cd->rc", grad_proj, w_proj, preferred_element_type=jnp.float32)
    grad_att_px = grad_att_px.astype(jnp.bfloat16).reshape(n_img, pixels_here, channels)
    grad_heads = to_heads(grad_att_px)
    grad_split = grad_heads.reshape(n_img, -1, local_heads, HEAD).transpose(0, 2, 1, 3)
    grad_q, grad_k, grad_v = attend_back(queries, keys, values, log_total, grad_split)
    grad_triples = jnp.stack([grad_q, grad_k, grad_v], 3).transpose(0, 2, 1, 3, 4)
    grad_triples = grad_triples.reshape(n_img, -1, local_heads * 3 * HEAD).astype(jnp.bfloat16)
    grad_triples = to_pixels(grad_triples)
    grad_rows = grad_triples.reshape(-1, 3 * channels)
    d_w_qkv = jnp.einsum(
        "rc,rd->cd", attn_in.reshape(-1, channels), grad_rows, preferred_element_type=jnp.float32
    )
    grad_attn_in = jnp.einsum(
        "rd,cd->rc", grad_rows, w_qkv, preferred_element_type=jnp.float32
    ).reshape(n_img, pixels_here, channels)
    d_gain_three = jnp.sum(grad_attn_in * normed_three, (0, 1))
    d_bias_three = jnp.sum(grad_attn_in, (0, 1))
    grad_middle = grad_output + group_backward(
        grad_attn_in * gains_one[4], normed_three, inverse_three, pixels_all
    )
    d_w_one, d_w_two, d_gains_one, d_scale_one, d_shift_one, unused_grad = res_back(
        grad_middle, kept_one, gains_one, scale_one, w_one, w_two, rows_local, pixels_all
    )
    grad_scale_shift = jnp.concatenate([d_scale_one, d_shift_one], 1)
    d_w_emb = jnp.dot(embedded.T, grad_scale_shift, precision=precise)
    grad_embedded = jnp.dot(grad_scale_shift, w_emb_wide.T, precision=precise)
    d_table = jnp.dot(one_hot.T, grad_embedded * silu_slope(pre_embed), precision=precise)
    d_norms_one = jnp.concatenate([d_gains_one, jnp.stack([d_gain_three, d_bias_three])], 0)
    flat_grad = jnp.concatenate(
        [
            d_w_one.ravel(),
            d_w_two.ravel(),
            d_w_qkv.ravel(),
            d_w_proj.ravel(),
            d_w_down.ravel(),
            d_w_emb.ravel(),
            d_table.ravel(),
            d_norms_one.ravel(),
            jnp.zeros((gathered.shape[0] - used_len,), jnp.float32),
        ]
    )
    own_grad = lax.psum_scatter(flat_grad, ("batch", "pix"), scatter_dimension=0, tiled=True)
    norm_before = jnp.sqrt(lax.psum(jnp.sum(own_grad * own_grad), ("batch", "pix")))
    clipped = own_grad * jnp.minimum(1.0, CLIP / norm_before)
    new_first = BETA_ONE * first_moment + (1.0 - BETA_ONE) * clipped
    new_second = BETA_TWO * second_moment + (1.0 - BETA_TWO) * clipped * clipped
    fixed_first = new_first / (1.0 - BETA_ONE**STEP)
    fixed_second = new_second / (1.0 - BETA_TWO**STEP)
    new_master = master - RATE * (
        fixed_first / (jnp.sqrt(fixed_second) + EPS_ADAM) + DECAY * master
    )
    level_sums = jnp.stack([level_pair[0], level_pair[1]])
    return (
        new_master,
        new_first,
        new_second,
        new_master.astype(jnp.bfloat16),
        norm_before,
        level_sums,
    )


MESH = pl.DeviceIdType.MESH
ROWS=537; BLK=560; HALF=288
PX=512
R_ONE,R_TWO,R_QKV,R_PROJ,R_DOWN,R_EMB,R_TAB,R_GAIN,R_END=0,3456,6912,8064,8448,13632,15168,17170,17184
f32=jnp.float32; bf=jnp.bfloat16
class Comm:
    def __init__(self): self.sent=[]
    def go(self, cond, src, dst, ssem, rsem, b, p):
        c = pltpu.make_async_remote_copy(src_ref=src,dst_ref=dst,send_sem=ssem,recv_sem=rsem,device_id=(b,p),device_id_type=MESH)
        if cond is None: c.start()
        else: pl.when(cond)(lambda: c.start())
        self.sent.append((cond,c))
    def drain(self):
        for cond,c in self.sent:
            if cond is None: c.wait_send()
            else: pl.when(cond)(lambda c=c: c.wait_send())
        self.sent=[]

def place():
    b=lax.axis_index("batch"); p=lax.axis_index("pix")
    core=lax.rem(b,2); y=lax.rem(lax.div(b,2),2); z=lax.div(b,4)
    return b,p,core,y,z

def base_of(s): return 16*((ROWS*s)//16)
def dg(a,b,ca,cb): return lax.dot_general(a,b,(((ca,),(cb,)),((),())),preferred_element_type=f32)
def nn(a,b): return dg(a,b,1,0)
def nt(a,b): return dg(a,b,1,1)
def tn(a,b): return dg(a,b,0,0)
def split3(v):
    hi=v.astype(bf); r=v-hi.astype(f32); mid=r.astype(bf); lo=(r-mid.astype(f32)).astype(bf)
    return hi,mid,lo
def exact(v,w,dot):
    hi,mid,lo=split3(v)
    return dot(hi,w)+dot(mid,w)+dot(lo,w)
def sigmoid(v): return 1.0/(1.0+jnp.exp(-v))
def silu(v): return v*sigmoid(v)
def slope(v):
    s=sigmoid(v)
    return s*(1.0+v*(1.0-s))
def cloop(n,chunk,body,init):
    return lax.fori_loop(0,n//chunk,lambda i,c: body(pl.multiple_of(i*chunk,chunk),c),init)
def col8(v): return jnp.sum(v.reshape(-1,8,v.shape[-1]),axis=0)
Z8=lambda: jnp.zeros((8,CH),f32)
class Blocks:
    def __init__(self,ref,n): self.ref=ref; self.n=n
def at_block(ref,j,sl):
    if isinstance(ref,Blocks): return ref.ref,(pl.ds(ref.n*j+sl.start,sl.size,stride=sl.stride),slice(None))
    return ref,(j,sl,slice(None))
def ld(ref,sl):
    out=[]
    for j in range(ref.ref.shape[0]//ref.n if isinstance(ref,Blocks) else ref.shape[0]):
        r,k=at_block(ref,j,sl)
        out.append(r[k])
    return jnp.concatenate(out,1)
def put3(ref,sl,v):
    for j in range(v.shape[1]//128):
        r,k=at_block(ref,j,sl)
        r[k]=v[:,128*j:128*j+128]
def every(start,n,step): return pl.ds(start,n,stride=step)
def row(v): return jnp.sum(v,axis=0,keepdims=True)


LAST=25
def step_kernel(images_all,
    mast,img,tgt,cln,vgg,lin,tvec,rowid,level,
    flat_ref,norm_ref,lev_ref,g_ref,
    wv,tails,cvt,cvt2,wd,wee,weo,wqT,x3a,x3b,z3,inner,middle,gout,gsec,ain,trT,dtrT,attT,xd,lse,dattT,ssend,srecv,hsend,hrecv,himg,dzs,dzr,geo,oth,wsem,tsem,xs,xr,total,blk,own_sem,azs,azr,axs,axr,ays,ayr,adar,adbr,ass,asr,pack_ref,lpk,ppk,red1,red2,tile,lps,lpr,pps,ppr,n1s,n1r,n2s,n2r,sibr,rb,rx,ry,zu,zd,s1s,s1r,dar,dbr,rxs,rxr,rys,ryr,zs,zur,zdr,acc,gtile,gls,glr,gps,gpr,rba,a2s,a2r,ads,ds_,hmid,esend,erecv,gm,a3s,a3r):
    b,p,core,y,z=place()
    q=1-p; xn=q; s=b*2+p
    pf=p.astype(f32); qf=1.0-pf
    yn=b+2-4*y; sib=b+1-2*core; oc=1-core
    up_ok=z<3; dn_ok=z>0
    top=z==3
    mine=(y*2+core)*2+p
    cvt3=Blocks(cvt,1536)
    mcopy=pltpu.make_async_copy(mast,cvt.at[pl.ds(0,1611)],own_sem)
    mcopy.start()
    barrier=pltpu.get_barrier_semaphore()
    plane=[]
    for dy in range(2):
        for dc in range(2):
            for dp in range(2):
                if dy+dc+dp: plane.append((4*dy+2*dc+dp,z*4+lax.rem(y+dy,2)*2+lax.rem(core+dc,2),lax.rem(p+dp,2)))
    line=[(k,lax.rem(z+k,4)) for k in range(1,4)]
    def sig(bb,pp): pl.semaphore_signal(barrier,inc=1,device_id=(bb,pp),device_id_type=MESH)
    for _,bb,pp in plane: sig(bb,pp)
    for _,zz in line: sig(b+4*(zz-z),p)
    def when(ok,f):
        if ok is None: f()
        else: pl.when(ok)(f)
    def AND(*c):
        r=None
        for k in c:
            if k is not None: r=k if r is None else r&k
        return r
    def wait_in(ref,sem):
        pltpu.make_async_remote_copy(src_ref=ref,dst_ref=ref,send_sem=sem,recv_sem=sem,device_id=(b,xn),device_id_type=MESH).wait_recv()
    def slot(zz,yy,pp,cc=core): return ((zz*2+yy)*2+cc)*2+pp
    A=pl.ds(0,HALF); B=pl.ds(HALF,BLK-HALF)
    cm=Comm()
    shift=lax.rem(9*s,16)
    total[ROWS-1:BLK]=jnp.zeros((BLK-ROWS+1,CH),f32)
    mcopy.wait()
    for j in range(3): total[0:ROWS,128*j:128*j+128]=cvt[pl.ds(j,ROWS,stride=3),:]
    at=lax.broadcasted_iota(jnp.int32,(BLK,CH),0)
    blk[...]=jnp.where(at==BLK-4,(level[...]==0).astype(f32),pltpu.roll(total[...],shift,0)).astype(bf)
    own=pltpu.make_async_copy(blk,g_ref.at[s],own_sem)
    own.start()
    pl.semaphore_wait(barrier,10)
    def valid(zz): return (zz>=0)&(zz<4)
    def pick(c0,c1,c2,c3): return jnp.where(z==0,c0,jnp.where(z==1,c1,jnp.where(z==2,c2,c3)))
    hs=(A,B)
    ends=(z==0)|(z==3); is1=z==1; is2=z==2; inner_z=jnp.logical_not(ends)
    def z_send(ok,zz,h,d,src=None):
        g=g_ref.at[slot(zz,y,p),hs[h]]
        cm.go(ok,g if src is None else src,g,azs.at[zz,(1-d)//2],azr.at[zz,h],b+4*d,p)
    def xy_send(ok,zz,h,src=None):
        g=g_ref.at[slot(zz,y,p),hs[h]]
        cm.go(ok,g if src is None else src,g,axs.at[zz],axr.at[zz,h],b,xn)
        cm.go(ok,g if src is None else src,g,ays.at[zz],ayr.at[zz,h],yn,p)
    def sib_send(ok,zz,yy,pp,h,src=None):
        g=g_ref.at[slot(zz,yy,pp),hs[h]]
        cm.go(ok,g if src is None else src,g,ass.at[zz],asr.at[zz],sib,p)
    def own_sends():
        for h in range(2):
            src=blk.at[hs[h]]
            z_send(z==0,z,h,1,src)
            z_send(z==3,z,h,-1,src)
            sib_send(None,z,y,p,h,src)
    def own_xy():
        for h in range(2): xy_send(z!=1,z,h,blk.at[hs[h]])
    four=((1-y,xn),(y,xn),(1-y,p),(y,p))
    def two_send(ok,i,d):
        yy,pp=four[i]
        for h in range(2):
            g=g_ref.at[slot(2,yy,pp),hs[h]]
            cm.go(ok,g,g,a2s.at[(1-d)//2],a2r.at[yy,pp,h],b+4*d,p)
    def two_in(i,ok):
        yy,pp=four[i]
        for h in range(2):
            g=g_ref.at[slot(2,yy,pp),hs[h]]
            when(ok,lambda: wait_in(g,a2r.at[yy,pp,h]))
            cm.go(ok&(z==1),g,g,a2s.at[1],a2r.at[yy,pp,h],b-4,p)
            sib_send(ok,2,yy,pp,h)
    def three_out(i):
        yy,pp=four[i]
        for h in range(2):
            g=g_ref.at[slot(3,yy,pp),hs[h]]
            cm.go(top,g,g,a3s,a3r.at[yy,pp,h],b-4,p)
    def three_in(i):
        yy,pp=four[i]
        for h in range(2):
            g=g_ref.at[slot(3,yy,pp),hs[h]]
            when(is2,lambda: wait_in(g,a3r.at[yy,pp,h]))
            sib_send(is2,3,yy,pp,h)
    def diag_in(ok,zz):
        sd=slot(zz,1-y,xn)
        def f():
            wait_in(g_ref.at[sd,A],adar.at[zz])
            wait_in(g_ref.at[sd,B],adbr.at[zz])
        when(ok,f)
        for h in range(2): sib_send(ok,zz,1-y,xn,h)
    def two_diag():
        sd=slot(2,1-y,xn)
        def f():
            wait_in(g_ref.at[sd,A],adar.at[2])
            wait_in(g_ref.at[sd,B],adbr.at[2])
        when(z==2,f)
        for h in range(2): sib_send(z==2,2,1-y,xn,h)
    def arrive0(h):
        ok=z!=0
        when(ok,lambda: wait_in(g_ref.at[slot(0,y,p),hs[h]],azr.at[0,h]))
        z_send(ok&up_ok,0,h,1)
        xy_send(ok,0,h)
        sib_send(ok,0,y,p,h)
    def arrive3(h,ok):
        when(ok,lambda: wait_in(g_ref.at[slot(3,y,p),hs[h]],azr.at[3,h]))
        z_send(ok&dn_ok,3,h,-1)
        sib_send(ok,3,y,p,h)
    def xy_arrive(ok,f,h):
        sx=slot(f,y,xn); sy=slot(f,1-y,p)
        when(ok,lambda: wait_in(g_ref.at[sx,hs[h]],axr.at[f,h]))
        if h==0: cm.go(ok,g_ref.at[sx,A],g_ref.at[sx,A],ads.at[f],adar.at[f],yn,p)
        sib_send(ok,f,y,xn,h)
        when(ok,lambda: wait_in(g_ref.at[sy,hs[h]],ayr.at[f,h]))
        if h==1: cm.go(ok,g_ref.at[sy,B],g_ref.at[sy,B],ads.at[f],adbr.at[f],b,xn)
        sib_send(ok,f,1-y,p,h)
    def later_sends():
        for h in range(2):
            src=blk.at[hs[h]]
            z_send(z==1,z,h,1,src)
            z_send(z==1,z,h,-1,src)
    def one_in(h,ok):
        when(ok,lambda: wait_in(g_ref.at[slot(1,y,p),hs[h]],azr.at[1,h]))
        z_send(ok&is2,1,h,1)
        sib_send(ok,1,y,p,h)
    def load(sl): return (pltpu.make_async_copy(g_ref.at[sl,pl.ds(0,528)],wv.at[pl.ds(pl.multiple_of(16*lax.div(ROWS*sl,16),16),528)],wsem.at[lax.div(sl,8)]),
                          pltpu.make_async_copy(g_ref.at[sl,pl.ds(528,32)],tails.at[sl],tsem.at[lax.div(sl,8)]))
    def d_arrive(zz):
        sd=slot(zz,1-y,xn)
        wait_in(g_ref.at[sd,A],adar.at[zz])
        sib_send(None,zz,1-y,xn,0)
        wait_in(g_ref.at[sd,B],adbr.at[zz])
        sib_send(None,zz,1-y,xn,1)
        for yy in range(2):
            for pp in range(2):
                for c in load(slot(zz,yy,pp)): c.start()
    def sib_arrive(zz):
        wait_in(g_ref.at[pl.ds(0,4)],asr.at[zz])
        for yy in range(2):
            for pp in range(2):
                sl=slot(zz,yy,pp,oc)
                for c in load(sl): c.start()
    has_gains=s==31
    gain_line=(y==1)&(core==1)&(p==1)
    def gain_sends():
        for k,zz in line: cm.go(has_gains,blk.at[pl.ds(528,16)],gtile,gls,glr,b+4*(zz-z),p)
    def gain_pass():
        pl.when(has_gains)(lambda: gtile.__setitem__(Ellipsis,blk[528:544]))
        pl.when(gain_line&jnp.logical_not(has_gains))(lambda: wait_in(gtile,glr))
        for d,bb,pp in plane: cm.go(gain_line,gtile,gtile,gps,gpr,bb,pp)
    def gain_wait():
        pl.when(jnp.logical_not(gain_line))(lambda: wait_in(gtile,gpr))
    seen=[]
    def take(shards):
        pltpu.make_async_copy(wv.at[pl.ds(0,8*528)],wv.at[pl.ds(0,8*528)],wsem.at[shards[0]//8]).wait()
        pltpu.make_async_copy(tails.at[pl.ds(0,8)],tails.at[pl.ds(0,8)],tsem.at[shards[0]//8]).wait()
        for k in shards:
            lo=base_of(k)
            if k<31 and base_of(k+1)-lo==544 or k==31: wv[lo+528:lo+544]=tails[k,0:16]
            seen.append(k)
        for k in range(1,32):
            if k in seen and k-1 in seen and (k in shards or k-1 in shards):
                off=base_of(k)-base_of(k-1)-528
                t=tails[k-1,off:off+16].astype(f32)
                if off: t=jnp.where(lax.broadcasted_iota(jnp.int32,(16,CH),0)<8,t,0.0)
                lo=base_of(k)
                wv[lo:lo+16]=(wv[lo:lo+16].astype(f32)+t).astype(bf)
    def rows(u,yy,pp,cc=core):
        at=pl.ds(pl.multiple_of(16*lax.div(ROWS*slot(u,yy,pp,cc),16),16),BLK)
        return wd.at[at,pl.ds(0,CH)] if u==0 else wv.at[at]
    def need(u,yy,pp,cc=core): return None if u<3 else slot(u,yy,pp,cc)<=LAST
    def sibsend(u):
        for yy,pp in four:
            cm.go(need(u,yy,pp,oc),rows(u,yy,pp,oc),sibr.at[4*u+2*yy+pp],s1s.at[u],s1r.at[u,yy,pp],sib,p)
    def both(u,yy,pp,lo,n):
        a=pl.multiple_of(16*lax.div(ROWS*slot(u,yy,pp),16)+lo,16)
        mine_=wd[pl.ds(a,n),0:CH] if u==0 else wv[pl.ds(a,n)]
        return mine_.astype(f32)+sibr[4*u+2*yy+pp,lo:lo+n].astype(f32)
    HA=(0,HALF); HB=(HALF,BLK-HALF)
    def sib_in(u,yy,pp): wait_in(sibr.at[4*u+2*yy+pp],s1r.at[u,yy,pp])
    def keep(u,yy,pp,half,more=None):
        t=both(u,yy,pp,*half)
        if more is not None: t=t+more.astype(f32)
        sibr[4*u+2*yy+pp,half[0]:half[0]+half[1]]=t.astype(bf)
    def diag(u):
        yy,pp=1-y,xn
        c=need(u,yy,pp)
        def f():
            sib_in(u,yy,pp)
            keep(u,yy,pp,HA); keep(u,yy,pp,HB)
        when(c,f)
        src=sibr.at[4*u+2*yy+pp]
        if u<2: cm.go(c,src.at[A],rba.at[u],ds_.at[u],dar.at[u],b,xn)
        else: cm.go(c,src.at[A],rba.at[u],ds_.at[u],dar.at[u],yn,p)
        cm.go(c,src.at[B],rb.at[u],ds_.at[u],dbr.at[u],yn,p)
    def ysend(u):
        c=need(u,1-y,p)
        def f():
            sib_in(u,1-y,p)
            keep(u,1-y,p,HA); keep(u,1-y,p,HB)
        when(c,f)
        for h in range(2): cm.go(c,sibr.at[4*u+2*(1-y)+p,hs[h]],ry.at[u,hs[h]],rys.at[u],ryr.at[u,h],yn,p)
    def xsend(u,only=None):
        c=AND(need(u,y,xn),only)
        def f():
            sib_in(u,y,xn)
            wait_in(rba.at[u],dar.at[u])
            keep(u,y,xn,HA,rba[u])
        when(c,f)
        cm.go(c,sibr.at[4*u+2*y+xn,A],rx.at[u,A],rxs.at[u],rxr.at[u,0],b,xn)
        def f2():
            wait_in(rb.at[u],dbr.at[u])
            keep(u,y,xn,HB,rb[u])
        when(c,f2)
        cm.go(c,sibr.at[4*u+2*y+xn,B],rx.at[u,B],rxs.at[u],rxr.at[u,1],b,xn)
    def put_x(u,half,h,more=None):
        keep(u,y,xn,half,more)
        cm.go(None,sibr.at[4*u+2*y+xn,hs[h]],rx.at[u,hs[h]],rxs.at[u],rxr.at[u,h],b,xn)
    def put_y(u,half,h,more=None):
        keep(u,1-y,p,half,more)
        cm.go(None,sibr.at[4*u+2*(1-y)+p,hs[h]],ry.at[u,hs[h]],rys.at[u],ryr.at[u,h],yn,p)
    def first_halves(u):
        sib_in(u,y,xn)
        put_x(u,HA,0)
        sib_in(u,1-y,p)
        if u>0: put_y(u,HB,1)
    def second_halves(u):
        wait_in(rba.at[u],dar.at[u])
        put_y(u,HA,0,rba[u])
        if u==0: put_y(u,HB,1)
        wait_in(rb.at[u],dbr.at[u])
        put_x(u,HB,1,rb[u])
    def chunks(u): return ((0,80,0),(80,80,0),(160,64,0),(224,64,0),(288,80,1),(368,64,1),(432,64,1),(496,64,1)) if u==0 else ((0,HALF,0),(HALF,BLK-HALF,1))
    def zur_at(u,k): return zur.at[2*(u-1)+k]
    def zdr_at(u,k): return zdr.at[k if u==0 else 8+2*(u-1)+k]
    def xy_in(u,h):
        wait_in(rx.at[u,hs[h]],rxr.at[u,h])
        wait_in(ry.at[u,hs[h]],ryr.at[u,h])
    def zstep(u,i):
        for d in (1,-1):
            at_z=i if d==1 else 3-i
            if not (at_z<u if d==1 else at_z>u): continue
            c=AND(need(u,y,p),z==at_z)
            buf,bsem=(zu.at[u-1],zur_at) if d==1 else (zd.at[u],zdr_at)
            own_at=4*u+2*y+p
            def first(): sib_in(u,y,p)
            when(c,first)
            seen_h=set()
            for k,(lo,n,h) in enumerate(chunks(u)):
                def f():
                    if h not in seen_h: xy_in(u,h)
                    t=both(u,y,p,lo,n)+rx[u,lo:lo+n].astype(f32)+ry[u,lo:lo+n].astype(f32)
                    if i>0:
                        wait_in(buf.at[pl.ds(lo,n)],bsem(u,k))
                        t=t+buf[lo:lo+n].astype(f32)
                    sibr[own_at,lo:lo+n]=t.astype(bf)
                when(c,f)
                seen_h.add(h)
                cm.go(c,sibr.at[own_at,pl.ds(lo,n)],buf.at[pl.ds(lo,n)],zs.at[u],bsem(u,k),b+4*d,p)
    def zend(u):
        def f():
            sib_in(u,y,p)
            done=set()
            for k,(lo,n,h) in enumerate(chunks(u)):
                if h not in done: xy_in(u,h); done.add(h)
                t=both(u,y,p,lo,n)+rx[u,lo:lo+n].astype(f32)+ry[u,lo:lo+n].astype(f32)
                if u>0:
                    wait_in(zu.at[u-1,pl.ds(lo,n)],zur_at(u,k))
                    t=t+zu[u-1,lo:lo+n].astype(f32)
                if u<3:
                    wait_in(zd.at[u,pl.ds(lo,n)],zdr_at(u,k))
                    t=t+zd[u,lo:lo+n].astype(f32)
                if u==3:
                    rr=16*lax.div(ROWS*s,16)+lo+lax.broadcasted_iota(jnp.int32,(n,CH),0)
                    t=jnp.where(rr<R_EMB,t,total[lo:lo+n])
                total[lo:lo+n]=t
        when(AND(need(u,y,p),z==u),f)
    state={"k":0}
    def xchg(src,dst,dst_like=None):
        k=state["k"]; state["k"]=k+1
        c=pltpu.make_async_remote_copy(src_ref=src,dst_ref=dst,send_sem=xs.at[k],recv_sem=xr.at[k],device_id=(b,q),device_id_type=MESH)
        c.start()
        return c
    edge=pl.ds(pl.multiple_of(q*480,32),32)
    gain_sends()
    c_img=xchg(img.at[edge],himg)
    def gsum(v): return exact(v,gm[...],nn)
    def swap_sums(k,s1,s2):
        ssend[k]=jnp.concatenate([s1,s2,jnp.zeros((6,CH),f32)],0)
        return xchg(ssend.at[k],srecv.at[k])
    def total_sums(k):
        t=gsum(ssend[k]+srecv[k])*(1.0/(12*2*PX))
        return t[0:1],t[1:2]
    def norm_of(t):
        mean,sq=t
        return mean,lax.rsqrt(sq-mean*mean+EPS_NORM)
    def fill3(dst,at,a):
        col=lax.broadcasted_iota(jnp.int32,a.shape,0)&31
        n=a.shape[0]
        dst[pl.ds(at,n),CH:2*CH]=a.astype(bf)
        dst[pl.ds(at,n),0:CH]=jnp.where(col==0,0.0,pltpu.roll(a,1,0)).astype(bf)
        dst[pl.ds(at,n),2*CH:3*CH]=jnp.where(col==31,0.0,pltpu.roll(a,n-1,0)).astype(bf)
    def fill_edges(dst,h):
        fill3(dst,0,h*pf); fill3(dst,544,h*qf)
    def conv_to(dst,x3,wrow,add=None):
        for dr in range(3):
            d=nn(x3[32*dr:32*dr+PX],wv[wrow+1152*dr:wrow+1152*dr+1152])
            if dr==0: dst[...]=d if add is None else add()+d
            else: dst[...]+=d
    def conv_dx(dst,wrow):
        first=True
        for dr in range(3):
            for dc in range(3):
                d=nt(z3[32*(2-dr):32*(2-dr)+PX,CH*(2-dc):CH*(2-dc)+CH],wv[wrow+CH*(3*dr+dc):wrow+CH*(3*dr+dc)+CH])
                if first: dst[...]=d
                else: dst[...]+=d
                first=False
    def st(i,c):
        v=img[pl.ds(i,64)].astype(f32)
        return c[0]+col8(v),c[1]+col8(v*v)
    a1,a2=cloop(PX,64,st,(Z8(),Z8()))
    c=swap_sums(0,row(a1),row(a2))
    own_sends()
    gain_pass()
    own_xy()
    group_of=lambda d: lax.shift_right_logical(lax.broadcasted_iota(jnp.int32,(CH,CH),d)*43691,19)
    gm[...]=(group_of(0)==group_of(1)).astype(f32).astype(bf)
    gain_wait()
    g6=gtile[...].astype(f32)
    g1,b1,g2,b2,g3,b3=[g6[2+i:3+i] for i in range(6)]
    c.wait()
    mean1,inv1=norm_of(total_sums(0))
    def act_of(v): return silu((v-mean1)*inv1*g1+b1)
    arrive3(0,is2)
    arrive3(1,is2)
    def fa(i,_):
        fill3(x3a,pl.multiple_of(i+32,32),act_of(img[pl.ds(i,64)].astype(f32)))
        return 0
    cloop(PX,64,fa,0)
    c_img.wait()
    fill_edges(x3a,act_of(himg[...].astype(f32)))
    own.wait()
    xy_arrive(z==3,3,0)
    xy_arrive(z==3,3,1)
    arrive0(0)
    xy_arrive(is2,2,0)
    three_out(1); three_out(2)
    arrive0(1)
    diag_in(top,3)
    three_out(0)
    xy_arrive(is2,2,1)
    arrive3(0,is1)
    arrive3(1,is1)
    later_sends()
    two_send(is2,3,-1)
    two_send(is2,1,-1); two_send(is2,2,-1)
    xy_arrive(None,0,0)
    one_in(0,is2)
    one_in(1,is2)
    xy_arrive(None,0,1)
    for h in range(2): xy_send(is1,3,h)
    for h in range(2): xy_send(is2,1,h)
    for h in range(2): one_in(h,top)
    for h in range(2): xy_send(top,1,h)
    for i in (3,1,2): two_send(is2,i,1)
    two_diag()
    two_send(is2,0,-1); two_send(is2,0,1)
    d_arrive(0)
    arrive3(0,z==0)
    xy_send(z==0,3,0)
    sib_arrive(0)
    take(range(0,8))
    conv_to(inner,x3a,R_ONE)
    def st2(i,c):
        v=inner[pl.ds(i,64)]
        return c[0]+col8(v),c[1]+col8(v*v)
    a1,a2=cloop(PX,64,st2,(Z8(),Z8()))
    c1=swap_sums(1,row(a1),row(a2))
    c2=xchg(inner.at[edge],hrecv.at[0])
    two_in(3,is1)
    xy_arrive(z>=2,1,0)
    arrive3(1,z==0)
    xy_send(z==0,3,1)
    xy_arrive(z<2,3,0)
    xy_arrive(z<2,3,1)
    for h in range(2): one_in(h,z==0)
    for h in range(2): xy_send(z<2,1,h)
    three_in(1); three_in(2)
    xy_arrive(z>=2,1,1)
    three_in(0)
    diag_in(z<2,3)
    for yy in range(2):
        for pp in range(2):
            for k in load(slot(3,yy,pp)): k.start()
    sib_arrive(3)
    two_in(1,is1)
    take(range(24,32))
    ids=rowid[...]
    pre=[]
    tcol=lax.broadcasted_iota(jnp.int32,(16,R_END-R_TAB),1)
    for h in range(2):
        hot=(tcol==2*ids+h).astype(f32).astype(bf)
        pre.append(nn(hot,wv[R_TAB:R_END])[0:1]+tvec[:,CH*h:CH*h+CH])
    emb=[silu(v) for v in pre]
    put3(cvt3,pl.ds(0,1536),wv[R_EMB:R_TAB].astype(f32))
    wee[...]=ld(cvt3,every(0,768,2)).astype(bf)
    weo[...]=ld(cvt3,every(1,768,2)).astype(bf)
    def emb_dot(w):
        r=None
        for h in range(2):
            e=jnp.broadcast_to(emb[h],(16,CH))
            d=exact(e,w[CH*h:CH*h+CH],nn)[0:1]
            r=d if r is None else r+d
        return r
    sc1=1.0+emb_dot(wee); sh=emb_dot(weo)
    c1.wait()
    xy_arrive(z<2,1,0)
    mean2,inv2=norm_of(total_sums(1))
    def pre_b(v):
        n=(v-mean2)*inv2
        af=n*g2+b2
        return n,af,af*sc1+sh
    def fb(i,_):
        fill3(x3b,pl.multiple_of(i+32,32),silu(pre_b(inner[pl.ds(i,64)])[2]))
        return 0
    cloop(PX,64,fb,0)
    c2.wait()
    fill_edges(x3b,silu(pre_b(hrecv[0])[2]))
    xy_arrive(z<2,1,1)
    two_in(2,is1)
    d_arrive(1)
    sib_arrive(1)
    two_in(0,is1)
    take(range(8,16))
    conv_to(middle,x3b,R_TWO,lambda: img[...].astype(f32))
    def st3(i,c):
        v=middle[pl.ds(i,64)]
        return c[0]+col8(v),c[1]+col8(v*v)
    a1,a2=cloop(PX,64,st3,(Z8(),Z8()))
    c1=swap_sums(2,row(a1),row(a2))
    put3(cvt3,pl.ds(0,1152),wv[R_QKV:R_PROJ].astype(f32))
    for j in range(3):
        wqT[CH*j:CH*j+CH]=ld(cvt3,every(j,CH,3)).T.astype(bf)
    c1.wait()
    mean3,inv3=norm_of(total_sums(2))
    def fc(i,_):
        n=(middle[pl.ds(i,64)]-mean3)*inv3
        ain[pl.ds(i,64)]=(n*g3+b3).astype(bf)
        return 0
    cloop(PX,64,fc,0)
    c_in=xchg(ain.at[pl.ds(0,PX)],ain.at[pl.ds(PX,PX)])
    c_mid=xchg(middle.at[edge],hmid)
    def triples(a):
        t=nt(wqT[...],a)
        is_q=lax.rem(lax.broadcasted_iota(jnp.int32,t.shape,0),192)<64
        return jnp.where(is_q,t*0.125,t).astype(bf)
    trT[:,0:PX]=triples(ain[0:PX])
    def head_rows(h):
        r0=pl.multiple_of(h*192,64)
        return r0,pl.multiple_of(r0+64,64),pl.multiple_of(r0+128,64)
    def fh1(h,_):
        r0,r1,r2=head_rows(h)
        sco=nn(trT[pl.ds(r1,64),0:PX].T,trT[pl.ds(r0,64),0:PX])
        m=jnp.max(sco,0,keepdims=True)
        e=jnp.exp(sco-m)
        lse[h,0:1]=m
        lse[h,1:2]=jnp.sum(e,0,keepdims=True)
        acc[h]=nn(trT[pl.ds(r2,64),0:PX],e.astype(bf))
        return 0
    lax.fori_loop(0,6,fh1,0)
    for i in (3,1,2): two_in(i,ends)
    c_in.wait()
    trT[:,PX:2*PX]=triples(ain[PX:2*PX])
    def fh(h,_):
        r0,r1,r2=head_rows(h)
        sco=nn(trT[pl.ds(r1,64),PX:2*PX].T,trT[pl.ds(r0,64),0:PX])
        m0=lse[h,0:1]
        m=jnp.maximum(m0,jnp.max(sco,0,keepdims=True))
        e=jnp.exp(sco-m)
        a=jnp.exp(m0-m)
        l=lse[h,1:2]*a+jnp.sum(e,0,keepdims=True)
        o=acc[h]*a+nn(trT[pl.ds(r2,64),PX:2*PX],e.astype(bf))
        attT[pl.ds(pl.multiple_of(h*64,64),64),:]=(o*(1.0/l)).astype(bf)
        lse[h,0:1]=m+jnp.log(l)
        return 0
    lax.fori_loop(0,6,fh,0)
    put3(gout,pl.ds(0,PX),middle[...]+tn(attT[...],wv[R_PROJ:R_DOWN]))
    hsend[0]=ld(gout,edge).astype(bf)
    c1=xchg(hsend.at[0],oth.at[0])
    two_in(0,ends)
    for yy in range(2):
        for pp in range(2):
            for k in load(slot(2,yy,pp)): k.start()
    sib_arrive(2)
    take(range(16,24))
    for off in range(9):
        put3(cvt3,pl.ds(0,576),wv[R_DOWN+576*off:R_DOWN+576*off+576].astype(f32))
        v0,v1,v2=[ld(cvt3,every(i,192,3)) for i in range(3)]
        put3(cvt2,every(0,192,2),jnp.concatenate([v0,v1[:,0:256]],1))
        w=jnp.concatenate([v1[:,128:384],v2],1)
        w=pltpu.roll(w,w.shape[1]-64,1)
        put3(cvt2,every(1,192,2),w)
        wd[CH*off:CH*off+CH]=ld(cvt2,pl.ds(0,CH))[:,0:576].astype(bf)
    def parts(ref,n):
        e=ld(ref,every(0,n//2,2)); o=ld(ref,every(1,n//2,2))
        col=lax.broadcasted_iota(jnp.int32,o.shape,0)&15
        return jnp.where(col==0,0.0,pltpu.roll(o,1,0)).astype(bf),e.astype(bf),o.astype(bf)
    for dc,v in enumerate(parts(gout,PX)):
        v=v.reshape(8,32,CH)
        even=v[:,0:16].reshape(128,CH); odd=v[:,16:32].reshape(128,CH)
        xd[:,CH*(3+dc):CH*(3+dc)+CH]=even
        xd[:,CH*(6+dc):CH*(6+dc)+CH]=odd
        xd[16:128,CH*dc:CH*dc+CH]=odd[0:112]
    c1.wait()
    put3(geo,pl.ds(0,32),oth[0].astype(f32)*pf)
    for dc,v in enumerate(parts(geo,32)):
        xd[0:16,CH*dc:CH*dc+CH]=v
    fin=nn(xd[...],wd[0:9*CH])
    feat=nn(fin.astype(bf),vgg[...]); tf=nn(tgt[...],vgg[...])
    ir=lax.rsqrt(jnp.mean(feat*feat,-1,keepdims=True)+EPS_FEAT)
    unit=feat*ir
    diff=unit-tf*lax.rsqrt(jnp.mean(tf*tf,-1,keepdims=True)+EPS_FEAT)
    wl=lin[...]*diff
    consist=jnp.sum(row(wl*diff),1,keepdims=True)*(1.0/(256*256))
    du=wl*(2.0/(256*256*images_all))
    dfeat=(ir*(du-unit*jnp.mean(du*unit,-1,keepdims=True))).astype(bf)
    zc=jnp.zeros((16,128),f32)
    for t_ in range(0,32,2): zc=zc+tails[t_,16:32,0:128].astype(f32)
    zc=zc[12:13,0:1]
    seed=(level[...]==0).astype(f32)/jnp.maximum(zc,1.0)*(2.0/(256*CH2))
    gfin=nt(dfeat,vgg[...])+seed*(fin-cln[...].astype(f32))
    dz=gfin.astype(bf)
    dzs[...]=dz[0:16]
    c1=xchg(dzs,dzr)
    for off in range(9):
        dw=tn(xd[:,CH*off:CH*off+CH],dz)
        put3(cvt2,pl.ds(0,CH),jnp.concatenate([dw,jnp.zeros((CH,64),f32)],1))
        e=ld(cvt2,every(0,192,2)); o_=pltpu.roll(ld(cvt2,every(1,192,2)),64,1)
        lane=lax.broadcasted_iota(jnp.int32,(192,128),1)
        put3(cvt3,every(0,192,3),e[:,0:384])
        put3(cvt3,every(1,192,3),jnp.concatenate([e[:,384:512],jnp.where(lane<64,e[:,512:640],o_[:,0:128]),o_[:,128:256]],1))
        put3(cvt3,every(2,192,3),o_[:,256:640])
        wv[R_DOWN+576*off:R_DOWN+576*off+576]=ld(cvt3,pl.ds(0,576)).astype(bf)
    sibsend(2); sibsend(3)
    c1.wait()
    z32=dz.astype(f32)
    down=jnp.concatenate([z32[16:128],dzr[...].astype(f32)*qf],0)
    def left(v):
        col=lax.broadcasted_iota(jnp.int32,v.shape,0)&15
        return jnp.where(col==15,0.0,pltpu.roll(v,127,0)).astype(bf)
    s00,s01,s10,s11=dz,left(z32),down.astype(bf),left(down)
    W=lambda a,c: wd[CH*(3*a+c):CH*(3*a+c)+CH]
    def put(a,c,v):
        for i in range(8):
            put3(gout,every((2*i+a)*32+c,16,2),v[16*i:16*i+16])
    put(0,0,nt(s00,W(1,1)))
    put(0,1,nt(s00,W(1,2))+nt(s01,W(1,0)))
    put(1,0,nt(s00,W(2,1))+nt(s10,W(0,1)))
    put(1,1,nt(s00,W(2,2))+nt(s01,W(2,0))+nt(s10,W(0,2))+nt(s11,W(0,0)))
    diag(2); diag(3); ysend(2); ysend(3)
    gp=ld(gout,pl.ds(0,PX)).astype(bf)
    dattT[...]=nt(wv[R_PROJ:R_DOWN],gp).astype(bf)
    wv[R_PROJ:R_DOWN]=nn(attT[...],gp).astype(bf)
    def bh_part(h,at):
        r0,r1,r2=head_rows(h)
        ra_=pl.ds(pl.multiple_of(h*64,64),64)
        qT=trT[pl.ds(r0,64),0:PX]
        kT=trT[pl.ds(r1,64),at:at+PX]
        gT=dattT[ra_,:]
        pr=jnp.exp(nn(kT.T,qT)-lse[h,0:1])
        de=jnp.sum(gT.astype(f32)*attT[ra_,:].astype(f32),0,keepdims=True)
        ds=(pr*(nn(trT[pl.ds(r2,64),at:at+PX].T,gT)-de)).astype(bf)
        dtrT[pl.ds(r1,64),at:at+PX]=nt(qT,ds).astype(bf)
        dtrT[pl.ds(r2,64),at:at+PX]=nt(gT,pr.astype(bf)).astype(bf)
        return r0,nn(kT,ds)*0.125
    def bh(h,_):
        r0,dqT=bh_part(h,PX)
        acc[h]=dqT
        dtrT[pl.ds(r0,64),PX:2*PX]=jnp.zeros((64,PX),bf)
        return 0
    lax.fori_loop(0,6,bh,0)
    oth[1:17]=tn(dtrT[:,PX:2*PX],wqT[...]).astype(bf).reshape(16,32,CH)
    c1=xchg(oth.at[pl.ds(1,16)],oth.at[pl.ds(17,16)])
    def bh2(h,_):
        r0,dqT=bh_part(h,0)
        dtrT[pl.ds(r0,64),0:PX]=(acc[h]+dqT).astype(bf)
        return 0
    lax.fori_loop(0,6,bh2,0)
    gsec[...]=tn(dtrT[:,0:PX],wqT[...])
    dq=nt(ain[...].T,dtrT[...])
    for j in range(3):
        put3(cvt3,every(j,CH,3),dq[:,CH*j:CH*j+CH])
    wv[R_QKV:R_PROJ]=ld(cvt3,pl.ds(0,1152)).astype(bf)
    c1.wait()
    def n3_of(i): return (middle[pl.ds(i,64)]-mean3)*inv3
    def s3(i,c):
        j=pl.multiple_of(17+lax.div(i,32),1)
        v=gsec[pl.ds(i,64)]+oth[pl.ds(j,2)].reshape(64,CH).astype(f32)
        gsec[pl.ds(i,64)]=v
        return c[0]+col8(v),c[1]+col8(v*n3_of(i))
    a1,a2=cloop(PX,64,s3,(Z8(),Z8()))
    db3,dg3=row(a1),row(a2)
    c1=swap_sums(3,db3*g3,dg3*g3)
    esend[0]=ld(gout,edge)+inv3*(gsec[edge]*g3)
    c2=xchg(esend.at[0],erecv.at[0])
    xsend(2)
    c1.wait()
    m1,m2=total_sums(3)
    def f3(i,_):
        v=ld(gout,pl.ds(i,64))+inv3*(gsec[pl.ds(i,64)]*g3-m1-n3_of(i)*m2)
        fill3(z3,pl.multiple_of(i+32,32),v)
        return 0
    cloop(PX,64,f3,0)
    c_mid.wait()
    c2.wait()
    fill_edges(z3,erecv[0]-inv3*(m1+(hmid[...]-mean3)*inv3*m2))
    conv_dx(gsec,R_TWO)
    for dr in range(3):
        d=tn(x3b[32*dr:32*dr+PX],z3[32:32+PX,CH:2*CH]).astype(bf)
        wv[R_TWO+1152*dr:R_TWO+1152*dr+1152]=d
        if dr==0: wd[R_TWO:4304,0:CH]=d[0:4304-R_TWO]
    sibsend(1)
    def s2(i,c):
        n,af,pb=pre_b(inner[pl.ds(i,64)])
        gpre=gsec[pl.ds(i,64)]*slope(pb)
        gaff=gpre*sc1
        gsec[pl.ds(i,64)]=gaff
        return c[0]+col8(gpre*af),c[1]+col8(gpre),c[2]+col8(gaff*n),c[3]+col8(gaff)
    a1,a2,a3,a4=cloop(PX,64,s2,(Z8(),Z8(),Z8(),Z8()))
    dsc,dsh,dg2,db2=row(a1),row(a2),row(a3),row(a4)
    c1=swap_sums(4,db2*g2,dg2*g2)
    esend[1]=gsec[edge]*g2
    c2=xchg(esend.at[1],erecv.at[1])
    diag(1)
    first_halves(1)
    c1.wait()
    m1,m2=total_sums(4)
    def f2(i,_):
        n=(inner[pl.ds(i,64)]-mean2)*inv2
        fill3(z3,pl.multiple_of(i+32,32),inv2*(gsec[pl.ds(i,64)]*g2-m1-n*m2))
        return 0
    cloop(PX,64,f2,0)
    c2.wait()
    fill_edges(z3,inv2*(erecv[1]-m1-(hrecv[0]-mean2)*inv2*m2))
    for dr in range(3):
        wd[1152*dr:1152*dr+1152,0:CH]=tn(x3a[32*dr:32*dr+PX],z3[32:32+PX,CH:2*CH]).astype(bf)
    sibsend(0)
    second_halves(1)
    xsend(3,z<2)
    zstep(2,0)
    conv_dx(gsec,R_ONE)
    diag(0)
    first_halves(0)
    def s1(i,c):
        n=(img[pl.ds(i,64)].astype(f32)-mean1)*inv1
        gpre=gsec[pl.ds(i,64)]*slope(n*g1+b1)
        return c[0]+col8(gpre*n),c[1]+col8(gpre)
    a1,a2=cloop(PX,64,s1,(Z8(),Z8()))
    ge=[]
    for h in range(2):
        d=exact(jnp.broadcast_to(dsc,(16,CH)),wee[CH*h:CH*h+CH],nt)+exact(jnp.broadcast_to(dsh,(16,CH)),weo[CH*h:CH*h+CH],nt)
        ge.append(d[0:1]*slope(pre[h]))
    hot_level=(lax.broadcasted_iota(jnp.int32,(1,CH),1)==level[...]).astype(f32)
    pack_ref[...]=jnp.concatenate([row(a1),row(a2),dg2,db2,dg3,db3,dsc,dsh,ge[0],ge[1],emb[0],emb[1],consist*hot_level,jnp.broadcast_to(ids.astype(f32),(1,CH)),0.5*hot_level,jnp.zeros((1,CH),f32)],0)
    low=jnp.logical_not(top)
    cm.go(low,pack_ref,lpk.at[z],lps,lpr,b+4*(3-z),p)
    zstep(1,0)
    zstep(3,0)
    second_halves(0)
    xsend(3,z>=2)
    zstep(2,1)
    zstep(1,1)
    zstep(0,0)
    zstep(3,1)
    zstep(0,1)
    zstep(3,2)
    def packs_line():
        lpk[3]=pack_ref[...]
        wait_in(lpk.at[pl.ds(0,3)],lpr)
    pl.when(top)(packs_line)
    for d,bb,pp in plane:
        cm.go(top,lpk,ppk.at[mine],pps,ppr,bb,pp)
    def packs_plane():
        ppk[mine]=lpk[...]
        wait_in(ppk.at[pl.ds(0,7)],ppr)
        a_s=16*lax.div(ROWS*s,16)
        rows_at=lambda k: ppk[:,:,k,:].reshape(32,384)
        zero=jnp.zeros((64,384),f32)
        for h in range(2):
            e=rows_at(10+h)
            t=jnp.concatenate([e,e,zero],0).T
            cvt[pl.ds(BLK+768*h,384,stride=2),:]=t
            cvt[pl.ds(BLK+768*h+1,384,stride=2),:]=t
        r=a_s+lax.broadcasted_iota(jnp.int32,(BLK,128),0)
        l=lax.broadcasted_iota(jnp.int32,(BLK,128),1)
        inside=(r>=R_EMB)&(r<R_TAB)
        start=pl.multiple_of(jnp.clip(a_s-R_EMB+BLK,0,BLK+1536),16)
        lf=jnp.where(inside&(((r&1)==1)==(l>=32))&(l<64),cvt[pl.ds(start,BLK),:],0.0)
        ids=rows_at(13)[:,0:128].astype(jnp.int32)
        ids=jnp.concatenate([ids]*4,0).astype(f32).T[0:1].astype(jnp.int32)
        hot=(r-R_TAB==2*ids+(l>=96).astype(jnp.int32))&(l>=64)&(r>=R_TAB)
        lf=jnp.where(hot,1.0,lf)
        rg=jnp.concatenate([rows_at(6),rows_at(7),rows_at(8),rows_at(9)],0)
        gains=[jnp.sum(rows_at(k),0,keepdims=True) for k in range(6)]
        hi=lax.Precision.HIGHEST
        add=lax.dot_general(lf,rg,(((1,),(0,)),((),())),precision=hi,preferred_element_type=f32)
        for k in range(6): add=add+jnp.where(r[:,0:1]-R_GAIN==k,gains[k],0.0)
        rr=a_s+lax.broadcasted_iota(jnp.int32,(BLK,384),0)
        total[...]=jnp.where(rr<R_EMB,0.0,add)
    pl.when(top)(packs_plane)
    zstep(0,2)
    zend(1); zend(2); zend(3)
    zend(0)
    shift=lax.rem(9*s,16)
    tr_=lax.broadcasted_iota(jnp.int32,(BLK,1),0)
    t=jnp.where((tr_>=shift)&(tr_<shift+ROWS),total[...],0.0)
    sq=jnp.sum(jnp.sum(t*t,0,keepdims=True),1,keepdims=True)
    tile[...]=jnp.concatenate([jnp.broadcast_to(sq,(1,128)),pack_ref[12:13,0:128],pack_ref[14:15,0:128],jnp.zeros((5,128),f32)],0)
    red1[mine]=tile[...]
    for d,bb,pp in plane: cm.go(None,tile,red1.at[mine],n1s,n1r,bb,pp)
    t=pltpu.roll(total[...],lax.rem(BLK-shift,BLK),0)[0:ROWS]
    for j in range(3): cvt[pl.ds(j,ROWS,stride=3),:]=t[:,128*j:128*j+128]
    fcopy=pltpu.make_async_copy(cvt.at[pl.ds(0,1611)],flat_ref,own_sem)
    fcopy.start()
    wait_in(red1.at[pl.ds(0,7)],n1r)
    v=red1[0]
    for k in range(1,8): v=v+red1[k]
    red2[z]=v
    for k,zz in line: cm.go(None,red2.at[z],red2.at[z],n2s,n2r,b+4*(zz-z),p)
    wait_in(red2.at[pl.ds(0,3)],n2r)
    sums=red2[0]+red2[1]+red2[2]+red2[3]
    norm_ref[...]=jnp.sqrt(sums[0:1,0:1])
    lev_ref[...]=sums[1:3,0:LEVELS]
    def sent(ok,ref,sem):
        when(ok,lambda: pltpu.make_async_copy(ref,ref,sem).wait())
    block=sibr.at[0]
    for zz in range(4):
        went=(None,None,is2,z!=2)[zz]
        for sem in (axs,ays,ads): sent(went,block,sem.at[zz])
        sent(None,sibr.at[pl.ds(0,4)],ass.at[zz])
        if zz<3:
            sent(None,sibr.at[pl.ds(0,4)],s1s.at[zz])
        else:
            sent(core==1,sibr.at[pl.ds(0,2)],s1s.at[zz])
        sent(need(zz,1-y,xn),block,ds_.at[zz])
        sent(need(zz,y,xn),block,rxs.at[zz])
        sent(need(zz,1-y,p),block,rys.at[zz])
        sent(AND(need(zz,y,p),z!=zz),block,zs.at[zz])
    sent(z<3,block,azs.at[0,0])
    sent(z>0,block,azs.at[3,1])
    sent(is1|is2,block,azs.at[1,0])
    sent(is1,block,azs.at[1,1])
    sent(is2,sibr.at[pl.ds(0,4)],a2s.at[0])
    sent(is1|is2,sibr.at[pl.ds(0,4)],a2s.at[1])
    sent(top,sibr.at[pl.ds(0,3)],a3s)
    sent(has_gains,blk.at[pl.ds(0,48)],gls)
    sent(gain_line,blk.at[pl.ds(0,112)],gps)
    sent(low,pack_ref,lps)
    sent(top,ppk.at[pl.ds(0,7)],pps)
    sent(None,red1.at[pl.ds(0,7)],n1s)
    sent(None,red2.at[pl.ds(0,3)],n2s)
    fcopy.wait()

def step(images_all,mast,img,tgt,cln,vgg,lin,tvec,rowid,level):
    D=pltpu.SemaphoreType.DMA
    V=lambda *s: pltpu.VMEM(s,bf)
    F=lambda *s: pltpu.VMEM(s,f32)
    vm=pl.BlockSpec(memory_space=pltpu.VMEM)
    return pl.pallas_call(functools.partial(step_kernel,images_all),
        out_shape=(jax.ShapeDtypeStruct((1611,128),f32),jax.ShapeDtypeStruct((1,1),f32),jax.ShapeDtypeStruct((2,LEVELS),f32),jax.ShapeDtypeStruct((32,BLK,CH),bf)),
        in_specs=[pl.BlockSpec(memory_space=pl.ANY)]+[vm]*8,
        out_specs=(pl.BlockSpec(memory_space=pl.ANY),vm,vm,pl.BlockSpec(memory_space=pl.ANY)),
        scratch_shapes=[V(17184,CH),V(32,32,CH),F(4608,128),F(5,CH,128),V(4304,CH2),V(768,CH),V(768,CH),V(1152,CH),V(576,1152),V(576,1152),V(576,1152),F(PX,CH),F(PX,CH),F(3,PX,128),F(PX,CH),V(1024,CH),V(1152,1024),V(1152,1024),V(CH,PX),V(128,3456),F(6,8,PX),V(CH,PX),F(5,8,CH),F(5,8,CH),V(1,32,CH),F(1,32,CH),V(32,CH),V(16,CH2),V(16,CH2),F(3,32,128),V(33,32,CH),D((4,)),D((4,)),D((15,)),D((15,)),F(BLK,CH),V(BLK,CH),D,D((4,2)),D((4,2)),D((4,)),D((4,2)),D((4,)),D((4,2)),D((4,)),D((4,)),D((4,)),D((4,)),F(16,CH),F(4,16,CH),F(8,4,16,CH),F(8,8,128),F(4,8,128),F(8,128),D,D,D,D,D,D,D,D,V(14,BLK,CH),V(4,BLK-HALF,CH),V(4,BLK,CH),V(4,BLK,CH),V(3,BLK,CH),V(3,BLK,CH),D((4,)),D((4,2,2)),D((4,)),D((4,)),D((4,)),D((4,2)),D((4,)),D((4,2)),D((4,)),D((6,)),D((12,)),F(6,64,PX),V(16,CH),D,D,D,D,V(4,HALF,CH),D((2,)),D((2,2,2)),D((4,)),D((4,)),F(32,CH),F(2,32,CH),F(2,32,CH),V(CH,CH),D,D((2,2,2))],
        compiler_params=pltpu.CompilerParams(collective_id=0,has_side_effects=True,vmem_limit_bytes=63<<20),
        name="train_step",
    )(mast,img,tgt,cln,vgg,lin,tvec,rowid,level)


def fast(images, target, clean_images, levels, labels, null_mask, vgg_proj, lpips_lin, master, first_moment, second_moment):
    row_index = jnp.where(null_mask == 1, CLASSES, labels).reshape(1, 1)
    tvec = time_vector(levels)
    own_grad, norm, level_sums, _ = step(
        16,
        master.reshape(1611, 128),
        images.reshape(PX, CH),
        target.reshape(128, CH2),
        clean_images.reshape(128, CH2),
        vgg_proj,
        lpips_lin.reshape(1, 256),
        tvec,
        row_index,
        levels.reshape(1, 1),
    )
    own_grad = own_grad.reshape(-1)
    norm_before = norm.reshape(())
    clipped = own_grad * jnp.minimum(1.0, CLIP / norm_before)
    new_first = BETA_ONE * first_moment + (1.0 - BETA_ONE) * clipped
    new_second = BETA_TWO * second_moment + (1.0 - BETA_TWO) * clipped * clipped
    fixed_first = new_first / (1.0 - BETA_ONE**STEP)
    fixed_second = new_second / (1.0 - BETA_TWO**STEP)
    new_master = master - RATE * (fixed_first / (jnp.sqrt(fixed_second) + EPS_ADAM) + DECAY * master)
    return (new_master, new_first, new_second, new_master.astype(jnp.bfloat16), norm_before, level_sums)


def solution(mesh):
    small = mesh.shape["batch"] == 16 and mesh.shape["pix"] == 2
    return jax.shard_map(
        fast if small else local,
        mesh=mesh,
        in_specs=(
            P("batch", "pix", None, None),
            P("batch", "pix", None, None),
            P("batch", "pix", None, None),
            P("batch"),
            P("batch"),
            P("batch"),
            P(),
            P(),
            P(("batch", "pix")),
            P(("batch", "pix")),
            P(("batch", "pix")),
        ),
        out_specs=(
            P(("batch", "pix")),
            P(("batch", "pix")),
            P(("batch", "pix")),
            P(("batch", "pix")),
            P(),
            P(),
        ),
        check_vma=False,
    )
```

```python
import functools
import math

import jax
import jax.numpy as jnp
from jax import lax
from jax.experimental import pallas as pl
from jax.experimental.pallas import tpu as pltpu
from jax.sharding import PartitionSpec as P

CH = 384
CH2 = 576
GROUPS = 32
HEAD = 64
TEMB = 768
CLASSES = 1000
LEVELS = 40
STEP = 10


EPS_NORM = 1e-05
EPS_FEAT = 1e-06
BETA_ONE = 0.9
BETA_TWO = 0.999
EPS_ADAM = 1e-08
RATE = 0.02
DECAY = 0.01
CLIP = 0.01
precise = lax.Precision.HIGHEST


def extended(shard, sides, width):
    for axis, dim in sides:
        size, length = (lax.axis_size(axis), shard.shape[dim])
        up = [(i, (i + 1) % size) for i in range(size - 1)]
        down = [(j, i) for i, j in up]
        last = lax.slice_in_dim(shard, length - width, length, axis=dim)
        initial = lax.slice_in_dim(shard, 0, width, axis=dim)
        before = lax.ppermute(last, axis, up)
        after = lax.ppermute(initial, axis, down)
        shard = jnp.concatenate([before, shard, after], axis=dim)
    return shard


def unpack(flat_vec):
    layout = [
        (9 * CH, CH),
        (9 * CH, CH),
        (CH, 3 * CH),
        (CH, CH),
        (9 * CH, CH2),
        (TEMB, 2 * CH),
        (CLASSES + 1, TEMB),
        (6, CH),
    ]
    pieces = []
    offset = 0
    for rows_n, cols_n in layout:
        pieces.append(flat_vec[offset : offset + rows_n * cols_n].reshape(rows_n, cols_n))
        offset += rows_n * cols_n
    return (pieces, offset)


def time_vector(level_ids):
    half_width = TEMB // 2
    frequency = jnp.exp(-math.log(10000.0) * jnp.arange(half_width, dtype=jnp.float32) / half_width)
    angles = level_ids.astype(jnp.float32)[..., None] * (1000.0 / LEVELS) * frequency
    return jnp.concatenate([jnp.cos(angles), jnp.sin(angles)], -1)


def silu_slope(values):
    sigmoid = jax.nn.sigmoid(values)
    return sigmoid * (1.0 + values * (1.0 - sigmoid))


def pix_sums(pair_sums):
    return lax.psum((pair_sums[0], pair_sums[1]), "pix")


def group_forward(values, pixels_all):
    grouped = values.reshape(values.shape[0], values.shape[1], GROUPS, -1)
    totals = pix_sums((jnp.sum(grouped, (1, 3)), jnp.sum(grouped * grouped, (1, 3))))
    per_group = pixels_all * grouped.shape[3]
    center = totals[0] / per_group
    spread = totals[1] / per_group - center * center
    inverse = lax.rsqrt(spread + EPS_NORM)
    normed = (grouped - center[:, None, :, None]) * inverse[:, None, :, None]
    return (normed.reshape(values.shape), inverse)


def group_backward(grad_normed, normed, inverse, pixels_all):
    grad_grouped = grad_normed.reshape(normed.shape[0], normed.shape[1], GROUPS, -1)
    val_grouped = normed.reshape(grad_grouped.shape)
    totals = pix_sums((jnp.sum(grad_grouped, (1, 3)), jnp.sum(grad_grouped * val_grouped, (1, 3))))
    per_group = pixels_all * grad_grouped.shape[3]
    result = (
        grad_grouped
        - (totals[0] / per_group)[:, None, :, None]
        - val_grouped * (totals[1] / per_group)[:, None, :, None]
    )
    return (result * inverse[:, None, :, None]).reshape(normed.shape)


def columns_of(values, stride):
    rows_out = values.shape[1] // stride
    cols_out = values.shape[2] // stride
    span_rows = stride * (rows_out - 1) + 1
    span_cols = stride * (cols_out - 1) + 1
    padded = extended(values, (("pix", 1),), 1)
    padded = jnp.pad(padded, ((0, 0), (0, 0), (1, 1), (0, 0)))
    return jnp.concatenate(
        [
            padded[
                :, row_off : row_off + span_rows : stride, col_off : col_off + span_cols : stride, :
            ]
            for row_off in range(3)
            for col_off in range(3)
        ],
        -1,
    )


def conv_forward(values, weight, rows_in, stride):
    n_img, pixels_in, in_chan = values.shape
    columns = columns_of(values.reshape(n_img, rows_in, -1, in_chan), stride)
    result = jnp.dot(columns.reshape(-1, 9 * in_chan), weight, preferred_element_type=jnp.float32)
    return (result.reshape(n_img, -1, weight.shape[1]), columns)


def conv_back(columns, grad_low, weight, rows_in, stride):
    n_img, pix_out, out_chan = grad_low.shape
    in_chan = weight.shape[0] // 9
    d_weight = jnp.einsum(
        "rk,rc->kc",
        columns.reshape(-1, 9 * in_chan),
        grad_low.reshape(-1, out_chan),
        preferred_element_type=jnp.float32,
    )
    flipped = (
        weight.reshape(3, 3, in_chan, out_chan)[::-1, ::-1]
        .transpose(0, 1, 3, 2)
        .reshape(9 * out_chan, in_chan)
    )
    rows_out = rows_in // stride
    grid_grad = grad_low.reshape(n_img, rows_out, pix_out // rows_out, out_chan)
    if stride > 1:
        grid_grad = jnp.pad(
            grid_grad[:, :, None, :, None, :],
            ((0, 0), (0, 0), (0, stride - 1), (0, 0), (0, stride - 1), (0, 0)),
        )
        grid_grad = grid_grad.reshape(n_img, rows_in, -1, out_chan)
    grad_columns = columns_of(grid_grad, 1)
    grad_input = jnp.dot(
        grad_columns.reshape(-1, 9 * out_chan), flipped, preferred_element_type=jnp.float32
    )
    return (d_weight, grad_input.reshape(n_img, -1, in_chan))


def res_forward(values, gain_rows, scale, shift, w_first, w_second, rows_in, pixels_all):
    normed_a, inverse_a = group_forward(values, pixels_all)
    pre_a = normed_a * gain_rows[0] + gain_rows[1]
    act_a = jax.nn.silu(pre_a).astype(jnp.bfloat16)
    inner, columns_a = conv_forward(act_a, w_first, rows_in, 1)
    normed_b, inverse_b = group_forward(inner, pixels_all)
    affine_b = normed_b * gain_rows[2] + gain_rows[3]
    pre_b = affine_b * (1.0 + scale) + shift
    second = jax.nn.silu(pre_b).astype(jnp.bfloat16)
    branch, columns_b = conv_forward(second, w_second, rows_in, 1)
    kept_state = (
        normed_a,
        inverse_a,
        pre_a,
        columns_a,
        normed_b,
        inverse_b,
        affine_b,
        pre_b,
        columns_b,
    )
    return (values + branch, kept_state)


def res_back(grad_result, kept_state, gain_rows, scale, w_first, w_second, rows_in, pixels_all):
    normed_a, inverse_a, pre_a, columns_a, normed_b, inverse_b, affine_b, pre_b, columns_b = (
        kept_state
    )
    d_w_second, grad_second = conv_back(
        columns_b, grad_result.astype(jnp.bfloat16), w_second, rows_in, 1
    )
    grad_pre_b = grad_second * silu_slope(pre_b)
    d_scale = jnp.sum(grad_pre_b * affine_b, 1)
    d_shift = jnp.sum(grad_pre_b, 1)
    grad_affine = grad_pre_b * (1.0 + scale)
    d_gain_b = jnp.sum(grad_affine * normed_b, (0, 1))
    d_bias_b = jnp.sum(grad_affine, (0, 1))
    grad_inner = group_backward(grad_affine * gain_rows[2], normed_b, inverse_b, pixels_all).astype(
        jnp.bfloat16
    )
    d_w_first, grad_act = conv_back(columns_a, grad_inner, w_first, rows_in, 1)
    grad_pre_a = grad_act * silu_slope(pre_a)
    d_gain_a = jnp.sum(grad_pre_a * normed_a, (0, 1))
    d_bias_a = jnp.sum(grad_pre_a, (0, 1))
    grad_values = None
    d_gains = jnp.stack([d_gain_a, d_bias_a, d_gain_b, d_bias_b])
    return (d_w_first, d_w_second, d_gains, d_scale, d_shift, grad_values)


def to_heads(values):
    return lax.all_to_all(values, "pix", split_axis=2, concat_axis=1, tiled=True)


def to_pixels(values):
    return lax.all_to_all(values, "pix", split_axis=1, concat_axis=2, tiled=True)


def flat_heads(values):
    return values.reshape(-1, values.shape[2], values.shape[3])


def attend(queries, keys, values):
    root_dim = math.sqrt(queries.shape[-1])

    def single(bundle):
        q_one, k_one, v_one = bundle
        scores = (
            jnp.einsum("qd,kd->qk", q_one, k_one, preferred_element_type=jnp.float32) / root_dim
        )
        row_peak = jnp.max(scores, -1, keepdims=True)
        exp_scores = jnp.exp(scores - row_peak)
        sum_exp = jnp.sum(exp_scores, -1, keepdims=True)
        probabilities = (exp_scores / sum_exp).astype(jnp.bfloat16)
        attended = jnp.einsum("qk,kd->qd", probabilities, v_one, preferred_element_type=jnp.float32)
        return (attended.astype(jnp.bfloat16), row_peak + jnp.log(sum_exp))

    attended, log_total = lax.map(
        single, (flat_heads(queries), flat_heads(keys), flat_heads(values))
    )
    return (attended.reshape(queries.shape), log_total)


def attend_back(queries, keys, values, log_total, grad_out):
    root_dim = math.sqrt(queries.shape[-1])

    def single(bundle):
        q_one, k_one, v_one, lse_one, g_one = bundle
        scores = (
            jnp.einsum("qd,kd->qk", q_one, k_one, preferred_element_type=jnp.float32) / root_dim
        )
        probabilities = jnp.exp(scores - lse_one)
        grad_v = jnp.einsum(
            "qk,qd->kd",
            probabilities.astype(jnp.bfloat16),
            g_one,
            preferred_element_type=jnp.float32,
        )
        grad_p = jnp.einsum("qd,kd->qk", g_one, v_one, preferred_element_type=jnp.float32)
        inner_sum = jnp.sum(probabilities * grad_p, -1, keepdims=True)
        grad_s = (probabilities * (grad_p - inner_sum)).astype(jnp.bfloat16)
        grad_q = (
            jnp.einsum("qk,kd->qd", grad_s, k_one, preferred_element_type=jnp.float32) / root_dim
        )
        grad_k = (
            jnp.einsum("qk,qd->kd", grad_s, q_one, preferred_element_type=jnp.float32) / root_dim
        )
        return (grad_q, grad_k, grad_v)

    grad_q, grad_k, grad_v = lax.map(
        single,
        (
            flat_heads(queries),
            flat_heads(keys),
            flat_heads(values),
            log_total,
            flat_heads(grad_out),
        ),
    )
    return (grad_q.reshape(queries.shape), grad_k.reshape(keys.shape), grad_v.reshape(values.shape))


def local(
    images,
    target,
    clean_images,
    levels,
    labels,
    null_mask,
    vgg_proj,
    lpips_lin,
    master,
    first_moment,
    second_moment,
):
    gathered = lax.all_gather(master.astype(jnp.bfloat16), ("batch", "pix"), axis=0, tiled=True)
    pieces, used_len = unpack(gathered)
    w_one, w_two, w_qkv, w_proj, w_down, w_emb, class_table, gains_low = pieces
    gains_one = gains_low.astype(jnp.float32)
    n_img, rows_local, cols_local, channels = images.shape
    wide_channels = w_down.shape[1]
    pix_count = lax.axis_size("pix")
    batch_count = lax.axis_size("batch")
    pixels_here = rows_local * cols_local
    pixels_all = pixels_here * pix_count
    pixels_all_two = pixels_all // 4
    images_all = n_img * batch_count
    row_index = jnp.where(null_mask == 1, class_table.shape[0] - 1, labels)
    one_hot = (
        row_index[:, None] == jnp.arange(class_table.shape[0], dtype=jnp.int32)[None, :]
    ).astype(jnp.float32)
    pre_embed = time_vector(levels) + jnp.dot(
        one_hot, class_table.astype(jnp.float32), precision=precise
    )
    embedded = jax.nn.silu(pre_embed)
    w_emb_wide = w_emb.astype(jnp.float32)
    scale_shift = jnp.dot(embedded, w_emb_wide, precision=precise)
    scale_one = scale_shift[:, None, :channels]
    shift_one = scale_shift[:, None, channels:]
    flat_in = images.astype(jnp.float32).reshape(n_img, pixels_here, channels)
    middle, kept_one = res_forward(
        flat_in, gains_one, scale_one, shift_one, w_one, w_two, rows_local, pixels_all
    )
    normed_three, inverse_three = group_forward(middle, pixels_all)
    attn_in = (normed_three * gains_one[4] + gains_one[5]).astype(jnp.bfloat16)
    triples = jnp.dot(attn_in.reshape(-1, channels), w_qkv, preferred_element_type=jnp.float32)
    triples = triples.astype(jnp.bfloat16).reshape(n_img, pixels_here, 3 * channels)
    spread_heads = to_heads(triples)
    local_heads = spread_heads.shape[2] // (3 * HEAD)
    split_heads = spread_heads.reshape(n_img, -1, local_heads, 3, HEAD).transpose(3, 0, 2, 1, 4)
    queries, keys, values = (split_heads[0], split_heads[1], split_heads[2])
    attended, log_total = attend(queries, keys, values)
    attended_px = to_pixels(attended.transpose(0, 2, 1, 3).reshape(n_img, -1, local_heads * HEAD))
    projected = jnp.dot(
        attended_px.reshape(-1, channels), w_proj, preferred_element_type=jnp.float32
    )
    output = middle + projected.reshape(n_img, pixels_here, channels)
    final_out, columns_down = conv_forward(output.astype(jnp.bfloat16), w_down, rows_local, 2)
    pixels_two = final_out.shape[1]
    feat_width = vgg_proj.shape[1]
    online_feat = jnp.dot(
        final_out.astype(jnp.bfloat16).reshape(-1, wide_channels),
        vgg_proj,
        preferred_element_type=jnp.float32,
    )
    online_feat = online_feat.reshape(n_img, pixels_two, feat_width)
    target_feat = jnp.dot(
        target.reshape(-1, wide_channels), vgg_proj, preferred_element_type=jnp.float32
    )
    target_feat = target_feat.reshape(n_img, pixels_two, feat_width)
    target_unit = target_feat * lax.rsqrt(
        jnp.mean(target_feat * target_feat, -1, keepdims=True) + EPS_FEAT
    )
    clean_wide = clean_images.astype(jnp.float32).reshape(n_img, pixels_two, wide_channels)

    def loss_terms(feature, out_value):
        unit = feature * lax.rsqrt(jnp.mean(feature * feature, -1, keepdims=True) + EPS_FEAT)
        consist = jnp.sum(lpips_lin * (unit - target_unit) ** 2, (1, 2)) / (
            feat_width * pixels_all_two
        )
        denoise = jnp.sum((out_value - clean_wide) ** 2, (1, 2)) / (pixels_all_two * wide_channels)
        return (consist, denoise)

    (consist, denoise), pullback = jax.vjp(loss_terms, online_feat, final_out)
    level_hot = (levels[:, None] == jnp.arange(LEVELS, dtype=jnp.int32)[None, :]).astype(
        jnp.float32
    )
    level_pair = lax.psum(
        (jnp.sum(consist[:, None] * level_hot, 0), jnp.sum(level_hot / pix_count, 0)),
        ("batch", "pix"),
    )
    zero_count = level_pair[1][0]
    is_zero = (levels == 0).astype(jnp.float32)
    grad_feat, grad_out = pullback(
        (jnp.full_like(consist, 1.0 / images_all), is_zero / jnp.maximum(zero_count, 1.0))
    )
    grad_feat_low = grad_feat.astype(jnp.bfloat16).reshape(-1, feat_width)
    grad_final = grad_out + jnp.einsum(
        "rf,cf->rc", grad_feat_low, vgg_proj, preferred_element_type=jnp.float32
    ).reshape(n_img, pixels_two, wide_channels)
    d_w_down, grad_output = conv_back(
        columns_down, grad_final.astype(jnp.bfloat16), w_down, rows_local, 2
    )
    grad_proj = grad_output.astype(jnp.bfloat16).reshape(-1, channels)
    d_w_proj = jnp.einsum(
        "rc,rd->cd",
        attended_px.reshape(-1, channels),
        grad_proj,
        preferred_element_type=jnp.float32,
    )
    grad_att_px = jnp.einsum("rd,cd->rc", grad_proj, w_proj, preferred_element_type=jnp.float32)
    grad_att_px = grad_att_px.astype(jnp.bfloat16).reshape(n_img, pixels_here, channels)
    grad_heads = to_heads(grad_att_px)
    grad_split = grad_heads.reshape(n_img, -1, local_heads, HEAD).transpose(0, 2, 1, 3)
    grad_q, grad_k, grad_v = attend_back(queries, keys, values, log_total, grad_split)
    grad_triples = jnp.stack([grad_q, grad_k, grad_v], 3).transpose(0, 2, 1, 3, 4)
    grad_triples = grad_triples.reshape(n_img, -1, local_heads * 3 * HEAD).astype(jnp.bfloat16)
    grad_triples = to_pixels(grad_triples)
    grad_rows = grad_triples.reshape(-1, 3 * channels)
    d_w_qkv = jnp.einsum(
        "rc,rd->cd", attn_in.reshape(-1, channels), grad_rows, preferred_element_type=jnp.float32
    )
    grad_attn_in = jnp.einsum(
        "rd,cd->rc", grad_rows, w_qkv, preferred_element_type=jnp.float32
    ).reshape(n_img, pixels_here, channels)
    d_gain_three = jnp.sum(grad_attn_in * normed_three, (0, 1))
    d_bias_three = jnp.sum(grad_attn_in, (0, 1))
    grad_middle = grad_output + group_backward(
        grad_attn_in * gains_one[4], normed_three, inverse_three, pixels_all
    )
    d_w_one, d_w_two, d_gains_one, d_scale_one, d_shift_one, unused_grad = res_back(
        grad_middle, kept_one, gains_one, scale_one, w_one, w_two, rows_local, pixels_all
    )
    grad_scale_shift = jnp.concatenate([d_scale_one, d_shift_one], 1)
    d_w_emb = jnp.dot(embedded.T, grad_scale_shift, precision=precise)
    grad_embedded = jnp.dot(grad_scale_shift, w_emb_wide.T, precision=precise)
    d_table = jnp.dot(one_hot.T, grad_embedded * silu_slope(pre_embed), precision=precise)
    d_norms_one = jnp.concatenate([d_gains_one, jnp.stack([d_gain_three, d_bias_three])], 0)
    flat_grad = jnp.concatenate(
        [
            d_w_one.ravel(),
            d_w_two.ravel(),
            d_w_qkv.ravel(),
            d_w_proj.ravel(),
            d_w_down.ravel(),
            d_w_emb.ravel(),
            d_table.ravel(),
            d_norms_one.ravel(),
            jnp.zeros((gathered.shape[0] - used_len,), jnp.float32),
        ]
    )
    own_grad = lax.psum_scatter(flat_grad, ("batch", "pix"), scatter_dimension=0, tiled=True)
    norm_before = jnp.sqrt(lax.psum(jnp.sum(own_grad * own_grad), ("batch", "pix")))
    clipped = own_grad * jnp.minimum(1.0, CLIP / norm_before)
    new_first = BETA_ONE * first_moment + (1.0 - BETA_ONE) * clipped
    new_second = BETA_TWO * second_moment + (1.0 - BETA_TWO) * clipped * clipped
    fixed_first = new_first / (1.0 - BETA_ONE**STEP)
    fixed_second = new_second / (1.0 - BETA_TWO**STEP)
    new_master = master - RATE * (
        fixed_first / (jnp.sqrt(fixed_second) + EPS_ADAM) + DECAY * master
    )
    level_sums = jnp.stack([level_pair[0], level_pair[1]])
    return (
        new_master,
        new_first,
        new_second,
        new_master.astype(jnp.bfloat16),
        norm_before,
        level_sums,
    )


MESH = pl.DeviceIdType.MESH
ROWS=537; BLK=560; HALF=288
PX=512
R_ONE,R_TWO,R_QKV,R_PROJ,R_DOWN,R_EMB,R_TAB,R_GAIN,R_END=0,3456,6912,8064,8448,13632,15168,17170,17184
f32=jnp.float32; bf=jnp.bfloat16
class Comm:
    def __init__(self): self.sent=[]
    def go(self, cond, src, dst, ssem, rsem, b, p):
        c = pltpu.make_async_remote_copy(src_ref=src,dst_ref=dst,send_sem=ssem,recv_sem=rsem,device_id=(b,p),device_id_type=MESH)
        if cond is None: c.start()
        else: pl.when(cond)(lambda: c.start())
        self.sent.append((cond,c))
    def drain(self):
        for cond,c in self.sent:
            if cond is None: c.wait_send()
            else: pl.when(cond)(lambda c=c: c.wait_send())
        self.sent=[]

def place():
    b=lax.axis_index("batch"); p=lax.axis_index("pix")
    core=lax.rem(b,2); y=lax.rem(lax.div(b,2),2); z=lax.div(b,4)
    return b,p,core,y,z

def base_of(s): return 16*((ROWS*s)//16)
def dg(a,b,ca,cb): return lax.dot_general(a,b,(((ca,),(cb,)),((),())),preferred_element_type=f32)
def nn(a,b): return dg(a,b,1,0)
def nt(a,b): return dg(a,b,1,1)
def tn(a,b): return dg(a,b,0,0)
def split3(v):
    hi=v.astype(bf); r=v-hi.astype(f32); mid=r.astype(bf); lo=(r-mid.astype(f32)).astype(bf)
    return hi,mid,lo
def exact(v,w,dot):
    hi,mid,lo=split3(v)
    return dot(hi,w)+dot(mid,w)+dot(lo,w)
def sigmoid(v): return 1.0/(1.0+jnp.exp(-v))
def silu(v): return v*sigmoid(v)
def slope(v):
    s=sigmoid(v)
    return s*(1.0+v*(1.0-s))
def cloop(n,chunk,body,init):
    return lax.fori_loop(0,n//chunk,lambda i,c: body(pl.multiple_of(i*chunk,chunk),c),init)
def col8(v): return jnp.sum(v.reshape(-1,8,v.shape[-1]),axis=0)
Z8=lambda: jnp.zeros((8,CH),f32)
class Blocks:
    def __init__(self,ref,n): self.ref=ref; self.n=n
def at_block(ref,j,sl):
    if isinstance(ref,Blocks): return ref.ref,(pl.ds(ref.n*j+sl.start,sl.size,stride=sl.stride),slice(None))
    return ref,(j,sl,slice(None))
def ld(ref,sl):
    out=[]
    for j in range(ref.ref.shape[0]//ref.n if isinstance(ref,Blocks) else ref.shape[0]):
        r,k=at_block(ref,j,sl)
        out.append(r[k])
    return jnp.concatenate(out,1)
def put3(ref,sl,v):
    for j in range(v.shape[1]//128):
        r,k=at_block(ref,j,sl)
        r[k]=v[:,128*j:128*j+128]
def every(start,n,step): return pl.ds(start,n,stride=step)
def row(v): return jnp.sum(v,axis=0,keepdims=True)


LAST=25
def step_kernel(images_all,
    mast,img,tgt,cln,vgg,lin,tvec,rowid,level,
    flat_ref,norm_ref,lev_ref,g_ref,
    wv,tails,cvt,cvt2,wd,wee,weo,wqT,x3a,x3b,z3,inner,middle,gout,gsec,ain,trT,dtrT,attT,xd,lse,dattT,ssend,srecv,hsend,hrecv,himg,dzs,dzr,geo,oth,wsem,tsem,xs,xr,total,blk,own_sem,azs,azr,axs,axr,ays,ayr,adar,adbr,ass,asr,pack_ref,lpk,ppk,red1,red2,tile,lps,lpr,pps,ppr,n1s,n1r,n2s,n2r,sibr,rb,rx,ry,zu,zd,s1s,s1r,dar,dbr,rxs,rxr,rys,ryr,zs,zur,zdr,acc,gtile,gls,glr,gps,gpr,rba,a2s,a2r,ads,ds_,hmid,esend,erecv,gm,a3s,a3r):
    b,p,core,y,z=place()
    q=1-p; xn=q; s=b*2+p
    pf=p.astype(f32); qf=1.0-pf
    yn=b+2-4*y; sib=b+1-2*core; oc=1-core
    up_ok=z<3; dn_ok=z>0
    top=z==3
    mine=(y*2+core)*2+p
    cvt3=Blocks(cvt,1536)
    mcopy=pltpu.make_async_copy(mast,cvt.at[pl.ds(0,1611)],own_sem)
    mcopy.start()
    barrier=pltpu.get_barrier_semaphore()
    plane=[]
    for dy in range(2):
        for dc in range(2):
            for dp in range(2):
                if dy+dc+dp: plane.append((4*dy+2*dc+dp,z*4+lax.rem(y+dy,2)*2+lax.rem(core+dc,2),lax.rem(p+dp,2)))
    line=[(k,lax.rem(z+k,4)) for k in range(1,4)]
    def sig(bb,pp): pl.semaphore_signal(barrier,inc=1,device_id=(bb,pp),device_id_type=MESH)
    for _,bb,pp in plane: sig(bb,pp)
    for _,zz in line: sig(b+4*(zz-z),p)
    def when(ok,f):
        if ok is None: f()
        else: pl.when(ok)(f)
    def AND(*c):
        r=None
        for k in c:
            if k is not None: r=k if r is None else r&k
        return r
    def wait_in(ref,sem):
        pltpu.make_async_remote_copy(src_ref=ref,dst_ref=ref,send_sem=sem,recv_sem=sem,device_id=(b,xn),device_id_type=MESH).wait_recv()
    def slot(zz,yy,pp,cc=core): return ((zz*2+yy)*2+cc)*2+pp
    A=pl.ds(0,HALF); B=pl.ds(HALF,BLK-HALF)
    cm=Comm()
    shift=lax.rem(9*s,16)
    total[ROWS-1:BLK]=jnp.zeros((BLK-ROWS+1,CH),f32)
    mcopy.wait()
    for j in range(3): total[0:ROWS,128*j:128*j+128]=cvt[pl.ds(j,ROWS,stride=3),:]
    at=lax.broadcasted_iota(jnp.int32,(BLK,CH),0)
    blk[...]=jnp.where(at==BLK-4,(level[...]==0).astype(f32),pltpu.roll(total[...],shift,0)).astype(bf)
    own=pltpu.make_async_copy(blk,g_ref.at[s],own_sem)
    own.start()
    pl.semaphore_wait(barrier,10)
    def valid(zz): return (zz>=0)&(zz<4)
    def pick(c0,c1,c2,c3): return jnp.where(z==0,c0,jnp.where(z==1,c1,jnp.where(z==2,c2,c3)))
    hs=(A,B)
    ends=(z==0)|(z==3); is1=z==1; is2=z==2; inner_z=jnp.logical_not(ends)
    def z_send(ok,zz,h,d,src=None):
        g=g_ref.at[slot(zz,y,p),hs[h]]
        cm.go(ok,g if src is None else src,g,azs.at[zz,(1-d)//2],azr.at[zz,h],b+4*d,p)
    def xy_send(ok,zz,h,src=None):
        g=g_ref.at[slot(zz,y,p),hs[h]]
        cm.go(ok,g if src is None else src,g,axs.at[zz],axr.at[zz,h],b,xn)
        cm.go(ok,g if src is None else src,g,ays.at[zz],ayr.at[zz,h],yn,p)
    def sib_send(ok,zz,yy,pp,h,src=None):
        sl=slot(zz,yy,pp)
        first=pl.multiple_of(16*lax.div(ROWS*sl,16),16)
        def part(lo,n):
            return g_ref.at[sl,pl.ds(lo,n)] if src is None else src.at[pl.ds(lo-(HALF if h else 0),n)]
        lo,n=(0,HALF) if h==0 else (HALF,528-HALF)
        cm.go(ok,part(lo,n),wv.at[pl.ds(first+lo,n)],ass.at[zz],asr.at[zz],sib,p)
        if h==1: cm.go(ok,part(528,32),tails.at[sl],ass.at[zz],asr.at[zz],sib,p)
    def own_sends():
        for h in range(2):
            src=blk.at[hs[h]]
            z_send(z==0,z,h,1,src)
            z_send(z==3,z,h,-1,src)
            sib_send(None,z,y,p,h,src)
    def own_xy():
        for h in range(2): xy_send(z!=1,z,h,blk.at[hs[h]])
    four=((1-y,xn),(y,xn),(1-y,p),(y,p))
    def two_send(ok,i,d):
        yy,pp=four[i]
        for h in range(2):
            g=g_ref.at[slot(2,yy,pp),hs[h]]
            cm.go(ok,g,g,a2s.at[(1-d)//2],a2r.at[yy,pp,h],b+4*d,p)
    def two_in(i,ok):
        yy,pp=four[i]
        for h in range(2):
            g=g_ref.at[slot(2,yy,pp),hs[h]]
            when(ok,lambda: wait_in(g,a2r.at[yy,pp,h]))
            cm.go(ok&(z==1),g,g,a2s.at[1],a2r.at[yy,pp,h],b-4,p)
            sib_send(ok,2,yy,pp,h)
    def three_out(i):
        yy,pp=four[i]
        for h in range(2):
            g=g_ref.at[slot(3,yy,pp),hs[h]]
            cm.go(top,g,g,a3s,a3r.at[yy,pp,h],b-4,p)
    def three_in(i):
        yy,pp=four[i]
        for h in range(2):
            g=g_ref.at[slot(3,yy,pp),hs[h]]
            when(is2,lambda: wait_in(g,a3r.at[yy,pp,h]))
            sib_send(is2,3,yy,pp,h)
    def diag_in(ok,zz):
        sd=slot(zz,1-y,xn)
        def f():
            wait_in(g_ref.at[sd,A],adar.at[zz])
            wait_in(g_ref.at[sd,B],adbr.at[zz])
        when(ok,f)
        for h in range(2): sib_send(ok,zz,1-y,xn,h)
    def two_diag():
        sd=slot(2,1-y,xn)
        def f():
            wait_in(g_ref.at[sd,A],adar.at[2])
            wait_in(g_ref.at[sd,B],adbr.at[2])
        when(z==2,f)
        for h in range(2): sib_send(z==2,2,1-y,xn,h)
    def arrive0(h):
        ok=z!=0
        when(ok,lambda: wait_in(g_ref.at[slot(0,y,p),hs[h]],azr.at[0,h]))
        z_send(ok&up_ok,0,h,1)
        xy_send(ok,0,h)
        sib_send(ok,0,y,p,h)
    def arrive3(h,ok):
        when(ok,lambda: wait_in(g_ref.at[slot(3,y,p),hs[h]],azr.at[3,h]))
        z_send(ok&dn_ok,3,h,-1)
        sib_send(ok,3,y,p,h)
    def xy_arrive(ok,f,h):
        sx=slot(f,y,xn); sy=slot(f,1-y,p)
        when(ok,lambda: wait_in(g_ref.at[sx,hs[h]],axr.at[f,h]))
        if h==0: cm.go(ok,g_ref.at[sx,A],g_ref.at[sx,A],ads.at[f],adar.at[f],yn,p)
        sib_send(ok,f,y,xn,h)
        when(ok,lambda: wait_in(g_ref.at[sy,hs[h]],ayr.at[f,h]))
        if h==1: cm.go(ok,g_ref.at[sy,B],g_ref.at[sy,B],ads.at[f],adbr.at[f],b,xn)
        sib_send(ok,f,1-y,p,h)
    def later_sends():
        for h in range(2):
            src=blk.at[hs[h]]
            z_send(z==1,z,h,1,src)
            z_send(z==1,z,h,-1,src)
    def one_in(h,ok):
        when(ok,lambda: wait_in(g_ref.at[slot(1,y,p),hs[h]],azr.at[1,h]))
        z_send(ok&is2,1,h,1)
        sib_send(ok,1,y,p,h)
    def load(sl): return (pltpu.make_async_copy(g_ref.at[sl,pl.ds(0,528)],wv.at[pl.ds(pl.multiple_of(16*lax.div(ROWS*sl,16),16),528)],wsem.at[lax.div(sl,8)]),
                          pltpu.make_async_copy(g_ref.at[sl,pl.ds(528,32)],tails.at[sl],tsem.at[lax.div(sl,8)]))
    def d_arrive(zz):
        sd=slot(zz,1-y,xn)
        wait_in(g_ref.at[sd,A],adar.at[zz])
        sib_send(None,zz,1-y,xn,0)
        wait_in(g_ref.at[sd,B],adbr.at[zz])
        sib_send(None,zz,1-y,xn,1)
        for yy in range(2):
            for pp in range(2):
                for c in load(slot(zz,yy,pp)): c.start()
    def sib_arrive(zz):
        wait_in(g_ref.at[pl.ds(0,4)],asr.at[zz])
    has_gains=s==31
    gain_line=(y==1)&(core==1)&(p==1)
    def gain_sends():
        for k,zz in line: cm.go(has_gains,blk.at[pl.ds(528,16)],gtile,gls,glr,b+4*(zz-z),p)
    def gain_pass():
        pl.when(has_gains)(lambda: gtile.__setitem__(Ellipsis,blk[528:544]))
        pl.when(gain_line&jnp.logical_not(has_gains))(lambda: wait_in(gtile,glr))
        for d,bb,pp in plane: cm.go(gain_line,gtile,gtile,gps,gpr,bb,pp)
    def gain_wait():
        pl.when(jnp.logical_not(gain_line))(lambda: wait_in(gtile,gpr))
    seen=[]
    def take(shards):
        pltpu.make_async_copy(wv.at[pl.ds(0,4*528)],wv.at[pl.ds(0,4*528)],wsem.at[shards[0]//8]).wait()
        pltpu.make_async_copy(tails.at[pl.ds(0,4)],tails.at[pl.ds(0,4)],tsem.at[shards[0]//8]).wait()
        for k in shards:
            lo=base_of(k)
            if k<31 and base_of(k+1)-lo==544 or k==31: wv[lo+528:lo+544]=tails[k,0:16]
            seen.append(k)
        for k in range(1,32):
            if k in seen and k-1 in seen and (k in shards or k-1 in shards):
                off=base_of(k)-base_of(k-1)-528
                t=tails[k-1,off:off+16].astype(f32)
                if off: t=jnp.where(lax.broadcasted_iota(jnp.int32,(16,CH),0)<8,t,0.0)
                lo=base_of(k)
                wv[lo:lo+16]=(wv[lo:lo+16].astype(f32)+t).astype(bf)
    def rows(u,yy,pp,cc=core):
        at=pl.ds(pl.multiple_of(16*lax.div(ROWS*slot(u,yy,pp,cc),16),16),BLK)
        return wd.at[at,pl.ds(0,CH)] if u==0 else wv.at[at]
    def need(u,yy,pp,cc=core): return None if u<3 else slot(u,yy,pp,cc)<=LAST
    def sibsend(u):
        for yy,pp in four:
            cm.go(need(u,yy,pp,oc),rows(u,yy,pp,oc),sibr.at[4*u+2*yy+pp],s1s.at[u],s1r.at[u,yy,pp],sib,p)
    def both(u,yy,pp,lo,n):
        a=pl.multiple_of(16*lax.div(ROWS*slot(u,yy,pp),16)+lo,16)
        mine_=wd[pl.ds(a,n),0:CH] if u==0 else wv[pl.ds(a,n)]
        return mine_.astype(f32)+sibr[4*u+2*yy+pp,lo:lo+n].astype(f32)
    HA=(0,HALF); HB=(HALF,BLK-HALF)
    def sib_in(u,yy,pp): wait_in(sibr.at[4*u+2*yy+pp],s1r.at[u,yy,pp])
    def keep(u,yy,pp,half,more=None):
        t=both(u,yy,pp,*half)
        if more is not None: t=t+more.astype(f32)
        sibr[4*u+2*yy+pp,half[0]:half[0]+half[1]]=t.astype(bf)
    def diag(u):
        yy,pp=1-y,xn
        c=need(u,yy,pp)
        def f():
            sib_in(u,yy,pp)
            keep(u,yy,pp,HA); keep(u,yy,pp,HB)
        when(c,f)
        src=sibr.at[4*u+2*yy+pp]
        if u<2: cm.go(c,src.at[A],rba.at[u],ds_.at[u],dar.at[u],b,xn)
        else: cm.go(c,src.at[A],rba.at[u],ds_.at[u],dar.at[u],yn,p)
        cm.go(c,src.at[B],rb.at[u],ds_.at[u],dbr.at[u],yn,p)
    def ysend(u):
        c=need(u,1-y,p)
        def f():
            sib_in(u,1-y,p)
            keep(u,1-y,p,HA); keep(u,1-y,p,HB)
        when(c,f)
        for h in range(2): cm.go(c,sibr.at[4*u+2*(1-y)+p,hs[h]],ry.at[u,hs[h]],rys.at[u],ryr.at[u,h],yn,p)
    def xsend(u,only=None):
        c=AND(need(u,y,xn),only)
        def f():
            sib_in(u,y,xn)
            wait_in(rba.at[u],dar.at[u])
            keep(u,y,xn,HA,rba[u])
        when(c,f)
        cm.go(c,sibr.at[4*u+2*y+xn,A],rx.at[u,A],rxs.at[u],rxr.at[u,0],b,xn)
        def f2():
            wait_in(rb.at[u],dbr.at[u])
            keep(u,y,xn,HB,rb[u])
        when(c,f2)
        cm.go(c,sibr.at[4*u+2*y+xn,B],rx.at[u,B],rxs.at[u],rxr.at[u,1],b,xn)
    def put_x(u,half,h,more=None):
        keep(u,y,xn,half,more)
        cm.go(None,sibr.at[4*u+2*y+xn,hs[h]],rx.at[u,hs[h]],rxs.at[u],rxr.at[u,h],b,xn)
    def put_y(u,half,h,more=None):
        keep(u,1-y,p,half,more)
        cm.go(None,sibr.at[4*u+2*(1-y)+p,hs[h]],ry.at[u,hs[h]],rys.at[u],ryr.at[u,h],yn,p)
    def first_halves(u):
        sib_in(u,y,xn)
        sib_in(u,1-y,p)
        if u>0:
            put_x(u,HA,0)
            put_y(u,HB,1)
    def second_halves(u):
        wait_in(rba.at[u],dar.at[u])
        put_y(u,HA,0,rba[u])
        if u==0:
            put_x(u,HA,0)
            put_y(u,HB,1)
        wait_in(rb.at[u],dbr.at[u])
        put_x(u,HB,1,rb[u])
    def chunks(u): return ((0,80,0),(80,80,0),(160,64,0),(224,64,0),(288,80,1),(368,64,1),(432,64,1),(496,64,1)) if u==0 else ((0,HALF,0),(HALF,BLK-HALF,1))
    def zur_at(u,k): return zur.at[2*(u-1)+k]
    def zdr_at(u,k): return zdr.at[k if u==0 else 8+2*(u-1)+k]
    def xy_in(u,h):
        wait_in(rx.at[u,hs[h]],rxr.at[u,h])
        wait_in(ry.at[u,hs[h]],ryr.at[u,h])
    def zstep(u,i):
        for d in (1,-1):
            at_z=i if d==1 else 3-i
            if not (at_z<u if d==1 else at_z>u): continue
            c=AND(need(u,y,p),z==at_z)
            buf,bsem=(zu.at[u-1],zur_at) if d==1 else (zd.at[u],zdr_at)
            own_at=4*u+2*y+p
            def first(): sib_in(u,y,p)
            when(c,first)
            seen_h=set()
            for k,(lo,n,h) in enumerate(chunks(u)):
                def f():
                    if h not in seen_h: xy_in(u,h)
                    t=both(u,y,p,lo,n)+rx[u,lo:lo+n].astype(f32)+ry[u,lo:lo+n].astype(f32)
                    if i>0:
                        wait_in(buf.at[pl.ds(lo,n)],bsem(u,k))
                        t=t+buf[lo:lo+n].astype(f32)
                    sibr[own_at,lo:lo+n]=t.astype(bf)
                when(c,f)
                seen_h.add(h)
                cm.go(c,sibr.at[own_at,pl.ds(lo,n)],buf.at[pl.ds(lo,n)],zs.at[u],bsem(u,k),b+4*d,p)
    def zend(u):
        def f():
            sib_in(u,y,p)
            done=set()
            for k,(lo,n,h) in enumerate(chunks(u)):
                if h not in done: xy_in(u,h); done.add(h)
                t=both(u,y,p,lo,n)+rx[u,lo:lo+n].astype(f32)+ry[u,lo:lo+n].astype(f32)
                if u>0:
                    wait_in(zu.at[u-1,pl.ds(lo,n)],zur_at(u,k))
                    t=t+zu[u-1,lo:lo+n].astype(f32)
                if u<3:
                    wait_in(zd.at[u,pl.ds(lo,n)],zdr_at(u,k))
                    t=t+zd[u,lo:lo+n].astype(f32)
                if u==3:
                    rr=16*lax.div(ROWS*s,16)+lo+lax.broadcasted_iota(jnp.int32,(n,CH),0)
                    t=jnp.where(rr<R_EMB,t,total[lo:lo+n])
                total[lo:lo+n]=t
        when(AND(need(u,y,p),z==u),f)
    state={"k":0}
    def xchg(src,dst,dst_like=None):
        k=state["k"]; state["k"]=k+1
        c=pltpu.make_async_remote_copy(src_ref=src,dst_ref=dst,send_sem=xs.at[k],recv_sem=xr.at[k],device_id=(b,q),device_id_type=MESH)
        c.start()
        return c
    edge=pl.ds(pl.multiple_of(q*480,32),32)
    gain_sends()
    c_img=xchg(img.at[edge],himg)
    def gsum(v): return exact(v,gm[...],nn)
    def swap_sums(k,s1,s2):
        ssend[k]=jnp.concatenate([s1,s2,jnp.zeros((6,CH),f32)],0)
        return xchg(ssend.at[k],srecv.at[k])
    def total_sums(k):
        t=gsum(ssend[k]+srecv[k])*(1.0/(12*2*PX))
        return t[0:1],t[1:2]
    def norm_of(t):
        mean,sq=t
        return mean,lax.rsqrt(sq-mean*mean+EPS_NORM)
    def fill3(dst,at,a):
        col=lax.broadcasted_iota(jnp.int32,a.shape,0)&31
        n=a.shape[0]
        dst[pl.ds(at,n),CH:2*CH]=a.astype(bf)
        dst[pl.ds(at,n),0:CH]=jnp.where(col==0,0.0,pltpu.roll(a,1,0)).astype(bf)
        dst[pl.ds(at,n),2*CH:3*CH]=jnp.where(col==31,0.0,pltpu.roll(a,n-1,0)).astype(bf)
    def fill_edges(dst,h):
        fill3(dst,0,h*pf); fill3(dst,544,h*qf)
    def conv_to(dst,x3,wrow,add=None):
        for dr in range(3):
            d=nn(x3[32*dr:32*dr+PX],wv[wrow+1152*dr:wrow+1152*dr+1152])
            if dr==0: dst[...]=d if add is None else add()+d
            else: dst[...]+=d
    def conv_dx(dst,wrow):
        first=True
        for dr in range(3):
            for dc in range(3):
                d=nt(z3[32*(2-dr):32*(2-dr)+PX,CH*(2-dc):CH*(2-dc)+CH],wv[wrow+CH*(3*dr+dc):wrow+CH*(3*dr+dc)+CH])
                if first: dst[...]=d
                else: dst[...]+=d
                first=False
    def st(i,c):
        v=img[pl.ds(i,64)].astype(f32)
        return c[0]+col8(v),c[1]+col8(v*v)
    a1,a2=cloop(PX,64,st,(Z8(),Z8()))
    c=swap_sums(0,row(a1),row(a2))
    own_sends()
    gain_pass()
    own_xy()
    group_of=lambda d: lax.shift_right_logical(lax.broadcasted_iota(jnp.int32,(CH,CH),d)*43691,19)
    gm[...]=(group_of(0)==group_of(1)).astype(f32).astype(bf)
    gain_wait()
    g6=gtile[...].astype(f32)
    g1,b1,g2,b2,g3,b3=[g6[2+i:3+i] for i in range(6)]
    c.wait()
    mean1,inv1=norm_of(total_sums(0))
    def act_of(v): return silu((v-mean1)*inv1*g1+b1)
    arrive3(0,is2)
    arrive3(1,is2)
    def fa(i,_):
        fill3(x3a,pl.multiple_of(i+32,32),act_of(img[pl.ds(i,64)].astype(f32)))
        return 0
    cloop(PX,64,fa,0)
    c_img.wait()
    fill_edges(x3a,act_of(himg[...].astype(f32)))
    own.wait()
    xy_arrive(z==3,3,0)
    xy_arrive(z==3,3,1)
    arrive0(0)
    xy_arrive(is2,2,0)
    three_out(1); three_out(2)
    arrive0(1)
    diag_in(top,3)
    three_out(0)
    xy_arrive(is2,2,1)
    arrive3(0,is1)
    arrive3(1,is1)
    later_sends()
    two_send(is2,3,-1)
    two_send(is2,1,-1); two_send(is2,2,-1)
    xy_arrive(None,0,0)
    one_in(0,is2)
    one_in(1,is2)
    xy_arrive(None,0,1)
    for h in range(2): xy_send(is1,3,h)
    for h in range(2): xy_send(is2,1,h)
    for h in range(2): one_in(h,top)
    for h in range(2): xy_send(top,1,h)
    for i in (3,1,2): two_send(is2,i,1)
    two_diag()
    two_send(is2,0,-1); two_send(is2,0,1)
    d_arrive(0)
    arrive3(0,z==0)
    xy_send(z==0,3,0)
    sib_arrive(0)
    take(range(0,8))
    conv_to(inner,x3a,R_ONE)
    def st2(i,c):
        v=inner[pl.ds(i,64)]
        return c[0]+col8(v),c[1]+col8(v*v)
    a1,a2=cloop(PX,64,st2,(Z8(),Z8()))
    c1=swap_sums(1,row(a1),row(a2))
    c2=xchg(inner.at[edge],hrecv.at[0])
    two_in(3,is1)
    xy_arrive(z>=2,1,0)
    arrive3(1,z==0)
    xy_send(z==0,3,1)
    xy_arrive(z<2,3,0)
    xy_arrive(z<2,3,1)
    for h in range(2): one_in(h,z==0)
    for h in range(2): xy_send(z<2,1,h)
    three_in(1); three_in(2)
    xy_arrive(z>=2,1,1)
    three_in(0)
    diag_in(z<2,3)
    for yy in range(2):
        for pp in range(2):
            for k in load(slot(3,yy,pp)): k.start()
    sib_arrive(3)
    two_in(1,is1)
    take(range(24,32))
    ids=rowid[...]
    pre=[]
    tcol=lax.broadcasted_iota(jnp.int32,(16,R_END-R_TAB),1)
    for h in range(2):
        hot=(tcol==2*ids+h).astype(f32).astype(bf)
        pre.append(nn(hot,wv[R_TAB:R_END])[0:1]+tvec[:,CH*h:CH*h+CH])
    emb=[silu(v) for v in pre]
    put3(cvt3,pl.ds(0,1536),wv[R_EMB:R_TAB].astype(f32))
    wee[...]=ld(cvt3,every(0,768,2)).astype(bf)
    weo[...]=ld(cvt3,every(1,768,2)).astype(bf)
    def emb_dot(w):
        r=None
        for h in range(2):
            e=jnp.broadcast_to(emb[h],(16,CH))
            d=exact(e,w[CH*h:CH*h+CH],nn)[0:1]
            r=d if r is None else r+d
        return r
    sc1=1.0+emb_dot(wee); sh=emb_dot(weo)
    c1.wait()
    xy_arrive(z<2,1,0)
    mean2,inv2=norm_of(total_sums(1))
    def pre_b(v):
        n=(v-mean2)*inv2
        af=n*g2+b2
        return n,af,af*sc1+sh
    def fb(i,_):
        fill3(x3b,pl.multiple_of(i+32,32),silu(pre_b(inner[pl.ds(i,64)])[2]))
        return 0
    cloop(PX,64,fb,0)
    c2.wait()
    fill_edges(x3b,silu(pre_b(hrecv[0])[2]))
    xy_arrive(z<2,1,1)
    two_in(2,is1)
    d_arrive(1)
    sib_arrive(1)
    two_in(0,is1)
    take(range(8,16))
    conv_to(middle,x3b,R_TWO,lambda: img[...].astype(f32))
    def st3(i,c):
        v=middle[pl.ds(i,64)]
        return c[0]+col8(v),c[1]+col8(v*v)
    a1,a2=cloop(PX,64,st3,(Z8(),Z8()))
    c1=swap_sums(2,row(a1),row(a2))
    put3(cvt3,pl.ds(0,1152),wv[R_QKV:R_PROJ].astype(f32))
    for j in range(3):
        wqT[CH*j:CH*j+CH]=ld(cvt3,every(j,CH,3)).T.astype(bf)
    c1.wait()
    mean3,inv3=norm_of(total_sums(2))
    def fc(i,_):
        n=(middle[pl.ds(i,64)]-mean3)*inv3
        ain[pl.ds(i,64)]=(n*g3+b3).astype(bf)
        return 0
    cloop(PX,64,fc,0)
    c_in=xchg(ain.at[pl.ds(0,PX)],ain.at[pl.ds(PX,PX)])
    c_mid=xchg(middle.at[edge],hmid)
    def triples(a):
        t=nt(wqT[...],a)
        is_q=lax.rem(lax.broadcasted_iota(jnp.int32,t.shape,0),192)<64
        return jnp.where(is_q,t*0.125,t).astype(bf)
    trT[:,0:PX]=triples(ain[0:PX])
    def head_rows(h):
        r0=pl.multiple_of(h*192,64)
        return r0,pl.multiple_of(r0+64,64),pl.multiple_of(r0+128,64)
    def fh1(h,_):
        r0,r1,r2=head_rows(h)
        sco=nn(trT[pl.ds(r1,64),0:PX].T,trT[pl.ds(r0,64),0:PX])
        m=jnp.max(sco,0,keepdims=True)
        e=jnp.exp(sco-m)
        lse[h,0:1]=m
        lse[h,1:2]=jnp.sum(e,0,keepdims=True)
        acc[h]=nn(trT[pl.ds(r2,64),0:PX],e.astype(bf))
        return 0
    lax.fori_loop(0,6,fh1,0)
    for i in (3,1,2): two_in(i,ends)
    c_in.wait()
    trT[:,PX:2*PX]=triples(ain[PX:2*PX])
    def fh(h,_):
        r0,r1,r2=head_rows(h)
        sco=nn(trT[pl.ds(r1,64),PX:2*PX].T,trT[pl.ds(r0,64),0:PX])
        m0=lse[h,0:1]
        m=jnp.maximum(m0,jnp.max(sco,0,keepdims=True))
        e=jnp.exp(sco-m)
        a=jnp.exp(m0-m)
        l=lse[h,1:2]*a+jnp.sum(e,0,keepdims=True)
        o=acc[h]*a+nn(trT[pl.ds(r2,64),PX:2*PX],e.astype(bf))
        attT[pl.ds(pl.multiple_of(h*64,64),64),:]=(o*(1.0/l)).astype(bf)
        lse[h,0:1]=m+jnp.log(l)
        return 0
    lax.fori_loop(0,6,fh,0)
    put3(gout,pl.ds(0,PX),middle[...]+tn(attT[...],wv[R_PROJ:R_DOWN]))
    hsend[0]=ld(gout,edge).astype(bf)
    c1=xchg(hsend.at[0],oth.at[0])
    two_in(0,ends)
    for yy in range(2):
        for pp in range(2):
            for k in load(slot(2,yy,pp)): k.start()
    sib_arrive(2)
    take(range(16,24))
    for off in range(9):
        put3(cvt3,pl.ds(0,576),wv[R_DOWN+576*off:R_DOWN+576*off+576].astype(f32))
        v0,v1,v2=[ld(cvt3,every(i,192,3)) for i in range(3)]
        put3(cvt2,every(0,192,2),jnp.concatenate([v0,v1[:,0:256]],1))
        w=jnp.concatenate([v1[:,128:384],v2],1)
        w=pltpu.roll(w,w.shape[1]-64,1)
        put3(cvt2,every(1,192,2),w)
        wd[CH*off:CH*off+CH]=ld(cvt2,pl.ds(0,CH))[:,0:576].astype(bf)
    def parts(ref,n):
        e=ld(ref,every(0,n//2,2)); o=ld(ref,every(1,n//2,2))
        col=lax.broadcasted_iota(jnp.int32,o.shape,0)&15
        return jnp.where(col==0,0.0,pltpu.roll(o,1,0)).astype(bf),e.astype(bf),o.astype(bf)
    for dc,v in enumerate(parts(gout,PX)):
        v=v.reshape(8,32,CH)
        even=v[:,0:16].reshape(128,CH); odd=v[:,16:32].reshape(128,CH)
        xd[:,CH*(3+dc):CH*(3+dc)+CH]=even
        xd[:,CH*(6+dc):CH*(6+dc)+CH]=odd
        xd[16:128,CH*dc:CH*dc+CH]=odd[0:112]
    c1.wait()
    put3(geo,pl.ds(0,32),oth[0].astype(f32)*pf)
    for dc,v in enumerate(parts(geo,32)):
        xd[0:16,CH*dc:CH*dc+CH]=v
    fin=nn(xd[...],wd[0:9*CH])
    feat=nn(fin.astype(bf),vgg[...]); tf=nn(tgt[...],vgg[...])
    ir=lax.rsqrt(jnp.mean(feat*feat,-1,keepdims=True)+EPS_FEAT)
    unit=feat*ir
    diff=unit-tf*lax.rsqrt(jnp.mean(tf*tf,-1,keepdims=True)+EPS_FEAT)
    wl=lin[...]*diff
    consist=jnp.sum(row(wl*diff),1,keepdims=True)*(1.0/(256*256))
    du=wl*(2.0/(256*256*images_all))
    dfeat=(ir*(du-unit*jnp.mean(du*unit,-1,keepdims=True))).astype(bf)
    zc=jnp.zeros((16,128),f32)
    for t_ in range(0,32,2): zc=zc+tails[t_,16:32,0:128].astype(f32)
    zc=zc[12:13,0:1]
    seed=(level[...]==0).astype(f32)/jnp.maximum(zc,1.0)*(2.0/(256*CH2))
    gfin=nt(dfeat,vgg[...])+seed*(fin-cln[...].astype(f32))
    dz=gfin.astype(bf)
    dzs[...]=dz[0:16]
    c1=xchg(dzs,dzr)
    for off in range(9):
        dw=tn(xd[:,CH*off:CH*off+CH],dz)
        put3(cvt2,pl.ds(0,CH),jnp.concatenate([dw,jnp.zeros((CH,64),f32)],1))
        e=ld(cvt2,every(0,192,2)); o_=pltpu.roll(ld(cvt2,every(1,192,2)),64,1)
        lane=lax.broadcasted_iota(jnp.int32,(192,128),1)
        put3(cvt3,every(0,192,3),e[:,0:384])
        put3(cvt3,every(1,192,3),jnp.concatenate([e[:,384:512],jnp.where(lane<64,e[:,512:640],o_[:,0:128]),o_[:,128:256]],1))
        put3(cvt3,every(2,192,3),o_[:,256:640])
        wv[R_DOWN+576*off:R_DOWN+576*off+576]=ld(cvt3,pl.ds(0,576)).astype(bf)
    sibsend(2); sibsend(3)
    c1.wait()
    z32=dz.astype(f32)
    down=jnp.concatenate([z32[16:128],dzr[...].astype(f32)*qf],0)
    def left(v):
        col=lax.broadcasted_iota(jnp.int32,v.shape,0)&15
        return jnp.where(col==15,0.0,pltpu.roll(v,127,0)).astype(bf)
    s00,s01,s10,s11=dz,left(z32),down.astype(bf),left(down)
    W=lambda a,c: wd[CH*(3*a+c):CH*(3*a+c)+CH]
    def put(a,c,v):
        for i in range(8):
            put3(gout,every((2*i+a)*32+c,16,2),v[16*i:16*i+16])
    put(0,0,nt(s00,W(1,1)))
    put(0,1,nt(s00,W(1,2))+nt(s01,W(1,0)))
    put(1,0,nt(s00,W(2,1))+nt(s10,W(0,1)))
    put(1,1,nt(s00,W(2,2))+nt(s01,W(2,0))+nt(s10,W(0,2))+nt(s11,W(0,0)))
    diag(2); diag(3); ysend(2); ysend(3)
    gp=ld(gout,pl.ds(0,PX)).astype(bf)
    dattT[...]=nt(wv[R_PROJ:R_DOWN],gp).astype(bf)
    wv[R_PROJ:R_DOWN]=nn(attT[...],gp).astype(bf)
    def bh_part(h,at):
        r0,r1,r2=head_rows(h)
        ra_=pl.ds(pl.multiple_of(h*64,64),64)
        qT=trT[pl.ds(r0,64),0:PX]
        kT=trT[pl.ds(r1,64),at:at+PX]
        gT=dattT[ra_,:]
        pr=jnp.exp(nn(kT.T,qT)-lse[h,0:1])
        de=jnp.sum(gT.astype(f32)*attT[ra_,:].astype(f32),0,keepdims=True)
        ds=(pr*(nn(trT[pl.ds(r2,64),at:at+PX].T,gT)-de)).astype(bf)
        dtrT[pl.ds(r1,64),at:at+PX]=nt(qT,ds).astype(bf)
        dtrT[pl.ds(r2,64),at:at+PX]=nt(gT,pr.astype(bf)).astype(bf)
        return r0,nn(kT,ds)*0.125
    def bh(h,_):
        r0,dqT=bh_part(h,PX)
        acc[h]=dqT
        dtrT[pl.ds(r0,64),PX:2*PX]=jnp.zeros((64,PX),bf)
        return 0
    lax.fori_loop(0,6,bh,0)
    oth[1:17]=tn(dtrT[:,PX:2*PX],wqT[...]).astype(bf).reshape(16,32,CH)
    c1=xchg(oth.at[pl.ds(1,16)],oth.at[pl.ds(17,16)])
    def bh2(h,_):
        r0,dqT=bh_part(h,0)
        dtrT[pl.ds(r0,64),0:PX]=(acc[h]+dqT).astype(bf)
        return 0
    lax.fori_loop(0,6,bh2,0)
    gsec[...]=tn(dtrT[:,0:PX],wqT[...])
    dq=nt(ain[...].T,dtrT[...])
    for j in range(3):
        put3(cvt3,every(j,CH,3),dq[:,CH*j:CH*j+CH])
    wv[R_QKV:R_PROJ]=ld(cvt3,pl.ds(0,1152)).astype(bf)
    c1.wait()
    def n3_of(i): return (middle[pl.ds(i,64)]-mean3)*inv3
    def s3(i,c):
        j=pl.multiple_of(17+lax.div(i,32),1)
        v=gsec[pl.ds(i,64)]+oth[pl.ds(j,2)].reshape(64,CH).astype(f32)
        gsec[pl.ds(i,64)]=v
        return c[0]+col8(v),c[1]+col8(v*n3_of(i))
    a1,a2=cloop(PX,64,s3,(Z8(),Z8()))
    db3,dg3=row(a1),row(a2)
    c1=swap_sums(3,db3*g3,dg3*g3)
    esend[0]=ld(gout,edge)+inv3*(gsec[edge]*g3)
    c2=xchg(esend.at[0],erecv.at[0])
    xsend(2)
    c1.wait()
    m1,m2=total_sums(3)
    def f3(i,_):
        v=ld(gout,pl.ds(i,64))+inv3*(gsec[pl.ds(i,64)]*g3-m1-n3_of(i)*m2)
        fill3(z3,pl.multiple_of(i+32,32),v)
        return 0
    cloop(PX,64,f3,0)
    c_mid.wait()
    c2.wait()
    fill_edges(z3,erecv[0]-inv3*(m1+(hmid[...]-mean3)*inv3*m2))
    conv_dx(gsec,R_TWO)
    for dr in range(3):
        d=tn(x3b[32*dr:32*dr+PX],z3[32:32+PX,CH:2*CH]).astype(bf)
        wv[R_TWO+1152*dr:R_TWO+1152*dr+1152]=d
        if dr==0: wd[R_TWO:4304,0:CH]=d[0:4304-R_TWO]
    sibsend(1)
    def s2(i,c):
        n,af,pb=pre_b(inner[pl.ds(i,64)])
        gpre=gsec[pl.ds(i,64)]*slope(pb)
        gaff=gpre*sc1
        gsec[pl.ds(i,64)]=gaff
        return c[0]+col8(gpre*af),c[1]+col8(gpre),c[2]+col8(gaff*n),c[3]+col8(gaff)
    a1,a2,a3,a4=cloop(PX,64,s2,(Z8(),Z8(),Z8(),Z8()))
    dsc,dsh,dg2,db2=row(a1),row(a2),row(a3),row(a4)
    c1=swap_sums(4,db2*g2,dg2*g2)
    esend[1]=gsec[edge]*g2
    c2=xchg(esend.at[1],erecv.at[1])
    diag(1)
    first_halves(1)
    c1.wait()
    m1,m2=total_sums(4)
    def f2(i,_):
        n=(inner[pl.ds(i,64)]-mean2)*inv2
        fill3(z3,pl.multiple_of(i+32,32),inv2*(gsec[pl.ds(i,64)]*g2-m1-n*m2))
        return 0
    cloop(PX,64,f2,0)
    c2.wait()
    fill_edges(z3,inv2*(erecv[1]-m1-(hrecv[0]-mean2)*inv2*m2))
    for dr in range(3):
        wd[1152*dr:1152*dr+1152,0:CH]=tn(x3a[32*dr:32*dr+PX],z3[32:32+PX,CH:2*CH]).astype(bf)
    sibsend(0)
    second_halves(1)
    xsend(3,z<2)
    zstep(2,0)
    diag(0)
    first_halves(0)
    conv_dx(gsec,R_ONE)
    def s1(i,c):
        n=(img[pl.ds(i,64)].astype(f32)-mean1)*inv1
        gpre=gsec[pl.ds(i,64)]*slope(n*g1+b1)
        return c[0]+col8(gpre*n),c[1]+col8(gpre)
    a1,a2=cloop(PX,64,s1,(Z8(),Z8()))
    ge=[]
    for h in range(2):
        d=exact(jnp.broadcast_to(dsc,(16,CH)),wee[CH*h:CH*h+CH],nt)+exact(jnp.broadcast_to(dsh,(16,CH)),weo[CH*h:CH*h+CH],nt)
        ge.append(d[0:1]*slope(pre[h]))
    hot_level=(lax.broadcasted_iota(jnp.int32,(1,CH),1)==level[...]).astype(f32)
    pack_ref[...]=jnp.concatenate([row(a1),row(a2),dg2,db2,dg3,db3,dsc,dsh,ge[0],ge[1],emb[0],emb[1],consist*hot_level,jnp.broadcast_to(ids.astype(f32),(1,CH)),0.5*hot_level,jnp.zeros((1,CH),f32)],0)
    low=jnp.logical_not(top)
    cm.go(low,pack_ref,lpk.at[z],lps,lpr,b+4*(3-z),p)
    zstep(1,0)
    zstep(3,0)
    second_halves(0)
    xsend(3,z>=2)
    zstep(2,1)
    zstep(1,1)
    zstep(0,0)
    zstep(3,1)
    zstep(0,1)
    zstep(3,2)
    def packs_line():
        lpk[3]=pack_ref[...]
        wait_in(lpk.at[pl.ds(0,3)],lpr)
    pl.when(top)(packs_line)
    for d,bb,pp in plane:
        cm.go(top,lpk,ppk.at[mine],pps,ppr,bb,pp)
    def packs_plane():
        ppk[mine]=lpk[...]
        wait_in(ppk.at[pl.ds(0,7)],ppr)
        a_s=16*lax.div(ROWS*s,16)
        rows_at=lambda k: ppk[:,:,k,:].reshape(32,384)
        zero=jnp.zeros((64,384),f32)
        for h in range(2):
            e=rows_at(10+h)
            t=jnp.concatenate([e,e,zero],0).T
            cvt[pl.ds(BLK+768*h,384,stride=2),:]=t
            cvt[pl.ds(BLK+768*h+1,384,stride=2),:]=t
        r=a_s+lax.broadcasted_iota(jnp.int32,(BLK,128),0)
        l=lax.broadcasted_iota(jnp.int32,(BLK,128),1)
        inside=(r>=R_EMB)&(r<R_TAB)
        start=pl.multiple_of(jnp.clip(a_s-R_EMB+BLK,0,BLK+1536),16)
        lf=jnp.where(inside&(((r&1)==1)==(l>=32))&(l<64),cvt[pl.ds(start,BLK),:],0.0)
        ids=rows_at(13)[:,0:128].astype(jnp.int32)
        ids=jnp.concatenate([ids]*4,0).astype(f32).T[0:1].astype(jnp.int32)
        hot=(r-R_TAB==2*ids+(l>=96).astype(jnp.int32))&(l>=64)&(r>=R_TAB)
        lf=jnp.where(hot,1.0,lf)
        rg=jnp.concatenate([rows_at(6),rows_at(7),rows_at(8),rows_at(9)],0)
        gains=[jnp.sum(rows_at(k),0,keepdims=True) for k in range(6)]
        hi=lax.Precision.HIGHEST
        add=lax.dot_general(lf,rg,(((1,),(0,)),((),())),precision=hi,preferred_element_type=f32)
        for k in range(6): add=add+jnp.where(r[:,0:1]-R_GAIN==k,gains[k],0.0)
        rr=a_s+lax.broadcasted_iota(jnp.int32,(BLK,384),0)
        total[...]=jnp.where(rr<R_EMB,0.0,add)
    pl.when(top)(packs_plane)
    zstep(0,2)
    zend(1); zend(2); zend(3)
    zend(0)
    shift=lax.rem(9*s,16)
    tr_=lax.broadcasted_iota(jnp.int32,(BLK,1),0)
    t=jnp.where((tr_>=shift)&(tr_<shift+ROWS),total[...],0.0)
    sq=jnp.sum(jnp.sum(t*t,0,keepdims=True),1,keepdims=True)
    tile[...]=jnp.concatenate([jnp.broadcast_to(sq,(1,128)),pack_ref[12:13,0:128],pack_ref[14:15,0:128],jnp.zeros((5,128),f32)],0)
    red1[mine]=tile[...]
    for d,bb,pp in plane: cm.go(None,tile,red1.at[mine],n1s,n1r,bb,pp)
    t=pltpu.roll(total[...],lax.rem(BLK-shift,BLK),0)[0:ROWS]
    for j in range(3): cvt[pl.ds(j,ROWS,stride=3),:]=t[:,128*j:128*j+128]
    fcopy=pltpu.make_async_copy(cvt.at[pl.ds(0,1611)],flat_ref,own_sem)
    fcopy.start()
    wait_in(red1.at[pl.ds(0,7)],n1r)
    v=red1[0]
    for k in range(1,8): v=v+red1[k]
    red2[z]=v
    for k,zz in line: cm.go(None,red2.at[z],red2.at[z],n2s,n2r,b+4*(zz-z),p)
    wait_in(red2.at[pl.ds(0,3)],n2r)
    sums=red2[0]+red2[1]+red2[2]+red2[3]
    norm_ref[...]=jnp.sqrt(sums[0:1,0:1])
    lev_ref[...]=sums[1:3,0:LEVELS]
    def sent(ok,ref,sem):
        when(ok,lambda: pltpu.make_async_copy(ref,ref,sem).wait())
    block=sibr.at[0]
    for zz in range(4):
        went=(None,None,is2,z!=2)[zz]
        for sem in (axs,ays,ads): sent(went,block,sem.at[zz])
        sent(None,sibr.at[pl.ds(0,4)],ass.at[zz])
        if zz<3:
            sent(None,sibr.at[pl.ds(0,4)],s1s.at[zz])
        else:
            sent(core==1,sibr.at[pl.ds(0,2)],s1s.at[zz])
        sent(need(zz,1-y,xn),block,ds_.at[zz])
        sent(need(zz,y,xn),block,rxs.at[zz])
        sent(need(zz,1-y,p),block,rys.at[zz])
        sent(AND(need(zz,y,p),z!=zz),block,zs.at[zz])
    sent(z<3,block,azs.at[0,0])
    sent(z>0,block,azs.at[3,1])
    sent(is1|is2,block,azs.at[1,0])
    sent(is1,block,azs.at[1,1])
    sent(is2,sibr.at[pl.ds(0,4)],a2s.at[0])
    sent(is1|is2,sibr.at[pl.ds(0,4)],a2s.at[1])
    sent(top,sibr.at[pl.ds(0,3)],a3s)
    sent(has_gains,blk.at[pl.ds(0,48)],gls)
    sent(gain_line,blk.at[pl.ds(0,112)],gps)
    sent(low,pack_ref,lps)
    sent(top,ppk.at[pl.ds(0,7)],pps)
    sent(None,red1.at[pl.ds(0,7)],n1s)
    sent(None,red2.at[pl.ds(0,3)],n2s)
    fcopy.wait()

def step(images_all,mast,img,tgt,cln,vgg,lin,tvec,rowid,level):
    D=pltpu.SemaphoreType.DMA
    V=lambda *s: pltpu.VMEM(s,bf)
    F=lambda *s: pltpu.VMEM(s,f32)
    vm=pl.BlockSpec(memory_space=pltpu.VMEM)
    return pl.pallas_call(functools.partial(step_kernel,images_all),
        out_shape=(jax.ShapeDtypeStruct((1611,128),f32),jax.ShapeDtypeStruct((1,1),f32),jax.ShapeDtypeStruct((2,LEVELS),f32),jax.ShapeDtypeStruct((32,BLK,CH),bf)),
        in_specs=[pl.BlockSpec(memory_space=pl.ANY)]+[vm]*8,
        out_specs=(pl.BlockSpec(memory_space=pl.ANY),vm,vm,pl.BlockSpec(memory_space=pl.ANY)),
        scratch_shapes=[V(17184,CH),V(32,32,CH),F(4608,128),F(5,CH,128),V(4304,CH2),V(768,CH),V(768,CH),V(1152,CH),V(576,1152),V(576,1152),V(576,1152),F(PX,CH),F(PX,CH),F(3,PX,128),F(PX,CH),V(1024,CH),V(1152,1024),V(1152,1024),V(CH,PX),V(128,3456),F(6,8,PX),V(CH,PX),F(5,8,CH),F(5,8,CH),V(1,32,CH),F(1,32,CH),V(32,CH),V(16,CH2),V(16,CH2),F(3,32,128),V(33,32,CH),D((4,)),D((4,)),D((15,)),D((15,)),F(BLK,CH),V(BLK,CH),D,D((4,2)),D((4,2)),D((4,)),D((4,2)),D((4,)),D((4,2)),D((4,)),D((4,)),D((4,)),D((4,)),F(16,CH),F(4,16,CH),F(8,4,16,CH),F(8,8,128),F(4,8,128),F(8,128),D,D,D,D,D,D,D,D,V(14,BLK,CH),V(4,BLK-HALF,CH),V(4,BLK,CH),V(4,BLK,CH),V(3,BLK,CH),V(3,BLK,CH),D((4,)),D((4,2,2)),D((4,)),D((4,)),D((4,)),D((4,2)),D((4,)),D((4,2)),D((4,)),D((6,)),D((12,)),F(6,64,PX),V(16,CH),D,D,D,D,V(4,HALF,CH),D((2,)),D((2,2,2)),D((4,)),D((4,)),F(32,CH),F(2,32,CH),F(2,32,CH),V(CH,CH),D,D((2,2,2))],
        compiler_params=pltpu.CompilerParams(collective_id=0,has_side_effects=True,vmem_limit_bytes=63<<20),
        name="train_step",
    )(mast,img,tgt,cln,vgg,lin,tvec,rowid,level)


def fast(images, target, clean_images, levels, labels, null_mask, vgg_proj, lpips_lin, master, first_moment, second_moment):
    row_index = jnp.where(null_mask == 1, CLASSES, labels).reshape(1, 1)
    tvec = time_vector(levels)
    own_grad, norm, level_sums, _ = step(
        16,
        master.reshape(1611, 128),
        images.reshape(PX, CH),
        target.reshape(128, CH2),
        clean_images.reshape(128, CH2),
        vgg_proj,
        lpips_lin.reshape(1, 256),
        tvec,
        row_index,
        levels.reshape(1, 1),
    )
    own_grad = own_grad.reshape(-1)
    norm_before = norm.reshape(())
    clipped = own_grad * jnp.minimum(1.0, CLIP / norm_before)
    new_first = BETA_ONE * first_moment + (1.0 - BETA_ONE) * clipped
    new_second = BETA_TWO * second_moment + (1.0 - BETA_TWO) * clipped * clipped
    fixed_first = new_first / (1.0 - BETA_ONE**STEP)
    fixed_second = new_second / (1.0 - BETA_TWO**STEP)
    new_master = master - RATE * (fixed_first / (jnp.sqrt(fixed_second) + EPS_ADAM) + DECAY * master)
    return (new_master, new_first, new_second, new_master.astype(jnp.bfloat16), norm_before, level_sums)


def solution(mesh):
    small = mesh.shape["batch"] == 16 and mesh.shape["pix"] == 2
    return jax.shard_map(
        fast if small else local,
        mesh=mesh,
        in_specs=(
            P("batch", "pix", None, None),
            P("batch", "pix", None, None),
            P("batch", "pix", None, None),
            P("batch"),
            P("batch"),
            P("batch"),
            P(),
            P(),
            P(("batch", "pix")),
            P(("batch", "pix")),
            P(("batch", "pix")),
        ),
        out_specs=(
            P(("batch", "pix")),
            P(("batch", "pix")),
            P(("batch", "pix")),
            P(("batch", "pix")),
            P(),
            P(),
        ),
        check_vma=False,
    )
```

```python
import functools
import math

import jax
import jax.numpy as jnp
from jax import lax
from jax.experimental import pallas as pl
from jax.experimental.pallas import tpu as pltpu
from jax.sharding import PartitionSpec as P

CH = 384
CH2 = 576
GROUPS = 32
HEAD = 64
TEMB = 768
CLASSES = 1000
LEVELS = 40
STEP = 10


EPS_NORM = 1e-05
EPS_FEAT = 1e-06
BETA_ONE = 0.9
BETA_TWO = 0.999
EPS_ADAM = 1e-08
RATE = 0.02
DECAY = 0.01
CLIP = 0.01
precise = lax.Precision.HIGHEST


def extended(shard, sides, width):
    for axis, dim in sides:
        size, length = (lax.axis_size(axis), shard.shape[dim])
        up = [(i, (i + 1) % size) for i in range(size - 1)]
        down = [(j, i) for i, j in up]
        last = lax.slice_in_dim(shard, length - width, length, axis=dim)
        initial = lax.slice_in_dim(shard, 0, width, axis=dim)
        before = lax.ppermute(last, axis, up)
        after = lax.ppermute(initial, axis, down)
        shard = jnp.concatenate([before, shard, after], axis=dim)
    return shard


def unpack(flat_vec):
    layout = [
        (9 * CH, CH),
        (9 * CH, CH),
        (CH, 3 * CH),
        (CH, CH),
        (9 * CH, CH2),
        (TEMB, 2 * CH),
        (CLASSES + 1, TEMB),
        (6, CH),
    ]
    pieces = []
    offset = 0
    for rows_n, cols_n in layout:
        pieces.append(flat_vec[offset : offset + rows_n * cols_n].reshape(rows_n, cols_n))
        offset += rows_n * cols_n
    return (pieces, offset)


def time_vector(level_ids):
    half_width = TEMB // 2
    frequency = jnp.exp(-math.log(10000.0) * jnp.arange(half_width, dtype=jnp.float32) / half_width)
    angles = level_ids.astype(jnp.float32)[..., None] * (1000.0 / LEVELS) * frequency
    return jnp.concatenate([jnp.cos(angles), jnp.sin(angles)], -1)


def silu_slope(values):
    sigmoid = jax.nn.sigmoid(values)
    return sigmoid * (1.0 + values * (1.0 - sigmoid))


def pix_sums(pair_sums):
    return lax.psum((pair_sums[0], pair_sums[1]), "pix")


def group_forward(values, pixels_all):
    grouped = values.reshape(values.shape[0], values.shape[1], GROUPS, -1)
    totals = pix_sums((jnp.sum(grouped, (1, 3)), jnp.sum(grouped * grouped, (1, 3))))
    per_group = pixels_all * grouped.shape[3]
    center = totals[0] / per_group
    spread = totals[1] / per_group - center * center
    inverse = lax.rsqrt(spread + EPS_NORM)
    normed = (grouped - center[:, None, :, None]) * inverse[:, None, :, None]
    return (normed.reshape(values.shape), inverse)


def group_backward(grad_normed, normed, inverse, pixels_all):
    grad_grouped = grad_normed.reshape(normed.shape[0], normed.shape[1], GROUPS, -1)
    val_grouped = normed.reshape(grad_grouped.shape)
    totals = pix_sums((jnp.sum(grad_grouped, (1, 3)), jnp.sum(grad_grouped * val_grouped, (1, 3))))
    per_group = pixels_all * grad_grouped.shape[3]
    result = (
        grad_grouped
        - (totals[0] / per_group)[:, None, :, None]
        - val_grouped * (totals[1] / per_group)[:, None, :, None]
    )
    return (result * inverse[:, None, :, None]).reshape(normed.shape)


def columns_of(values, stride):
    rows_out = values.shape[1] // stride
    cols_out = values.shape[2] // stride
    span_rows = stride * (rows_out - 1) + 1
    span_cols = stride * (cols_out - 1) + 1
    padded = extended(values, (("pix", 1),), 1)
    padded = jnp.pad(padded, ((0, 0), (0, 0), (1, 1), (0, 0)))
    return jnp.concatenate(
        [
            padded[
                :, row_off : row_off + span_rows : stride, col_off : col_off + span_cols : stride, :
            ]
            for row_off in range(3)
            for col_off in range(3)
        ],
        -1,
    )


def conv_forward(values, weight, rows_in, stride):
    n_img, pixels_in, in_chan = values.shape
    columns = columns_of(values.reshape(n_img, rows_in, -1, in_chan), stride)
    result = jnp.dot(columns.reshape(-1, 9 * in_chan), weight, preferred_element_type=jnp.float32)
    return (result.reshape(n_img, -1, weight.shape[1]), columns)


def conv_back(columns, grad_low, weight, rows_in, stride):
    n_img, pix_out, out_chan = grad_low.shape
    in_chan = weight.shape[0] // 9
    d_weight = jnp.einsum(
        "rk,rc->kc",
        columns.reshape(-1, 9 * in_chan),
        grad_low.reshape(-1, out_chan),
        preferred_element_type=jnp.float32,
    )
    flipped = (
        weight.reshape(3, 3, in_chan, out_chan)[::-1, ::-1]
        .transpose(0, 1, 3, 2)
        .reshape(9 * out_chan, in_chan)
    )
    rows_out = rows_in // stride
    grid_grad = grad_low.reshape(n_img, rows_out, pix_out // rows_out, out_chan)
    if stride > 1:
        grid_grad = jnp.pad(
            grid_grad[:, :, None, :, None, :],
            ((0, 0), (0, 0), (0, stride - 1), (0, 0), (0, stride - 1), (0, 0)),
        )
        grid_grad = grid_grad.reshape(n_img, rows_in, -1, out_chan)
    grad_columns = columns_of(grid_grad, 1)
    grad_input = jnp.dot(
        grad_columns.reshape(-1, 9 * out_chan), flipped, preferred_element_type=jnp.float32
    )
    return (d_weight, grad_input.reshape(n_img, -1, in_chan))


def res_forward(values, gain_rows, scale, shift, w_first, w_second, rows_in, pixels_all):
    normed_a, inverse_a = group_forward(values, pixels_all)
    pre_a = normed_a * gain_rows[0] + gain_rows[1]
    act_a = jax.nn.silu(pre_a).astype(jnp.bfloat16)
    inner, columns_a = conv_forward(act_a, w_first, rows_in, 1)
    normed_b, inverse_b = group_forward(inner, pixels_all)
    affine_b = normed_b * gain_rows[2] + gain_rows[3]
    pre_b = affine_b * (1.0 + scale) + shift
    second = jax.nn.silu(pre_b).astype(jnp.bfloat16)
    branch, columns_b = conv_forward(second, w_second, rows_in, 1)
    kept_state = (
        normed_a,
        inverse_a,
        pre_a,
        columns_a,
        normed_b,
        inverse_b,
        affine_b,
        pre_b,
        columns_b,
    )
    return (values + branch, kept_state)


def res_back(grad_result, kept_state, gain_rows, scale, w_first, w_second, rows_in, pixels_all):
    normed_a, inverse_a, pre_a, columns_a, normed_b, inverse_b, affine_b, pre_b, columns_b = (
        kept_state
    )
    d_w_second, grad_second = conv_back(
        columns_b, grad_result.astype(jnp.bfloat16), w_second, rows_in, 1
    )
    grad_pre_b = grad_second * silu_slope(pre_b)
    d_scale = jnp.sum(grad_pre_b * affine_b, 1)
    d_shift = jnp.sum(grad_pre_b, 1)
    grad_affine = grad_pre_b * (1.0 + scale)
    d_gain_b = jnp.sum(grad_affine * normed_b, (0, 1))
    d_bias_b = jnp.sum(grad_affine, (0, 1))
    grad_inner = group_backward(grad_affine * gain_rows[2], normed_b, inverse_b, pixels_all).astype(
        jnp.bfloat16
    )
    d_w_first, grad_act = conv_back(columns_a, grad_inner, w_first, rows_in, 1)
    grad_pre_a = grad_act * silu_slope(pre_a)
    d_gain_a = jnp.sum(grad_pre_a * normed_a, (0, 1))
    d_bias_a = jnp.sum(grad_pre_a, (0, 1))
    grad_values = None
    d_gains = jnp.stack([d_gain_a, d_bias_a, d_gain_b, d_bias_b])
    return (d_w_first, d_w_second, d_gains, d_scale, d_shift, grad_values)


def to_heads(values):
    return lax.all_to_all(values, "pix", split_axis=2, concat_axis=1, tiled=True)


def to_pixels(values):
    return lax.all_to_all(values, "pix", split_axis=1, concat_axis=2, tiled=True)


def flat_heads(values):
    return values.reshape(-1, values.shape[2], values.shape[3])


def attend(queries, keys, values):
    root_dim = math.sqrt(queries.shape[-1])

    def single(bundle):
        q_one, k_one, v_one = bundle
        scores = (
            jnp.einsum("qd,kd->qk", q_one, k_one, preferred_element_type=jnp.float32) / root_dim
        )
        row_peak = jnp.max(scores, -1, keepdims=True)
        exp_scores = jnp.exp(scores - row_peak)
        sum_exp = jnp.sum(exp_scores, -1, keepdims=True)
        probabilities = (exp_scores / sum_exp).astype(jnp.bfloat16)
        attended = jnp.einsum("qk,kd->qd", probabilities, v_one, preferred_element_type=jnp.float32)
        return (attended.astype(jnp.bfloat16), row_peak + jnp.log(sum_exp))

    attended, log_total = lax.map(
        single, (flat_heads(queries), flat_heads(keys), flat_heads(values))
    )
    return (attended.reshape(queries.shape), log_total)


def attend_back(queries, keys, values, log_total, grad_out):
    root_dim = math.sqrt(queries.shape[-1])

    def single(bundle):
        q_one, k_one, v_one, lse_one, g_one = bundle
        scores = (
            jnp.einsum("qd,kd->qk", q_one, k_one, preferred_element_type=jnp.float32) / root_dim
        )
        probabilities = jnp.exp(scores - lse_one)
        grad_v = jnp.einsum(
            "qk,qd->kd",
            probabilities.astype(jnp.bfloat16),
            g_one,
            preferred_element_type=jnp.float32,
        )
        grad_p = jnp.einsum("qd,kd->qk", g_one, v_one, preferred_element_type=jnp.float32)
        inner_sum = jnp.sum(probabilities * grad_p, -1, keepdims=True)
        grad_s = (probabilities * (grad_p - inner_sum)).astype(jnp.bfloat16)
        grad_q = (
            jnp.einsum("qk,kd->qd", grad_s, k_one, preferred_element_type=jnp.float32) / root_dim
        )
        grad_k = (
            jnp.einsum("qk,qd->kd", grad_s, q_one, preferred_element_type=jnp.float32) / root_dim
        )
        return (grad_q, grad_k, grad_v)

    grad_q, grad_k, grad_v = lax.map(
        single,
        (
            flat_heads(queries),
            flat_heads(keys),
            flat_heads(values),
            log_total,
            flat_heads(grad_out),
        ),
    )
    return (grad_q.reshape(queries.shape), grad_k.reshape(keys.shape), grad_v.reshape(values.shape))


def local(
    images,
    target,
    clean_images,
    levels,
    labels,
    null_mask,
    vgg_proj,
    lpips_lin,
    master,
    first_moment,
    second_moment,
):
    gathered = lax.all_gather(master.astype(jnp.bfloat16), ("batch", "pix"), axis=0, tiled=True)
    pieces, used_len = unpack(gathered)
    w_one, w_two, w_qkv, w_proj, w_down, w_emb, class_table, gains_low = pieces
    gains_one = gains_low.astype(jnp.float32)
    n_img, rows_local, cols_local, channels = images.shape
    wide_channels = w_down.shape[1]
    pix_count = lax.axis_size("pix")
    batch_count = lax.axis_size("batch")
    pixels_here = rows_local * cols_local
    pixels_all = pixels_here * pix_count
    pixels_all_two = pixels_all // 4
    images_all = n_img * batch_count
    row_index = jnp.where(null_mask == 1, class_table.shape[0] - 1, labels)
    one_hot = (
        row_index[:, None] == jnp.arange(class_table.shape[0], dtype=jnp.int32)[None, :]
    ).astype(jnp.float32)
    pre_embed = time_vector(levels) + jnp.dot(
        one_hot, class_table.astype(jnp.float32), precision=precise
    )
    embedded = jax.nn.silu(pre_embed)
    w_emb_wide = w_emb.astype(jnp.float32)
    scale_shift = jnp.dot(embedded, w_emb_wide, precision=precise)
    scale_one = scale_shift[:, None, :channels]
    shift_one = scale_shift[:, None, channels:]
    flat_in = images.astype(jnp.float32).reshape(n_img, pixels_here, channels)
    middle, kept_one = res_forward(
        flat_in, gains_one, scale_one, shift_one, w_one, w_two, rows_local, pixels_all
    )
    normed_three, inverse_three = group_forward(middle, pixels_all)
    attn_in = (normed_three * gains_one[4] + gains_one[5]).astype(jnp.bfloat16)
    triples = jnp.dot(attn_in.reshape(-1, channels), w_qkv, preferred_element_type=jnp.float32)
    triples = triples.astype(jnp.bfloat16).reshape(n_img, pixels_here, 3 * channels)
    spread_heads = to_heads(triples)
    local_heads = spread_heads.shape[2] // (3 * HEAD)
    split_heads = spread_heads.reshape(n_img, -1, local_heads, 3, HEAD).transpose(3, 0, 2, 1, 4)
    queries, keys, values = (split_heads[0], split_heads[1], split_heads[2])
    attended, log_total = attend(queries, keys, values)
    attended_px = to_pixels(attended.transpose(0, 2, 1, 3).reshape(n_img, -1, local_heads * HEAD))
    projected = jnp.dot(
        attended_px.reshape(-1, channels), w_proj, preferred_element_type=jnp.float32
    )
    output = middle + projected.reshape(n_img, pixels_here, channels)
    final_out, columns_down = conv_forward(output.astype(jnp.bfloat16), w_down, rows_local, 2)
    pixels_two = final_out.shape[1]
    feat_width = vgg_proj.shape[1]
    online_feat = jnp.dot(
        final_out.astype(jnp.bfloat16).reshape(-1, wide_channels),
        vgg_proj,
        preferred_element_type=jnp.float32,
    )
    online_feat = online_feat.reshape(n_img, pixels_two, feat_width)
    target_feat = jnp.dot(
        target.reshape(-1, wide_channels), vgg_proj, preferred_element_type=jnp.float32
    )
    target_feat = target_feat.reshape(n_img, pixels_two, feat_width)
    target_unit = target_feat * lax.rsqrt(
        jnp.mean(target_feat * target_feat, -1, keepdims=True) + EPS_FEAT
    )
    clean_wide = clean_images.astype(jnp.float32).reshape(n_img, pixels_two, wide_channels)

    def loss_terms(feature, out_value):
        unit = feature * lax.rsqrt(jnp.mean(feature * feature, -1, keepdims=True) + EPS_FEAT)
        consist = jnp.sum(lpips_lin * (unit - target_unit) ** 2, (1, 2)) / (
            feat_width * pixels_all_two
        )
        denoise = jnp.sum((out_value - clean_wide) ** 2, (1, 2)) / (pixels_all_two * wide_channels)
        return (consist, denoise)

    (consist, denoise), pullback = jax.vjp(loss_terms, online_feat, final_out)
    level_hot = (levels[:, None] == jnp.arange(LEVELS, dtype=jnp.int32)[None, :]).astype(
        jnp.float32
    )
    level_pair = lax.psum(
        (jnp.sum(consist[:, None] * level_hot, 0), jnp.sum(level_hot / pix_count, 0)),
        ("batch", "pix"),
    )
    zero_count = level_pair[1][0]
    is_zero = (levels == 0).astype(jnp.float32)
    grad_feat, grad_out = pullback(
        (jnp.full_like(consist, 1.0 / images_all), is_zero / jnp.maximum(zero_count, 1.0))
    )
    grad_feat_low = grad_feat.astype(jnp.bfloat16).reshape(-1, feat_width)
    grad_final = grad_out + jnp.einsum(
        "rf,cf->rc", grad_feat_low, vgg_proj, preferred_element_type=jnp.float32
    ).reshape(n_img, pixels_two, wide_channels)
    d_w_down, grad_output = conv_back(
        columns_down, grad_final.astype(jnp.bfloat16), w_down, rows_local, 2
    )
    grad_proj = grad_output.astype(jnp.bfloat16).reshape(-1, channels)
    d_w_proj = jnp.einsum(
        "rc,rd->cd",
        attended_px.reshape(-1, channels),
        grad_proj,
        preferred_element_type=jnp.float32,
    )
    grad_att_px = jnp.einsum("rd,cd->rc", grad_proj, w_proj, preferred_element_type=jnp.float32)
    grad_att_px = grad_att_px.astype(jnp.bfloat16).reshape(n_img, pixels_here, channels)
    grad_heads = to_heads(grad_att_px)
    grad_split = grad_heads.reshape(n_img, -1, local_heads, HEAD).transpose(0, 2, 1, 3)
    grad_q, grad_k, grad_v = attend_back(queries, keys, values, log_total, grad_split)
    grad_triples = jnp.stack([grad_q, grad_k, grad_v], 3).transpose(0, 2, 1, 3, 4)
    grad_triples = grad_triples.reshape(n_img, -1, local_heads * 3 * HEAD).astype(jnp.bfloat16)
    grad_triples = to_pixels(grad_triples)
    grad_rows = grad_triples.reshape(-1, 3 * channels)
    d_w_qkv = jnp.einsum(
        "rc,rd->cd", attn_in.reshape(-1, channels), grad_rows, preferred_element_type=jnp.float32
    )
    grad_attn_in = jnp.einsum(
        "rd,cd->rc", grad_rows, w_qkv, preferred_element_type=jnp.float32
    ).reshape(n_img, pixels_here, channels)
    d_gain_three = jnp.sum(grad_attn_in * normed_three, (0, 1))
    d_bias_three = jnp.sum(grad_attn_in, (0, 1))
    grad_middle = grad_output + group_backward(
        grad_attn_in * gains_one[4], normed_three, inverse_three, pixels_all
    )
    d_w_one, d_w_two, d_gains_one, d_scale_one, d_shift_one, unused_grad = res_back(
        grad_middle, kept_one, gains_one, scale_one, w_one, w_two, rows_local, pixels_all
    )
    grad_scale_shift = jnp.concatenate([d_scale_one, d_shift_one], 1)
    d_w_emb = jnp.dot(embedded.T, grad_scale_shift, precision=precise)
    grad_embedded = jnp.dot(grad_scale_shift, w_emb_wide.T, precision=precise)
    d_table = jnp.dot(one_hot.T, grad_embedded * silu_slope(pre_embed), precision=precise)
    d_norms_one = jnp.concatenate([d_gains_one, jnp.stack([d_gain_three, d_bias_three])], 0)
    flat_grad = jnp.concatenate(
        [
            d_w_one.ravel(),
            d_w_two.ravel(),
            d_w_qkv.ravel(),
            d_w_proj.ravel(),
            d_w_down.ravel(),
            d_w_emb.ravel(),
            d_table.ravel(),
            d_norms_one.ravel(),
            jnp.zeros((gathered.shape[0] - used_len,), jnp.float32),
        ]
    )
    own_grad = lax.psum_scatter(flat_grad, ("batch", "pix"), scatter_dimension=0, tiled=True)
    norm_before = jnp.sqrt(lax.psum(jnp.sum(own_grad * own_grad), ("batch", "pix")))
    clipped = own_grad * jnp.minimum(1.0, CLIP / norm_before)
    new_first = BETA_ONE * first_moment + (1.0 - BETA_ONE) * clipped
    new_second = BETA_TWO * second_moment + (1.0 - BETA_TWO) * clipped * clipped
    fixed_first = new_first / (1.0 - BETA_ONE**STEP)
    fixed_second = new_second / (1.0 - BETA_TWO**STEP)
    new_master = master - RATE * (
        fixed_first / (jnp.sqrt(fixed_second) + EPS_ADAM) + DECAY * master
    )
    level_sums = jnp.stack([level_pair[0], level_pair[1]])
    return (
        new_master,
        new_first,
        new_second,
        new_master.astype(jnp.bfloat16),
        norm_before,
        level_sums,
    )


MESH = pl.DeviceIdType.MESH
ROWS=537; BLK=560; HALF=288
PX=512
R_ONE,R_TWO,R_QKV,R_PROJ,R_DOWN,R_EMB,R_TAB,R_GAIN,R_END=0,3456,6912,8064,8448,13632,15168,17170,17184
f32=jnp.float32; bf=jnp.bfloat16
class Comm:
    def __init__(self): self.sent=[]
    def go(self, cond, src, dst, ssem, rsem, b, p):
        c = pltpu.make_async_remote_copy(src_ref=src,dst_ref=dst,send_sem=ssem,recv_sem=rsem,device_id=(b,p),device_id_type=MESH)
        if cond is None: c.start()
        else: pl.when(cond)(lambda: c.start())
        self.sent.append((cond,c))
    def drain(self):
        for cond,c in self.sent:
            if cond is None: c.wait_send()
            else: pl.when(cond)(lambda c=c: c.wait_send())
        self.sent=[]

def place():
    b=lax.axis_index("batch"); p=lax.axis_index("pix")
    core=lax.rem(b,2); y=lax.rem(lax.div(b,2),2); z=lax.div(b,4)
    return b,p,core,y,z

def base_of(s): return 16*((ROWS*s)//16)
def dg(a,b,ca,cb): return lax.dot_general(a,b,(((ca,),(cb,)),((),())),preferred_element_type=f32)
def nn(a,b): return dg(a,b,1,0)
def nt(a,b): return dg(a,b,1,1)
def tn(a,b): return dg(a,b,0,0)
def split3(v):
    hi=v.astype(bf); r=v-hi.astype(f32); mid=r.astype(bf); lo=(r-mid.astype(f32)).astype(bf)
    return hi,mid,lo
def exact(v,w,dot):
    hi,mid,lo=split3(v)
    return dot(hi,w)+dot(mid,w)+dot(lo,w)
def sigmoid(v): return 1.0/(1.0+jnp.exp(-v))
def silu(v): return v*sigmoid(v)
def slope(v):
    s=sigmoid(v)
    return s*(1.0+v*(1.0-s))
def cloop(n,chunk,body,init):
    return lax.fori_loop(0,n//chunk,lambda i,c: body(pl.multiple_of(i*chunk,chunk),c),init)
def col8(v): return jnp.sum(v.reshape(-1,8,v.shape[-1]),axis=0)
Z8=lambda: jnp.zeros((8,CH),f32)
class Blocks:
    def __init__(self,ref,n): self.ref=ref; self.n=n
def at_block(ref,j,sl):
    if isinstance(ref,Blocks): return ref.ref,(pl.ds(ref.n*j+sl.start,sl.size,stride=sl.stride),slice(None))
    return ref,(j,sl,slice(None))
def ld(ref,sl):
    out=[]
    for j in range(ref.ref.shape[0]//ref.n if isinstance(ref,Blocks) else ref.shape[0]):
        r,k=at_block(ref,j,sl)
        out.append(r[k])
    return jnp.concatenate(out,1)
def put3(ref,sl,v):
    for j in range(v.shape[1]//128):
        r,k=at_block(ref,j,sl)
        r[k]=v[:,128*j:128*j+128]
def every(start,n,step): return pl.ds(start,n,stride=step)
def row(v): return jnp.sum(v,axis=0,keepdims=True)


LAST=25
def step_kernel(images_all,
    mast,img,tgt,cln,vgg,lin,tvec,rowid,level,
    flat_ref,norm_ref,lev_ref,g_ref,
    wv,tails,cvt,cvt2,wd,wee,weo,wqT,x3a,x3b,z3,inner,middle,gout,gsec,ain,trT,dtrT,attT,xd,lse,dattT,ssend,srecv,hsend,hrecv,himg,dzs,dzr,geo,oth,wsem,tsem,xs,xr,total,blk,own_sem,azs,azr,axs,axr,ays,ayr,adar,adbr,ass,asr,pack_ref,lpk,ppk,red1,red2,tile,lps,lpr,pps,ppr,n1s,n1r,n2s,n2r,sibr,rb,rx,ry,zu,zd,s1s,s1r,dar,dbr,rxs,rxr,rys,ryr,zs,zur,zdr,acc,gtile,gls,glr,gps,gpr,rba,a2s,a2r,ads,ds_,hmid,esend,erecv,gm,a3s,a3r):
    b,p,core,y,z=place()
    q=1-p; xn=q; s=b*2+p
    pf=p.astype(f32); qf=1.0-pf
    yn=b+2-4*y; sib=b+1-2*core; oc=1-core
    up_ok=z<3; dn_ok=z>0
    top=z==3
    mine=(y*2+core)*2+p
    cvt3=Blocks(cvt,1536)
    mcopy=pltpu.make_async_copy(mast,cvt.at[pl.ds(0,1611)],own_sem)
    mcopy.start()
    barrier=pltpu.get_barrier_semaphore()
    plane=[]
    for dy in range(2):
        for dc in range(2):
            for dp in range(2):
                if dy+dc+dp: plane.append((4*dy+2*dc+dp,z*4+lax.rem(y+dy,2)*2+lax.rem(core+dc,2),lax.rem(p+dp,2)))
    line=[(k,lax.rem(z+k,4)) for k in range(1,4)]
    def sig(bb,pp): pl.semaphore_signal(barrier,inc=1,device_id=(bb,pp),device_id_type=MESH)
    for _,bb,pp in plane: sig(bb,pp)
    for _,zz in line: sig(b+4*(zz-z),p)
    def when(ok,f):
        if ok is None: f()
        else: pl.when(ok)(f)
    def AND(*c):
        r=None
        for k in c:
            if k is not None: r=k if r is None else r&k
        return r
    def wait_in(ref,sem):
        pltpu.make_async_remote_copy(src_ref=ref,dst_ref=ref,send_sem=sem,recv_sem=sem,device_id=(b,xn),device_id_type=MESH).wait_recv()
    def slot(zz,yy,pp,cc=core): return ((zz*2+yy)*2+cc)*2+pp
    A=pl.ds(0,HALF); B=pl.ds(HALF,BLK-HALF)
    cm=Comm()
    shift=lax.rem(9*s,16)
    total[ROWS-1:BLK]=jnp.zeros((BLK-ROWS+1,CH),f32)
    mcopy.wait()
    for j in range(3): total[0:ROWS,128*j:128*j+128]=cvt[pl.ds(j,ROWS,stride=3),:]
    at=lax.broadcasted_iota(jnp.int32,(BLK,CH),0)
    blk[...]=jnp.where(at==BLK-4,(level[...]==0).astype(f32),pltpu.roll(total[...],shift,0)).astype(bf)
    own=pltpu.make_async_copy(blk,g_ref.at[s],own_sem)
    own.start()
    pl.semaphore_wait(barrier,10)
    def valid(zz): return (zz>=0)&(zz<4)
    def pick(c0,c1,c2,c3): return jnp.where(z==0,c0,jnp.where(z==1,c1,jnp.where(z==2,c2,c3)))
    hs=(A,B)
    ends=(z==0)|(z==3); is1=z==1; is2=z==2; inner_z=jnp.logical_not(ends)
    def z_send(ok,zz,h,d,src=None):
        g=g_ref.at[slot(zz,y,p),hs[h]]
        cm.go(ok,g if src is None else src,g,azs.at[zz,(1-d)//2],azr.at[zz,h],b+4*d,p)
    def xy_send(ok,zz,h,src=None):
        g=g_ref.at[slot(zz,y,p),hs[h]]
        cm.go(ok,g if src is None else src,g,axs.at[zz],axr.at[zz,h],b,xn)
        cm.go(ok,g if src is None else src,g,ays.at[zz],ayr.at[zz,h],yn,p)
    def sib_send(ok,zz,yy,pp,h,src=None):
        sl=slot(zz,yy,pp)
        first=pl.multiple_of(16*lax.div(ROWS*sl,16),16)
        def part(lo,n):
            return g_ref.at[sl,pl.ds(lo,n)] if src is None else src.at[pl.ds(lo-(HALF if h else 0),n)]
        lo,n=(0,HALF) if h==0 else (HALF,528-HALF)
        cm.go(ok,part(lo,n),wv.at[pl.ds(first+lo,n)],ass.at[zz],asr.at[zz],sib,p)
        if h==1: cm.go(ok,part(528,32),tails.at[sl],ass.at[zz],asr.at[zz],sib,p)
    def own_sends():
        for h in range(2):
            src=blk.at[hs[h]]
            z_send(z==0,z,h,1,src)
            z_send(z==3,z,h,-1,src)
            sib_send(None,z,y,p,h,src)
    def own_xy():
        for h in range(2): xy_send(z!=1,z,h,blk.at[hs[h]])
    four=((1-y,xn),(y,xn),(1-y,p),(y,p))
    def two_send(ok,i,d):
        yy,pp=four[i]
        for h in range(2):
            g=g_ref.at[slot(2,yy,pp),hs[h]]
            cm.go(ok,g,g,a2s.at[(1-d)//2],a2r.at[yy,pp,h],b+4*d,p)
    def two_in(i,ok):
        yy,pp=four[i]
        for h in range(2):
            g=g_ref.at[slot(2,yy,pp),hs[h]]
            when(ok,lambda: wait_in(g,a2r.at[yy,pp,h]))
            cm.go(ok&(z==1),g,g,a2s.at[1],a2r.at[yy,pp,h],b-4,p)
            sib_send(ok,2,yy,pp,h)
    def three_out(i):
        yy,pp=four[i]
        for h in range(2):
            g=g_ref.at[slot(3,yy,pp),hs[h]]
            cm.go(top,g,g,a3s,a3r.at[yy,pp,h],b-4,p)
    def three_in(i):
        yy,pp=four[i]
        for h in range(2):
            g=g_ref.at[slot(3,yy,pp),hs[h]]
            when(is2,lambda: wait_in(g,a3r.at[yy,pp,h]))
            sib_send(is2,3,yy,pp,h)
    def diag_in(ok,zz):
        sd=slot(zz,1-y,xn)
        def f():
            wait_in(g_ref.at[sd,A],adar.at[zz])
            wait_in(g_ref.at[sd,B],adbr.at[zz])
        when(ok,f)
        for h in range(2): sib_send(ok,zz,1-y,xn,h)
    def two_diag():
        sd=slot(2,1-y,xn)
        def f():
            wait_in(g_ref.at[sd,A],adar.at[2])
            wait_in(g_ref.at[sd,B],adbr.at[2])
        when(z==2,f)
        for h in range(2): sib_send(z==2,2,1-y,xn,h)
    def arrive0(h):
        ok=z!=0
        when(ok,lambda: wait_in(g_ref.at[slot(0,y,p),hs[h]],azr.at[0,h]))
        z_send(ok&up_ok,0,h,1)
        xy_send(ok,0,h)
        sib_send(ok,0,y,p,h)
    def arrive3(h,ok):
        when(ok,lambda: wait_in(g_ref.at[slot(3,y,p),hs[h]],azr.at[3,h]))
        z_send(ok&dn_ok,3,h,-1)
        sib_send(ok,3,y,p,h)
    def xy_arrive(ok,f,h):
        sx=slot(f,y,xn); sy=slot(f,1-y,p)
        when(ok,lambda: wait_in(g_ref.at[sx,hs[h]],axr.at[f,h]))
        if h==0: cm.go(ok,g_ref.at[sx,A],g_ref.at[sx,A],ads.at[f],adar.at[f],yn,p)
        sib_send(ok,f,y,xn,h)
        when(ok,lambda: wait_in(g_ref.at[sy,hs[h]],ayr.at[f,h]))
        if h==1: cm.go(ok,g_ref.at[sy,B],g_ref.at[sy,B],ads.at[f],adbr.at[f],b,xn)
        sib_send(ok,f,1-y,p,h)
    def later_sends():
        for h in range(2):
            src=blk.at[hs[h]]
            z_send(z==1,z,h,1,src)
            z_send(z==1,z,h,-1,src)
    def one_in(h,ok):
        when(ok,lambda: wait_in(g_ref.at[slot(1,y,p),hs[h]],azr.at[1,h]))
        z_send(ok&is2,1,h,1)
        sib_send(ok,1,y,p,h)
    def load(sl): return (pltpu.make_async_copy(g_ref.at[sl,pl.ds(0,528)],wv.at[pl.ds(pl.multiple_of(16*lax.div(ROWS*sl,16),16),528)],wsem.at[lax.div(sl,8)]),
                          pltpu.make_async_copy(g_ref.at[sl,pl.ds(528,32)],tails.at[sl],tsem.at[lax.div(sl,8)]))
    def d_arrive(zz):
        sd=slot(zz,1-y,xn)
        wait_in(g_ref.at[sd,A],adar.at[zz])
        sib_send(None,zz,1-y,xn,0)
        wait_in(g_ref.at[sd,B],adbr.at[zz])
        sib_send(None,zz,1-y,xn,1)
        for yy in range(2):
            for pp in range(2):
                for c in load(slot(zz,yy,pp)): c.start()
    def sib_arrive(zz):
        wait_in(g_ref.at[pl.ds(0,4)],asr.at[zz])
    has_gains=s==31
    gain_line=(y==1)&(core==1)&(p==1)
    def gain_sends():
        for k,zz in line: cm.go(has_gains,blk.at[pl.ds(528,16)],gtile,gls,glr,b+4*(zz-z),p)
    def gain_pass():
        pl.when(has_gains)(lambda: gtile.__setitem__(Ellipsis,blk[528:544]))
        pl.when(gain_line&jnp.logical_not(has_gains))(lambda: wait_in(gtile,glr))
        for d,bb,pp in plane: cm.go(gain_line,gtile,gtile,gps,gpr,bb,pp)
    def gain_wait():
        pl.when(jnp.logical_not(gain_line))(lambda: wait_in(gtile,gpr))
    seen=[]
    def take(shards):
        pltpu.make_async_copy(wv.at[pl.ds(0,4*528)],wv.at[pl.ds(0,4*528)],wsem.at[shards[0]//8]).wait()
        pltpu.make_async_copy(tails.at[pl.ds(0,4)],tails.at[pl.ds(0,4)],tsem.at[shards[0]//8]).wait()
        for k in shards:
            lo=base_of(k)
            if k<31 and base_of(k+1)-lo==544 or k==31: wv[lo+528:lo+544]=tails[k,0:16]
            seen.append(k)
        for k in range(1,32):
            if k in seen and k-1 in seen and (k in shards or k-1 in shards):
                off=base_of(k)-base_of(k-1)-528
                t=tails[k-1,off:off+16].astype(f32)
                if off: t=jnp.where(lax.broadcasted_iota(jnp.int32,(16,CH),0)<8,t,0.0)
                lo=base_of(k)
                wv[lo:lo+16]=(wv[lo:lo+16].astype(f32)+t).astype(bf)
    def rows(u,yy,pp,cc=core):
        at=pl.ds(pl.multiple_of(16*lax.div(ROWS*slot(u,yy,pp,cc),16),16),BLK)
        return wd.at[at,pl.ds(0,CH)] if u==0 else wv.at[at]
    def need(u,yy,pp,cc=core): return None if u<3 else slot(u,yy,pp,cc)<=LAST
    def sibsend(u):
        for yy,pp in four:
            cm.go(need(u,yy,pp,oc),rows(u,yy,pp,oc),sibr.at[4*u+2*yy+pp],s1s.at[u],s1r.at[u,yy,pp],sib,p)
    def both(u,yy,pp,lo,n):
        a=pl.multiple_of(16*lax.div(ROWS*slot(u,yy,pp),16)+lo,16)
        mine_=wd[pl.ds(a,n),0:CH] if u==0 else wv[pl.ds(a,n)]
        return mine_.astype(f32)+sibr[4*u+2*yy+pp,lo:lo+n].astype(f32)
    HA=(0,HALF); HB=(HALF,BLK-HALF)
    def sib_in(u,yy,pp): wait_in(sibr.at[4*u+2*yy+pp],s1r.at[u,yy,pp])
    def keep(u,yy,pp,half,more=None):
        t=both(u,yy,pp,*half)
        if more is not None: t=t+more.astype(f32)
        sibr[4*u+2*yy+pp,half[0]:half[0]+half[1]]=t.astype(bf)
    def diag(u):
        yy,pp=1-y,xn
        c=need(u,yy,pp)
        def f():
            sib_in(u,yy,pp)
            keep(u,yy,pp,HA); keep(u,yy,pp,HB)
        when(c,f)
        src=sibr.at[4*u+2*yy+pp]
        if u<2: cm.go(c,src.at[A],rba.at[u],ds_.at[u],dar.at[u],b,xn)
        else: cm.go(c,src.at[A],rba.at[u],ds_.at[u],dar.at[u],yn,p)
        cm.go(c,src.at[B],rb.at[u],ds_.at[u],dbr.at[u],yn,p)
    def ysend(u):
        c=need(u,1-y,p)
        def f():
            sib_in(u,1-y,p)
            keep(u,1-y,p,HA); keep(u,1-y,p,HB)
        when(c,f)
        for h in range(2): cm.go(c,sibr.at[4*u+2*(1-y)+p,hs[h]],ry.at[u,hs[h]],rys.at[u],ryr.at[u,h],yn,p)
    def xsend(u,only=None):
        c=AND(need(u,y,xn),only)
        def f():
            sib_in(u,y,xn)
            wait_in(rba.at[u],dar.at[u])
            keep(u,y,xn,HA,rba[u])
        when(c,f)
        cm.go(c,sibr.at[4*u+2*y+xn,A],rx.at[u,A],rxs.at[u],rxr.at[u,0],b,xn)
        def f2():
            wait_in(rb.at[u],dbr.at[u])
            keep(u,y,xn,HB,rb[u])
        when(c,f2)
        cm.go(c,sibr.at[4*u+2*y+xn,B],rx.at[u,B],rxs.at[u],rxr.at[u,1],b,xn)
    def put_x(u,half,h,more=None):
        keep(u,y,xn,half,more)
        cm.go(None,sibr.at[4*u+2*y+xn,hs[h]],rx.at[u,hs[h]],rxs.at[u],rxr.at[u,h],b,xn)
    def put_y(u,half,h,more=None):
        keep(u,1-y,p,half,more)
        cm.go(None,sibr.at[4*u+2*(1-y)+p,hs[h]],ry.at[u,hs[h]],rys.at[u],ryr.at[u,h],yn,p)
    def first_halves(u):
        sib_in(u,y,xn)
        sib_in(u,1-y,p)
        if u>0:
            put_x(u,HA,0)
            put_y(u,HB,1)
    def second_halves(u):
        wait_in(rba.at[u],dar.at[u])
        put_y(u,HA,0,rba[u])
        if u==0: put_y(u,HB,1)
        wait_in(rb.at[u],dbr.at[u])
        put_x(u,HB,1,rb[u])
    def chunks(u): return ((0,80,0),(80,80,0),(160,64,0),(224,64,0),(288,80,1),(368,64,1),(432,64,1),(496,64,1)) if u==0 else ((0,HALF,0),(HALF,BLK-HALF,1))
    def zur_at(u,k): return zur.at[2*(u-1)+k]
    def zdr_at(u,k): return zdr.at[k if u==0 else 8+2*(u-1)+k]
    def xy_in(u,h):
        wait_in(rx.at[u,hs[h]],rxr.at[u,h])
        wait_in(ry.at[u,hs[h]],ryr.at[u,h])
    def zstep(u,i):
        for d in (1,-1):
            at_z=i if d==1 else 3-i
            if not (at_z<u if d==1 else at_z>u): continue
            c=AND(need(u,y,p),z==at_z)
            buf,bsem=(zu.at[u-1],zur_at) if d==1 else (zd.at[u],zdr_at)
            own_at=4*u+2*y+p
            def first(): sib_in(u,y,p)
            when(c,first)
            seen_h=set()
            for k,(lo,n,h) in enumerate(chunks(u)):
                def f():
                    if h not in seen_h: xy_in(u,h)
                    t=both(u,y,p,lo,n)+rx[u,lo:lo+n].astype(f32)+ry[u,lo:lo+n].astype(f32)
                    if i>0:
                        wait_in(buf.at[pl.ds(lo,n)],bsem(u,k))
                        t=t+buf[lo:lo+n].astype(f32)
                    sibr[own_at,lo:lo+n]=t.astype(bf)
                when(c,f)
                seen_h.add(h)
                cm.go(c,sibr.at[own_at,pl.ds(lo,n)],buf.at[pl.ds(lo,n)],zs.at[u],bsem(u,k),b+4*d,p)
    def zend(u):
        def f():
            sib_in(u,y,p)
            done=set()
            for k,(lo,n,h) in enumerate(chunks(u)):
                if h not in done: xy_in(u,h); done.add(h)
                t=both(u,y,p,lo,n)+rx[u,lo:lo+n].astype(f32)+ry[u,lo:lo+n].astype(f32)
                if u>0:
                    wait_in(zu.at[u-1,pl.ds(lo,n)],zur_at(u,k))
                    t=t+zu[u-1,lo:lo+n].astype(f32)
                if u<3:
                    wait_in(zd.at[u,pl.ds(lo,n)],zdr_at(u,k))
                    t=t+zd[u,lo:lo+n].astype(f32)
                if u==3:
                    rr=16*lax.div(ROWS*s,16)+lo+lax.broadcasted_iota(jnp.int32,(n,CH),0)
                    t=jnp.where(rr<R_EMB,t,total[lo:lo+n])
                total[lo:lo+n]=t
        when(AND(need(u,y,p),z==u),f)
    state={"k":0}
    def xchg(src,dst,dst_like=None):
        k=state["k"]; state["k"]=k+1
        c=pltpu.make_async_remote_copy(src_ref=src,dst_ref=dst,send_sem=xs.at[k],recv_sem=xr.at[k],device_id=(b,q),device_id_type=MESH)
        c.start()
        return c
    edge=pl.ds(pl.multiple_of(q*480,32),32)
    gain_sends()
    c_img=xchg(img.at[edge],himg)
    def gsum(v): return exact(v,gm[...],nn)
    def swap_sums(k,s1,s2):
        ssend[k]=jnp.concatenate([s1,s2,jnp.zeros((6,CH),f32)],0)
        return xchg(ssend.at[k],srecv.at[k])
    def total_sums(k):
        t=gsum(ssend[k]+srecv[k])*(1.0/(12*2*PX))
        return t[0:1],t[1:2]
    def norm_of(t):
        mean,sq=t
        return mean,lax.rsqrt(sq-mean*mean+EPS_NORM)
    def fill3(dst,at,a):
        col=lax.broadcasted_iota(jnp.int32,a.shape,0)&31
        n=a.shape[0]
        dst[pl.ds(at,n),CH:2*CH]=a.astype(bf)
        dst[pl.ds(at,n),0:CH]=jnp.where(col==0,0.0,pltpu.roll(a,1,0)).astype(bf)
        dst[pl.ds(at,n),2*CH:3*CH]=jnp.where(col==31,0.0,pltpu.roll(a,n-1,0)).astype(bf)
    def fill_edges(dst,h):
        fill3(dst,0,h*pf); fill3(dst,544,h*qf)
    def conv_to(dst,x3,wrow,add=None):
        for dr in range(3):
            d=nn(x3[32*dr:32*dr+PX],wv[wrow+1152*dr:wrow+1152*dr+1152])
            if dr==0: dst[...]=d if add is None else add()+d
            else: dst[...]+=d
    def conv_dx(dst,wrow):
        first=True
        for dr in range(3):
            for dc in range(3):
                d=nt(z3[32*(2-dr):32*(2-dr)+PX,CH*(2-dc):CH*(2-dc)+CH],wv[wrow+CH*(3*dr+dc):wrow+CH*(3*dr+dc)+CH])
                if first: dst[...]=d
                else: dst[...]+=d
                first=False
    def st(i,c):
        v=img[pl.ds(i,64)].astype(f32)
        return c[0]+col8(v),c[1]+col8(v*v)
    a1,a2=cloop(PX,64,st,(Z8(),Z8()))
    c=swap_sums(0,row(a1),row(a2))
    own_sends()
    gain_pass()
    own_xy()
    group_of=lambda d: lax.shift_right_logical(lax.broadcasted_iota(jnp.int32,(CH,CH),d)*43691,19)
    gm[...]=(group_of(0)==group_of(1)).astype(f32).astype(bf)
    gain_wait()
    g6=gtile[...].astype(f32)
    g1,b1,g2,b2,g3,b3=[g6[2+i:3+i] for i in range(6)]
    c.wait()
    mean1,inv1=norm_of(total_sums(0))
    def act_of(v): return silu((v-mean1)*inv1*g1+b1)
    arrive3(0,is2)
    arrive3(1,is2)
    def fa(i,_):
        fill3(x3a,pl.multiple_of(i+32,32),act_of(img[pl.ds(i,64)].astype(f32)))
        return 0
    cloop(PX,64,fa,0)
    c_img.wait()
    fill_edges(x3a,act_of(himg[...].astype(f32)))
    own.wait()
    xy_arrive(z==3,3,0)
    xy_arrive(z==3,3,1)
    arrive0(0)
    xy_arrive(is2,2,0)
    three_out(1); three_out(2)
    arrive0(1)
    diag_in(top,3)
    three_out(0)
    xy_arrive(is2,2,1)
    arrive3(0,is1)
    arrive3(1,is1)
    later_sends()
    two_send(is2,3,-1)
    two_send(is2,1,-1); two_send(is2,2,-1)
    xy_arrive(None,0,0)
    one_in(0,is2)
    one_in(1,is2)
    xy_arrive(None,0,1)
    for h in range(2): xy_send(is1,3,h)
    for h in range(2): xy_send(is2,1,h)
    for h in range(2): one_in(h,top)
    for h in range(2): xy_send(top,1,h)
    for i in (3,1,2): two_send(is2,i,1)
    two_diag()
    two_send(is2,0,-1); two_send(is2,0,1)
    d_arrive(0)
    arrive3(0,z==0)
    xy_send(z==0,3,0)
    sib_arrive(0)
    take(range(0,8))
    conv_to(inner,x3a,R_ONE)
    def st2(i,c):
        v=inner[pl.ds(i,64)]
        return c[0]+col8(v),c[1]+col8(v*v)
    a1,a2=cloop(PX,64,st2,(Z8(),Z8()))
    c1=swap_sums(1,row(a1),row(a2))
    c2=xchg(inner.at[edge],hrecv.at[0])
    two_in(3,is1)
    xy_arrive(z>=2,1,0)
    arrive3(1,z==0)
    xy_send(z==0,3,1)
    xy_arrive(z<2,3,0)
    xy_arrive(z<2,3,1)
    for h in range(2): one_in(h,z==0)
    for h in range(2): xy_send(z<2,1,h)
    three_in(1); three_in(2)
    xy_arrive(z>=2,1,1)
    three_in(0)
    diag_in(z<2,3)
    for yy in range(2):
        for pp in range(2):
            for k in load(slot(3,yy,pp)): k.start()
    sib_arrive(3)
    two_in(1,is1)
    take(range(24,32))
    ids=rowid[...]
    pre=[]
    tcol=lax.broadcasted_iota(jnp.int32,(16,R_END-R_TAB),1)
    for h in range(2):
        hot=(tcol==2*ids+h).astype(f32).astype(bf)
        pre.append(nn(hot,wv[R_TAB:R_END])[0:1]+tvec[:,CH*h:CH*h+CH])
    emb=[silu(v) for v in pre]
    put3(cvt3,pl.ds(0,1536),wv[R_EMB:R_TAB].astype(f32))
    wee[...]=ld(cvt3,every(0,768,2)).astype(bf)
    weo[...]=ld(cvt3,every(1,768,2)).astype(bf)
    def emb_dot(w):
        r=None
        for h in range(2):
            e=jnp.broadcast_to(emb[h],(16,CH))
            d=exact(e,w[CH*h:CH*h+CH],nn)[0:1]
            r=d if r is None else r+d
        return r
    sc1=1.0+emb_dot(wee); sh=emb_dot(weo)
    c1.wait()
    xy_arrive(z<2,1,0)
    mean2,inv2=norm_of(total_sums(1))
    def pre_b(v):
        n=(v-mean2)*inv2
        af=n*g2+b2
        return n,af,af*sc1+sh
    def fb(i,_):
        fill3(x3b,pl.multiple_of(i+32,32),silu(pre_b(inner[pl.ds(i,64)])[2]))
        return 0
    cloop(PX,64,fb,0)
    c2.wait()
    fill_edges(x3b,silu(pre_b(hrecv[0])[2]))
    xy_arrive(z<2,1,1)
    two_in(2,is1)
    d_arrive(1)
    sib_arrive(1)
    two_in(0,is1)
    take(range(8,16))
    conv_to(middle,x3b,R_TWO,lambda: img[...].astype(f32))
    def st3(i,c):
        v=middle[pl.ds(i,64)]
        return c[0]+col8(v),c[1]+col8(v*v)
    a1,a2=cloop(PX,64,st3,(Z8(),Z8()))
    c1=swap_sums(2,row(a1),row(a2))
    put3(cvt3,pl.ds(0,1152),wv[R_QKV:R_PROJ].astype(f32))
    for j in range(3):
        wqT[CH*j:CH*j+CH]=ld(cvt3,every(j,CH,3)).T.astype(bf)
    c1.wait()
    mean3,inv3=norm_of(total_sums(2))
    def fc(i,_):
        n=(middle[pl.ds(i,64)]-mean3)*inv3
        ain[pl.ds(i,64)]=(n*g3+b3).astype(bf)
        return 0
    cloop(PX,64,fc,0)
    c_in=xchg(ain.at[pl.ds(0,PX)],ain.at[pl.ds(PX,PX)])
    c_mid=xchg(middle.at[edge],hmid)
    def triples(a):
        t=nt(wqT[...],a)
        is_q=lax.rem(lax.broadcasted_iota(jnp.int32,t.shape,0),192)<64
        return jnp.where(is_q,t*0.125,t).astype(bf)
    trT[:,0:PX]=triples(ain[0:PX])
    def head_rows(h):
        r0=pl.multiple_of(h*192,64)
        return r0,pl.multiple_of(r0+64,64),pl.multiple_of(r0+128,64)
    def fh1(h,_):
        r0,r1,r2=head_rows(h)
        sco=nn(trT[pl.ds(r1,64),0:PX].T,trT[pl.ds(r0,64),0:PX])
        m=jnp.max(sco,0,keepdims=True)
        e=jnp.exp(sco-m)
        lse[h,0:1]=m
        lse[h,1:2]=jnp.sum(e,0,keepdims=True)
        acc[h]=nn(trT[pl.ds(r2,64),0:PX],e.astype(bf))
        return 0
    lax.fori_loop(0,6,fh1,0)
    for i in (3,1,2): two_in(i,ends)
    c_in.wait()
    trT[:,PX:2*PX]=triples(ain[PX:2*PX])
    def fh(h,_):
        r0,r1,r2=head_rows(h)
        sco=nn(trT[pl.ds(r1,64),PX:2*PX].T,trT[pl.ds(r0,64),0:PX])
        m0=lse[h,0:1]
        m=jnp.maximum(m0,jnp.max(sco,0,keepdims=True))
        e=jnp.exp(sco-m)
        a=jnp.exp(m0-m)
        l=lse[h,1:2]*a+jnp.sum(e,0,keepdims=True)
        o=acc[h]*a+nn(trT[pl.ds(r2,64),PX:2*PX],e.astype(bf))
        attT[pl.ds(pl.multiple_of(h*64,64),64),:]=(o*(1.0/l)).astype(bf)
        lse[h,0:1]=m+jnp.log(l)
        return 0
    lax.fori_loop(0,6,fh,0)
    put3(gout,pl.ds(0,PX),middle[...]+tn(attT[...],wv[R_PROJ:R_DOWN]))
    hsend[0]=ld(gout,edge).astype(bf)
    c1=xchg(hsend.at[0],oth.at[0])
    two_in(0,ends)
    for yy in range(2):
        for pp in range(2):
            for k in load(slot(2,yy,pp)): k.start()
    sib_arrive(2)
    take(range(16,24))
    for off in range(9):
        put3(cvt3,pl.ds(0,576),wv[R_DOWN+576*off:R_DOWN+576*off+576].astype(f32))
        v0,v1,v2=[ld(cvt3,every(i,192,3)) for i in range(3)]
        put3(cvt2,every(0,192,2),jnp.concatenate([v0,v1[:,0:256]],1))
        w=jnp.concatenate([v1[:,128:384],v2],1)
        w=pltpu.roll(w,w.shape[1]-64,1)
        put3(cvt2,every(1,192,2),w)
        wd[CH*off:CH*off+CH]=ld(cvt2,pl.ds(0,CH))[:,0:576].astype(bf)
    def parts(ref,n):
        e=ld(ref,every(0,n//2,2)); o=ld(ref,every(1,n//2,2))
        col=lax.broadcasted_iota(jnp.int32,o.shape,0)&15
        return jnp.where(col==0,0.0,pltpu.roll(o,1,0)).astype(bf),e.astype(bf),o.astype(bf)
    for dc,v in enumerate(parts(gout,PX)):
        v=v.reshape(8,32,CH)
        even=v[:,0:16].reshape(128,CH); odd=v[:,16:32].reshape(128,CH)
        xd[:,CH*(3+dc):CH*(3+dc)+CH]=even
        xd[:,CH*(6+dc):CH*(6+dc)+CH]=odd
        xd[16:128,CH*dc:CH*dc+CH]=odd[0:112]
    c1.wait()
    put3(geo,pl.ds(0,32),oth[0].astype(f32)*pf)
    for dc,v in enumerate(parts(geo,32)):
        xd[0:16,CH*dc:CH*dc+CH]=v
    fin=nn(xd[...],wd[0:9*CH])
    feat=nn(fin.astype(bf),vgg[...]); tf=nn(tgt[...],vgg[...])
    ir=lax.rsqrt(jnp.mean(feat*feat,-1,keepdims=True)+EPS_FEAT)
    unit=feat*ir
    diff=unit-tf*lax.rsqrt(jnp.mean(tf*tf,-1,keepdims=True)+EPS_FEAT)
    wl=lin[...]*diff
    consist=jnp.sum(row(wl*diff),1,keepdims=True)*(1.0/(256*256))
    du=wl*(2.0/(256*256*images_all))
    dfeat=(ir*(du-unit*jnp.mean(du*unit,-1,keepdims=True))).astype(bf)
    zc=jnp.zeros((16,128),f32)
    for t_ in range(0,32,2): zc=zc+tails[t_,16:32,0:128].astype(f32)
    zc=zc[12:13,0:1]
    seed=(level[...]==0).astype(f32)/jnp.maximum(zc,1.0)*(2.0/(256*CH2))
    gfin=nt(dfeat,vgg[...])+seed*(fin-cln[...].astype(f32))
    dz=gfin.astype(bf)
    dzs[...]=dz[0:16]
    c1=xchg(dzs,dzr)
    for off in range(9):
        dw=tn(xd[:,CH*off:CH*off+CH],dz)
        put3(cvt2,pl.ds(0,CH),jnp.concatenate([dw,jnp.zeros((CH,64),f32)],1))
        e=ld(cvt2,every(0,192,2)); o_=pltpu.roll(ld(cvt2,every(1,192,2)),64,1)
        lane=lax.broadcasted_iota(jnp.int32,(192,128),1)
        put3(cvt3,every(0,192,3),e[:,0:384])
        put3(cvt3,every(1,192,3),jnp.concatenate([e[:,384:512],jnp.where(lane<64,e[:,512:640],o_[:,0:128]),o_[:,128:256]],1))
        put3(cvt3,every(2,192,3),o_[:,256:640])
        wv[R_DOWN+576*off:R_DOWN+576*off+576]=ld(cvt3,pl.ds(0,576)).astype(bf)
    sibsend(2); sibsend(3)
    c1.wait()
    z32=dz.astype(f32)
    down=jnp.concatenate([z32[16:128],dzr[...].astype(f32)*qf],0)
    def left(v):
        col=lax.broadcasted_iota(jnp.int32,v.shape,0)&15
        return jnp.where(col==15,0.0,pltpu.roll(v,127,0)).astype(bf)
    s00,s01,s10,s11=dz,left(z32),down.astype(bf),left(down)
    W=lambda a,c: wd[CH*(3*a+c):CH*(3*a+c)+CH]
    def put(a,c,v):
        for i in range(8):
            put3(gout,every((2*i+a)*32+c,16,2),v[16*i:16*i+16])
    put(0,0,nt(s00,W(1,1)))
    put(0,1,nt(s00,W(1,2))+nt(s01,W(1,0)))
    put(1,0,nt(s00,W(2,1))+nt(s10,W(0,1)))
    put(1,1,nt(s00,W(2,2))+nt(s01,W(2,0))+nt(s10,W(0,2))+nt(s11,W(0,0)))
    diag(2); diag(3); ysend(2); ysend(3)
    gp=ld(gout,pl.ds(0,PX)).astype(bf)
    dattT[...]=nt(wv[R_PROJ:R_DOWN],gp).astype(bf)
    wv[R_PROJ:R_DOWN]=nn(attT[...],gp).astype(bf)
    def bh_part(h,at,n):
        r0,r1,r2=head_rows(h)
        ra_=pl.ds(pl.multiple_of(h*64,64),64)
        qT=trT[pl.ds(r0,64),0:PX]
        kT=trT[pl.ds(r1,64),at:at+n]
        gT=dattT[ra_,:]
        pr=jnp.exp(nn(kT.T,qT)-lse[h,0:1])
        de=jnp.sum(gT.astype(f32)*attT[ra_,:].astype(f32),0,keepdims=True)
        ds=(pr*(nn(trT[pl.ds(r2,64),at:at+n].T,gT)-de)).astype(bf)
        dtrT[pl.ds(r1,64),at:at+n]=nt(qT,ds).astype(bf)
        dtrT[pl.ds(r2,64),at:at+n]=nt(gT,pr.astype(bf)).astype(bf)
        return r0,nn(kT,ds)*0.125
    def bh(at,first):
        def f(h,_):
            r0,dqT=bh_part(h,at,256)
            if first:
                acc[h]=dqT
                dtrT[pl.ds(r0,64),PX:2*PX]=jnp.zeros((64,PX),bf)
            else: acc[h]+=dqT
            return 0
        return f
    c_g=[]
    for i in range(2):
        at=PX+256*i
        lax.fori_loop(0,6,bh(at,i==0),0)
        oth[1+8*i:9+8*i]=tn(dtrT[:,at:at+256],wqT[...]).astype(bf).reshape(8,32,CH)
        c_g.append(xchg(oth.at[pl.ds(1+8*i,8)],oth.at[pl.ds(17+8*i,8)]))
    def bh2(h,_):
        r0,dqT=bh_part(h,0,PX)
        dtrT[pl.ds(r0,64),0:PX]=(acc[h]+dqT).astype(bf)
        return 0
    lax.fori_loop(0,6,bh2,0)
    gsec[...]=tn(dtrT[:,0:PX],wqT[...])
    for c in c_g: c.wait()
    def n3_of(i): return (middle[pl.ds(i,64)]-mean3)*inv3
    def s3(i,c):
        j=pl.multiple_of(17+lax.div(i,32),1)
        v=gsec[pl.ds(i,64)]+oth[pl.ds(j,2)].reshape(64,CH).astype(f32)
        gsec[pl.ds(i,64)]=v
        return c[0]+col8(v),c[1]+col8(v*n3_of(i))
    a1,a2=cloop(PX,64,s3,(Z8(),Z8()))
    db3,dg3=row(a1),row(a2)
    c1=swap_sums(3,db3*g3,dg3*g3)
    esend[0]=ld(gout,edge)+inv3*(gsec[edge]*g3)
    c2=xchg(esend.at[0],erecv.at[0])
    xsend(2)
    dq=nt(ain[...].T,dtrT[...])
    for j in range(3):
        put3(cvt3,every(j,CH,3),dq[:,CH*j:CH*j+CH])
    wv[R_QKV:R_PROJ]=ld(cvt3,pl.ds(0,1152)).astype(bf)
    c1.wait()
    m1,m2=total_sums(3)
    def f3(i,_):
        v=ld(gout,pl.ds(i,64))+inv3*(gsec[pl.ds(i,64)]*g3-m1-n3_of(i)*m2)
        fill3(z3,pl.multiple_of(i+32,32),v)
        return 0
    cloop(PX,64,f3,0)
    c_mid.wait()
    c2.wait()
    fill_edges(z3,erecv[0]-inv3*(m1+(hmid[...]-mean3)*inv3*m2))
    conv_dx(gsec,R_TWO)
    for dr in range(3):
        d=tn(x3b[32*dr:32*dr+PX],z3[32:32+PX,CH:2*CH]).astype(bf)
        wv[R_TWO+1152*dr:R_TWO+1152*dr+1152]=d
        if dr==0: wd[R_TWO:4304,0:CH]=d[0:4304-R_TWO]
    sibsend(1)
    def s2(i,c):
        n,af,pb=pre_b(inner[pl.ds(i,64)])
        gpre=gsec[pl.ds(i,64)]*slope(pb)
        gaff=gpre*sc1
        gsec[pl.ds(i,64)]=gaff
        return c[0]+col8(gpre*af),c[1]+col8(gpre),c[2]+col8(gaff*n),c[3]+col8(gaff)
    a1,a2,a3,a4=cloop(PX,64,s2,(Z8(),Z8(),Z8(),Z8()))
    dsc,dsh,dg2,db2=row(a1),row(a2),row(a3),row(a4)
    c1=swap_sums(4,db2*g2,dg2*g2)
    esend[1]=gsec[edge]*g2
    c2=xchg(esend.at[1],erecv.at[1])
    diag(1)
    first_halves(1)
    c1.wait()
    m1,m2=total_sums(4)
    def f2(i,_):
        n=(inner[pl.ds(i,64)]-mean2)*inv2
        fill3(z3,pl.multiple_of(i+32,32),inv2*(gsec[pl.ds(i,64)]*g2-m1-n*m2))
        return 0
    cloop(PX,64,f2,0)
    c2.wait()
    fill_edges(z3,inv2*(erecv[1]-m1-(hrecv[0]-mean2)*inv2*m2))
    for dr in range(3):
        wd[1152*dr:1152*dr+1152,0:CH]=tn(x3a[32*dr:32*dr+PX],z3[32:32+PX,CH:2*CH]).astype(bf)
    sibsend(0)
    second_halves(1)
    xsend(3,z<2)
    zstep(2,0)
    diag(0)
    first_halves(0)
    conv_dx(gsec,R_ONE)
    def s1(i,c):
        n=(img[pl.ds(i,64)].astype(f32)-mean1)*inv1
        gpre=gsec[pl.ds(i,64)]*slope(n*g1+b1)
        return c[0]+col8(gpre*n),c[1]+col8(gpre)
    a1,a2=cloop(PX,64,s1,(Z8(),Z8()))
    ge=[]
    for h in range(2):
        d=exact(jnp.broadcast_to(dsc,(16,CH)),wee[CH*h:CH*h+CH],nt)+exact(jnp.broadcast_to(dsh,(16,CH)),weo[CH*h:CH*h+CH],nt)
        ge.append(d[0:1]*slope(pre[h]))
    hot_level=(lax.broadcasted_iota(jnp.int32,(1,CH),1)==level[...]).astype(f32)
    pack_ref[...]=jnp.concatenate([row(a1),row(a2),dg2,db2,dg3,db3,dsc,dsh,ge[0],ge[1],emb[0],emb[1],consist*hot_level,jnp.broadcast_to(ids.astype(f32),(1,CH)),0.5*hot_level,jnp.zeros((1,CH),f32)],0)
    low=jnp.logical_not(top)
    cm.go(low,pack_ref,lpk.at[z],lps,lpr,b+4*(3-z),p)
    put_x(0,HA,0)
    zstep(1,0)
    zstep(3,0)
    second_halves(0)
    xsend(3,z>=2)
    zstep(2,1)
    zstep(1,1)
    zstep(0,0)
    zstep(3,1)
    zstep(0,1)
    zstep(3,2)
    def packs_line():
        lpk[3]=pack_ref[...]
        wait_in(lpk.at[pl.ds(0,3)],lpr)
    pl.when(top)(packs_line)
    for d,bb,pp in plane:
        cm.go(top,lpk,ppk.at[mine],pps,ppr,bb,pp)
    def packs_plane():
        ppk[mine]=lpk[...]
        wait_in(ppk.at[pl.ds(0,7)],ppr)
        a_s=16*lax.div(ROWS*s,16)
        rows_at=lambda k: ppk[:,:,k,:].reshape(32,384)
        zero=jnp.zeros((64,384),f32)
        for h in range(2):
            e=rows_at(10+h)
            t=jnp.concatenate([e,e,zero],0).T
            cvt[pl.ds(BLK+768*h,384,stride=2),:]=t
            cvt[pl.ds(BLK+768*h+1,384,stride=2),:]=t
        r=a_s+lax.broadcasted_iota(jnp.int32,(BLK,128),0)
        l=lax.broadcasted_iota(jnp.int32,(BLK,128),1)
        inside=(r>=R_EMB)&(r<R_TAB)
        start=pl.multiple_of(jnp.clip(a_s-R_EMB+BLK,0,BLK+1536),16)
        lf=jnp.where(inside&(((r&1)==1)==(l>=32))&(l<64),cvt[pl.ds(start,BLK),:],0.0)
        ids=rows_at(13)[:,0:128].astype(jnp.int32)
        ids=jnp.concatenate([ids]*4,0).astype(f32).T[0:1].astype(jnp.int32)
        hot=(r-R_TAB==2*ids+(l>=96).astype(jnp.int32))&(l>=64)&(r>=R_TAB)
        lf=jnp.where(hot,1.0,lf)
        rg=jnp.concatenate([rows_at(6),rows_at(7),rows_at(8),rows_at(9)],0)
        gains=[jnp.sum(rows_at(k),0,keepdims=True) for k in range(6)]
        hi=lax.Precision.HIGHEST
        add=lax.dot_general(lf,rg,(((1,),(0,)),((),())),precision=hi,preferred_element_type=f32)
        for k in range(6): add=add+jnp.where(r[:,0:1]-R_GAIN==k,gains[k],0.0)
        rr=a_s+lax.broadcasted_iota(jnp.int32,(BLK,384),0)
        total[...]=jnp.where(rr<R_EMB,0.0,add)
    pl.when(top)(packs_plane)
    zstep(0,2)
    zend(1); zend(2); zend(3)
    zend(0)
    shift=lax.rem(9*s,16)
    tr_=lax.broadcasted_iota(jnp.int32,(BLK,1),0)
    t=jnp.where((tr_>=shift)&(tr_<shift+ROWS),total[...],0.0)
    sq=jnp.sum(jnp.sum(t*t,0,keepdims=True),1,keepdims=True)
    tile[...]=jnp.concatenate([jnp.broadcast_to(sq,(1,128)),pack_ref[12:13,0:128],pack_ref[14:15,0:128],jnp.zeros((5,128),f32)],0)
    red1[mine]=tile[...]
    for d,bb,pp in plane: cm.go(None,tile,red1.at[mine],n1s,n1r,bb,pp)
    t=pltpu.roll(total[...],lax.rem(BLK-shift,BLK),0)[0:ROWS]
    for j in range(3): cvt[pl.ds(j,ROWS,stride=3),:]=t[:,128*j:128*j+128]
    fcopy=pltpu.make_async_copy(cvt.at[pl.ds(0,1611)],flat_ref,own_sem)
    fcopy.start()
    wait_in(red1.at[pl.ds(0,7)],n1r)
    v=red1[0]
    for k in range(1,8): v=v+red1[k]
    red2[z]=v
    for k,zz in line: cm.go(None,red2.at[z],red2.at[z],n2s,n2r,b+4*(zz-z),p)
    wait_in(red2.at[pl.ds(0,3)],n2r)
    sums=red2[0]+red2[1]+red2[2]+red2[3]
    norm_ref[...]=jnp.sqrt(sums[0:1,0:1])
    lev_ref[...]=sums[1:3,0:LEVELS]
    def sent(ok,ref,sem):
        when(ok,lambda: pltpu.make_async_copy(ref,ref,sem).wait())
    block=sibr.at[0]
    for zz in range(4):
        went=(None,None,is2,z!=2)[zz]
        for sem in (axs,ays,ads): sent(went,block,sem.at[zz])
        sent(None,sibr.at[pl.ds(0,4)],ass.at[zz])
        if zz<3:
            sent(None,sibr.at[pl.ds(0,4)],s1s.at[zz])
        else:
            sent(core==1,sibr.at[pl.ds(0,2)],s1s.at[zz])
        sent(need(zz,1-y,xn),block,ds_.at[zz])
        sent(need(zz,y,xn),block,rxs.at[zz])
        sent(need(zz,1-y,p),block,rys.at[zz])
        sent(AND(need(zz,y,p),z!=zz),block,zs.at[zz])
    sent(z<3,block,azs.at[0,0])
    sent(z>0,block,azs.at[3,1])
    sent(is1|is2,block,azs.at[1,0])
    sent(is1,block,azs.at[1,1])
    sent(is2,sibr.at[pl.ds(0,4)],a2s.at[0])
    sent(is1|is2,sibr.at[pl.ds(0,4)],a2s.at[1])
    sent(top,sibr.at[pl.ds(0,3)],a3s)
    sent(has_gains,blk.at[pl.ds(0,48)],gls)
    sent(gain_line,blk.at[pl.ds(0,112)],gps)
    sent(low,pack_ref,lps)
    sent(top,ppk.at[pl.ds(0,7)],pps)
    sent(None,red1.at[pl.ds(0,7)],n1s)
    sent(None,red2.at[pl.ds(0,3)],n2s)
    fcopy.wait()

def step(images_all,mast,img,tgt,cln,vgg,lin,tvec,rowid,level):
    D=pltpu.SemaphoreType.DMA
    V=lambda *s: pltpu.VMEM(s,bf)
    F=lambda *s: pltpu.VMEM(s,f32)
    vm=pl.BlockSpec(memory_space=pltpu.VMEM)
    return pl.pallas_call(functools.partial(step_kernel,images_all),
        out_shape=(jax.ShapeDtypeStruct((1611,128),f32),jax.ShapeDtypeStruct((1,1),f32),jax.ShapeDtypeStruct((2,LEVELS),f32),jax.ShapeDtypeStruct((32,BLK,CH),bf)),
        in_specs=[pl.BlockSpec(memory_space=pl.ANY)]+[vm]*8,
        out_specs=(pl.BlockSpec(memory_space=pl.ANY),vm,vm,pl.BlockSpec(memory_space=pl.ANY)),
        scratch_shapes=[V(17184,CH),V(32,32,CH),F(4608,128),F(5,CH,128),V(4304,CH2),V(768,CH),V(768,CH),V(1152,CH),V(576,1152),V(576,1152),V(576,1152),F(PX,CH),F(PX,CH),F(3,PX,128),F(PX,CH),V(1024,CH),V(1152,1024),V(1152,1024),V(CH,PX),V(128,3456),F(6,8,PX),V(CH,PX),F(5,8,CH),F(5,8,CH),V(1,32,CH),F(1,32,CH),V(32,CH),V(16,CH2),V(16,CH2),F(3,32,128),V(33,32,CH),D((4,)),D((4,)),D((15,)),D((15,)),F(BLK,CH),V(BLK,CH),D,D((4,2)),D((4,2)),D((4,)),D((4,2)),D((4,)),D((4,2)),D((4,)),D((4,)),D((4,)),D((4,)),F(16,CH),F(4,16,CH),F(8,4,16,CH),F(8,8,128),F(4,8,128),F(8,128),D,D,D,D,D,D,D,D,V(14,BLK,CH),V(4,BLK-HALF,CH),V(4,BLK,CH),V(4,BLK,CH),V(3,BLK,CH),V(3,BLK,CH),D((4,)),D((4,2,2)),D((4,)),D((4,)),D((4,)),D((4,2)),D((4,)),D((4,2)),D((4,)),D((6,)),D((12,)),F(6,64,PX),V(16,CH),D,D,D,D,V(4,HALF,CH),D((2,)),D((2,2,2)),D((4,)),D((4,)),F(32,CH),F(2,32,CH),F(2,32,CH),V(CH,CH),D,D((2,2,2))],
        compiler_params=pltpu.CompilerParams(collective_id=0,has_side_effects=True,vmem_limit_bytes=63<<20),
        name="train_step",
    )(mast,img,tgt,cln,vgg,lin,tvec,rowid,level)


def fast(images, target, clean_images, levels, labels, null_mask, vgg_proj, lpips_lin, master, first_moment, second_moment):
    row_index = jnp.where(null_mask == 1, CLASSES, labels).reshape(1, 1)
    tvec = time_vector(levels)
    own_grad, norm, level_sums, _ = step(
        16,
        master.reshape(1611, 128),
        images.reshape(PX, CH),
        target.reshape(128, CH2),
        clean_images.reshape(128, CH2),
        vgg_proj,
        lpips_lin.reshape(1, 256),
        tvec,
        row_index,
        levels.reshape(1, 1),
    )
    own_grad = own_grad.reshape(-1)
    norm_before = norm.reshape(())
    clipped = own_grad * jnp.minimum(1.0, CLIP / norm_before)
    new_first = BETA_ONE * first_moment + (1.0 - BETA_ONE) * clipped
    new_second = BETA_TWO * second_moment + (1.0 - BETA_TWO) * clipped * clipped
    fixed_first = new_first / (1.0 - BETA_ONE**STEP)
    fixed_second = new_second / (1.0 - BETA_TWO**STEP)
    new_master = master - RATE * (fixed_first / (jnp.sqrt(fixed_second) + EPS_ADAM) + DECAY * master)
    return (new_master, new_first, new_second, new_master.astype(jnp.bfloat16), norm_before, level_sums)


def solution(mesh):
    small = mesh.shape["batch"] == 16 and mesh.shape["pix"] == 2
    return jax.shard_map(
        fast if small else local,
        mesh=mesh,
        in_specs=(
            P("batch", "pix", None, None),
            P("batch", "pix", None, None),
            P("batch", "pix", None, None),
            P("batch"),
            P("batch"),
            P("batch"),
            P(),
            P(),
            P(("batch", "pix")),
            P(("batch", "pix")),
            P(("batch", "pix")),
        ),
        out_specs=(
            P(("batch", "pix")),
            P(("batch", "pix")),
            P(("batch", "pix")),
            P(("batch", "pix")),
            P(),
            P(),
        ),
        check_vma=False,
    )
```

```python
import functools
import math

import jax
import jax.numpy as jnp
from jax import lax
from jax.experimental import pallas as pl
from jax.experimental.pallas import tpu as pltpu
from jax.sharding import PartitionSpec as P

CH = 384
CH2 = 576
GROUPS = 32
HEAD = 64
TEMB = 768
CLASSES = 1000
LEVELS = 40
STEP = 10


EPS_NORM = 1e-05
EPS_FEAT = 1e-06
BETA_ONE = 0.9
BETA_TWO = 0.999
EPS_ADAM = 1e-08
RATE = 0.02
DECAY = 0.01
CLIP = 0.01
precise = lax.Precision.HIGHEST


def extended(shard, sides, width):
    for axis, dim in sides:
        size, length = (lax.axis_size(axis), shard.shape[dim])
        up = [(i, (i + 1) % size) for i in range(size - 1)]
        down = [(j, i) for i, j in up]
        last = lax.slice_in_dim(shard, length - width, length, axis=dim)
        initial = lax.slice_in_dim(shard, 0, width, axis=dim)
        before = lax.ppermute(last, axis, up)
        after = lax.ppermute(initial, axis, down)
        shard = jnp.concatenate([before, shard, after], axis=dim)
    return shard


def unpack(flat_vec):
    layout = [
        (9 * CH, CH),
        (9 * CH, CH),
        (CH, 3 * CH),
        (CH, CH),
        (9 * CH, CH2),
        (TEMB, 2 * CH),
        (CLASSES + 1, TEMB),
        (6, CH),
    ]
    pieces = []
    offset = 0
    for rows_n, cols_n in layout:
        pieces.append(flat_vec[offset : offset + rows_n * cols_n].reshape(rows_n, cols_n))
        offset += rows_n * cols_n
    return (pieces, offset)


def time_vector(level_ids):
    half_width = TEMB // 2
    frequency = jnp.exp(-math.log(10000.0) * jnp.arange(half_width, dtype=jnp.float32) / half_width)
    angles = level_ids.astype(jnp.float32)[..., None] * (1000.0 / LEVELS) * frequency
    return jnp.concatenate([jnp.cos(angles), jnp.sin(angles)], -1)


def silu_slope(values):
    sigmoid = jax.nn.sigmoid(values)
    return sigmoid * (1.0 + values * (1.0 - sigmoid))


def pix_sums(pair_sums):
    return lax.psum((pair_sums[0], pair_sums[1]), "pix")


def group_forward(values, pixels_all):
    grouped = values.reshape(values.shape[0], values.shape[1], GROUPS, -1)
    totals = pix_sums((jnp.sum(grouped, (1, 3)), jnp.sum(grouped * grouped, (1, 3))))
    per_group = pixels_all * grouped.shape[3]
    center = totals[0] / per_group
    spread = totals[1] / per_group - center * center
    inverse = lax.rsqrt(spread + EPS_NORM)
    normed = (grouped - center[:, None, :, None]) * inverse[:, None, :, None]
    return (normed.reshape(values.shape), inverse)


def group_backward(grad_normed, normed, inverse, pixels_all):
    grad_grouped = grad_normed.reshape(normed.shape[0], normed.shape[1], GROUPS, -1)
    val_grouped = normed.reshape(grad_grouped.shape)
    totals = pix_sums((jnp.sum(grad_grouped, (1, 3)), jnp.sum(grad_grouped * val_grouped, (1, 3))))
    per_group = pixels_all * grad_grouped.shape[3]
    result = (
        grad_grouped
        - (totals[0] / per_group)[:, None, :, None]
        - val_grouped * (totals[1] / per_group)[:, None, :, None]
    )
    return (result * inverse[:, None, :, None]).reshape(normed.shape)


def columns_of(values, stride):
    rows_out = values.shape[1] // stride
    cols_out = values.shape[2] // stride
    span_rows = stride * (rows_out - 1) + 1
    span_cols = stride * (cols_out - 1) + 1
    padded = extended(values, (("pix", 1),), 1)
    padded = jnp.pad(padded, ((0, 0), (0, 0), (1, 1), (0, 0)))
    return jnp.concatenate(
        [
            padded[
                :, row_off : row_off + span_rows : stride, col_off : col_off + span_cols : stride, :
            ]
            for row_off in range(3)
            for col_off in range(3)
        ],
        -1,
    )


def conv_forward(values, weight, rows_in, stride):
    n_img, pixels_in, in_chan = values.shape
    columns = columns_of(values.reshape(n_img, rows_in, -1, in_chan), stride)
    result = jnp.dot(columns.reshape(-1, 9 * in_chan), weight, preferred_element_type=jnp.float32)
    return (result.reshape(n_img, -1, weight.shape[1]), columns)


def conv_back(columns, grad_low, weight, rows_in, stride):
    n_img, pix_out, out_chan = grad_low.shape
    in_chan = weight.shape[0] // 9
    d_weight = jnp.einsum(
        "rk,rc->kc",
        columns.reshape(-1, 9 * in_chan),
        grad_low.reshape(-1, out_chan),
        preferred_element_type=jnp.float32,
    )
    flipped = (
        weight.reshape(3, 3, in_chan, out_chan)[::-1, ::-1]
        .transpose(0, 1, 3, 2)
        .reshape(9 * out_chan, in_chan)
    )
    rows_out = rows_in // stride
    grid_grad = grad_low.reshape(n_img, rows_out, pix_out // rows_out, out_chan)
    if stride > 1:
        grid_grad = jnp.pad(
            grid_grad[:, :, None, :, None, :],
            ((0, 0), (0, 0), (0, stride - 1), (0, 0), (0, stride - 1), (0, 0)),
        )
        grid_grad = grid_grad.reshape(n_img, rows_in, -1, out_chan)
    grad_columns = columns_of(grid_grad, 1)
    grad_input = jnp.dot(
        grad_columns.reshape(-1, 9 * out_chan), flipped, preferred_element_type=jnp.float32
    )
    return (d_weight, grad_input.reshape(n_img, -1, in_chan))


def res_forward(values, gain_rows, scale, shift, w_first, w_second, rows_in, pixels_all):
    normed_a, inverse_a = group_forward(values, pixels_all)
    pre_a = normed_a * gain_rows[0] + gain_rows[1]
    act_a = jax.nn.silu(pre_a).astype(jnp.bfloat16)
    inner, columns_a = conv_forward(act_a, w_first, rows_in, 1)
    normed_b, inverse_b = group_forward(inner, pixels_all)
    affine_b = normed_b * gain_rows[2] + gain_rows[3]
    pre_b = affine_b * (1.0 + scale) + shift
    second = jax.nn.silu(pre_b).astype(jnp.bfloat16)
    branch, columns_b = conv_forward(second, w_second, rows_in, 1)
    kept_state = (
        normed_a,
        inverse_a,
        pre_a,
        columns_a,
        normed_b,
        inverse_b,
        affine_b,
        pre_b,
        columns_b,
    )
    return (values + branch, kept_state)


def res_back(grad_result, kept_state, gain_rows, scale, w_first, w_second, rows_in, pixels_all):
    normed_a, inverse_a, pre_a, columns_a, normed_b, inverse_b, affine_b, pre_b, columns_b = (
        kept_state
    )
    d_w_second, grad_second = conv_back(
        columns_b, grad_result.astype(jnp.bfloat16), w_second, rows_in, 1
    )
    grad_pre_b = grad_second * silu_slope(pre_b)
    d_scale = jnp.sum(grad_pre_b * affine_b, 1)
    d_shift = jnp.sum(grad_pre_b, 1)
    grad_affine = grad_pre_b * (1.0 + scale)
    d_gain_b = jnp.sum(grad_affine * normed_b, (0, 1))
    d_bias_b = jnp.sum(grad_affine, (0, 1))
    grad_inner = group_backward(grad_affine * gain_rows[2], normed_b, inverse_b, pixels_all).astype(
        jnp.bfloat16
    )
    d_w_first, grad_act = conv_back(columns_a, grad_inner, w_first, rows_in, 1)
    grad_pre_a = grad_act * silu_slope(pre_a)
    d_gain_a = jnp.sum(grad_pre_a * normed_a, (0, 1))
    d_bias_a = jnp.sum(grad_pre_a, (0, 1))
    grad_values = None
    d_gains = jnp.stack([d_gain_a, d_bias_a, d_gain_b, d_bias_b])
    return (d_w_first, d_w_second, d_gains, d_scale, d_shift, grad_values)


def to_heads(values):
    return lax.all_to_all(values, "pix", split_axis=2, concat_axis=1, tiled=True)


def to_pixels(values):
    return lax.all_to_all(values, "pix", split_axis=1, concat_axis=2, tiled=True)


def flat_heads(values):
    return values.reshape(-1, values.shape[2], values.shape[3])


def attend(queries, keys, values):
    root_dim = math.sqrt(queries.shape[-1])

    def single(bundle):
        q_one, k_one, v_one = bundle
        scores = (
            jnp.einsum("qd,kd->qk", q_one, k_one, preferred_element_type=jnp.float32) / root_dim
        )
        row_peak = jnp.max(scores, -1, keepdims=True)
        exp_scores = jnp.exp(scores - row_peak)
        sum_exp = jnp.sum(exp_scores, -1, keepdims=True)
        probabilities = (exp_scores / sum_exp).astype(jnp.bfloat16)
        attended = jnp.einsum("qk,kd->qd", probabilities, v_one, preferred_element_type=jnp.float32)
        return (attended.astype(jnp.bfloat16), row_peak + jnp.log(sum_exp))

    attended, log_total = lax.map(
        single, (flat_heads(queries), flat_heads(keys), flat_heads(values))
    )
    return (attended.reshape(queries.shape), log_total)


def attend_back(queries, keys, values, log_total, grad_out):
    root_dim = math.sqrt(queries.shape[-1])

    def single(bundle):
        q_one, k_one, v_one, lse_one, g_one = bundle
        scores = (
            jnp.einsum("qd,kd->qk", q_one, k_one, preferred_element_type=jnp.float32) / root_dim
        )
        probabilities = jnp.exp(scores - lse_one)
        grad_v = jnp.einsum(
            "qk,qd->kd",
            probabilities.astype(jnp.bfloat16),
            g_one,
            preferred_element_type=jnp.float32,
        )
        grad_p = jnp.einsum("qd,kd->qk", g_one, v_one, preferred_element_type=jnp.float32)
        inner_sum = jnp.sum(probabilities * grad_p, -1, keepdims=True)
        grad_s = (probabilities * (grad_p - inner_sum)).astype(jnp.bfloat16)
        grad_q = (
            jnp.einsum("qk,kd->qd", grad_s, k_one, preferred_element_type=jnp.float32) / root_dim
        )
        grad_k = (
            jnp.einsum("qk,qd->kd", grad_s, q_one, preferred_element_type=jnp.float32) / root_dim
        )
        return (grad_q, grad_k, grad_v)

    grad_q, grad_k, grad_v = lax.map(
        single,
        (
            flat_heads(queries),
            flat_heads(keys),
            flat_heads(values),
            log_total,
            flat_heads(grad_out),
        ),
    )
    return (grad_q.reshape(queries.shape), grad_k.reshape(keys.shape), grad_v.reshape(values.shape))


def local(
    images,
    target,
    clean_images,
    levels,
    labels,
    null_mask,
    vgg_proj,
    lpips_lin,
    master,
    first_moment,
    second_moment,
):
    gathered = lax.all_gather(master.astype(jnp.bfloat16), ("batch", "pix"), axis=0, tiled=True)
    pieces, used_len = unpack(gathered)
    w_one, w_two, w_qkv, w_proj, w_down, w_emb, class_table, gains_low = pieces
    gains_one = gains_low.astype(jnp.float32)
    n_img, rows_local, cols_local, channels = images.shape
    wide_channels = w_down.shape[1]
    pix_count = lax.axis_size("pix")
    batch_count = lax.axis_size("batch")
    pixels_here = rows_local * cols_local
    pixels_all = pixels_here * pix_count
    pixels_all_two = pixels_all // 4
    images_all = n_img * batch_count
    row_index = jnp.where(null_mask == 1, class_table.shape[0] - 1, labels)
    one_hot = (
        row_index[:, None] == jnp.arange(class_table.shape[0], dtype=jnp.int32)[None, :]
    ).astype(jnp.float32)
    pre_embed = time_vector(levels) + jnp.dot(
        one_hot, class_table.astype(jnp.float32), precision=precise
    )
    embedded = jax.nn.silu(pre_embed)
    w_emb_wide = w_emb.astype(jnp.float32)
    scale_shift = jnp.dot(embedded, w_emb_wide, precision=precise)
    scale_one = scale_shift[:, None, :channels]
    shift_one = scale_shift[:, None, channels:]
    flat_in = images.astype(jnp.float32).reshape(n_img, pixels_here, channels)
    middle, kept_one = res_forward(
        flat_in, gains_one, scale_one, shift_one, w_one, w_two, rows_local, pixels_all
    )
    normed_three, inverse_three = group_forward(middle, pixels_all)
    attn_in = (normed_three * gains_one[4] + gains_one[5]).astype(jnp.bfloat16)
    triples = jnp.dot(attn_in.reshape(-1, channels), w_qkv, preferred_element_type=jnp.float32)
    triples = triples.astype(jnp.bfloat16).reshape(n_img, pixels_here, 3 * channels)
    spread_heads = to_heads(triples)
    local_heads = spread_heads.shape[2] // (3 * HEAD)
    split_heads = spread_heads.reshape(n_img, -1, local_heads, 3, HEAD).transpose(3, 0, 2, 1, 4)
    queries, keys, values = (split_heads[0], split_heads[1], split_heads[2])
    attended, log_total = attend(queries, keys, values)
    attended_px = to_pixels(attended.transpose(0, 2, 1, 3).reshape(n_img, -1, local_heads * HEAD))
    projected = jnp.dot(
        attended_px.reshape(-1, channels), w_proj, preferred_element_type=jnp.float32
    )
    output = middle + projected.reshape(n_img, pixels_here, channels)
    final_out, columns_down = conv_forward(output.astype(jnp.bfloat16), w_down, rows_local, 2)
    pixels_two = final_out.shape[1]
    feat_width = vgg_proj.shape[1]
    online_feat = jnp.dot(
        final_out.astype(jnp.bfloat16).reshape(-1, wide_channels),
        vgg_proj,
        preferred_element_type=jnp.float32,
    )
    online_feat = online_feat.reshape(n_img, pixels_two, feat_width)
    target_feat = jnp.dot(
        target.reshape(-1, wide_channels), vgg_proj, preferred_element_type=jnp.float32
    )
    target_feat = target_feat.reshape(n_img, pixels_two, feat_width)
    target_unit = target_feat * lax.rsqrt(
        jnp.mean(target_feat * target_feat, -1, keepdims=True) + EPS_FEAT
    )
    clean_wide = clean_images.astype(jnp.float32).reshape(n_img, pixels_two, wide_channels)

    def loss_terms(feature, out_value):
        unit = feature * lax.rsqrt(jnp.mean(feature * feature, -1, keepdims=True) + EPS_FEAT)
        consist = jnp.sum(lpips_lin * (unit - target_unit) ** 2, (1, 2)) / (
            feat_width * pixels_all_two
        )
        denoise = jnp.sum((out_value - clean_wide) ** 2, (1, 2)) / (pixels_all_two * wide_channels)
        return (consist, denoise)

    (consist, denoise), pullback = jax.vjp(loss_terms, online_feat, final_out)
    level_hot = (levels[:, None] == jnp.arange(LEVELS, dtype=jnp.int32)[None, :]).astype(
        jnp.float32
    )
    level_pair = lax.psum(
        (jnp.sum(consist[:, None] * level_hot, 0), jnp.sum(level_hot / pix_count, 0)),
        ("batch", "pix"),
    )
    zero_count = level_pair[1][0]
    is_zero = (levels == 0).astype(jnp.float32)
    grad_feat, grad_out = pullback(
        (jnp.full_like(consist, 1.0 / images_all), is_zero / jnp.maximum(zero_count, 1.0))
    )
    grad_feat_low = grad_feat.astype(jnp.bfloat16).reshape(-1, feat_width)
    grad_final = grad_out + jnp.einsum(
        "rf,cf->rc", grad_feat_low, vgg_proj, preferred_element_type=jnp.float32
    ).reshape(n_img, pixels_two, wide_channels)
    d_w_down, grad_output = conv_back(
        columns_down, grad_final.astype(jnp.bfloat16), w_down, rows_local, 2
    )
    grad_proj = grad_output.astype(jnp.bfloat16).reshape(-1, channels)
    d_w_proj = jnp.einsum(
        "rc,rd->cd",
        attended_px.reshape(-1, channels),
        grad_proj,
        preferred_element_type=jnp.float32,
    )
    grad_att_px = jnp.einsum("rd,cd->rc", grad_proj, w_proj, preferred_element_type=jnp.float32)
    grad_att_px = grad_att_px.astype(jnp.bfloat16).reshape(n_img, pixels_here, channels)
    grad_heads = to_heads(grad_att_px)
    grad_split = grad_heads.reshape(n_img, -1, local_heads, HEAD).transpose(0, 2, 1, 3)
    grad_q, grad_k, grad_v = attend_back(queries, keys, values, log_total, grad_split)
    grad_triples = jnp.stack([grad_q, grad_k, grad_v], 3).transpose(0, 2, 1, 3, 4)
    grad_triples = grad_triples.reshape(n_img, -1, local_heads * 3 * HEAD).astype(jnp.bfloat16)
    grad_triples = to_pixels(grad_triples)
    grad_rows = grad_triples.reshape(-1, 3 * channels)
    d_w_qkv = jnp.einsum(
        "rc,rd->cd", attn_in.reshape(-1, channels), grad_rows, preferred_element_type=jnp.float32
    )
    grad_attn_in = jnp.einsum(
        "rd,cd->rc", grad_rows, w_qkv, preferred_element_type=jnp.float32
    ).reshape(n_img, pixels_here, channels)
    d_gain_three = jnp.sum(grad_attn_in * normed_three, (0, 1))
    d_bias_three = jnp.sum(grad_attn_in, (0, 1))
    grad_middle = grad_output + group_backward(
        grad_attn_in * gains_one[4], normed_three, inverse_three, pixels_all
    )
    d_w_one, d_w_two, d_gains_one, d_scale_one, d_shift_one, unused_grad = res_back(
        grad_middle, kept_one, gains_one, scale_one, w_one, w_two, rows_local, pixels_all
    )
    grad_scale_shift = jnp.concatenate([d_scale_one, d_shift_one], 1)
    d_w_emb = jnp.dot(embedded.T, grad_scale_shift, precision=precise)
    grad_embedded = jnp.dot(grad_scale_shift, w_emb_wide.T, precision=precise)
    d_table = jnp.dot(one_hot.T, grad_embedded * silu_slope(pre_embed), precision=precise)
    d_norms_one = jnp.concatenate([d_gains_one, jnp.stack([d_gain_three, d_bias_three])], 0)
    flat_grad = jnp.concatenate(
        [
            d_w_one.ravel(),
            d_w_two.ravel(),
            d_w_qkv.ravel(),
            d_w_proj.ravel(),
            d_w_down.ravel(),
            d_w_emb.ravel(),
            d_table.ravel(),
            d_norms_one.ravel(),
            jnp.zeros((gathered.shape[0] - used_len,), jnp.float32),
        ]
    )
    own_grad = lax.psum_scatter(flat_grad, ("batch", "pix"), scatter_dimension=0, tiled=True)
    norm_before = jnp.sqrt(lax.psum(jnp.sum(own_grad * own_grad), ("batch", "pix")))
    clipped = own_grad * jnp.minimum(1.0, CLIP / norm_before)
    new_first = BETA_ONE * first_moment + (1.0 - BETA_ONE) * clipped
    new_second = BETA_TWO * second_moment + (1.0 - BETA_TWO) * clipped * clipped
    fixed_first = new_first / (1.0 - BETA_ONE**STEP)
    fixed_second = new_second / (1.0 - BETA_TWO**STEP)
    new_master = master - RATE * (
        fixed_first / (jnp.sqrt(fixed_second) + EPS_ADAM) + DECAY * master
    )
    level_sums = jnp.stack([level_pair[0], level_pair[1]])
    return (
        new_master,
        new_first,
        new_second,
        new_master.astype(jnp.bfloat16),
        norm_before,
        level_sums,
    )


MESH = pl.DeviceIdType.MESH
ROWS=537; BLK=560; HALF=288
PX=512
R_ONE,R_TWO,R_QKV,R_PROJ,R_DOWN,R_EMB,R_TAB,R_GAIN,R_END=0,3456,6912,8064,8448,13632,15168,17170,17184
f32=jnp.float32; bf=jnp.bfloat16
class Comm:
    def __init__(self): self.sent=[]
    def go(self, cond, src, dst, ssem, rsem, b, p):
        c = pltpu.make_async_remote_copy(src_ref=src,dst_ref=dst,send_sem=ssem,recv_sem=rsem,device_id=(b,p),device_id_type=MESH)
        if cond is None: c.start()
        else: pl.when(cond)(lambda: c.start())
        self.sent.append((cond,c))
    def drain(self):
        for cond,c in self.sent:
            if cond is None: c.wait_send()
            else: pl.when(cond)(lambda c=c: c.wait_send())
        self.sent=[]

def place():
    b=lax.axis_index("batch"); p=lax.axis_index("pix")
    core=lax.rem(b,2); y=lax.rem(lax.div(b,2),2); z=lax.div(b,4)
    return b,p,core,y,z

def base_of(s): return 16*((ROWS*s)//16)
def dg(a,b,ca,cb): return lax.dot_general(a,b,(((ca,),(cb,)),((),())),preferred_element_type=f32)
def nn(a,b): return dg(a,b,1,0)
def nt(a,b): return dg(a,b,1,1)
def tn(a,b): return dg(a,b,0,0)
def split3(v):
    hi=v.astype(bf); r=v-hi.astype(f32); mid=r.astype(bf); lo=(r-mid.astype(f32)).astype(bf)
    return hi,mid,lo
def exact(v,w,dot):
    hi,mid,lo=split3(v)
    return dot(hi,w)+dot(mid,w)+dot(lo,w)
def sigmoid(v): return 1.0/(1.0+jnp.exp(-v))
def silu(v): return v*sigmoid(v)
def slope(v):
    s=sigmoid(v)
    return s*(1.0+v*(1.0-s))
def cloop(n,chunk,body,init):
    return lax.fori_loop(0,n//chunk,lambda i,c: body(pl.multiple_of(i*chunk,chunk),c),init)
def col8(v): return jnp.sum(v.reshape(-1,8,v.shape[-1]),axis=0)
Z8=lambda: jnp.zeros((8,CH),f32)
class Blocks:
    def __init__(self,ref,n): self.ref=ref; self.n=n
def at_block(ref,j,sl):
    if isinstance(ref,Blocks): return ref.ref,(pl.ds(ref.n*j+sl.start,sl.size,stride=sl.stride),slice(None))
    return ref,(j,sl,slice(None))
def ld(ref,sl):
    out=[]
    for j in range(ref.ref.shape[0]//ref.n if isinstance(ref,Blocks) else ref.shape[0]):
        r,k=at_block(ref,j,sl)
        out.append(r[k])
    return jnp.concatenate(out,1)
def put3(ref,sl,v):
    for j in range(v.shape[1]//128):
        r,k=at_block(ref,j,sl)
        r[k]=v[:,128*j:128*j+128]
def every(start,n,step): return pl.ds(start,n,stride=step)
def row(v): return jnp.sum(v,axis=0,keepdims=True)


LAST=25
def step_kernel(images_all,
    mast,img,tgt,cln,vgg,lin,tvec,rowid,level,
    flat_ref,norm_ref,lev_ref,g_ref,
    wv,tails,cvt,cvt2,wd,wee,weo,wqT,x3a,x3b,z3,inner,middle,gout,gsec,ain,trT,dtrT,attT,xd,lse,dattT,ssend,srecv,hsend,hrecv,himg,dzs,dzr,geo,oth,wsem,tsem,xs,xr,total,blk,own_sem,azs,azr,axs,axr,ays,ayr,adar,adbr,ass,asr,pack_ref,lpk,ppk,red1,red2,tile,lps,lpr,pps,ppr,n1s,n1r,n2s,n2r,sibr,rb,rx,ry,zu,zd,s1s,s1r,dar,dbr,rxs,rxr,rys,ryr,zs,zur,zdr,acc,gtile,gls,glr,gps,gpr,rba,a2s,a2r,ads,ds_,hmid,esend,erecv,gm,a3s,a3r):
    b,p,core,y,z=place()
    q=1-p; xn=q; s=b*2+p
    pf=p.astype(f32); qf=1.0-pf
    yn=b+2-4*y; sib=b+1-2*core; oc=1-core
    up_ok=z<3; dn_ok=z>0
    top=z==3
    mine=(y*2+core)*2+p
    cvt3=Blocks(cvt,1536)
    mcopy=pltpu.make_async_copy(mast,cvt.at[pl.ds(0,1611)],own_sem)
    mcopy.start()
    barrier=pltpu.get_barrier_semaphore()
    plane=[]
    for dy in range(2):
        for dc in range(2):
            for dp in range(2):
                if dy+dc+dp: plane.append((4*dy+2*dc+dp,z*4+lax.rem(y+dy,2)*2+lax.rem(core+dc,2),lax.rem(p+dp,2)))
    line=[(k,lax.rem(z+k,4)) for k in range(1,4)]
    def sig(bb,pp): pl.semaphore_signal(barrier,inc=1,device_id=(bb,pp),device_id_type=MESH)
    for _,bb,pp in plane: sig(bb,pp)
    for _,zz in line: sig(b+4*(zz-z),p)
    def when(ok,f):
        if ok is None: f()
        else: pl.when(ok)(f)
    def AND(*c):
        r=None
        for k in c:
            if k is not None: r=k if r is None else r&k
        return r
    def wait_in(ref,sem):
        pltpu.make_async_remote_copy(src_ref=ref,dst_ref=ref,send_sem=sem,recv_sem=sem,device_id=(b,xn),device_id_type=MESH).wait_recv()
    def slot(zz,yy,pp,cc=core): return ((zz*2+yy)*2+cc)*2+pp
    A=pl.ds(0,HALF); B=pl.ds(HALF,BLK-HALF)
    cm=Comm()
    shift=lax.rem(9*s,16)
    total[ROWS-1:BLK]=jnp.zeros((BLK-ROWS+1,CH),f32)
    mcopy.wait()
    for j in range(3): total[0:ROWS,128*j:128*j+128]=cvt[pl.ds(j,ROWS,stride=3),:]
    at=lax.broadcasted_iota(jnp.int32,(BLK,CH),0)
    blk[...]=jnp.where(at==BLK-4,(level[...]==0).astype(f32),pltpu.roll(total[...],shift,0)).astype(bf)
    own=pltpu.make_async_copy(blk,g_ref.at[s],own_sem)
    own.start()
    pl.semaphore_wait(barrier,10)
    def valid(zz): return (zz>=0)&(zz<4)
    def pick(c0,c1,c2,c3): return jnp.where(z==0,c0,jnp.where(z==1,c1,jnp.where(z==2,c2,c3)))
    hs=(A,B)
    ends=(z==0)|(z==3); is1=z==1; is2=z==2; inner_z=jnp.logical_not(ends)
    def z_send(ok,zz,h,d,src=None):
        g=g_ref.at[slot(zz,y,p),hs[h]]
        cm.go(ok,g if src is None else src,g,azs.at[zz,(1-d)//2],azr.at[zz,h],b+4*d,p)
    def xy_send(ok,zz,h,src=None):
        g=g_ref.at[slot(zz,y,p),hs[h]]
        cm.go(ok,g if src is None else src,g,axs.at[zz],axr.at[zz,h],b,xn)
        cm.go(ok,g if src is None else src,g,ays.at[zz],ayr.at[zz,h],yn,p)
    def sib_send(ok,zz,yy,pp,h,src=None):
        sl=slot(zz,yy,pp)
        first=pl.multiple_of(16*lax.div(ROWS*sl,16),16)
        def part(lo,n):
            return g_ref.at[sl,pl.ds(lo,n)] if src is None else src.at[pl.ds(lo-(HALF if h else 0),n)]
        lo,n=(0,HALF) if h==0 else (HALF,528-HALF)
        cm.go(ok,part(lo,n),wv.at[pl.ds(first+lo,n)],ass.at[zz],asr.at[zz],sib,p)
        if h==1: cm.go(ok,part(528,32),tails.at[sl],ass.at[zz],asr.at[zz],sib,p)
    def own_sends():
        for h in range(2):
            src=blk.at[hs[h]]
            z_send(z==0,z,h,1,src)
            z_send(z==3,z,h,-1,src)
            sib_send(None,z,y,p,h,src)
    def own_xy():
        for h in range(2): xy_send(z!=1,z,h,blk.at[hs[h]])
    four=((1-y,xn),(y,xn),(1-y,p),(y,p))
    def two_send(ok,i,d):
        yy,pp=four[i]
        for h in range(2):
            g=g_ref.at[slot(2,yy,pp),hs[h]]
            cm.go(ok,g,g,a2s.at[(1-d)//2],a2r.at[yy,pp,h],b+4*d,p)
    def two_in(i,ok):
        yy,pp=four[i]
        for h in range(2):
            g=g_ref.at[slot(2,yy,pp),hs[h]]
            when(ok,lambda: wait_in(g,a2r.at[yy,pp,h]))
            cm.go(ok&(z==1),g,g,a2s.at[1],a2r.at[yy,pp,h],b-4,p)
            sib_send(ok,2,yy,pp,h)
    def three_out(i):
        yy,pp=four[i]
        for h in range(2):
            g=g_ref.at[slot(3,yy,pp),hs[h]]
            cm.go(top,g,g,a3s,a3r.at[yy,pp,h],b-4,p)
    def three_in(i):
        yy,pp=four[i]
        for h in range(2):
            g=g_ref.at[slot(3,yy,pp),hs[h]]
            when(is2,lambda: wait_in(g,a3r.at[yy,pp,h]))
            sib_send(is2,3,yy,pp,h)
    def diag_in(ok,zz):
        sd=slot(zz,1-y,xn)
        def f():
            wait_in(g_ref.at[sd,A],adar.at[zz])
            wait_in(g_ref.at[sd,B],adbr.at[zz])
        when(ok,f)
        for h in range(2): sib_send(ok,zz,1-y,xn,h)
    def two_diag():
        sd=slot(2,1-y,xn)
        def f():
            wait_in(g_ref.at[sd,A],adar.at[2])
            wait_in(g_ref.at[sd,B],adbr.at[2])
        when(z==2,f)
        for h in range(2): sib_send(z==2,2,1-y,xn,h)
    def arrive0(h):
        ok=z!=0
        when(ok,lambda: wait_in(g_ref.at[slot(0,y,p),hs[h]],azr.at[0,h]))
        z_send(ok&up_ok,0,h,1)
        xy_send(ok,0,h)
        sib_send(ok,0,y,p,h)
    def arrive3(h,ok):
        when(ok,lambda: wait_in(g_ref.at[slot(3,y,p),hs[h]],azr.at[3,h]))
        z_send(ok&dn_ok,3,h,-1)
        sib_send(ok,3,y,p,h)
    def xy_arrive(ok,f,h):
        sx=slot(f,y,xn); sy=slot(f,1-y,p)
        when(ok,lambda: wait_in(g_ref.at[sx,hs[h]],axr.at[f,h]))
        if h==0: cm.go(ok,g_ref.at[sx,A],g_ref.at[sx,A],ads.at[f],adar.at[f],yn,p)
        sib_send(ok,f,y,xn,h)
        when(ok,lambda: wait_in(g_ref.at[sy,hs[h]],ayr.at[f,h]))
        if h==1: cm.go(ok,g_ref.at[sy,B],g_ref.at[sy,B],ads.at[f],adbr.at[f],b,xn)
        sib_send(ok,f,1-y,p,h)
    def later_sends():
        for h in range(2):
            src=blk.at[hs[h]]
            z_send(z==1,z,h,1,src)
            z_send(z==1,z,h,-1,src)
    def one_in(h,ok):
        when(ok,lambda: wait_in(g_ref.at[slot(1,y,p),hs[h]],azr.at[1,h]))
        z_send(ok&is2,1,h,1)
        sib_send(ok,1,y,p,h)
    def load(sl): return (pltpu.make_async_copy(g_ref.at[sl,pl.ds(0,528)],wv.at[pl.ds(pl.multiple_of(16*lax.div(ROWS*sl,16),16),528)],wsem.at[lax.div(sl,8)]),
                          pltpu.make_async_copy(g_ref.at[sl,pl.ds(528,32)],tails.at[sl],tsem.at[lax.div(sl,8)]))
    def d_arrive(zz):
        sd=slot(zz,1-y,xn)
        wait_in(g_ref.at[sd,A],adar.at[zz])
        sib_send(None,zz,1-y,xn,0)
        wait_in(g_ref.at[sd,B],adbr.at[zz])
        sib_send(None,zz,1-y,xn,1)
        for yy in range(2):
            for pp in range(2):
                for c in load(slot(zz,yy,pp)): c.start()
    def sib_arrive(zz):
        wait_in(g_ref.at[pl.ds(0,4)],asr.at[zz])
    has_gains=s==31
    gain_line=(y==1)&(core==1)&(p==1)
    def gain_sends():
        for k,zz in line: cm.go(has_gains,blk.at[pl.ds(528,16)],gtile,gls,glr,b+4*(zz-z),p)
    def gain_pass():
        pl.when(has_gains)(lambda: gtile.__setitem__(Ellipsis,blk[528:544]))
        pl.when(gain_line&jnp.logical_not(has_gains))(lambda: wait_in(gtile,glr))
        for d,bb,pp in plane: cm.go(gain_line,gtile,gtile,gps,gpr,bb,pp)
    def gain_wait():
        pl.when(jnp.logical_not(gain_line))(lambda: wait_in(gtile,gpr))
    seen=[]
    def take(shards):
        pltpu.make_async_copy(wv.at[pl.ds(0,4*528)],wv.at[pl.ds(0,4*528)],wsem.at[shards[0]//8]).wait()
        pltpu.make_async_copy(tails.at[pl.ds(0,4)],tails.at[pl.ds(0,4)],tsem.at[shards[0]//8]).wait()
        for k in shards:
            lo=base_of(k)
            if k<31 and base_of(k+1)-lo==544 or k==31: wv[lo+528:lo+544]=tails[k,0:16]
            seen.append(k)
        for k in range(1,32):
            if k in seen and k-1 in seen and (k in shards or k-1 in shards):
                off=base_of(k)-base_of(k-1)-528
                t=tails[k-1,off:off+16].astype(f32)
                if off: t=jnp.where(lax.broadcasted_iota(jnp.int32,(16,CH),0)<8,t,0.0)
                lo=base_of(k)
                wv[lo:lo+16]=(wv[lo:lo+16].astype(f32)+t).astype(bf)
    def rows(u,yy,pp,cc=core):
        at=pl.ds(pl.multiple_of(16*lax.div(ROWS*slot(u,yy,pp,cc),16),16),BLK)
        return wd.at[at,pl.ds(0,CH)] if u==0 else wv.at[at]
    def need(u,yy,pp,cc=core): return None if u<3 else slot(u,yy,pp,cc)<=LAST
    def sibsend(u):
        for yy,pp in four:
            cm.go(need(u,yy,pp,oc),rows(u,yy,pp,oc),sibr.at[4*u+2*yy+pp],s1s.at[u],s1r.at[u,yy,pp],sib,p)
    def both(u,yy,pp,lo,n):
        a=pl.multiple_of(16*lax.div(ROWS*slot(u,yy,pp),16)+lo,16)
        mine_=wd[pl.ds(a,n),0:CH] if u==0 else wv[pl.ds(a,n)]
        return mine_.astype(f32)+sibr[4*u+2*yy+pp,lo:lo+n].astype(f32)
    HA=(0,HALF); HB=(HALF,BLK-HALF)
    def sib_in(u,yy,pp): wait_in(sibr.at[4*u+2*yy+pp],s1r.at[u,yy,pp])
    def keep(u,yy,pp,half,more=None):
        t=both(u,yy,pp,*half)
        if more is not None: t=t+more.astype(f32)
        sibr[4*u+2*yy+pp,half[0]:half[0]+half[1]]=t.astype(bf)
    def diag(u):
        yy,pp=1-y,xn
        c=need(u,yy,pp)
        def f():
            sib_in(u,yy,pp)
            keep(u,yy,pp,HA); keep(u,yy,pp,HB)
        when(c,f)
        src=sibr.at[4*u+2*yy+pp]
        if u<2: cm.go(c,src.at[A],rba.at[u],ds_.at[u],dar.at[u],b,xn)
        else: cm.go(c,src.at[A],rba.at[u],ds_.at[u],dar.at[u],yn,p)
        cm.go(c,src.at[B],rb.at[u],ds_.at[u],dbr.at[u],yn,p)
    def ysend(u):
        c=need(u,1-y,p)
        def f():
            sib_in(u,1-y,p)
            keep(u,1-y,p,HA); keep(u,1-y,p,HB)
        when(c,f)
        for h in range(2): cm.go(c,sibr.at[4*u+2*(1-y)+p,hs[h]],ry.at[u,hs[h]],rys.at[u],ryr.at[u,h],yn,p)
    def xsend(u,only=None):
        c=AND(need(u,y,xn),only)
        def f():
            sib_in(u,y,xn)
            wait_in(rba.at[u],dar.at[u])
            keep(u,y,xn,HA,rba[u])
        when(c,f)
        cm.go(c,sibr.at[4*u+2*y+xn,A],rx.at[u,A],rxs.at[u],rxr.at[u,0],b,xn)
        def f2():
            wait_in(rb.at[u],dbr.at[u])
            keep(u,y,xn,HB,rb[u])
        when(c,f2)
        cm.go(c,sibr.at[4*u+2*y+xn,B],rx.at[u,B],rxs.at[u],rxr.at[u,1],b,xn)
    def put_x(u,half,h,more=None):
        keep(u,y,xn,half,more)
        cm.go(None,sibr.at[4*u+2*y+xn,hs[h]],rx.at[u,hs[h]],rxs.at[u],rxr.at[u,h],b,xn)
    def put_y(u,half,h,more=None):
        keep(u,1-y,p,half,more)
        cm.go(None,sibr.at[4*u+2*(1-y)+p,hs[h]],ry.at[u,hs[h]],rys.at[u],ryr.at[u,h],yn,p)
    def first_halves(u):
        sib_in(u,y,xn)
        sib_in(u,1-y,p)
        if u>0:
            put_x(u,HA,0)
            put_y(u,HB,1)
    def second_halves(u):
        wait_in(rba.at[u],dar.at[u])
        put_y(u,HA,0,rba[u])
        if u==0: put_y(u,HB,1)
        wait_in(rb.at[u],dbr.at[u])
        put_x(u,HB,1,rb[u])
    def chunks(u): return ((0,80,0),(80,80,0),(160,64,0),(224,64,0),(288,80,1),(368,64,1),(432,64,1),(496,64,1)) if u==0 else ((0,HALF,0),(HALF,BLK-HALF,1))
    def zur_at(u,k): return zur.at[2*(u-1)+k]
    def zdr_at(u,k): return zdr.at[k if u==0 else 8+2*(u-1)+k]
    def xy_in(u,h):
        wait_in(rx.at[u,hs[h]],rxr.at[u,h])
        wait_in(ry.at[u,hs[h]],ryr.at[u,h])
    def zstep(u,i):
        for d in (1,-1):
            at_z=i if d==1 else 3-i
            if not (at_z<u if d==1 else at_z>u): continue
            c=AND(need(u,y,p),z==at_z)
            buf,bsem=(zu.at[u-1],zur_at) if d==1 else (zd.at[u],zdr_at)
            own_at=4*u+2*y+p
            def first(): sib_in(u,y,p)
            when(c,first)
            seen_h=set()
            for k,(lo,n,h) in enumerate(chunks(u)):
                def f():
                    if h not in seen_h: xy_in(u,h)
                    t=both(u,y,p,lo,n)+rx[u,lo:lo+n].astype(f32)+ry[u,lo:lo+n].astype(f32)
                    if i>0:
                        wait_in(buf.at[pl.ds(lo,n)],bsem(u,k))
                        t=t+buf[lo:lo+n].astype(f32)
                    sibr[own_at,lo:lo+n]=t.astype(bf)
                when(c,f)
                seen_h.add(h)
                cm.go(c,sibr.at[own_at,pl.ds(lo,n)],buf.at[pl.ds(lo,n)],zs.at[u],bsem(u,k),b+4*d,p)
    def zend(u):
        def f():
            sib_in(u,y,p)
            done=set()
            for k,(lo,n,h) in enumerate(chunks(u)):
                if h not in done: xy_in(u,h); done.add(h)
                t=both(u,y,p,lo,n)+rx[u,lo:lo+n].astype(f32)+ry[u,lo:lo+n].astype(f32)
                if u>0:
                    wait_in(zu.at[u-1,pl.ds(lo,n)],zur_at(u,k))
                    t=t+zu[u-1,lo:lo+n].astype(f32)
                if u<3:
                    wait_in(zd.at[u,pl.ds(lo,n)],zdr_at(u,k))
                    t=t+zd[u,lo:lo+n].astype(f32)
                if u==3:
                    rr=16*lax.div(ROWS*s,16)+lo+lax.broadcasted_iota(jnp.int32,(n,CH),0)
                    t=jnp.where(rr<R_EMB,t,total[lo:lo+n])
                total[lo:lo+n]=t
        when(AND(need(u,y,p),z==u),f)
    state={"k":0}
    def xchg(src,dst,dst_like=None):
        k=state["k"]; state["k"]=k+1
        c=pltpu.make_async_remote_copy(src_ref=src,dst_ref=dst,send_sem=xs.at[k],recv_sem=xr.at[k],device_id=(b,q),device_id_type=MESH)
        c.start()
        return c
    edge=pl.ds(pl.multiple_of(q*480,32),32)
    gain_sends()
    c_img=xchg(img.at[edge],himg)
    def gsum(v): return exact(v,gm[...],nn)
    def swap_sums(k,s1,s2):
        ssend[k]=jnp.concatenate([s1,s2,jnp.zeros((6,CH),f32)],0)
        return xchg(ssend.at[k],srecv.at[k])
    def total_sums(k):
        t=gsum(ssend[k]+srecv[k])/(12.0*2*PX)
        return t[0:1],t[1:2]
    def norm_of(t):
        mean,sq=t
        return mean,lax.rsqrt(jnp.maximum(sq-mean*mean,0.0)+EPS_NORM)
    def fill3(dst,at,a):
        col=lax.broadcasted_iota(jnp.int32,a.shape,0)&31
        n=a.shape[0]
        dst[pl.ds(at,n),CH:2*CH]=a.astype(bf)
        dst[pl.ds(at,n),0:CH]=jnp.where(col==0,0.0,pltpu.roll(a,1,0)).astype(bf)
        dst[pl.ds(at,n),2*CH:3*CH]=jnp.where(col==31,0.0,pltpu.roll(a,n-1,0)).astype(bf)
    def fill_edges(dst,h):
        fill3(dst,0,h*pf); fill3(dst,544,h*qf)
    def conv_to(dst,x3,wrow,add=None):
        for dr in range(3):
            d=nn(x3[32*dr:32*dr+PX],wv[wrow+1152*dr:wrow+1152*dr+1152])
            if dr==0: dst[...]=d if add is None else add()+d
            else: dst[...]+=d
    def conv_dx(dst,wrow):
        first=True
        for dr in range(3):
            for dc in range(3):
                d=nt(z3[32*(2-dr):32*(2-dr)+PX,CH*(2-dc):CH*(2-dc)+CH],wv[wrow+CH*(3*dr+dc):wrow+CH*(3*dr+dc)+CH])
                if first: dst[...]=d
                else: dst[...]+=d
                first=False
    def st(i,c):
        v=img[pl.ds(i,64)].astype(f32)
        return c[0]+col8(v),c[1]+col8(v*v)
    a1,a2=cloop(PX,64,st,(Z8(),Z8()))
    c=swap_sums(0,row(a1),row(a2))
    own_sends()
    gain_pass()
    own_xy()
    group_of=lambda d: lax.shift_right_logical(lax.broadcasted_iota(jnp.int32,(CH,CH),d)*43691,19)
    gm[...]=(group_of(0)==group_of(1)).astype(f32).astype(bf)
    gain_wait()
    g6=gtile[...].astype(f32)
    g1,b1,g2,b2,g3,b3=[g6[2+i:3+i] for i in range(6)]
    c.wait()
    mean1,inv1=norm_of(total_sums(0))
    def act_of(v): return silu((v-mean1)*inv1*g1+b1)
    arrive3(0,is2)
    arrive3(1,is2)
    def fa(i,_):
        fill3(x3a,pl.multiple_of(i+32,32),act_of(img[pl.ds(i,64)].astype(f32)))
        return 0
    cloop(PX,64,fa,0)
    c_img.wait()
    fill_edges(x3a,act_of(himg[...].astype(f32)))
    own.wait()
    xy_arrive(z==3,3,0)
    xy_arrive(z==3,3,1)
    arrive0(0)
    xy_arrive(is2,2,0)
    three_out(1); three_out(2)
    arrive0(1)
    diag_in(top,3)
    three_out(0)
    xy_arrive(is2,2,1)
    arrive3(0,is1)
    arrive3(1,is1)
    later_sends()
    two_send(is2,3,-1)
    two_send(is2,1,-1); two_send(is2,2,-1)
    xy_arrive(None,0,0)
    one_in(0,is2)
    one_in(1,is2)
    xy_arrive(None,0,1)
    for h in range(2): xy_send(is1,3,h)
    for h in range(2): xy_send(is2,1,h)
    for h in range(2): one_in(h,top)
    for h in range(2): xy_send(top,1,h)
    for i in (3,1,2): two_send(is2,i,1)
    two_diag()
    two_send(is2,0,-1); two_send(is2,0,1)
    d_arrive(0)
    arrive3(0,z==0)
    xy_send(z==0,3,0)
    sib_arrive(0)
    take(range(0,8))
    conv_to(inner,x3a,R_ONE)
    def st2(i,c):
        v=inner[pl.ds(i,64)]
        return c[0]+col8(v),c[1]+col8(v*v)
    a1,a2=cloop(PX,64,st2,(Z8(),Z8()))
    c1=swap_sums(1,row(a1),row(a2))
    c2=xchg(inner.at[edge],hrecv.at[0])
    two_in(3,is1)
    xy_arrive(z>=2,1,0)
    arrive3(1,z==0)
    xy_send(z==0,3,1)
    xy_arrive(z<2,3,0)
    xy_arrive(z<2,3,1)
    for h in range(2): one_in(h,z==0)
    for h in range(2): xy_send(z<2,1,h)
    three_in(1); three_in(2)
    xy_arrive(z>=2,1,1)
    three_in(0)
    diag_in(z<2,3)
    for yy in range(2):
        for pp in range(2):
            for k in load(slot(3,yy,pp)): k.start()
    sib_arrive(3)
    two_in(1,is1)
    take(range(24,32))
    ids=rowid[...]
    pre=[]
    tcol=lax.broadcasted_iota(jnp.int32,(16,R_END-R_TAB),1)
    for h in range(2):
        hot=(tcol==2*ids+h).astype(f32).astype(bf)
        pre.append(nn(hot,wv[R_TAB:R_END])[0:1]+tvec[:,CH*h:CH*h+CH])
    emb=[silu(v) for v in pre]
    put3(cvt3,pl.ds(0,1536),wv[R_EMB:R_TAB].astype(f32))
    wee[...]=ld(cvt3,every(0,768,2)).astype(bf)
    weo[...]=ld(cvt3,every(1,768,2)).astype(bf)
    def emb_dot(w):
        r=None
        for h in range(2):
            e=jnp.broadcast_to(emb[h],(16,CH))
            d=exact(e,w[CH*h:CH*h+CH],nn)[0:1]
            r=d if r is None else r+d
        return r
    sc1=1.0+emb_dot(wee); sh=emb_dot(weo)
    c1.wait()
    xy_arrive(z<2,1,0)
    mean2,inv2=norm_of(total_sums(1))
    def pre_b(v):
        n=(v-mean2)*inv2
        af=n*g2+b2
        return n,af,af*sc1+sh
    def fb(i,_):
        fill3(x3b,pl.multiple_of(i+32,32),silu(pre_b(inner[pl.ds(i,64)])[2]))
        return 0
    cloop(PX,64,fb,0)
    c2.wait()
    fill_edges(x3b,silu(pre_b(hrecv[0])[2]))
    xy_arrive(z<2,1,1)
    two_in(2,is1)
    d_arrive(1)
    sib_arrive(1)
    two_in(0,is1)
    take(range(8,16))
    conv_to(middle,x3b,R_TWO,lambda: img[...].astype(f32))
    def st3(i,c):
        v=middle[pl.ds(i,64)]
        return c[0]+col8(v),c[1]+col8(v*v)
    a1,a2=cloop(PX,64,st3,(Z8(),Z8()))
    c1=swap_sums(2,row(a1),row(a2))
    put3(cvt3,pl.ds(0,1152),wv[R_QKV:R_PROJ].astype(f32))
    for j in range(3):
        wqT[CH*j:CH*j+CH]=ld(cvt3,every(j,CH,3)).T.astype(bf)
    c1.wait()
    mean3,inv3=norm_of(total_sums(2))
    def fc(i,_):
        n=(middle[pl.ds(i,64)]-mean3)*inv3
        ain[pl.ds(i,64)]=(n*g3+b3).astype(bf)
        return 0
    cloop(PX,64,fc,0)
    c_in=xchg(ain.at[pl.ds(0,PX)],ain.at[pl.ds(PX,PX)])
    c_mid=xchg(middle.at[edge],hmid)
    def triples(a):
        t=nt(wqT[...],a)
        is_q=lax.rem(lax.broadcasted_iota(jnp.int32,t.shape,0),192)<64
        return jnp.where(is_q,t*0.125,t).astype(bf)
    trT[:,0:PX]=triples(ain[0:PX])
    def head_rows(h):
        r0=pl.multiple_of(h*192,64)
        return r0,pl.multiple_of(r0+64,64),pl.multiple_of(r0+128,64)
    def fh1(h,_):
        r0,r1,r2=head_rows(h)
        sco=nn(trT[pl.ds(r1,64),0:PX].T,trT[pl.ds(r0,64),0:PX])
        m=jnp.max(sco,0,keepdims=True)
        e=jnp.exp(sco-m)
        lse[h,0:1]=m
        lse[h,1:2]=jnp.sum(e,0,keepdims=True)
        acc[h]=nn(trT[pl.ds(r2,64),0:PX],e.astype(bf))
        return 0
    lax.fori_loop(0,6,fh1,0)
    for i in (3,1,2): two_in(i,ends)
    c_in.wait()
    trT[:,PX:2*PX]=triples(ain[PX:2*PX])
    def fh(h,_):
        r0,r1,r2=head_rows(h)
        sco=nn(trT[pl.ds(r1,64),PX:2*PX].T,trT[pl.ds(r0,64),0:PX])
        m0=lse[h,0:1]
        m=jnp.maximum(m0,jnp.max(sco,0,keepdims=True))
        e=jnp.exp(sco-m)
        a=jnp.exp(m0-m)
        l=lse[h,1:2]*a+jnp.sum(e,0,keepdims=True)
        o=acc[h]*a+nn(trT[pl.ds(r2,64),PX:2*PX],e.astype(bf))
        attT[pl.ds(pl.multiple_of(h*64,64),64),:]=(o*(1.0/l)).astype(bf)
        lse[h,0:1]=m+jnp.log(l)
        return 0
    lax.fori_loop(0,6,fh,0)
    put3(gout,pl.ds(0,PX),middle[...]+tn(attT[...],wv[R_PROJ:R_DOWN]))
    hsend[0]=ld(gout,edge).astype(bf)
    c1=xchg(hsend.at[0],oth.at[0])
    two_in(0,ends)
    for yy in range(2):
        for pp in range(2):
            for k in load(slot(2,yy,pp)): k.start()
    sib_arrive(2)
    take(range(16,24))
    for off in range(9):
        put3(cvt3,pl.ds(0,576),wv[R_DOWN+576*off:R_DOWN+576*off+576].astype(f32))
        v0,v1,v2=[ld(cvt3,every(i,192,3)) for i in range(3)]
        put3(cvt2,every(0,192,2),jnp.concatenate([v0,v1[:,0:256]],1))
        w=jnp.concatenate([v1[:,128:384],v2],1)
        w=pltpu.roll(w,w.shape[1]-64,1)
        put3(cvt2,every(1,192,2),w)
        wd[CH*off:CH*off+CH]=ld(cvt2,pl.ds(0,CH))[:,0:576].astype(bf)
    def parts(ref,n):
        e=ld(ref,every(0,n//2,2)); o=ld(ref,every(1,n//2,2))
        col=lax.broadcasted_iota(jnp.int32,o.shape,0)&15
        return jnp.where(col==0,0.0,pltpu.roll(o,1,0)).astype(bf),e.astype(bf),o.astype(bf)
    for dc,v in enumerate(parts(gout,PX)):
        v=v.reshape(8,32,CH)
        even=v[:,0:16].reshape(128,CH); odd=v[:,16:32].reshape(128,CH)
        xd[:,CH*(3+dc):CH*(3+dc)+CH]=even
        xd[:,CH*(6+dc):CH*(6+dc)+CH]=odd
        xd[16:128,CH*dc:CH*dc+CH]=odd[0:112]
    c1.wait()
    put3(geo,pl.ds(0,32),oth[0].astype(f32)*pf)
    for dc,v in enumerate(parts(geo,32)):
        xd[0:16,CH*dc:CH*dc+CH]=v
    fin=nn(xd[...],wd[0:9*CH])
    feat=nn(fin.astype(bf),vgg[...]); tf=nn(tgt[...],vgg[...])
    ir=lax.rsqrt(jnp.mean(feat*feat,-1,keepdims=True)+EPS_FEAT)
    unit=feat*ir
    diff=unit-tf*lax.rsqrt(jnp.mean(tf*tf,-1,keepdims=True)+EPS_FEAT)
    wl=lin[...]*diff
    consist=jnp.sum(row(wl*diff),1,keepdims=True)*(1.0/(256*256))
    du=wl*(2.0/(256*256*images_all))
    dfeat=(ir*(du-unit*jnp.mean(du*unit,-1,keepdims=True))).astype(bf)
    zc=jnp.zeros((16,128),f32)
    for t_ in range(0,32,2): zc=zc+tails[t_,16:32,0:128].astype(f32)
    zc=zc[12:13,0:1]
    seed=(level[...]==0).astype(f32)/jnp.maximum(zc,1.0)*(2.0/(256*CH2))
    gfin=nt(dfeat,vgg[...])+seed*(fin-cln[...].astype(f32))
    dz=gfin.astype(bf)
    dzs[...]=dz[0:16]
    c1=xchg(dzs,dzr)
    for off in range(9):
        dw=tn(xd[:,CH*off:CH*off+CH],dz)
        put3(cvt2,pl.ds(0,CH),jnp.concatenate([dw,jnp.zeros((CH,64),f32)],1))
        e=ld(cvt2,every(0,192,2)); o_=pltpu.roll(ld(cvt2,every(1,192,2)),64,1)
        lane=lax.broadcasted_iota(jnp.int32,(192,128),1)
        put3(cvt3,every(0,192,3),e[:,0:384])
        put3(cvt3,every(1,192,3),jnp.concatenate([e[:,384:512],jnp.where(lane<64,e[:,512:640],o_[:,0:128]),o_[:,128:256]],1))
        put3(cvt3,every(2,192,3),o_[:,256:640])
        wv[R_DOWN+576*off:R_DOWN+576*off+576]=ld(cvt3,pl.ds(0,576)).astype(bf)
    sibsend(2); sibsend(3)
    c1.wait()
    z32=dz.astype(f32)
    down=jnp.concatenate([z32[16:128],dzr[...].astype(f32)*qf],0)
    def left(v):
        col=lax.broadcasted_iota(jnp.int32,v.shape,0)&15
        return jnp.where(col==15,0.0,pltpu.roll(v,127,0)).astype(bf)
    s00,s01,s10,s11=dz,left(z32),down.astype(bf),left(down)
    W=lambda a,c: wd[CH*(3*a+c):CH*(3*a+c)+CH]
    def put(a,c,v):
        for i in range(8):
            put3(gout,every((2*i+a)*32+c,16,2),v[16*i:16*i+16])
    put(0,0,nt(s00,W(1,1)))
    put(0,1,nt(s00,W(1,2))+nt(s01,W(1,0)))
    put(1,0,nt(s00,W(2,1))+nt(s10,W(0,1)))
    put(1,1,nt(s00,W(2,2))+nt(s01,W(2,0))+nt(s10,W(0,2))+nt(s11,W(0,0)))
    diag(2); diag(3); ysend(2); ysend(3)
    gp=ld(gout,pl.ds(0,PX)).astype(bf)
    dattT[...]=nt(wv[R_PROJ:R_DOWN],gp).astype(bf)
    wv[R_PROJ:R_DOWN]=nn(attT[...],gp).astype(bf)
    def bh_part(h,at,n):
        r0,r1,r2=head_rows(h)
        ra_=pl.ds(pl.multiple_of(h*64,64),64)
        qT=trT[pl.ds(r0,64),0:PX]
        kT=trT[pl.ds(r1,64),at:at+n]
        gT=dattT[ra_,:]
        pr=jnp.exp(nn(kT.T,qT)-lse[h,0:1])
        de=jnp.sum(gT.astype(f32)*attT[ra_,:].astype(f32),0,keepdims=True)
        ds=(pr*(nn(trT[pl.ds(r2,64),at:at+n].T,gT)-de)).astype(bf)
        dtrT[pl.ds(r1,64),at:at+n]=nt(qT,ds).astype(bf)
        dtrT[pl.ds(r2,64),at:at+n]=nt(gT,pr.astype(bf)).astype(bf)
        return r0,nn(kT,ds)*0.125
    def bh(at,first):
        def f(h,_):
            r0,dqT=bh_part(h,at,256)
            if first:
                acc[h]=dqT
                dtrT[pl.ds(r0,64),PX:2*PX]=jnp.zeros((64,PX),bf)
            else: acc[h]+=dqT
            return 0
        return f
    c_g=[]
    for i in range(2):
        at=PX+256*i
        lax.fori_loop(0,6,bh(at,i==0),0)
        oth[1+8*i:9+8*i]=tn(dtrT[:,at:at+256],wqT[...]).astype(bf).reshape(8,32,CH)
        c_g.append(xchg(oth.at[pl.ds(1+8*i,8)],oth.at[pl.ds(17+8*i,8)]))
    def bh2(h,_):
        r0,dqT=bh_part(h,0,PX)
        dtrT[pl.ds(r0,64),0:PX]=(acc[h]+dqT).astype(bf)
        return 0
    lax.fori_loop(0,6,bh2,0)
    gsec[...]=tn(dtrT[:,0:PX],wqT[...])
    for c in c_g: c.wait()
    def n3_of(i): return (middle[pl.ds(i,64)]-mean3)*inv3
    def s3(i,c):
        j=pl.multiple_of(17+lax.div(i,32),1)
        v=gsec[pl.ds(i,64)]+oth[pl.ds(j,2)].reshape(64,CH).astype(f32)
        gsec[pl.ds(i,64)]=v
        return c[0]+col8(v),c[1]+col8(v*n3_of(i))
    a1,a2=cloop(PX,64,s3,(Z8(),Z8()))
    db3,dg3=row(a1),row(a2)
    c1=swap_sums(3,db3*g3,dg3*g3)
    esend[0]=ld(gout,edge)+inv3*(gsec[edge]*g3)
    c2=xchg(esend.at[0],erecv.at[0])
    xsend(2)
    dq=nt(ain[...].T,dtrT[...])
    for j in range(3):
        put3(cvt3,every(j,CH,3),dq[:,CH*j:CH*j+CH])
    wv[R_QKV:R_PROJ]=ld(cvt3,pl.ds(0,1152)).astype(bf)
    c1.wait()
    m1,m2=total_sums(3)
    def f3(i,_):
        v=ld(gout,pl.ds(i,64))+inv3*(gsec[pl.ds(i,64)]*g3-m1-n3_of(i)*m2)
        fill3(z3,pl.multiple_of(i+32,32),v)
        return 0
    cloop(PX,64,f3,0)
    c_mid.wait()
    c2.wait()
    fill_edges(z3,erecv[0]-inv3*(m1+(hmid[...]-mean3)*inv3*m2))
    conv_dx(gsec,R_TWO)
    for dr in range(3):
        d=tn(x3b[32*dr:32*dr+PX],z3[32:32+PX,CH:2*CH]).astype(bf)
        wv[R_TWO+1152*dr:R_TWO+1152*dr+1152]=d
        if dr==0: wd[R_TWO:4304,0:CH]=d[0:4304-R_TWO]
    sibsend(1)
    def s2(i,c):
        n,af,pb=pre_b(inner[pl.ds(i,64)])
        gpre=gsec[pl.ds(i,64)]*slope(pb)
        gaff=gpre*sc1
        gsec[pl.ds(i,64)]=gaff
        return c[0]+col8(gpre*af),c[1]+col8(gpre),c[2]+col8(gaff*n),c[3]+col8(gaff)
    a1,a2,a3,a4=cloop(PX,64,s2,(Z8(),Z8(),Z8(),Z8()))
    dsc,dsh,dg2,db2=row(a1),row(a2),row(a3),row(a4)
    c1=swap_sums(4,db2*g2,dg2*g2)
    esend[1]=gsec[edge]*g2
    c2=xchg(esend.at[1],erecv.at[1])
    diag(1)
    first_halves(1)
    c1.wait()
    m1,m2=total_sums(4)
    def f2(i,_):
        n=(inner[pl.ds(i,64)]-mean2)*inv2
        fill3(z3,pl.multiple_of(i+32,32),inv2*(gsec[pl.ds(i,64)]*g2-m1-n*m2))
        return 0
    cloop(PX,64,f2,0)
    c2.wait()
    fill_edges(z3,inv2*(erecv[1]-m1-(hrecv[0]-mean2)*inv2*m2))
    for dr in range(3):
        wd[1152*dr:1152*dr+1152,0:CH]=tn(x3a[32*dr:32*dr+PX],z3[32:32+PX,CH:2*CH]).astype(bf)
    sibsend(0)
    second_halves(1)
    xsend(3,z<2)
    zstep(2,0)
    diag(0)
    first_halves(0)
    conv_dx(gsec,R_ONE)
    def s1(i,c):
        n=(img[pl.ds(i,64)].astype(f32)-mean1)*inv1
        gpre=gsec[pl.ds(i,64)]*slope(n*g1+b1)
        return c[0]+col8(gpre*n),c[1]+col8(gpre)
    a1,a2=cloop(PX,64,s1,(Z8(),Z8()))
    ge=[]
    for h in range(2):
        d=exact(jnp.broadcast_to(dsc,(16,CH)),wee[CH*h:CH*h+CH],nt)+exact(jnp.broadcast_to(dsh,(16,CH)),weo[CH*h:CH*h+CH],nt)
        ge.append(d[0:1]*slope(pre[h]))
    hot_level=(lax.broadcasted_iota(jnp.int32,(1,CH),1)==level[...]).astype(f32)
    pack_ref[...]=jnp.concatenate([row(a1),row(a2),dg2,db2,dg3,db3,dsc,dsh,ge[0],ge[1],emb[0],emb[1],consist*hot_level,jnp.broadcast_to(ids.astype(f32),(1,CH)),0.5*hot_level,jnp.zeros((1,CH),f32)],0)
    low=jnp.logical_not(top)
    cm.go(low,pack_ref,lpk.at[z],lps,lpr,b+4*(3-z),p)
    put_x(0,HA,0)
    zstep(1,0)
    zstep(3,0)
    second_halves(0)
    xsend(3,z>=2)
    zstep(2,1)
    zstep(1,1)
    zstep(0,0)
    zstep(3,1)
    zstep(0,1)
    zstep(3,2)
    def packs_line():
        lpk[3]=pack_ref[...]
        wait_in(lpk.at[pl.ds(0,3)],lpr)
    pl.when(top)(packs_line)
    for d,bb,pp in plane:
        cm.go(top,lpk,ppk.at[mine],pps,ppr,bb,pp)
    def packs_plane():
        ppk[mine]=lpk[...]
        wait_in(ppk.at[pl.ds(0,7)],ppr)
        a_s=16*lax.div(ROWS*s,16)
        rows_at=lambda k: ppk[:,:,k,:].reshape(32,384)
        zero=jnp.zeros((64,384),f32)
        for h in range(2):
            e=rows_at(10+h)
            t=jnp.concatenate([e,e,zero],0).T
            cvt[pl.ds(BLK+768*h,384,stride=2),:]=t
            cvt[pl.ds(BLK+768*h+1,384,stride=2),:]=t
        r=a_s+lax.broadcasted_iota(jnp.int32,(BLK,128),0)
        l=lax.broadcasted_iota(jnp.int32,(BLK,128),1)
        inside=(r>=R_EMB)&(r<R_TAB)
        start=pl.multiple_of(jnp.clip(a_s-R_EMB+BLK,0,BLK+1536),16)
        lf=jnp.where(inside&(((r&1)==1)==(l>=32))&(l<64),cvt[pl.ds(start,BLK),:],0.0)
        ids=rows_at(13)[:,0:128].astype(jnp.int32)
        ids=jnp.concatenate([ids]*4,0).astype(f32).T[0:1].astype(jnp.int32)
        hot=(r-R_TAB==2*ids+(l>=96).astype(jnp.int32))&(l>=64)&(r>=R_TAB)
        lf=jnp.where(hot,1.0,lf)
        rg=jnp.concatenate([rows_at(6),rows_at(7),rows_at(8),rows_at(9)],0)
        gains=[jnp.sum(rows_at(k),0,keepdims=True) for k in range(6)]
        hi=lax.Precision.HIGHEST
        add=lax.dot_general(lf,rg,(((1,),(0,)),((),())),precision=hi,preferred_element_type=f32)
        for k in range(6): add=add+jnp.where(r[:,0:1]-R_GAIN==k,gains[k],0.0)
        rr=a_s+lax.broadcasted_iota(jnp.int32,(BLK,384),0)
        total[...]=jnp.where(rr<R_EMB,0.0,add)
    pl.when(top)(packs_plane)
    zstep(0,2)
    zend(1); zend(2); zend(3)
    zend(0)
    shift=lax.rem(9*s,16)
    tr_=lax.broadcasted_iota(jnp.int32,(BLK,1),0)
    t=jnp.where((tr_>=shift)&(tr_<shift+ROWS),total[...],0.0)
    sq=jnp.sum(jnp.sum(t*t,0,keepdims=True),1,keepdims=True)
    tile[...]=jnp.concatenate([jnp.broadcast_to(sq,(1,128)),pack_ref[12:13,0:128],pack_ref[14:15,0:128],jnp.zeros((5,128),f32)],0)
    red1[mine]=tile[...]
    for d,bb,pp in plane: cm.go(None,tile,red1.at[mine],n1s,n1r,bb,pp)
    t=pltpu.roll(total[...],lax.rem(BLK-shift,BLK),0)[0:ROWS]
    for j in range(3): cvt[pl.ds(j,ROWS,stride=3),:]=t[:,128*j:128*j+128]
    fcopy=pltpu.make_async_copy(cvt.at[pl.ds(0,1611)],flat_ref,own_sem)
    fcopy.start()
    wait_in(red1.at[pl.ds(0,7)],n1r)
    v=red1[0]
    for k in range(1,8): v=v+red1[k]
    red2[z]=v
    for k,zz in line: cm.go(None,red2.at[z],red2.at[z],n2s,n2r,b+4*(zz-z),p)
    wait_in(red2.at[pl.ds(0,3)],n2r)
    sums=red2[0]+red2[1]+red2[2]+red2[3]
    norm_ref[...]=jnp.sqrt(sums[0:1,0:1])
    lev_ref[...]=sums[1:3,0:LEVELS]
    def sent(ok,ref,sem):
        when(ok,lambda: pltpu.make_async_copy(ref,ref,sem).wait())
    block=sibr.at[0]
    for zz in range(4):
        went=(None,None,is2,z!=2)[zz]
        for sem in (axs,ays,ads): sent(went,block,sem.at[zz])
        sent(None,sibr.at[pl.ds(0,4)],ass.at[zz])
        if zz<3:
            sent(None,sibr.at[pl.ds(0,4)],s1s.at[zz])
        else:
            sent(core==1,sibr.at[pl.ds(0,2)],s1s.at[zz])
        sent(need(zz,1-y,xn),block,ds_.at[zz])
        sent(need(zz,y,xn),block,rxs.at[zz])
        sent(need(zz,1-y,p),block,rys.at[zz])
        sent(AND(need(zz,y,p),z!=zz),block,zs.at[zz])
    sent(z<3,block,azs.at[0,0])
    sent(z>0,block,azs.at[3,1])
    sent(is1|is2,block,azs.at[1,0])
    sent(is1,block,azs.at[1,1])
    sent(is2,sibr.at[pl.ds(0,4)],a2s.at[0])
    sent(is1|is2,sibr.at[pl.ds(0,4)],a2s.at[1])
    sent(top,sibr.at[pl.ds(0,3)],a3s)
    sent(has_gains,blk.at[pl.ds(0,48)],gls)
    sent(gain_line,blk.at[pl.ds(0,112)],gps)
    sent(low,pack_ref,lps)
    sent(top,ppk.at[pl.ds(0,7)],pps)
    sent(None,red1.at[pl.ds(0,7)],n1s)
    sent(None,red2.at[pl.ds(0,3)],n2s)
    fcopy.wait()

def step(images_all,mast,img,tgt,cln,vgg,lin,tvec,rowid,level):
    D=pltpu.SemaphoreType.DMA
    V=lambda *s: pltpu.VMEM(s,bf)
    F=lambda *s: pltpu.VMEM(s,f32)
    vm=pl.BlockSpec(memory_space=pltpu.VMEM)
    return pl.pallas_call(functools.partial(step_kernel,images_all),
        out_shape=(jax.ShapeDtypeStruct((1611,128),f32),jax.ShapeDtypeStruct((1,1),f32),jax.ShapeDtypeStruct((2,LEVELS),f32),jax.ShapeDtypeStruct((32,BLK,CH),bf)),
        in_specs=[pl.BlockSpec(memory_space=pl.ANY)]+[vm]*8,
        out_specs=(pl.BlockSpec(memory_space=pl.ANY),vm,vm,pl.BlockSpec(memory_space=pl.ANY)),
        scratch_shapes=[V(17184,CH),V(32,32,CH),F(4608,128),F(5,CH,128),V(4304,CH2),V(768,CH),V(768,CH),V(1152,CH),V(576,1152),V(576,1152),V(576,1152),F(PX,CH),F(PX,CH),F(3,PX,128),F(PX,CH),V(1024,CH),V(1152,1024),V(1152,1024),V(CH,PX),V(128,3456),F(6,8,PX),V(CH,PX),F(5,8,CH),F(5,8,CH),V(1,32,CH),F(1,32,CH),V(32,CH),V(16,CH2),V(16,CH2),F(3,32,128),V(33,32,CH),D((4,)),D((4,)),D((15,)),D((15,)),F(BLK,CH),V(BLK,CH),D,D((4,2)),D((4,2)),D((4,)),D((4,2)),D((4,)),D((4,2)),D((4,)),D((4,)),D((4,)),D((4,)),F(16,CH),F(4,16,CH),F(8,4,16,CH),F(8,8,128),F(4,8,128),F(8,128),D,D,D,D,D,D,D,D,V(14,BLK,CH),V(4,BLK-HALF,CH),V(4,BLK,CH),V(4,BLK,CH),V(3,BLK,CH),V(3,BLK,CH),D((4,)),D((4,2,2)),D((4,)),D((4,)),D((4,)),D((4,2)),D((4,)),D((4,2)),D((4,)),D((6,)),D((12,)),F(6,64,PX),V(16,CH),D,D,D,D,V(4,HALF,CH),D((2,)),D((2,2,2)),D((4,)),D((4,)),F(32,CH),F(2,32,CH),F(2,32,CH),V(CH,CH),D,D((2,2,2))],
        compiler_params=pltpu.CompilerParams(collective_id=0,has_side_effects=True,vmem_limit_bytes=63<<20),
        name="train_step",
    )(mast,img,tgt,cln,vgg,lin,tvec,rowid,level)


def fast(images, target, clean_images, levels, labels, null_mask, vgg_proj, lpips_lin, master, first_moment, second_moment):
    row_index = jnp.where(null_mask == 1, CLASSES, labels).reshape(1, 1)
    tvec = time_vector(levels)
    own_grad, norm, level_sums, _ = step(
        16,
        master.reshape(1611, 128),
        images.reshape(PX, CH),
        target.reshape(128, CH2),
        clean_images.reshape(128, CH2),
        vgg_proj,
        lpips_lin.reshape(1, 256),
        tvec,
        row_index,
        levels.reshape(1, 1),
    )
    own_grad = own_grad.reshape(-1)
    norm_before = norm.reshape(())
    clipped = own_grad * jnp.minimum(1.0, CLIP / norm_before)
    new_first = BETA_ONE * first_moment + (1.0 - BETA_ONE) * clipped
    new_second = BETA_TWO * second_moment + (1.0 - BETA_TWO) * clipped * clipped
    fixed_first = new_first / (1.0 - BETA_ONE**STEP)
    fixed_second = new_second / (1.0 - BETA_TWO**STEP)
    new_master = master - RATE * (fixed_first / (jnp.sqrt(fixed_second) + EPS_ADAM) + DECAY * master)
    return (new_master, new_first, new_second, new_master.astype(jnp.bfloat16), norm_before, level_sums)


def solution(mesh):
    small = mesh.shape["batch"] == 16 and mesh.shape["pix"] == 2
    return jax.shard_map(
        fast if small else local,
        mesh=mesh,
        in_specs=(
            P("batch", "pix", None, None),
            P("batch", "pix", None, None),
            P("batch", "pix", None, None),
            P("batch"),
            P("batch"),
            P("batch"),
            P(),
            P(),
            P(("batch", "pix")),
            P(("batch", "pix")),
            P(("batch", "pix")),
        ),
        out_specs=(
            P(("batch", "pix")),
            P(("batch", "pix")),
            P(("batch", "pix")),
            P(("batch", "pix")),
            P(),
            P(),
        ),
        check_vma=False,
    )
```

```python
import functools
import math

import jax
import jax.numpy as jnp
import numpy as np
from jax import lax
from jax.experimental import pallas as pl
from jax.experimental.pallas import tpu as pltpu
from jax.sharding import PartitionSpec as P

CH = 384
CH2 = 576
GROUPS = 32
HEAD = 64
TEMB = 768
CLASSES = 1000
LEVELS = 40
STEP = 10


EPS_NORM = 1e-05
EPS_FEAT = 1e-06
BETA_ONE = 0.9
BETA_TWO = 0.999
EPS_ADAM = 1e-08
RATE = 0.02
DECAY = 0.01
CLIP = 0.01
precise = lax.Precision.HIGHEST


def extended(shard, sides, width):
    for axis, dim in sides:
        size, length = (lax.axis_size(axis), shard.shape[dim])
        up = [(i, (i + 1) % size) for i in range(size - 1)]
        down = [(j, i) for i, j in up]
        last = lax.slice_in_dim(shard, length - width, length, axis=dim)
        initial = lax.slice_in_dim(shard, 0, width, axis=dim)
        before = lax.ppermute(last, axis, up)
        after = lax.ppermute(initial, axis, down)
        shard = jnp.concatenate([before, shard, after], axis=dim)
    return shard


def unpack(flat_vec):
    layout = [
        (9 * CH, CH),
        (9 * CH, CH),
        (CH, 3 * CH),
        (CH, CH),
        (9 * CH, CH2),
        (TEMB, 2 * CH),
        (CLASSES + 1, TEMB),
        (6, CH),
    ]
    pieces = []
    offset = 0
    for rows_n, cols_n in layout:
        pieces.append(flat_vec[offset : offset + rows_n * cols_n].reshape(rows_n, cols_n))
        offset += rows_n * cols_n
    return (pieces, offset)


def time_vector(level_ids):
    half_width = TEMB // 2
    frequency = jnp.exp(-math.log(10000.0) * jnp.arange(half_width, dtype=jnp.float32) / half_width)
    angles = level_ids.astype(jnp.float32)[..., None] * (1000.0 / LEVELS) * frequency
    return jnp.concatenate([jnp.cos(angles), jnp.sin(angles)], -1)


def silu_slope(values):
    sigmoid = jax.nn.sigmoid(values)
    return sigmoid * (1.0 + values * (1.0 - sigmoid))


def pix_sums(pair_sums):
    return lax.psum((pair_sums[0], pair_sums[1]), "pix")


def group_forward(values, pixels_all):
    grouped = values.reshape(values.shape[0], values.shape[1], GROUPS, -1)
    totals = pix_sums((jnp.sum(grouped, (1, 3)), jnp.sum(grouped * grouped, (1, 3))))
    per_group = pixels_all * grouped.shape[3]
    center = totals[0] / per_group
    spread = totals[1] / per_group - center * center
    inverse = lax.rsqrt(spread + EPS_NORM)
    normed = (grouped - center[:, None, :, None]) * inverse[:, None, :, None]
    return (normed.reshape(values.shape), inverse)


def group_backward(grad_normed, normed, inverse, pixels_all):
    grad_grouped = grad_normed.reshape(normed.shape[0], normed.shape[1], GROUPS, -1)
    val_grouped = normed.reshape(grad_grouped.shape)
    totals = pix_sums((jnp.sum(grad_grouped, (1, 3)), jnp.sum(grad_grouped * val_grouped, (1, 3))))
    per_group = pixels_all * grad_grouped.shape[3]
    result = (
        grad_grouped
        - (totals[0] / per_group)[:, None, :, None]
        - val_grouped * (totals[1] / per_group)[:, None, :, None]
    )
    return (result * inverse[:, None, :, None]).reshape(normed.shape)


def columns_of(values, stride):
    rows_out = values.shape[1] // stride
    cols_out = values.shape[2] // stride
    span_rows = stride * (rows_out - 1) + 1
    span_cols = stride * (cols_out - 1) + 1
    padded = extended(values, (("pix", 1),), 1)
    padded = jnp.pad(padded, ((0, 0), (0, 0), (1, 1), (0, 0)))
    return jnp.concatenate(
        [
            padded[
                :, row_off : row_off + span_rows : stride, col_off : col_off + span_cols : stride, :
            ]
            for row_off in range(3)
            for col_off in range(3)
        ],
        -1,
    )


def conv_forward(values, weight, rows_in, stride):
    n_img, pixels_in, in_chan = values.shape
    columns = columns_of(values.reshape(n_img, rows_in, -1, in_chan), stride)
    result = jnp.dot(columns.reshape(-1, 9 * in_chan), weight, preferred_element_type=jnp.float32)
    return (result.reshape(n_img, -1, weight.shape[1]), columns)


def conv_back(columns, grad_low, weight, rows_in, stride):
    n_img, pix_out, out_chan = grad_low.shape
    in_chan = weight.shape[0] // 9
    d_weight = jnp.einsum(
        "rk,rc->kc",
        columns.reshape(-1, 9 * in_chan),
        grad_low.reshape(-1, out_chan),
        preferred_element_type=jnp.float32,
    )
    flipped = (
        weight.reshape(3, 3, in_chan, out_chan)[::-1, ::-1]
        .transpose(0, 1, 3, 2)
        .reshape(9 * out_chan, in_chan)
    )
    rows_out = rows_in // stride
    grid_grad = grad_low.reshape(n_img, rows_out, pix_out // rows_out, out_chan)
    if stride > 1:
        grid_grad = jnp.pad(
            grid_grad[:, :, None, :, None, :],
            ((0, 0), (0, 0), (0, stride - 1), (0, 0), (0, stride - 1), (0, 0)),
        )
        grid_grad = grid_grad.reshape(n_img, rows_in, -1, out_chan)
    grad_columns = columns_of(grid_grad, 1)
    grad_input = jnp.dot(
        grad_columns.reshape(-1, 9 * out_chan), flipped, preferred_element_type=jnp.float32
    )
    return (d_weight, grad_input.reshape(n_img, -1, in_chan))


def res_forward(values, gain_rows, scale, shift, w_first, w_second, rows_in, pixels_all):
    normed_a, inverse_a = group_forward(values, pixels_all)
    pre_a = normed_a * gain_rows[0] + gain_rows[1]
    act_a = jax.nn.silu(pre_a).astype(jnp.bfloat16)
    inner, columns_a = conv_forward(act_a, w_first, rows_in, 1)
    normed_b, inverse_b = group_forward(inner, pixels_all)
    affine_b = normed_b * gain_rows[2] + gain_rows[3]
    pre_b = affine_b * (1.0 + scale) + shift
    second = jax.nn.silu(pre_b).astype(jnp.bfloat16)
    branch, columns_b = conv_forward(second, w_second, rows_in, 1)
    kept_state = (
        normed_a,
        inverse_a,
        pre_a,
        columns_a,
        normed_b,
        inverse_b,
        affine_b,
        pre_b,
        columns_b,
    )
    return (values + branch, kept_state)


def res_back(grad_result, kept_state, gain_rows, scale, w_first, w_second, rows_in, pixels_all):
    normed_a, inverse_a, pre_a, columns_a, normed_b, inverse_b, affine_b, pre_b, columns_b = (
        kept_state
    )
    d_w_second, grad_second = conv_back(
        columns_b, grad_result.astype(jnp.bfloat16), w_second, rows_in, 1
    )
    grad_pre_b = grad_second * silu_slope(pre_b)
    d_scale = jnp.sum(grad_pre_b * affine_b, 1)
    d_shift = jnp.sum(grad_pre_b, 1)
    grad_affine = grad_pre_b * (1.0 + scale)
    d_gain_b = jnp.sum(grad_affine * normed_b, (0, 1))
    d_bias_b = jnp.sum(grad_affine, (0, 1))
    grad_inner = group_backward(grad_affine * gain_rows[2], normed_b, inverse_b, pixels_all).astype(
        jnp.bfloat16
    )
    d_w_first, grad_act = conv_back(columns_a, grad_inner, w_first, rows_in, 1)
    grad_pre_a = grad_act * silu_slope(pre_a)
    d_gain_a = jnp.sum(grad_pre_a * normed_a, (0, 1))
    d_bias_a = jnp.sum(grad_pre_a, (0, 1))
    grad_values = None
    d_gains = jnp.stack([d_gain_a, d_bias_a, d_gain_b, d_bias_b])
    return (d_w_first, d_w_second, d_gains, d_scale, d_shift, grad_values)


def to_heads(values):
    return lax.all_to_all(values, "pix", split_axis=2, concat_axis=1, tiled=True)


def to_pixels(values):
    return lax.all_to_all(values, "pix", split_axis=1, concat_axis=2, tiled=True)


def flat_heads(values):
    return values.reshape(-1, values.shape[2], values.shape[3])


def attend(queries, keys, values):
    root_dim = math.sqrt(queries.shape[-1])

    def single(bundle):
        q_one, k_one, v_one = bundle
        scores = (
            jnp.einsum("qd,kd->qk", q_one, k_one, preferred_element_type=jnp.float32) / root_dim
        )
        row_peak = jnp.max(scores, -1, keepdims=True)
        exp_scores = jnp.exp(scores - row_peak)
        sum_exp = jnp.sum(exp_scores, -1, keepdims=True)
        probabilities = (exp_scores / sum_exp).astype(jnp.bfloat16)
        attended = jnp.einsum("qk,kd->qd", probabilities, v_one, preferred_element_type=jnp.float32)
        return (attended.astype(jnp.bfloat16), row_peak + jnp.log(sum_exp))

    attended, log_total = lax.map(
        single, (flat_heads(queries), flat_heads(keys), flat_heads(values))
    )
    return (attended.reshape(queries.shape), log_total)


def attend_back(queries, keys, values, log_total, grad_out):
    root_dim = math.sqrt(queries.shape[-1])

    def single(bundle):
        q_one, k_one, v_one, lse_one, g_one = bundle
        scores = (
            jnp.einsum("qd,kd->qk", q_one, k_one, preferred_element_type=jnp.float32) / root_dim
        )
        probabilities = jnp.exp(scores - lse_one)
        grad_v = jnp.einsum(
            "qk,qd->kd",
            probabilities.astype(jnp.bfloat16),
            g_one,
            preferred_element_type=jnp.float32,
        )
        grad_p = jnp.einsum("qd,kd->qk", g_one, v_one, preferred_element_type=jnp.float32)
        inner_sum = jnp.sum(probabilities * grad_p, -1, keepdims=True)
        grad_s = (probabilities * (grad_p - inner_sum)).astype(jnp.bfloat16)
        grad_q = (
            jnp.einsum("qk,kd->qd", grad_s, k_one, preferred_element_type=jnp.float32) / root_dim
        )
        grad_k = (
            jnp.einsum("qk,qd->kd", grad_s, q_one, preferred_element_type=jnp.float32) / root_dim
        )
        return (grad_q, grad_k, grad_v)

    grad_q, grad_k, grad_v = lax.map(
        single,
        (
            flat_heads(queries),
            flat_heads(keys),
            flat_heads(values),
            log_total,
            flat_heads(grad_out),
        ),
    )
    return (grad_q.reshape(queries.shape), grad_k.reshape(keys.shape), grad_v.reshape(values.shape))


def local(
    images,
    target,
    clean_images,
    levels,
    labels,
    null_mask,
    vgg_proj,
    lpips_lin,
    master,
    first_moment,
    second_moment,
):
    gathered = lax.all_gather(master.astype(jnp.bfloat16), ("batch", "pix"), axis=0, tiled=True)
    pieces, used_len = unpack(gathered)
    w_one, w_two, w_qkv, w_proj, w_down, w_emb, class_table, gains_low = pieces
    gains_one = gains_low.astype(jnp.float32)
    n_img, rows_local, cols_local, channels = images.shape
    wide_channels = w_down.shape[1]
    pix_count = lax.axis_size("pix")
    batch_count = lax.axis_size("batch")
    pixels_here = rows_local * cols_local
    pixels_all = pixels_here * pix_count
    pixels_all_two = pixels_all // 4
    images_all = n_img * batch_count
    row_index = jnp.where(null_mask == 1, class_table.shape[0] - 1, labels)
    one_hot = (
        row_index[:, None] == jnp.arange(class_table.shape[0], dtype=jnp.int32)[None, :]
    ).astype(jnp.float32)
    pre_embed = time_vector(levels) + jnp.dot(
        one_hot, class_table.astype(jnp.float32), precision=precise
    )
    embedded = jax.nn.silu(pre_embed)
    w_emb_wide = w_emb.astype(jnp.float32)
    scale_shift = jnp.dot(embedded, w_emb_wide, precision=precise)
    scale_one = scale_shift[:, None, :channels]
    shift_one = scale_shift[:, None, channels:]
    flat_in = images.astype(jnp.float32).reshape(n_img, pixels_here, channels)
    middle, kept_one = res_forward(
        flat_in, gains_one, scale_one, shift_one, w_one, w_two, rows_local, pixels_all
    )
    normed_three, inverse_three = group_forward(middle, pixels_all)
    attn_in = (normed_three * gains_one[4] + gains_one[5]).astype(jnp.bfloat16)
    triples = jnp.dot(attn_in.reshape(-1, channels), w_qkv, preferred_element_type=jnp.float32)
    triples = triples.astype(jnp.bfloat16).reshape(n_img, pixels_here, 3 * channels)
    spread_heads = to_heads(triples)
    local_heads = spread_heads.shape[2] // (3 * HEAD)
    split_heads = spread_heads.reshape(n_img, -1, local_heads, 3, HEAD).transpose(3, 0, 2, 1, 4)
    queries, keys, values = (split_heads[0], split_heads[1], split_heads[2])
    attended, log_total = attend(queries, keys, values)
    attended_px = to_pixels(attended.transpose(0, 2, 1, 3).reshape(n_img, -1, local_heads * HEAD))
    projected = jnp.dot(
        attended_px.reshape(-1, channels), w_proj, preferred_element_type=jnp.float32
    )
    output = middle + projected.reshape(n_img, pixels_here, channels)
    final_out, columns_down = conv_forward(output.astype(jnp.bfloat16), w_down, rows_local, 2)
    pixels_two = final_out.shape[1]
    feat_width = vgg_proj.shape[1]
    online_feat = jnp.dot(
        final_out.astype(jnp.bfloat16).reshape(-1, wide_channels),
        vgg_proj,
        preferred_element_type=jnp.float32,
    )
    online_feat = online_feat.reshape(n_img, pixels_two, feat_width)
    target_feat = jnp.dot(
        target.reshape(-1, wide_channels), vgg_proj, preferred_element_type=jnp.float32
    )
    target_feat = target_feat.reshape(n_img, pixels_two, feat_width)
    target_unit = target_feat * lax.rsqrt(
        jnp.mean(target_feat * target_feat, -1, keepdims=True) + EPS_FEAT
    )
    clean_wide = clean_images.astype(jnp.float32).reshape(n_img, pixels_two, wide_channels)

    def loss_terms(feature, out_value):
        unit = feature * lax.rsqrt(jnp.mean(feature * feature, -1, keepdims=True) + EPS_FEAT)
        consist = jnp.sum(lpips_lin * (unit - target_unit) ** 2, (1, 2)) / (
            feat_width * pixels_all_two
        )
        denoise = jnp.sum((out_value - clean_wide) ** 2, (1, 2)) / (pixels_all_two * wide_channels)
        return (consist, denoise)

    (consist, denoise), pullback = jax.vjp(loss_terms, online_feat, final_out)
    level_hot = (levels[:, None] == jnp.arange(LEVELS, dtype=jnp.int32)[None, :]).astype(
        jnp.float32
    )
    level_pair = lax.psum(
        (jnp.sum(consist[:, None] * level_hot, 0), jnp.sum(level_hot / pix_count, 0)),
        ("batch", "pix"),
    )
    zero_count = level_pair[1][0]
    is_zero = (levels == 0).astype(jnp.float32)
    grad_feat, grad_out = pullback(
        (jnp.full_like(consist, 1.0 / images_all), is_zero / jnp.maximum(zero_count, 1.0))
    )
    grad_feat_low = grad_feat.astype(jnp.bfloat16).reshape(-1, feat_width)
    grad_final = grad_out + jnp.einsum(
        "rf,cf->rc", grad_feat_low, vgg_proj, preferred_element_type=jnp.float32
    ).reshape(n_img, pixels_two, wide_channels)
    d_w_down, grad_output = conv_back(
        columns_down, grad_final.astype(jnp.bfloat16), w_down, rows_local, 2
    )
    grad_proj = grad_output.astype(jnp.bfloat16).reshape(-1, channels)
    d_w_proj = jnp.einsum(
        "rc,rd->cd",
        attended_px.reshape(-1, channels),
        grad_proj,
        preferred_element_type=jnp.float32,
    )
    grad_att_px = jnp.einsum("rd,cd->rc", grad_proj, w_proj, preferred_element_type=jnp.float32)
    grad_att_px = grad_att_px.astype(jnp.bfloat16).reshape(n_img, pixels_here, channels)
    grad_heads = to_heads(grad_att_px)
    grad_split = grad_heads.reshape(n_img, -1, local_heads, HEAD).transpose(0, 2, 1, 3)
    grad_q, grad_k, grad_v = attend_back(queries, keys, values, log_total, grad_split)
    grad_triples = jnp.stack([grad_q, grad_k, grad_v], 3).transpose(0, 2, 1, 3, 4)
    grad_triples = grad_triples.reshape(n_img, -1, local_heads * 3 * HEAD).astype(jnp.bfloat16)
    grad_triples = to_pixels(grad_triples)
    grad_rows = grad_triples.reshape(-1, 3 * channels)
    d_w_qkv = jnp.einsum(
        "rc,rd->cd", attn_in.reshape(-1, channels), grad_rows, preferred_element_type=jnp.float32
    )
    grad_attn_in = jnp.einsum(
        "rd,cd->rc", grad_rows, w_qkv, preferred_element_type=jnp.float32
    ).reshape(n_img, pixels_here, channels)
    d_gain_three = jnp.sum(grad_attn_in * normed_three, (0, 1))
    d_bias_three = jnp.sum(grad_attn_in, (0, 1))
    grad_middle = grad_output + group_backward(
        grad_attn_in * gains_one[4], normed_three, inverse_three, pixels_all
    )
    d_w_one, d_w_two, d_gains_one, d_scale_one, d_shift_one, unused_grad = res_back(
        grad_middle, kept_one, gains_one, scale_one, w_one, w_two, rows_local, pixels_all
    )
    grad_scale_shift = jnp.concatenate([d_scale_one, d_shift_one], 1)
    d_w_emb = jnp.dot(embedded.T, grad_scale_shift, precision=precise)
    grad_embedded = jnp.dot(grad_scale_shift, w_emb_wide.T, precision=precise)
    d_table = jnp.dot(one_hot.T, grad_embedded * silu_slope(pre_embed), precision=precise)
    d_norms_one = jnp.concatenate([d_gains_one, jnp.stack([d_gain_three, d_bias_three])], 0)
    flat_grad = jnp.concatenate(
        [
            d_w_one.ravel(),
            d_w_two.ravel(),
            d_w_qkv.ravel(),
            d_w_proj.ravel(),
            d_w_down.ravel(),
            d_w_emb.ravel(),
            d_table.ravel(),
            d_norms_one.ravel(),
            jnp.zeros((gathered.shape[0] - used_len,), jnp.float32),
        ]
    )
    own_grad = lax.psum_scatter(flat_grad, ("batch", "pix"), scatter_dimension=0, tiled=True)
    norm_before = jnp.sqrt(lax.psum(jnp.sum(own_grad * own_grad), ("batch", "pix")))
    clipped = own_grad * jnp.minimum(1.0, CLIP / norm_before)
    new_first = BETA_ONE * first_moment + (1.0 - BETA_ONE) * clipped
    new_second = BETA_TWO * second_moment + (1.0 - BETA_TWO) * clipped * clipped
    fixed_first = new_first / (1.0 - BETA_ONE**STEP)
    fixed_second = new_second / (1.0 - BETA_TWO**STEP)
    new_master = master - RATE * (
        fixed_first / (jnp.sqrt(fixed_second) + EPS_ADAM) + DECAY * master
    )
    level_sums = jnp.stack([level_pair[0], level_pair[1]])
    return (
        new_master,
        new_first,
        new_second,
        new_master.astype(jnp.bfloat16),
        norm_before,
        level_sums,
    )


MESH = pl.DeviceIdType.MESH
ROWS=537; BLK=560; HALF=288
PX=512
R_ONE,R_TWO,R_QKV,R_PROJ,R_DOWN,R_EMB,R_TAB,R_GAIN,R_END=0,3456,6912,8064,8448,13632,15168,17170,17184
f32=jnp.float32; bf=jnp.bfloat16
class Comm:
    def __init__(self): self.sent=[]
    def go(self, cond, src, dst, ssem, rsem, b, p):
        c = pltpu.make_async_remote_copy(src_ref=src,dst_ref=dst,send_sem=ssem,recv_sem=rsem,device_id=(b,p),device_id_type=MESH)
        if cond is None: c.start()
        else: pl.when(cond)(lambda: c.start())
        self.sent.append((cond,c))
    def drain(self):
        for cond,c in self.sent:
            if cond is None: c.wait_send()
            else: pl.when(cond)(lambda c=c: c.wait_send())
        self.sent=[]

def place():
    b=lax.axis_index("batch"); p=lax.axis_index("pix")
    core=lax.rem(b,2); y=lax.rem(lax.div(b,2),2); z=lax.div(b,4)
    return b,p,core,y,z

def base_of(s): return 16*((ROWS*s)//16)
def dg(a,b,ca,cb): return lax.dot_general(a,b,(((ca,),(cb,)),((),())),preferred_element_type=f32)
def nn(a,b): return dg(a,b,1,0)
def nt(a,b): return dg(a,b,1,1)
def tn(a,b): return dg(a,b,0,0)
def split3(v):
    hi=v.astype(bf); r=v-hi.astype(f32); mid=r.astype(bf); lo=(r-mid.astype(f32)).astype(bf)
    return hi,mid,lo
def exact(v,w,dot):
    hi,mid,lo=split3(v)
    return dot(hi,w)+dot(mid,w)+dot(lo,w)
def sigmoid(v): return 1.0/(1.0+jnp.exp(-v))
def silu(v): return v*sigmoid(v)
def slope(v):
    s=sigmoid(v)
    return s*(1.0+v*(1.0-s))
def cloop(n,chunk,body,init):
    return lax.fori_loop(0,n//chunk,lambda i,c: body(pl.multiple_of(i*chunk,chunk),c),init)
def col8(v): return jnp.sum(v.reshape(-1,8,v.shape[-1]),axis=0)
Z8=lambda: jnp.zeros((8,CH),f32)
class Blocks:
    def __init__(self,ref,n): self.ref=ref; self.n=n
def at_block(ref,j,sl):
    if isinstance(ref,Blocks): return ref.ref,(pl.ds(ref.n*j+sl.start,sl.size,stride=sl.stride),slice(None))
    return ref,(j,sl,slice(None))
def ld(ref,sl):
    out=[]
    for j in range(ref.ref.shape[0]//ref.n if isinstance(ref,Blocks) else ref.shape[0]):
        r,k=at_block(ref,j,sl)
        out.append(r[k])
    return jnp.concatenate(out,1)
def put3(ref,sl,v):
    for j in range(v.shape[1]//128):
        r,k=at_block(ref,j,sl)
        r[k]=v[:,128*j:128*j+128]
def every(start,n,step): return pl.ds(start,n,stride=step)
def row(v): return jnp.sum(v,axis=0,keepdims=True)


LAST=25
def step_kernel(images_all,
    mast,img,tgt,cln,vgg,lin,tvec,rowid,level,
    flat_ref,norm_ref,lev_ref,g_ref,
    wv,tails,cvt,cvt2,wd,wee,weo,wqT,x3a,x3b,z3,inner,middle,gout,gsec,ain,trT,dtrT,attT,xd,lse,dattT,ssend,srecv,hsend,hrecv,himg,dzs,dzr,geo,oth,wsem,tsem,xs,xr,total,blk,own_sem,azs,azr,axs,axr,ays,ayr,adar,adbr,ass,asr,pack_ref,lpk,ppk,red1,red2,tile,lps,lpr,pps,ppr,n1s,n1r,n2s,n2r,sibr,rb,rx,ry,zu,zd,s1s,s1r,dar,dbr,rxs,rxr,rys,ryr,zs,zur,zdr,acc,gtile,gls,glr,gps,gpr,rba,a2s,a2r,ads,ds_,hmid,esend,erecv,gm,a3s,a3r):
    b,p,core,y,z=place()
    q=1-p; xn=q; s=b*2+p
    pf=p.astype(f32); qf=1.0-pf
    yn=b+2-4*y; sib=b+1-2*core; oc=1-core
    up_ok=z<3; dn_ok=z>0
    top=z==3
    mine=(y*2+core)*2+p
    cvt3=Blocks(cvt,1536)
    mcopy=pltpu.make_async_copy(mast,cvt.at[pl.ds(0,1611)],own_sem)
    mcopy.start()
    barrier=pltpu.get_barrier_semaphore()
    plane=[]
    for dy in range(2):
        for dc in range(2):
            for dp in range(2):
                if dy+dc+dp: plane.append((4*dy+2*dc+dp,z*4+lax.rem(y+dy,2)*2+lax.rem(core+dc,2),lax.rem(p+dp,2)))
    line=[(k,lax.rem(z+k,4)) for k in range(1,4)]
    def sig(bb,pp): pl.semaphore_signal(barrier,inc=1,device_id=(bb,pp),device_id_type=MESH)
    for _,bb,pp in plane: sig(bb,pp)
    for _,zz in line: sig(b+4*(zz-z),p)
    def when(ok,f):
        if ok is None: f()
        else: pl.when(ok)(f)
    def AND(*c):
        r=None
        for k in c:
            if k is not None: r=k if r is None else r&k
        return r
    def wait_in(ref,sem):
        pltpu.make_async_remote_copy(src_ref=ref,dst_ref=ref,send_sem=sem,recv_sem=sem,device_id=(b,xn),device_id_type=MESH).wait_recv()
    def slot(zz,yy,pp,cc=core): return ((zz*2+yy)*2+cc)*2+pp
    A=pl.ds(0,HALF); B=pl.ds(HALF,BLK-HALF)
    cm=Comm()
    shift=lax.rem(9*s,16)
    total[ROWS-1:BLK]=jnp.zeros((BLK-ROWS+1,CH),f32)
    mcopy.wait()
    for j in range(3): total[0:ROWS,128*j:128*j+128]=cvt[pl.ds(j,ROWS,stride=3),:]
    at=lax.broadcasted_iota(jnp.int32,(BLK,CH),0)
    blk[...]=jnp.where(at==BLK-4,(level[...]==0).astype(f32),pltpu.roll(total[...],shift,0)).astype(bf)
    own=pltpu.make_async_copy(blk,g_ref.at[s],own_sem)
    own.start()
    pl.semaphore_wait(barrier,10)
    def valid(zz): return (zz>=0)&(zz<4)
    def pick(c0,c1,c2,c3): return jnp.where(z==0,c0,jnp.where(z==1,c1,jnp.where(z==2,c2,c3)))
    hs=(A,B)
    ends=(z==0)|(z==3); is1=z==1; is2=z==2; inner_z=jnp.logical_not(ends)
    def z_send(ok,zz,h,d,src=None):
        g=g_ref.at[slot(zz,y,p),hs[h]]
        cm.go(ok,g if src is None else src,g,azs.at[zz,(1-d)//2],azr.at[zz,h],b+4*d,p)
    def xy_send(ok,zz,h,src=None):
        g=g_ref.at[slot(zz,y,p),hs[h]]
        cm.go(ok,g if src is None else src,g,axs.at[zz],axr.at[zz,h],b,xn)
        cm.go(ok,g if src is None else src,g,ays.at[zz],ayr.at[zz,h],yn,p)
    def sib_send(ok,zz,yy,pp,h,src=None):
        sl=slot(zz,yy,pp)
        first=pl.multiple_of(16*lax.div(ROWS*sl,16),16)
        def part(lo,n):
            return g_ref.at[sl,pl.ds(lo,n)] if src is None else src.at[pl.ds(lo-(HALF if h else 0),n)]
        lo,n=(0,HALF) if h==0 else (HALF,528-HALF)
        cm.go(ok,part(lo,n),wv.at[pl.ds(first+lo,n)],ass.at[zz],asr.at[zz],sib,p)
        if h==1: cm.go(ok,part(528,32),tails.at[sl],ass.at[zz],asr.at[zz],sib,p)
    def own_sends():
        for h in range(2):
            src=blk.at[hs[h]]
            z_send(z==0,z,h,1,src)
            z_send(z==3,z,h,-1,src)
            sib_send(None,z,y,p,h,src)
    def own_xy():
        for h in range(2): xy_send(z!=1,z,h,blk.at[hs[h]])
    four=((1-y,xn),(y,xn),(1-y,p),(y,p))
    def two_send(ok,i,d):
        yy,pp=four[i]
        for h in range(2):
            g=g_ref.at[slot(2,yy,pp),hs[h]]
            cm.go(ok,g,g,a2s.at[(1-d)//2],a2r.at[yy,pp,h],b+4*d,p)
    def two_in(i,ok):
        yy,pp=four[i]
        for h in range(2):
            g=g_ref.at[slot(2,yy,pp),hs[h]]
            when(ok,lambda: wait_in(g,a2r.at[yy,pp,h]))
            cm.go(ok&(z==1),g,g,a2s.at[1],a2r.at[yy,pp,h],b-4,p)
            sib_send(ok,2,yy,pp,h)
    def three_out(i):
        yy,pp=four[i]
        for h in range(2):
            g=g_ref.at[slot(3,yy,pp),hs[h]]
            cm.go(top,g,g,a3s,a3r.at[yy,pp,h],b-4,p)
    def three_in(i):
        yy,pp=four[i]
        for h in range(2):
            g=g_ref.at[slot(3,yy,pp),hs[h]]
            when(is2,lambda: wait_in(g,a3r.at[yy,pp,h]))
            sib_send(is2,3,yy,pp,h)
    def diag_in(ok,zz):
        sd=slot(zz,1-y,xn)
        def f():
            wait_in(g_ref.at[sd,A],adar.at[zz])
            wait_in(g_ref.at[sd,B],adbr.at[zz])
        when(ok,f)
        for h in range(2): sib_send(ok,zz,1-y,xn,h)
    def two_diag():
        sd=slot(2,1-y,xn)
        def f():
            wait_in(g_ref.at[sd,A],adar.at[2])
            wait_in(g_ref.at[sd,B],adbr.at[2])
        when(z==2,f)
        for h in range(2): sib_send(z==2,2,1-y,xn,h)
    def arrive0(h):
        ok=z!=0
        when(ok,lambda: wait_in(g_ref.at[slot(0,y,p),hs[h]],azr.at[0,h]))
        z_send(ok&up_ok,0,h,1)
        xy_send(ok,0,h)
        sib_send(ok,0,y,p,h)
    def arrive3(h,ok):
        when(ok,lambda: wait_in(g_ref.at[slot(3,y,p),hs[h]],azr.at[3,h]))
        z_send(ok&dn_ok,3,h,-1)
        sib_send(ok,3,y,p,h)
    def xy_arrive(ok,f,h):
        sx=slot(f,y,xn); sy=slot(f,1-y,p)
        when(ok,lambda: wait_in(g_ref.at[sx,hs[h]],axr.at[f,h]))
        if h==0: cm.go(ok,g_ref.at[sx,A],g_ref.at[sx,A],ads.at[f],adar.at[f],yn,p)
        sib_send(ok,f,y,xn,h)
        when(ok,lambda: wait_in(g_ref.at[sy,hs[h]],ayr.at[f,h]))
        if h==1: cm.go(ok,g_ref.at[sy,B],g_ref.at[sy,B],ads.at[f],adbr.at[f],b,xn)
        sib_send(ok,f,1-y,p,h)
    def later_sends():
        for h in range(2):
            src=blk.at[hs[h]]
            z_send(z==1,z,h,1,src)
            z_send(z==1,z,h,-1,src)
    def one_in(h,ok):
        when(ok,lambda: wait_in(g_ref.at[slot(1,y,p),hs[h]],azr.at[1,h]))
        z_send(ok&is2,1,h,1)
        sib_send(ok,1,y,p,h)
    def load(sl): return (pltpu.make_async_copy(g_ref.at[sl,pl.ds(0,528)],wv.at[pl.ds(pl.multiple_of(16*lax.div(ROWS*sl,16),16),528)],wsem.at[lax.div(sl,8)]),
                          pltpu.make_async_copy(g_ref.at[sl,pl.ds(528,32)],tails.at[sl],tsem.at[lax.div(sl,8)]))
    def d_arrive(zz):
        sd=slot(zz,1-y,xn)
        wait_in(g_ref.at[sd,A],adar.at[zz])
        sib_send(None,zz,1-y,xn,0)
        wait_in(g_ref.at[sd,B],adbr.at[zz])
        sib_send(None,zz,1-y,xn,1)
        for yy in range(2):
            for pp in range(2):
                for c in load(slot(zz,yy,pp)): c.start()
    def sib_arrive(zz):
        wait_in(g_ref.at[pl.ds(0,4)],asr.at[zz])
    has_gains=s==31
    gain_line=(y==1)&(core==1)&(p==1)
    def gain_sends():
        for k,zz in line: cm.go(has_gains,blk.at[pl.ds(528,16)],gtile,gls,glr,b+4*(zz-z),p)
    def gain_pass():
        pl.when(has_gains)(lambda: gtile.__setitem__(Ellipsis,blk[528:544]))
        pl.when(gain_line&jnp.logical_not(has_gains))(lambda: wait_in(gtile,glr))
        for d,bb,pp in plane: cm.go(gain_line,gtile,gtile,gps,gpr,bb,pp)
    def gain_wait():
        pl.when(jnp.logical_not(gain_line))(lambda: wait_in(gtile,gpr))
    seen=[]
    def take(shards):
        pltpu.make_async_copy(wv.at[pl.ds(0,4*528)],wv.at[pl.ds(0,4*528)],wsem.at[shards[0]//8]).wait()
        pltpu.make_async_copy(tails.at[pl.ds(0,4)],tails.at[pl.ds(0,4)],tsem.at[shards[0]//8]).wait()
        for k in shards:
            lo=base_of(k)
            if k<31 and base_of(k+1)-lo==544 or k==31: wv[lo+528:lo+544]=tails[k,0:16]
            seen.append(k)
        for k in range(1,32):
            if k in seen and k-1 in seen and (k in shards or k-1 in shards):
                off=base_of(k)-base_of(k-1)-528
                t=tails[k-1,off:off+16].astype(f32)
                if off: t=jnp.where(lax.broadcasted_iota(jnp.int32,(16,CH),0)<8,t,0.0)
                lo=base_of(k)
                wv[lo:lo+16]=(wv[lo:lo+16].astype(f32)+t).astype(bf)
    def rows(u,yy,pp,cc=core):
        at=pl.ds(pl.multiple_of(16*lax.div(ROWS*slot(u,yy,pp,cc),16),16),BLK)
        return wd.at[at,pl.ds(0,CH)] if u==0 else wv.at[at]
    def need(u,yy,pp,cc=core): return None if u<3 else slot(u,yy,pp,cc)<=LAST
    def sibsend(u):
        for yy,pp in four:
            cm.go(need(u,yy,pp,oc),rows(u,yy,pp,oc),sibr.at[4*u+2*yy+pp],s1s.at[u],s1r.at[u,yy,pp],sib,p)
    def both(u,yy,pp,lo,n):
        a=pl.multiple_of(16*lax.div(ROWS*slot(u,yy,pp),16)+lo,16)
        mine_=wd[pl.ds(a,n),0:CH] if u==0 else wv[pl.ds(a,n)]
        return mine_.astype(f32)+sibr[4*u+2*yy+pp,lo:lo+n].astype(f32)
    HA=(0,HALF); HB=(HALF,BLK-HALF)
    def sib_in(u,yy,pp): wait_in(sibr.at[4*u+2*yy+pp],s1r.at[u,yy,pp])
    def keep(u,yy,pp,half,more=None):
        t=both(u,yy,pp,*half)
        if more is not None: t=t+more.astype(f32)
        sibr[4*u+2*yy+pp,half[0]:half[0]+half[1]]=t.astype(bf)
    def diag(u):
        yy,pp=1-y,xn
        c=need(u,yy,pp)
        def f():
            sib_in(u,yy,pp)
            keep(u,yy,pp,HA); keep(u,yy,pp,HB)
        when(c,f)
        src=sibr.at[4*u+2*yy+pp]
        if u<2: cm.go(c,src.at[A],rba.at[u],ds_.at[u],dar.at[u],b,xn)
        else: cm.go(c,src.at[A],rba.at[u],ds_.at[u],dar.at[u],yn,p)
        cm.go(c,src.at[B],rb.at[u],ds_.at[u],dbr.at[u],yn,p)
    def ysend(u):
        c=need(u,1-y,p)
        def f():
            sib_in(u,1-y,p)
            keep(u,1-y,p,HA); keep(u,1-y,p,HB)
        when(c,f)
        for h in range(2): cm.go(c,sibr.at[4*u+2*(1-y)+p,hs[h]],ry.at[u,hs[h]],rys.at[u],ryr.at[u,h],yn,p)
    def xsend(u,only=None):
        c=AND(need(u,y,xn),only)
        def f():
            sib_in(u,y,xn)
            wait_in(rba.at[u],dar.at[u])
            keep(u,y,xn,HA,rba[u])
        when(c,f)
        cm.go(c,sibr.at[4*u+2*y+xn,A],rx.at[u,A],rxs.at[u],rxr.at[u,0],b,xn)
        def f2():
            wait_in(rb.at[u],dbr.at[u])
            keep(u,y,xn,HB,rb[u])
        when(c,f2)
        cm.go(c,sibr.at[4*u+2*y+xn,B],rx.at[u,B],rxs.at[u],rxr.at[u,1],b,xn)
    def put_x(u,half,h,more=None):
        keep(u,y,xn,half,more)
        cm.go(None,sibr.at[4*u+2*y+xn,hs[h]],rx.at[u,hs[h]],rxs.at[u],rxr.at[u,h],b,xn)
    def put_y(u,half,h,more=None):
        keep(u,1-y,p,half,more)
        cm.go(None,sibr.at[4*u+2*(1-y)+p,hs[h]],ry.at[u,hs[h]],rys.at[u],ryr.at[u,h],yn,p)
    def first_halves(u):
        sib_in(u,y,xn)
        sib_in(u,1-y,p)
        if u>0:
            put_x(u,HA,0)
            put_y(u,HB,1)
    def second_halves(u):
        wait_in(rba.at[u],dar.at[u])
        put_y(u,HA,0,rba[u])
        if u==0: put_y(u,HB,1)
        wait_in(rb.at[u],dbr.at[u])
        put_x(u,HB,1,rb[u])
    def chunks(u): return ((0,80,0),(80,80,0),(160,64,0),(224,64,0),(288,80,1),(368,64,1),(432,64,1),(496,64,1)) if u==0 else ((0,HALF,0),(HALF,BLK-HALF,1))
    def zur_at(u,k): return zur.at[2*(u-1)+k]
    def zdr_at(u,k): return zdr.at[k if u==0 else 8+2*(u-1)+k]
    def xy_in(u,h):
        wait_in(rx.at[u,hs[h]],rxr.at[u,h])
        wait_in(ry.at[u,hs[h]],ryr.at[u,h])
    def zstep(u,i):
        for d in (1,-1):
            at_z=i if d==1 else 3-i
            if not (at_z<u if d==1 else at_z>u): continue
            c=AND(need(u,y,p),z==at_z)
            buf,bsem=(zu.at[u-1],zur_at) if d==1 else (zd.at[u],zdr_at)
            own_at=4*u+2*y+p
            def first(): sib_in(u,y,p)
            when(c,first)
            seen_h=set()
            for k,(lo,n,h) in enumerate(chunks(u)):
                def f():
                    if h not in seen_h: xy_in(u,h)
                    t=both(u,y,p,lo,n)+rx[u,lo:lo+n].astype(f32)+ry[u,lo:lo+n].astype(f32)
                    if i>0:
                        wait_in(buf.at[pl.ds(lo,n)],bsem(u,k))
                        t=t+buf[lo:lo+n].astype(f32)
                    sibr[own_at,lo:lo+n]=t.astype(bf)
                when(c,f)
                seen_h.add(h)
                cm.go(c,sibr.at[own_at,pl.ds(lo,n)],buf.at[pl.ds(lo,n)],zs.at[u],bsem(u,k),b+4*d,p)
    def zend(u):
        def f():
            sib_in(u,y,p)
            done=set()
            for k,(lo,n,h) in enumerate(chunks(u)):
                if h not in done: xy_in(u,h); done.add(h)
                t=both(u,y,p,lo,n)+rx[u,lo:lo+n].astype(f32)+ry[u,lo:lo+n].astype(f32)
                if u>0:
                    wait_in(zu.at[u-1,pl.ds(lo,n)],zur_at(u,k))
                    t=t+zu[u-1,lo:lo+n].astype(f32)
                if u<3:
                    wait_in(zd.at[u,pl.ds(lo,n)],zdr_at(u,k))
                    t=t+zd[u,lo:lo+n].astype(f32)
                if u==3:
                    rr=16*lax.div(ROWS*s,16)+lo+lax.broadcasted_iota(jnp.int32,(n,CH),0)
                    t=jnp.where(rr<R_EMB,t,total[lo:lo+n])
                total[lo:lo+n]=t
        when(AND(need(u,y,p),z==u),f)
    state={"k":0}
    def xchg(src,dst,dst_like=None):
        k=state["k"]; state["k"]=k+1
        c=pltpu.make_async_remote_copy(src_ref=src,dst_ref=dst,send_sem=xs.at[k],recv_sem=xr.at[k],device_id=(b,q),device_id_type=MESH)
        c.start()
        return c
    edge=pl.ds(pl.multiple_of(q*480,32),32)
    gain_sends()
    c_img=xchg(img.at[edge],himg)
    def gsum(v): return exact(v,gm[...],nn)
    def swap_sums(k,s1,s2):
        ssend[k]=jnp.concatenate([s1,s2,jnp.zeros((6,CH),f32)],0)
        return xchg(ssend.at[k],srecv.at[k])
    def total_sums(k):
        t=gsum(ssend[k]+srecv[k])/(12.0*2*PX)
        return t[0:1],t[1:2]
    def norm_of(t):
        mean,sq=t
        return mean,lax.rsqrt(jnp.maximum(sq-mean*mean,0.0)+EPS_NORM)
    def fill3(dst,at,a):
        col=lax.broadcasted_iota(jnp.int32,a.shape,0)&31
        n=a.shape[0]
        dst[pl.ds(at,n),CH:2*CH]=a.astype(bf)
        dst[pl.ds(at,n),0:CH]=jnp.where(col==0,0.0,pltpu.roll(a,1,0)).astype(bf)
        dst[pl.ds(at,n),2*CH:3*CH]=jnp.where(col==31,0.0,pltpu.roll(a,n-1,0)).astype(bf)
    def fill_edges(dst,h):
        fill3(dst,0,h*pf); fill3(dst,544,h*qf)
    def conv_to(dst,x3,wrow,add=None):
        for dr in range(3):
            d=nn(x3[32*dr:32*dr+PX],wv[wrow+1152*dr:wrow+1152*dr+1152])
            if dr==0: dst[...]=d if add is None else add()+d
            else: dst[...]+=d
    def conv_dx(dst,wrow):
        first=True
        for dr in range(3):
            for dc in range(3):
                d=nt(z3[32*(2-dr):32*(2-dr)+PX,CH*(2-dc):CH*(2-dc)+CH],wv[wrow+CH*(3*dr+dc):wrow+CH*(3*dr+dc)+CH])
                if first: dst[...]=d
                else: dst[...]+=d
                first=False
    def st(i,c):
        v=img[pl.ds(i,64)].astype(f32)
        return c[0]+col8(v),c[1]+col8(v*v)
    a1,a2=cloop(PX,64,st,(Z8(),Z8()))
    c=swap_sums(0,row(a1),row(a2))
    own_sends()
    gain_pass()
    own_xy()
    group_of=lambda d: lax.shift_right_logical(lax.broadcasted_iota(jnp.int32,(CH,CH),d)*43691,19)
    gm[...]=(group_of(0)==group_of(1)).astype(f32).astype(bf)
    gain_wait()
    g6=gtile[...].astype(f32)
    g1,b1,g2,b2,g3,b3=[g6[2+i:3+i] for i in range(6)]
    c.wait()
    mean1,inv1=norm_of(total_sums(0))
    def act_of(v): return silu((v-mean1)*inv1*g1+b1)
    arrive3(0,is2)
    arrive3(1,is2)
    def fa(i,_):
        fill3(x3a,pl.multiple_of(i+32,32),act_of(img[pl.ds(i,64)].astype(f32)))
        return 0
    cloop(PX,64,fa,0)
    c_img.wait()
    fill_edges(x3a,act_of(himg[...].astype(f32)))
    own.wait()
    xy_arrive(z==3,3,0)
    xy_arrive(z==3,3,1)
    arrive0(0)
    xy_arrive(is2,2,0)
    three_out(1); three_out(2)
    arrive0(1)
    diag_in(top,3)
    three_out(0)
    xy_arrive(is2,2,1)
    arrive3(0,is1)
    arrive3(1,is1)
    later_sends()
    two_send(is2,3,-1)
    two_send(is2,1,-1); two_send(is2,2,-1)
    xy_arrive(None,0,0)
    one_in(0,is2)
    one_in(1,is2)
    xy_arrive(None,0,1)
    for h in range(2): xy_send(is1,3,h)
    for h in range(2): xy_send(is2,1,h)
    for h in range(2): one_in(h,top)
    for h in range(2): xy_send(top,1,h)
    for i in (3,1,2): two_send(is2,i,1)
    two_diag()
    two_send(is2,0,-1); two_send(is2,0,1)
    d_arrive(0)
    arrive3(0,z==0)
    xy_send(z==0,3,0)
    sib_arrive(0)
    take(range(0,8))
    conv_to(inner,x3a,R_ONE)
    def st2(i,c):
        v=inner[pl.ds(i,64)]
        return c[0]+col8(v),c[1]+col8(v*v)
    a1,a2=cloop(PX,64,st2,(Z8(),Z8()))
    c1=swap_sums(1,row(a1),row(a2))
    c2=xchg(inner.at[edge],hrecv.at[0])
    two_in(3,is1)
    xy_arrive(z>=2,1,0)
    arrive3(1,z==0)
    xy_send(z==0,3,1)
    xy_arrive(z<2,3,0)
    xy_arrive(z<2,3,1)
    for h in range(2): one_in(h,z==0)
    for h in range(2): xy_send(z<2,1,h)
    three_in(1); three_in(2)
    xy_arrive(z>=2,1,1)
    three_in(0)
    diag_in(z<2,3)
    for yy in range(2):
        for pp in range(2):
            for k in load(slot(3,yy,pp)): k.start()
    sib_arrive(3)
    two_in(1,is1)
    take(range(24,32))
    ids=rowid[...]
    here=lax.broadcasted_iota(jnp.int32,(LEVELS,TEMB),0)==level[...]
    time_row=jnp.sum(jnp.where(here,tvec[...],0.0),0,keepdims=True)
    pre=[]
    tcol=lax.broadcasted_iota(jnp.int32,(16,R_END-R_TAB),1)
    for h in range(2):
        hot=(tcol==2*ids+h).astype(f32).astype(bf)
        pre.append(nn(hot,wv[R_TAB:R_END])[0:1]+time_row[:,CH*h:CH*h+CH])
    emb=[silu(v) for v in pre]
    put3(cvt3,pl.ds(0,1536),wv[R_EMB:R_TAB].astype(f32))
    wee[...]=ld(cvt3,every(0,768,2)).astype(bf)
    weo[...]=ld(cvt3,every(1,768,2)).astype(bf)
    def emb_dot(w):
        r=None
        for h in range(2):
            e=jnp.broadcast_to(emb[h],(16,CH))
            d=exact(e,w[CH*h:CH*h+CH],nn)[0:1]
            r=d if r is None else r+d
        return r
    sc1=1.0+emb_dot(wee); sh=emb_dot(weo)
    c1.wait()
    xy_arrive(z<2,1,0)
    mean2,inv2=norm_of(total_sums(1))
    def pre_b(v):
        n=(v-mean2)*inv2
        af=n*g2+b2
        return n,af,af*sc1+sh
    def fb(i,_):
        fill3(x3b,pl.multiple_of(i+32,32),silu(pre_b(inner[pl.ds(i,64)])[2]))
        return 0
    cloop(PX,64,fb,0)
    c2.wait()
    fill_edges(x3b,silu(pre_b(hrecv[0])[2]))
    xy_arrive(z<2,1,1)
    two_in(2,is1)
    d_arrive(1)
    sib_arrive(1)
    two_in(0,is1)
    take(range(8,16))
    conv_to(middle,x3b,R_TWO,lambda: img[...].astype(f32))
    def st3(i,c):
        v=middle[pl.ds(i,64)]
        return c[0]+col8(v),c[1]+col8(v*v)
    a1,a2=cloop(PX,64,st3,(Z8(),Z8()))
    c1=swap_sums(2,row(a1),row(a2))
    put3(cvt3,pl.ds(0,1152),wv[R_QKV:R_PROJ].astype(f32))
    for j in range(3):
        wqT[CH*j:CH*j+CH]=ld(cvt3,every(j,CH,3)).T.astype(bf)
    c1.wait()
    mean3,inv3=norm_of(total_sums(2))
    def fc(i,_):
        n=(middle[pl.ds(i,64)]-mean3)*inv3
        ain[pl.ds(i,64)]=(n*g3+b3).astype(bf)
        return 0
    cloop(PX,64,fc,0)
    c_in=xchg(ain.at[pl.ds(0,PX)],ain.at[pl.ds(PX,PX)])
    c_mid=xchg(middle.at[edge],hmid)
    def triples(a):
        t=nt(wqT[...],a)
        is_q=lax.rem(lax.broadcasted_iota(jnp.int32,t.shape,0),192)<64
        return jnp.where(is_q,t*0.125,t).astype(bf)
    trT[:,0:PX]=triples(ain[0:PX])
    def head_rows(h):
        r0=pl.multiple_of(h*192,64)
        return r0,pl.multiple_of(r0+64,64),pl.multiple_of(r0+128,64)
    def fh1(h,_):
        r0,r1,r2=head_rows(h)
        sco=nn(trT[pl.ds(r1,64),0:PX].T,trT[pl.ds(r0,64),0:PX])
        m=jnp.max(sco,0,keepdims=True)
        e=jnp.exp(sco-m)
        lse[h,0:1]=m
        lse[h,1:2]=jnp.sum(e,0,keepdims=True)
        acc[h]=nn(trT[pl.ds(r2,64),0:PX],e.astype(bf))
        return 0
    lax.fori_loop(0,6,fh1,0)
    for i in (3,1,2): two_in(i,ends)
    c_in.wait()
    trT[:,PX:2*PX]=triples(ain[PX:2*PX])
    def fh(h,_):
        r0,r1,r2=head_rows(h)
        sco=nn(trT[pl.ds(r1,64),PX:2*PX].T,trT[pl.ds(r0,64),0:PX])
        m0=lse[h,0:1]
        m=jnp.maximum(m0,jnp.max(sco,0,keepdims=True))
        e=jnp.exp(sco-m)
        a=jnp.exp(m0-m)
        l=lse[h,1:2]*a+jnp.sum(e,0,keepdims=True)
        o=acc[h]*a+nn(trT[pl.ds(r2,64),PX:2*PX],e.astype(bf))
        attT[pl.ds(pl.multiple_of(h*64,64),64),:]=(o*(1.0/l)).astype(bf)
        lse[h,0:1]=m+jnp.log(l)
        return 0
    lax.fori_loop(0,6,fh,0)
    put3(gout,pl.ds(0,PX),middle[...]+tn(attT[...],wv[R_PROJ:R_DOWN]))
    hsend[0]=ld(gout,edge).astype(bf)
    c1=xchg(hsend.at[0],oth.at[0])
    two_in(0,ends)
    for yy in range(2):
        for pp in range(2):
            for k in load(slot(2,yy,pp)): k.start()
    sib_arrive(2)
    take(range(16,24))
    for off in range(9):
        put3(cvt3,pl.ds(0,576),wv[R_DOWN+576*off:R_DOWN+576*off+576].astype(f32))
        v0,v1,v2=[ld(cvt3,every(i,192,3)) for i in range(3)]
        put3(cvt2,every(0,192,2),jnp.concatenate([v0,v1[:,0:256]],1))
        w=jnp.concatenate([v1[:,128:384],v2],1)
        w=pltpu.roll(w,w.shape[1]-64,1)
        put3(cvt2,every(1,192,2),w)
        wd[CH*off:CH*off+CH]=ld(cvt2,pl.ds(0,CH))[:,0:576].astype(bf)
    def parts(ref,n):
        e=ld(ref,every(0,n//2,2)); o=ld(ref,every(1,n//2,2))
        col=lax.broadcasted_iota(jnp.int32,o.shape,0)&15
        return jnp.where(col==0,0.0,pltpu.roll(o,1,0)).astype(bf),e.astype(bf),o.astype(bf)
    for dc,v in enumerate(parts(gout,PX)):
        v=v.reshape(8,32,CH)
        even=v[:,0:16].reshape(128,CH); odd=v[:,16:32].reshape(128,CH)
        xd[:,CH*(3+dc):CH*(3+dc)+CH]=even
        xd[:,CH*(6+dc):CH*(6+dc)+CH]=odd
        xd[16:128,CH*dc:CH*dc+CH]=odd[0:112]
    c1.wait()
    put3(geo,pl.ds(0,32),oth[0].astype(f32)*pf)
    for dc,v in enumerate(parts(geo,32)):
        xd[0:16,CH*dc:CH*dc+CH]=v
    fin=nn(xd[...],wd[0:9*CH])
    feat=nn(fin.astype(bf),vgg[...]); tf=nn(tgt[...],vgg[...])
    ir=lax.rsqrt(jnp.mean(feat*feat,-1,keepdims=True)+EPS_FEAT)
    unit=feat*ir
    diff=unit-tf*lax.rsqrt(jnp.mean(tf*tf,-1,keepdims=True)+EPS_FEAT)
    wl=lin[...]*diff
    consist=jnp.sum(row(wl*diff),1,keepdims=True)*(1.0/(256*256))
    du=wl*(2.0/(256*256*images_all))
    dfeat=(ir*(du-unit*jnp.mean(du*unit,-1,keepdims=True))).astype(bf)
    zc=jnp.zeros((16,128),f32)
    for t_ in range(0,32,2): zc=zc+tails[t_,16:32,0:128].astype(f32)
    zc=zc[12:13,0:1]
    seed=(level[...]==0).astype(f32)/jnp.maximum(zc,1.0)*(2.0/(256*CH2))
    gfin=nt(dfeat,vgg[...])+seed*(fin-cln[...].astype(f32))
    dz=gfin.astype(bf)
    dzs[...]=dz[0:16]
    c1=xchg(dzs,dzr)
    for off in range(9):
        dw=tn(xd[:,CH*off:CH*off+CH],dz)
        put3(cvt2,pl.ds(0,CH),jnp.concatenate([dw,jnp.zeros((CH,64),f32)],1))
        e=ld(cvt2,every(0,192,2)); o_=pltpu.roll(ld(cvt2,every(1,192,2)),64,1)
        lane=lax.broadcasted_iota(jnp.int32,(192,128),1)
        put3(cvt3,every(0,192,3),e[:,0:384])
        put3(cvt3,every(1,192,3),jnp.concatenate([e[:,384:512],jnp.where(lane<64,e[:,512:640],o_[:,0:128]),o_[:,128:256]],1))
        put3(cvt3,every(2,192,3),o_[:,256:640])
        wv[R_DOWN+576*off:R_DOWN+576*off+576]=ld(cvt3,pl.ds(0,576)).astype(bf)
    sibsend(2); sibsend(3)
    c1.wait()
    z32=dz.astype(f32)
    down=jnp.concatenate([z32[16:128],dzr[...].astype(f32)*qf],0)
    def left(v):
        col=lax.broadcasted_iota(jnp.int32,v.shape,0)&15
        return jnp.where(col==15,0.0,pltpu.roll(v,127,0)).astype(bf)
    s00,s01,s10,s11=dz,left(z32),down.astype(bf),left(down)
    W=lambda a,c: wd[CH*(3*a+c):CH*(3*a+c)+CH]
    def put(a,c,v):
        for i in range(8):
            put3(gout,every((2*i+a)*32+c,16,2),v[16*i:16*i+16])
    put(0,0,nt(s00,W(1,1)))
    put(0,1,nt(s00,W(1,2))+nt(s01,W(1,0)))
    put(1,0,nt(s00,W(2,1))+nt(s10,W(0,1)))
    put(1,1,nt(s00,W(2,2))+nt(s01,W(2,0))+nt(s10,W(0,2))+nt(s11,W(0,0)))
    diag(2); diag(3); ysend(2); ysend(3)
    gp=ld(gout,pl.ds(0,PX)).astype(bf)
    dattT[...]=nt(wv[R_PROJ:R_DOWN],gp).astype(bf)
    wv[R_PROJ:R_DOWN]=nn(attT[...],gp).astype(bf)
    def bh_part(h,at,n):
        r0,r1,r2=head_rows(h)
        ra_=pl.ds(pl.multiple_of(h*64,64),64)
        qT=trT[pl.ds(r0,64),0:PX]
        kT=trT[pl.ds(r1,64),at:at+n]
        gT=dattT[ra_,:]
        pr=jnp.exp(nn(kT.T,qT)-lse[h,0:1])
        de=jnp.sum(gT.astype(f32)*attT[ra_,:].astype(f32),0,keepdims=True)
        ds=(pr*(nn(trT[pl.ds(r2,64),at:at+n].T,gT)-de)).astype(bf)
        dtrT[pl.ds(r1,64),at:at+n]=nt(qT,ds).astype(bf)
        dtrT[pl.ds(r2,64),at:at+n]=nt(gT,pr.astype(bf)).astype(bf)
        return r0,nn(kT,ds)*0.125
    def bh(at,first):
        def f(h,_):
            r0,dqT=bh_part(h,at,256)
            if first:
                acc[h]=dqT
                dtrT[pl.ds(r0,64),PX:2*PX]=jnp.zeros((64,PX),bf)
            else: acc[h]+=dqT
            return 0
        return f
    c_g=[]
    for i in range(2):
        at=PX+256*i
        lax.fori_loop(0,6,bh(at,i==0),0)
        oth[1+8*i:9+8*i]=tn(dtrT[:,at:at+256],wqT[...]).astype(bf).reshape(8,32,CH)
        c_g.append(xchg(oth.at[pl.ds(1+8*i,8)],oth.at[pl.ds(17+8*i,8)]))
    def bh2(h,_):
        r0,dqT=bh_part(h,0,PX)
        dtrT[pl.ds(r0,64),0:PX]=(acc[h]+dqT).astype(bf)
        return 0
    lax.fori_loop(0,6,bh2,0)
    gsec[...]=tn(dtrT[:,0:PX],wqT[...])
    for c in c_g: c.wait()
    def n3_of(i): return (middle[pl.ds(i,64)]-mean3)*inv3
    def s3(i,c):
        j=pl.multiple_of(17+lax.div(i,32),1)
        v=gsec[pl.ds(i,64)]+oth[pl.ds(j,2)].reshape(64,CH).astype(f32)
        gsec[pl.ds(i,64)]=v
        return c[0]+col8(v),c[1]+col8(v*n3_of(i))
    a1,a2=cloop(PX,64,s3,(Z8(),Z8()))
    db3,dg3=row(a1),row(a2)
    c1=swap_sums(3,db3*g3,dg3*g3)
    esend[0]=ld(gout,edge)+inv3*(gsec[edge]*g3)
    c2=xchg(esend.at[0],erecv.at[0])
    xsend(2)
    dq=nt(ain[...].T,dtrT[...])
    for j in range(3):
        put3(cvt3,every(j,CH,3),dq[:,CH*j:CH*j+CH])
    wv[R_QKV:R_PROJ]=ld(cvt3,pl.ds(0,1152)).astype(bf)
    c1.wait()
    m1,m2=total_sums(3)
    def f3(i,_):
        v=ld(gout,pl.ds(i,64))+inv3*(gsec[pl.ds(i,64)]*g3-m1-n3_of(i)*m2)
        fill3(z3,pl.multiple_of(i+32,32),v)
        return 0
    cloop(PX,64,f3,0)
    c_mid.wait()
    c2.wait()
    fill_edges(z3,erecv[0]-inv3*(m1+(hmid[...]-mean3)*inv3*m2))
    conv_dx(gsec,R_TWO)
    for dr in range(3):
        d=tn(x3b[32*dr:32*dr+PX],z3[32:32+PX,CH:2*CH]).astype(bf)
        wv[R_TWO+1152*dr:R_TWO+1152*dr+1152]=d
        if dr==0: wd[R_TWO:4304,0:CH]=d[0:4304-R_TWO]
    sibsend(1)
    def s2(i,c):
        n,af,pb=pre_b(inner[pl.ds(i,64)])
        gpre=gsec[pl.ds(i,64)]*slope(pb)
        gaff=gpre*sc1
        gsec[pl.ds(i,64)]=gaff
        return c[0]+col8(gpre*af),c[1]+col8(gpre),c[2]+col8(gaff*n),c[3]+col8(gaff)
    a1,a2,a3,a4=cloop(PX,64,s2,(Z8(),Z8(),Z8(),Z8()))
    dsc,dsh,dg2,db2=row(a1),row(a2),row(a3),row(a4)
    c1=swap_sums(4,db2*g2,dg2*g2)
    esend[1]=gsec[edge]*g2
    c2=xchg(esend.at[1],erecv.at[1])
    diag(1)
    first_halves(1)
    c1.wait()
    m1,m2=total_sums(4)
    def f2(i,_):
        n=(inner[pl.ds(i,64)]-mean2)*inv2
        fill3(z3,pl.multiple_of(i+32,32),inv2*(gsec[pl.ds(i,64)]*g2-m1-n*m2))
        return 0
    cloop(PX,64,f2,0)
    c2.wait()
    fill_edges(z3,inv2*(erecv[1]-m1-(hrecv[0]-mean2)*inv2*m2))
    for dr in range(3):
        wd[1152*dr:1152*dr+1152,0:CH]=tn(x3a[32*dr:32*dr+PX],z3[32:32+PX,CH:2*CH]).astype(bf)
    sibsend(0)
    second_halves(1)
    xsend(3,z<2)
    zstep(2,0)
    diag(0)
    first_halves(0)
    conv_dx(gsec,R_ONE)
    def s1(i,c):
        n=(img[pl.ds(i,64)].astype(f32)-mean1)*inv1
        gpre=gsec[pl.ds(i,64)]*slope(n*g1+b1)
        return c[0]+col8(gpre*n),c[1]+col8(gpre)
    a1,a2=cloop(PX,64,s1,(Z8(),Z8()))
    ge=[]
    for h in range(2):
        d=exact(jnp.broadcast_to(dsc,(16,CH)),wee[CH*h:CH*h+CH],nt)+exact(jnp.broadcast_to(dsh,(16,CH)),weo[CH*h:CH*h+CH],nt)
        ge.append(d[0:1]*slope(pre[h]))
    hot_level=(lax.broadcasted_iota(jnp.int32,(1,CH),1)==level[...]).astype(f32)
    pack_ref[...]=jnp.concatenate([row(a1),row(a2),dg2,db2,dg3,db3,dsc,dsh,ge[0],ge[1],emb[0],emb[1],consist*hot_level,jnp.broadcast_to(ids.astype(f32),(1,CH)),0.5*hot_level,jnp.zeros((1,CH),f32)],0)
    low=jnp.logical_not(top)
    cm.go(low,pack_ref,lpk.at[z],lps,lpr,b+4*(3-z),p)
    put_x(0,HA,0)
    zstep(1,0)
    zstep(3,0)
    second_halves(0)
    xsend(3,z>=2)
    zstep(2,1)
    zstep(1,1)
    zstep(0,0)
    zstep(3,1)
    zstep(0,1)
    zstep(3,2)
    def packs_line():
        lpk[3]=pack_ref[...]
        wait_in(lpk.at[pl.ds(0,3)],lpr)
    pl.when(top)(packs_line)
    for d,bb,pp in plane:
        cm.go(top,lpk,ppk.at[mine],pps,ppr,bb,pp)
    def packs_plane():
        ppk[mine]=lpk[...]
        wait_in(ppk.at[pl.ds(0,7)],ppr)
        a_s=16*lax.div(ROWS*s,16)
        rows_at=lambda k: ppk[:,:,k,:].reshape(32,384)
        zero=jnp.zeros((64,384),f32)
        for h in range(2):
            e=rows_at(10+h)
            t=jnp.concatenate([e,e,zero],0).T
            cvt[pl.ds(BLK+768*h,384,stride=2),:]=t
            cvt[pl.ds(BLK+768*h+1,384,stride=2),:]=t
        r=a_s+lax.broadcasted_iota(jnp.int32,(BLK,128),0)
        l=lax.broadcasted_iota(jnp.int32,(BLK,128),1)
        inside=(r>=R_EMB)&(r<R_TAB)
        start=pl.multiple_of(jnp.clip(a_s-R_EMB+BLK,0,BLK+1536),16)
        lf=jnp.where(inside&(((r&1)==1)==(l>=32))&(l<64),cvt[pl.ds(start,BLK),:],0.0)
        ids=rows_at(13)[:,0:128].astype(jnp.int32)
        ids=jnp.concatenate([ids]*4,0).astype(f32).T[0:1].astype(jnp.int32)
        hot=(r-R_TAB==2*ids+(l>=96).astype(jnp.int32))&(l>=64)&(r>=R_TAB)
        lf=jnp.where(hot,1.0,lf)
        rg=jnp.concatenate([rows_at(6),rows_at(7),rows_at(8),rows_at(9)],0)
        gains=[jnp.sum(rows_at(k),0,keepdims=True) for k in range(6)]
        hi=lax.Precision.HIGHEST
        add=lax.dot_general(lf,rg,(((1,),(0,)),((),())),precision=hi,preferred_element_type=f32)
        for k in range(6): add=add+jnp.where(r[:,0:1]-R_GAIN==k,gains[k],0.0)
        rr=a_s+lax.broadcasted_iota(jnp.int32,(BLK,384),0)
        total[...]=jnp.where(rr<R_EMB,0.0,add)
    pl.when(top)(packs_plane)
    zstep(0,2)
    zend(1); zend(2); zend(3)
    zend(0)
    shift=lax.rem(9*s,16)
    tr_=lax.broadcasted_iota(jnp.int32,(BLK,1),0)
    t=jnp.where((tr_>=shift)&(tr_<shift+ROWS),total[...],0.0)
    sq=jnp.sum(jnp.sum(t*t,0,keepdims=True),1,keepdims=True)
    tile[...]=jnp.concatenate([jnp.broadcast_to(sq,(1,128)),pack_ref[12:13,0:128],pack_ref[14:15,0:128],jnp.zeros((5,128),f32)],0)
    red1[mine]=tile[...]
    for d,bb,pp in plane: cm.go(None,tile,red1.at[mine],n1s,n1r,bb,pp)
    t=pltpu.roll(total[...],lax.rem(BLK-shift,BLK),0)[0:ROWS]
    for j in range(3): cvt[pl.ds(j,ROWS,stride=3),:]=t[:,128*j:128*j+128]
    fcopy=pltpu.make_async_copy(cvt.at[pl.ds(0,1611)],flat_ref,own_sem)
    fcopy.start()
    wait_in(red1.at[pl.ds(0,7)],n1r)
    v=red1[0]
    for k in range(1,8): v=v+red1[k]
    red2[z]=v
    for k,zz in line: cm.go(None,red2.at[z],red2.at[z],n2s,n2r,b+4*(zz-z),p)
    wait_in(red2.at[pl.ds(0,3)],n2r)
    sums=red2[0]+red2[1]+red2[2]+red2[3]
    norm_ref[...]=jnp.sqrt(sums[0:1,0:1])
    lev_ref[...]=sums[1:3,0:LEVELS]
    def sent(ok,ref,sem):
        when(ok,lambda: pltpu.make_async_copy(ref,ref,sem).wait())
    block=sibr.at[0]
    for zz in range(4):
        went=(None,None,is2,z!=2)[zz]
        for sem in (axs,ays,ads): sent(went,block,sem.at[zz])
        sent(None,sibr.at[pl.ds(0,4)],ass.at[zz])
        if zz<3:
            sent(None,sibr.at[pl.ds(0,4)],s1s.at[zz])
        else:
            sent(core==1,sibr.at[pl.ds(0,2)],s1s.at[zz])
        sent(need(zz,1-y,xn),block,ds_.at[zz])
        sent(need(zz,y,xn),block,rxs.at[zz])
        sent(need(zz,1-y,p),block,rys.at[zz])
        sent(AND(need(zz,y,p),z!=zz),block,zs.at[zz])
    sent(z<3,block,azs.at[0,0])
    sent(z>0,block,azs.at[3,1])
    sent(is1|is2,block,azs.at[1,0])
    sent(is1,block,azs.at[1,1])
    sent(is2,sibr.at[pl.ds(0,4)],a2s.at[0])
    sent(is1|is2,sibr.at[pl.ds(0,4)],a2s.at[1])
    sent(top,sibr.at[pl.ds(0,3)],a3s)
    sent(has_gains,blk.at[pl.ds(0,48)],gls)
    sent(gain_line,blk.at[pl.ds(0,112)],gps)
    sent(low,pack_ref,lps)
    sent(top,ppk.at[pl.ds(0,7)],pps)
    sent(None,red1.at[pl.ds(0,7)],n1s)
    sent(None,red2.at[pl.ds(0,3)],n2s)
    fcopy.wait()

def step(images_all,mast,img,tgt,cln,vgg,lin,tvec,rowid,level):
    D=pltpu.SemaphoreType.DMA
    V=lambda *s: pltpu.VMEM(s,bf)
    F=lambda *s: pltpu.VMEM(s,f32)
    vm=pl.BlockSpec(memory_space=pltpu.VMEM)
    return pl.pallas_call(functools.partial(step_kernel,images_all),
        out_shape=(jax.ShapeDtypeStruct((1611,128),f32),jax.ShapeDtypeStruct((1,1),f32),jax.ShapeDtypeStruct((2,LEVELS),f32),jax.ShapeDtypeStruct((32,BLK,CH),bf)),
        in_specs=[pl.BlockSpec(memory_space=pl.ANY)]+[vm]*8,
        out_specs=(pl.BlockSpec(memory_space=pl.ANY),vm,vm,pl.BlockSpec(memory_space=pl.ANY)),
        scratch_shapes=[V(17184,CH),V(32,32,CH),F(4608,128),F(5,CH,128),V(4304,CH2),V(768,CH),V(768,CH),V(1152,CH),V(576,1152),V(576,1152),V(576,1152),F(PX,CH),F(PX,CH),F(3,PX,128),F(PX,CH),V(1024,CH),V(1152,1024),V(1152,1024),V(CH,PX),V(128,3456),F(6,8,PX),V(CH,PX),F(5,8,CH),F(5,8,CH),V(1,32,CH),F(1,32,CH),V(32,CH),V(16,CH2),V(16,CH2),F(3,32,128),V(33,32,CH),D((4,)),D((4,)),D((15,)),D((15,)),F(BLK,CH),V(BLK,CH),D,D((4,2)),D((4,2)),D((4,)),D((4,2)),D((4,)),D((4,2)),D((4,)),D((4,)),D((4,)),D((4,)),F(16,CH),F(4,16,CH),F(8,4,16,CH),F(8,8,128),F(4,8,128),F(8,128),D,D,D,D,D,D,D,D,V(14,BLK,CH),V(4,BLK-HALF,CH),V(4,BLK,CH),V(4,BLK,CH),V(3,BLK,CH),V(3,BLK,CH),D((4,)),D((4,2,2)),D((4,)),D((4,)),D((4,)),D((4,2)),D((4,)),D((4,2)),D((4,)),D((6,)),D((12,)),F(6,64,PX),V(16,CH),D,D,D,D,V(4,HALF,CH),D((2,)),D((2,2,2)),D((4,)),D((4,)),F(32,CH),F(2,32,CH),F(2,32,CH),V(CH,CH),D,D((2,2,2))],
        compiler_params=pltpu.CompilerParams(collective_id=0,has_side_effects=True,vmem_limit_bytes=63<<20),
        name="train_step",
    )(mast,img,tgt,cln,vgg,lin,tvec,rowid,level)


def time_rows():
    half = np.arange(TEMB // 2, dtype=np.float32)
    frequency = np.exp(np.float32(-math.log(10000.0)) * half / np.float32(TEMB // 2))
    angles = np.arange(LEVELS, dtype=np.float32)[:, None] * np.float32(1000.0 / LEVELS) * frequency
    return np.concatenate([np.cos(angles), np.sin(angles)], -1).astype(np.float32)


def fast(images, target, clean_images, levels, labels, null_mask, vgg_proj, lpips_lin, master, first_moment, second_moment):
    row_index = jnp.where(null_mask == 1, CLASSES, labels).reshape(1, 1)
    tvec = jnp.asarray(time_rows())
    own_grad, norm, level_sums, _ = step(
        16,
        master.reshape(1611, 128),
        images.reshape(PX, CH),
        target.reshape(128, CH2),
        clean_images.reshape(128, CH2),
        vgg_proj,
        lpips_lin.reshape(1, 256),
        tvec,
        row_index,
        levels.reshape(1, 1),
    )
    own_grad = own_grad.reshape(-1)
    norm_before = norm.reshape(())
    clipped = own_grad * jnp.minimum(1.0, CLIP / norm_before)
    new_first = BETA_ONE * first_moment + (1.0 - BETA_ONE) * clipped
    new_second = BETA_TWO * second_moment + (1.0 - BETA_TWO) * clipped * clipped
    fixed_first = new_first / (1.0 - BETA_ONE**STEP)
    fixed_second = new_second / (1.0 - BETA_TWO**STEP)
    new_master = master - RATE * (fixed_first / (jnp.sqrt(fixed_second) + EPS_ADAM) + DECAY * master)
    return (new_master, new_first, new_second, new_master.astype(jnp.bfloat16), norm_before, level_sums)


def solution(mesh):
    small = mesh.shape["batch"] == 16 and mesh.shape["pix"] == 2
    return jax.shard_map(
        fast if small else local,
        mesh=mesh,
        in_specs=(
            P("batch", "pix", None, None),
            P("batch", "pix", None, None),
            P("batch", "pix", None, None),
            P("batch"),
            P("batch"),
            P("batch"),
            P(),
            P(),
            P(("batch", "pix")),
            P(("batch", "pix")),
            P(("batch", "pix")),
        ),
        out_specs=(
            P(("batch", "pix")),
            P(("batch", "pix")),
            P(("batch", "pix")),
            P(("batch", "pix")),
            P(),
            P(),
        ),
        check_vma=False,
    )
```
